32 devices in a mesh: grp: 2 (over x), fsdp: 16 (over z, y, core).
Axes of the slice: x: 2, y: 2, z: 4, core: 2. Of those that a mesh axis runs over, the one named last changes fastest.
Arguments:
- tokens: bfloat16 [64, 64, 1280], P('grp', 'fsdp'), may hold values from -6 to 6
- cotangent: bfloat16 [64, 64, 1280], P('grp', 'fsdp'), may hold values from -6 to 6
- lengths: int32 [2, 32], P('grp'), may hold values from 32 to 64, as said below
- placement: int32 [2, 32], P('grp'), may hold values from 0 to 31, each once within a row
- query_weight: bfloat16 [1280, 1280], P('fsdp'), may hold values from -0.15625 to 0.15625
- key_weight: bfloat16 [1280, 1280], P('fsdp'), may hold values from -0.15625 to 0.15625
- value_weight: bfloat16 [1280, 1280], P('fsdp'), may hold values from -0.15625 to 0.15625
- out_weight: bfloat16 [1280, 1280], P('fsdp'), may hold values from -0.15625 to 0.15625
- up_weight: bfloat16 [1280, 5120], P('fsdp'), may hold values from -0.15625 to 0.15625
- gate_weight: bfloat16 [1280, 5120], P('fsdp'), may hold values from -0.15625 to 0.15625
- down_weight: bfloat16 [5120, 1280], P('fsdp'), may hold values from -0.078125 to 0.078125
- scoring: bfloat16 [1280], P('fsdp'), may hold values from 0.69921875 to 1.5
- upscale: bfloat16 [5120], P('fsdp'), may hold values from 0.5 to 1.5
- gatescale: bfloat16 [5120], P('fsdp'), may hold values from 0.5 to 1.5
- attention_rate: bfloat16 [1280], P('fsdp'), may hold values from 0.099609375 to 0.5
- feedforward_rate: bfloat16 [1280], P('fsdp'), may hold values from 0.099609375 to 0.5
Outputs:
- layer_out: bfloat16 [64, 64, 1280], P('grp', 'fsdp')
- input_grad: bfloat16 [64, 64, 1280], P('grp', 'fsdp')
- query_grad: float32 [1280, 1280], P('fsdp', 'grp')
- key_grad: float32 [1280, 1280], P('fsdp', 'grp')
- value_grad: float32 [1280, 1280], P('fsdp', 'grp')
- out_grad: float32 [1280, 1280], P('fsdp', 'grp')
- up_grad: float32 [1280, 5120], P('fsdp', 'grp')
- gate_grad: float32 [1280, 5120], P('fsdp', 'grp')
- down_grad: float32 [5120, 1280], P('fsdp', 'grp')
- scoring_grad: float32 [1280], P('fsdp')
- upscale_grad: float32 [5120], P('fsdp')
- gatescale_grad: float32 [5120], P('fsdp')
- attention_grad: float32 [1280], P('fsdp')
- feedforward_grad: float32 [1280], P('fsdp')
The draws below stay inside these ranges and needn't reach their ends.
Inputs may be any that keep to these rules, and one draw needn't show every extreme that they name: lengths[g, t] is the length of the sequence in slot t of group g; in each group some slot holds the full 64. Each row of placement is a permutation of the group's 32 slots.
All inputs are finite; a program needn't handle non-finite values.
Results may differ from the reference program's by a relative error of at most 0.015.
Values may be sent and summed in bfloat16 or wider, within the bound.
No kernel may reach another device: no remote copies, remote signals or barrier semaphores. Data moves between devices by JAX's collectives and lax.ppermute only.
A program may use at most 256 MiB of HBM per device.

```python
import math
import jax
import jax.numpy as jnp
from jax import lax

D = 1280
H = 20
DK = 64
FF = 5120
SLOT = 64
GSEQ = 32
SEQS = 64
N_GRP = 2


def draw_lengths(key, part):
    key = jax.random.fold_in(key, 7)
    first_key, second_key = jax.random.split(key)
    group_count = SEQS // GSEQ
    drawn_lengths = jax.random.randint(first_key, (group_count, GSEQ), SLOT // 2, SLOT + 1, dtype=jnp.int32)
    chosen = jax.random.randint(second_key, (group_count, 1), 0, GSEQ, dtype=jnp.int32)
    columns = jnp.arange(GSEQ, dtype=jnp.int32)[None, :]
    return jnp.where(columns == chosen, SLOT, drawn_lengths).astype(jnp.int32)


def steps_of(key, extent, pieces, smallest, high):
    level = 1.0
    for dim, blocks in pieces:
        heights = jax.random.uniform(jax.random.fold_in(jax.random.fold_in(key, 6), dim), (blocks,), jnp.float32, smallest / len(pieces), high / len(pieces))
        level = level * jnp.repeat(jnp.exp(heights), extent[dim] // blocks).reshape((-1,) + (1,) * (len(extent) - 1 - dim))
    return level


def scatter_about(key, extent, deviation, limit, cuts=(), held_as=jnp.bfloat16):
    values = deviation * jax.random.normal(key, extent, jnp.float32)
    if cuts:
        values = values * steps_of(key, extent, cuts, -0.22, 0.18)
    return jnp.clip(values, -limit, limit).astype(held_as)


def setup_inputs(seed: int = 0) -> dict:
    key_list = jax.random.split(jax.random.key(seed), 17)
    return {
        "tokens": scatter_about(key_list[0], (SEQS, SLOT, D), 1.0, 6.0, ((0, 2), (1, 16))),
        "cotangent": scatter_about(key_list[1], (SEQS, SLOT, D), 1.0, 6.0, ((0, 2), (1, 16))),
        "lengths": draw_lengths(jax.random.fold_in(key_list[16], 71), 0),
        "placement": jax.vmap(lambda own: jax.random.permutation(own, GSEQ))(jax.random.split(key_list[3], N_GRP)).reshape((N_GRP, GSEQ)).astype(jnp.int32),
        "query_weight": scatter_about(key_list[4], (D, D), D ** -0.5, 0.15625, ((0, 16),)),
        "key_weight": scatter_about(key_list[5], (D, D), D ** -0.5, 0.15625, ((0, 16),)),
        "value_weight": scatter_about(key_list[6], (D, D), D ** -0.5, 0.15625, ((0, 16),)),
        "out_weight": scatter_about(key_list[7], (D, D), D ** -0.5, 0.15625, ((0, 16),)),
        "up_weight": scatter_about(key_list[8], (D, FF), D ** -0.5, 0.15625, ((0, 16),)),
        "gate_weight": scatter_about(key_list[9], (D, FF), D ** -0.5, 0.15625, ((0, 16),)),
        "down_weight": scatter_about(key_list[10], (FF, D), FF ** -0.5, 0.078125, ((0, 16),)),
        "scoring": jnp.clip(0.69921875 + 0.80078125 * jax.random.uniform(key_list[11], (D,), jnp.float32) ** steps_of(key_list[11], (D,), ((0, 16),), -0.2, 0.2), 0.69921875, 1.5).astype(jnp.bfloat16),
        "upscale": jnp.clip(0.5 + 1.0 * jax.random.uniform(key_list[12], (FF,), jnp.float32) ** steps_of(key_list[12], (FF,), ((0, 16),), -0.2, 0.2), 0.5, 1.5).astype(jnp.bfloat16),
        "gatescale": jnp.clip(0.5 + 1.0 * jax.random.uniform(key_list[13], (FF,), jnp.float32) ** steps_of(key_list[13], (FF,), ((0, 16),), -0.2, 0.2), 0.5, 1.5).astype(jnp.bfloat16),
        "attention_rate": jnp.clip(0.099609375 + 0.40039062 * jax.random.uniform(key_list[14], (D,), jnp.float32) ** steps_of(key_list[14], (D,), ((0, 16),), -0.2, 0.2), 0.099609375, 0.5).astype(jnp.bfloat16),
        "feedforward_rate": jnp.clip(0.099609375 + 0.40039062 * jax.random.uniform(key_list[15], (D,), jnp.float32) ** steps_of(key_list[15], (D,), ((0, 16),), -0.2, 0.2), 0.099609375, 0.5).astype(jnp.bfloat16),
    }


highest = lax.Precision.HIGHEST

@jax.custom_vjp
def low(v):
    return lax.optimization_barrier(v.astype(jnp.bfloat16)).astype(jnp.float32)

@jax.custom_vjp
def low_back(v):
    return v

def low_keep(v):
    return (low(v), None)

def low_pass(kept, grad):
    return (grad,)

def back_keep(v):
    return (v, None)

def back_low(kept, grad):
    return (low(grad),)
low.defvjp(low_keep, low_pass)
low_back.defvjp(back_keep, back_low)

def rms_norm(vector):
    return vector * lax.rsqrt(lax.optimization_barrier(jnp.mean(vector * vector, axis=-1, keepdims=True)) + 1e-06)

def head_norm(vector, scaling):
    split_heads = vector.reshape(vector.shape[:-1] + (H, DK))
    unit_heads = split_heads * lax.rsqrt(lax.optimization_barrier(jnp.sum(split_heads * split_heads, axis=-1, keepdims=True)) + 1e-06)
    return unit_heads.reshape(vector.shape) * scaling

def project(left_side, right_side):
    return jnp.einsum('bsd,de->bse', left_side, right_side, precision=highest)

def forward(params, inputs, valid_rows):
    query_weight, key_weight, value_weight, out_weight, up_weight, gate_weight, down_weight, scoring, upscale, gatescale, attention_rate, feedforward_rate = params
    batch_size = inputs.shape[0]
    length = inputs.shape[1]
    queries = low_back(project(inputs, query_weight))
    key_rows = low_back(project(inputs, key_weight))
    values = low_back(low(project(inputs, value_weight)))
    query_unit = low(head_norm(queries, scoring)).reshape(batch_size, length, H, DK)
    key_unit = low(head_norm(key_rows, scoring)).reshape(batch_size, length, H, DK)
    scores = low_back(jnp.einsum('bqhd,bkhd->bhqk', query_unit, key_unit, precision=highest) * math.sqrt(DK))
    causal = jnp.arange(length)[:, None] >= jnp.arange(length)[None, :]
    scores = jnp.where(causal, scores, -1e+30)
    row_max = lax.optimization_barrier(jnp.max(scores, axis=-1, keepdims=True))
    exp_scores = jnp.exp(scores - row_max)
    softmax_weights = low(exp_scores / lax.optimization_barrier(jnp.sum(exp_scores, axis=-1, keepdims=True)))
    mixed_heads = jnp.einsum('bhqk,bkhd->bqhd', softmax_weights, values.reshape(batch_size, length, H, DK), precision=highest).reshape(batch_size, length, H * DK)
    mixed_heads = low_back(low(mixed_heads))
    attended = low_back(project(mixed_heads, out_weight))
    first_state = rms_norm(inputs + attention_rate * (rms_norm(attended) - inputs))
    first_low = low(first_state)
    up_proj = low_back(project(first_low, up_weight))
    gate_proj = low_back(project(first_low, gate_weight))
    scaled = gatescale * gate_proj
    hidden = low(scaled * jax.nn.sigmoid(scaled) * (upscale * up_proj))
    down_proj = low_back(project(hidden, down_weight))
    second = rms_norm(first_state + feedforward_rate * (rms_norm(down_proj) - first_state))
    return second * valid_rows

def reference(tokens, cotangent, lengths, placement, query_weight, key_weight, value_weight, out_weight, up_weight, gate_weight, down_weight, scoring, upscale, gatescale, attention_rate, feedforward_rate):
    params = tuple((member.astype(jnp.float32) for member in (query_weight, key_weight, value_weight, out_weight, up_weight, gate_weight, down_weight, scoring, upscale, gatescale, attention_rate, feedforward_rate)))
    seq_lengths = jnp.take_along_axis(lengths, placement, axis=1).reshape(SEQS)
    valid_rows = (jnp.arange(SLOT, dtype=jnp.int32)[None, :] < seq_lengths[:, None]).astype(jnp.float32)
    block_count = SEQS // 4
    inputs = tokens.astype(jnp.float32).reshape(block_count, 4, SLOT, D)
    cot_rows = cotangent.astype(jnp.float32).reshape(block_count, 4, SLOT, D)
    valid_blocks = valid_rows.reshape(block_count, 4, SLOT, 1)

    def scan_step(totals, seq_block):
        block_inputs, block_cot, block_valid = seq_block

        def layer_of(weights, rows):
            return forward(weights, rows, block_valid)
        outputs, pullback = jax.vjp(layer_of, params, block_inputs)
        weight_grads, row_grads = pullback(block_cot)
        return (jax.tree.map(jnp.add, totals, weight_grads), (outputs.astype(jnp.bfloat16), row_grads.astype(jnp.bfloat16)))
    zero_grads = jax.tree.map(jnp.zeros_like, params)
    totals, (layer_out, input_grad) = lax.scan(scan_step, zero_grads, (inputs, cot_rows, valid_blocks))
    return (layer_out.reshape(SEQS, SLOT, D), input_grad.reshape(SEQS, SLOT, D), totals[0], totals[1], totals[2], totals[3], totals[4], totals[5], totals[6], totals[7], totals[8], totals[9], totals[10], totals[11])
```

```python
import math

import jax
import jax.numpy as jnp
from jax import lax
from jax.experimental import pallas as pl
from jax.experimental.pallas import tpu as pltpu
from jax.sharding import PartitionSpec as P

H = 20
DK = 64
BF = jnp.bfloat16
F32 = jnp.float32


def rms_norm(vector):
    return vector * lax.rsqrt(jnp.mean(vector * vector, axis=-1, keepdims=True) + 1e-06)


def head_norm(vector, scaling):
    split_heads = vector.reshape(vector.shape[0], -1, DK)
    unit_heads = split_heads * lax.rsqrt(
        jnp.sum(split_heads * split_heads, axis=-1, keepdims=True) + 1e-06
    )
    return unit_heads.reshape(vector.shape) * scaling


def residual_mix(base_rows, branch_rows, blending):
    return rms_norm(base_rows + blending * (rms_norm(branch_rows) - base_rows))


def swiglu(up_proj, gate_proj, upscale, gatescale):
    scaled = gatescale * gate_proj
    return scaled * jax.nn.sigmoid(scaled) * (upscale * up_proj)


def matmul(left_side, right_side):
    return jnp.dot(left_side, right_side, preferred_element_type=F32)


def weight_grad(left_side, right_side):
    return lax.dot_general(
        left_side, right_side, (((0,), (0,)), ((), ())), preferred_element_type=F32
    )


def back_matmul(grad_rows, weight_rows):
    return lax.dot_general(
        grad_rows, weight_rows, (((1,), (1,)), ((), ())), preferred_element_type=F32
    )


def assemble(parts, places, cuts):
    wholes = []
    for low, high in cuts:
        whole = jnp.zeros((len(parts), parts[0].shape[0], high - low), parts[0].dtype)
        for i, part in enumerate(parts):
            whole = lax.dynamic_update_index_in_dim(whole, part[:, low:high], places[i], 0)
        wholes.append(whole.reshape(-1, high - low))
    return wholes


def attention_forward(queries, key_rows, value_low, scoring, seq_len):
    rows = queries.shape[0]
    count = rows // seq_len
    query_unit = head_norm(queries, scoring).astype(BF)
    key_unit = head_norm(key_rows, scoring).astype(BF)
    probs = attention_probs(query_unit, key_unit, seq_len)
    value_heads = value_low.reshape(count, seq_len, -1, DK)
    mixed = jnp.einsum(
        "bhqk,bkhd->bqhd", probs.astype(BF), value_heads, preferred_element_type=F32
    )
    return query_unit, key_unit, mixed.reshape(rows, -1).astype(BF)


def attention_probs(query_unit, key_unit, seq_len):
    count = query_unit.shape[0] // seq_len
    positions = jnp.arange(seq_len, dtype=jnp.int32)
    causal = positions[:, None] >= positions[None, :]
    scores = jnp.einsum(
        "bqhd,bkhd->bhqk",
        query_unit.reshape(count, seq_len, -1, DK),
        key_unit.reshape(count, seq_len, -1, DK),
        preferred_element_type=F32,
    ) * math.sqrt(DK)
    scores = jnp.where(causal, scores, -1e30)
    exp_scores = jnp.exp(scores - jnp.max(scores, axis=-1, keepdims=True))
    return exp_scores / jnp.sum(exp_scores, axis=-1, keepdims=True)


def attention_backward(grad_mixed, queries, key_rows, value_low, query_unit, key_unit, scoring, seq_len):
    rows = queries.shape[0]
    count = rows // seq_len
    probs = attention_probs(query_unit, key_unit, seq_len)
    grad_heads = grad_mixed.reshape(count, seq_len, -1, DK)
    value_heads = value_low.reshape(count, seq_len, -1, DK)
    grad_value = jnp.einsum(
        "bhqk,bqhd->bkhd", probs.astype(BF), grad_heads, preferred_element_type=F32
    ).reshape(rows, -1)
    grad_probs = jnp.einsum(
        "bqhd,bkhd->bhqk", grad_heads, value_heads, preferred_element_type=F32
    )
    grad_scores = (
        probs * (grad_probs - jnp.sum(grad_probs * probs, axis=-1, keepdims=True))
    ).astype(BF)
    grad_qunit = jnp.einsum(
        "bhqk,bkhd->bqhd",
        grad_scores,
        key_unit.reshape(count, seq_len, -1, DK),
        preferred_element_type=F32,
    ) * math.sqrt(DK)
    grad_kunit = jnp.einsum(
        "bhqk,bqhd->bkhd",
        grad_scores,
        query_unit.reshape(count, seq_len, -1, DK),
        preferred_element_type=F32,
    ) * math.sqrt(DK)
    _, pullback = jax.vjp(head_norm, queries, scoring)
    grad_query, scoring_query = pullback(grad_qunit.reshape(rows, -1))
    _, pullback = jax.vjp(head_norm, key_rows, scoring)
    grad_key, scoring_key = pullback(grad_kunit.reshape(rows, -1))
    return (
        grad_query.astype(BF),
        grad_key.astype(BF),
        grad_value.astype(BF),
        scoring_query + scoring_key,
    )


def per_device(
    tokens,
    cotangent,
    lengths,
    placement,
    query_weight,
    key_weight,
    value_weight,
    out_weight,
    up_weight,
    gate_weight,
    down_weight,
    scoring,
    upscale,
    gatescale,
    attention_rate,
    feedforward_rate,
):
    size = lax.axis_size("fsdp")
    planes = size // 4
    half = lax.axis_index("grp")
    me = lax.axis_index("fsdp")
    core = me % 2
    side = (me // 2) % 2
    plane = me // 4
    local_seqs = tokens.shape[0] // size
    seq_len = tokens.shape[1] * size
    width = tokens.shape[2]
    own_rows = local_seqs * seq_len
    shard = query_weight.shape[0]
    hidden_shard = down_weight.shape[0]
    part = hidden_shard // 2
    half_width = width // 2

    def swap_core(array):
        return lax.ppermute(array, "fsdp", [(i, i ^ 1) for i in range(size)])

    def swap_side(array):
        return lax.ppermute(array, "fsdp", [(i, i ^ 2) for i in range(size)])

    def next_plane(array):
        return lax.ppermute(array, "fsdp", [(i, (i + 4) % size) for i in range(size)])

    def swap_half(array):
        return lax.ppermute(array, "grp", [(0, 1), (1, 0)])

    def pick(array, index, axis):
        return lax.dynamic_index_in_dim(array, index, axis, keepdims=False)

    ring = [(plane - k) % planes for k in range(planes)]
    places = []
    hidden_places = []
    for b in range(2):
        for a in range(2):
            for k in range(planes):
                there_core = core if b == 0 else 1 - core
                there_side = side if a == 0 else 1 - side
                places.append((ring[k] * 2 + there_side) * 2 + there_core)
                hidden_places.append((there_core * 2 + there_side) * planes + ring[k])
    places = jnp.stack(places).astype(jnp.int32)
    hidden_places = jnp.stack(hidden_places).astype(jnp.int32)

    def gather(own):
        held = [own]
        for _ in range(planes - 1):
            held.append(next_plane(held[-1]))
        other = [swap_side(array) for array in held]
        mine = held + other
        return mine + [swap_core(array) for array in mine]

    def column_half(weight):
        return pick(weight.reshape(shard, 2, half_width), half, 1)

    def hidden_half(weight):
        blocks = weight.reshape(shard, planes, 2, 2, 2, part)
        mine = pick(blocks, half, 4)
        return jnp.transpose(mine, (0, 3, 2, 1, 4)).reshape(shard, -1)

    per_row = hidden_shard // shard
    scales = jnp.concatenate(
        [
            scoring.reshape(shard, 1),
            attention_rate.reshape(shard, 1),
            feedforward_rate.reshape(shard, 1),
            upscale.reshape(shard, per_row),
            gatescale.reshape(shard, per_row),
        ],
        axis=1,
    )
    scales = jnp.pad(scales, ((0, 0), (0, 128 - scales.shape[1])))
    first_group = jnp.concatenate(
        [
            column_half(query_weight),
            column_half(key_weight),
            column_half(value_weight),
            out_weight,
            scales,
        ],
        axis=1,
    )
    second_group = jnp.concatenate([hidden_half(up_weight), hidden_half(gate_weight)], axis=1)
    third_group = pick(down_weight.reshape(2, part, width), half, 0)

    cols = 3 * half_width
    qkv_weight, out_full, scale_full = assemble(
        gather(first_group),
        places,
        [(0, cols), (cols, cols + width), (cols + width, cols + width + 128)],
    )
    hidden_width = second_group.shape[1] // 2
    (up_gate,) = assemble(gather(second_group), places, [(0, 2 * hidden_width)])
    (down_full,) = assemble(gather(third_group), hidden_places, [(0, width)])

    scale_float = scale_full.astype(F32)
    scoring_half = lax.dynamic_slice_in_dim(scale_float[:, 0], half * half_width, half_width)
    attention_mix = scale_float[:, 1]
    feed_mix = scale_float[:, 2]

    def hidden_scale(columns):
        blocks = columns.reshape(planes, 2, 2, 2, part)
        return jnp.transpose(pick(blocks, half, 3), (2, 1, 0, 3)).reshape(-1)

    up_scale = hidden_scale(scale_float[:, 3 : 3 + per_row])
    gate_scale = hidden_scale(scale_float[:, 3 + per_row : 3 + 2 * per_row])

    both = jnp.stack([tokens, cotangent])
    arrived = lax.all_to_all(both, "fsdp", split_axis=1, concat_axis=2, tiled=True)
    group_order = placement[0]
    own_slots = lax.dynamic_slice_in_dim(group_order, me * local_seqs, local_seqs)
    own_lengths = jnp.take(lengths[0], own_slots)
    valid = (jnp.arange(seq_len, dtype=jnp.int32)[None, :] < own_lengths[:, None]).reshape(
        own_rows, 1
    )
    own_tokens = arrived[0].reshape(own_rows, width)
    own_cot = jnp.where(valid, arrived[1].reshape(own_rows, width), jnp.zeros((), BF))
    token_rows = jnp.concatenate([own_tokens, swap_half(own_tokens)])
    cot_rows = jnp.concatenate([own_cot, swap_half(own_cot)])

    def turned(array):
        return jnp.concatenate([array[own_rows:], array[:own_rows]])

    def whole_sum(partial):
        return partial + swap_half(turned(partial).astype(BF)).astype(F32)

    token_float = token_rows.astype(F32)
    qkv = matmul(token_rows, qkv_weight)
    queries = qkv[:, :half_width]
    key_rows = qkv[:, half_width : 2 * half_width]
    value_low = qkv[:, 2 * half_width :].astype(BF)
    query_unit, key_unit, mixed_half = attention_forward(
        queries, key_rows, value_low, scoring_half, seq_len
    )
    mixed_other = swap_half(turned(mixed_half))
    mixed_low = jnp.where(
        half == 0,
        jnp.concatenate([mixed_half, mixed_other], axis=1),
        jnp.concatenate([mixed_other, mixed_half], axis=1),
    )
    attended = matmul(mixed_low, out_full)
    first_state = residual_mix(token_float, attended, attention_mix)
    first_low = first_state.astype(BF)
    up_gate_proj = matmul(first_low, up_gate)
    up_proj = up_gate_proj[:, :hidden_width]
    gate_proj = up_gate_proj[:, hidden_width:]
    hidden_low = swiglu(up_proj, gate_proj, up_scale, gate_scale).astype(BF)
    down_proj = whole_sum(matmul(hidden_low, down_full))

    feed_rows = jnp.broadcast_to(feed_mix, down_proj.shape)
    second, pullback = jax.vjp(residual_mix, first_state, down_proj, feed_rows)
    layer_own = jnp.where(valid, second[:own_rows], 0.0).astype(BF)
    grad_first, grad_down, feed_grad = pullback(cot_rows.astype(F32))
    feed_grad = jnp.sum(feed_grad[:own_rows], axis=0)
    down_low = grad_down.astype(BF)
    grad_hidden = back_matmul(down_low, down_full)
    _, pullback = jax.vjp(swiglu, up_proj, gate_proj, up_scale, gate_scale)
    grad_up, grad_gate, upscale_grad, gatescale_grad = pullback(grad_hidden)
    up_gate_low = jnp.concatenate([grad_up.astype(BF), grad_gate.astype(BF)], axis=1)
    grad_first = grad_first + whole_sum(back_matmul(up_gate_low, up_gate))
    attention_rows = jnp.broadcast_to(attention_mix, attended.shape)
    _, pullback = jax.vjp(residual_mix, token_float, attended, attention_rows)
    grad_tokens, grad_attended, attention_grad = pullback(grad_first)
    attention_grad = jnp.sum(attention_grad[:own_rows], axis=0)
    attended_low = grad_attended.astype(BF)
    out_half = pick(out_full.reshape(2, half_width, width), half, 0)
    grad_mixed = back_matmul(attended_low, out_half).astype(BF)
    grad_query, grad_key, grad_value, scoring_grad = attention_backward(
        grad_mixed, queries, key_rows, value_low, query_unit, key_unit, scoring_half, seq_len
    )
    qkv_low = jnp.concatenate([grad_query, grad_key, grad_value], axis=1)
    token_partial = back_matmul(qkv_low, qkv_weight)
    input_own = (
        grad_tokens[:own_rows]
        + token_partial[:own_rows]
        + swap_half(token_partial[own_rows:].astype(BF)).astype(F32)
    ).astype(BF)
    outgoing = jnp.stack([layer_own, input_own]).reshape(2, local_seqs, seq_len, width)
    returned = lax.all_to_all(outgoing, "fsdp", split_axis=2, concat_axis=1, tiled=True)

    order = [(plane - 1 - k) % planes for k in range(planes)]
    feature = jnp.arange(width, dtype=jnp.int32)
    block = []
    for b in range(2):
        for a in range(2):
            for k in range(planes):
                there_core = core if b == 0 else 1 - core
                there_side = 1 - side if a == 0 else side
                block.append((order[k] * 2 + there_side) * 2 + there_core)
    block = jnp.stack(block).astype(jnp.int32)
    wanted = (block[:, None] * shard + jnp.arange(shard, dtype=jnp.int32)[None, :]).reshape(-1)
    chooser = (feature[:, None] == wanted[None, :]).astype(BF)

    def share(array):
        return jnp.concatenate([array, swap_core(array)])

    def share_columns(array):
        chosen = matmul(array, chooser).astype(BF)
        return jnp.concatenate([chosen[:, :half_width], swap_core(chosen[:, half_width:])])

    def scatter(grads, height):
        grads = grads.astype(BF)
        total = None
        for k in range(planes):
            sent = grads[k * height : (k + 1) * height]
            kept = grads[(planes + k) * height : (planes + k + 1) * height]
            total_here = kept.astype(F32) + swap_side(sent).astype(F32)
            if total is not None:
                total_here = total_here + next_plane(total.astype(BF)).astype(F32)
            total = total_here
        return total

    hidden_blocks = hidden_low.reshape(hidden_low.shape[0], 2, 2 * planes * part)
    hidden_both = jnp.concatenate(
        [pick(hidden_blocks, core, 1), swap_core(pick(hidden_blocks, 1 - core, 1))]
    )
    down_wgrad = weight_grad(hidden_both, share(down_low)).astype(BF)
    down_blocks = down_wgrad.reshape(2, planes, part, width)
    down_sent = pick(down_blocks, 1 - side, 0)
    down_kept = pick(down_blocks, side, 0)
    down_order = jnp.concatenate(
        [pick(down_sent, order[k], 0) for k in range(planes)]
        + [pick(down_kept, order[k], 0) for k in range(planes)]
    )
    down_total = scatter(down_order, part)
    first_both = share_columns(first_low)
    up_gate_total = scatter(weight_grad(first_both, share(up_gate_low)), shard)
    mixed_both = share_columns(mixed_low)
    attended_cols = pick(attended_low.reshape(-1, 2, half_width), half, 1)
    out_total = scatter(weight_grad(mixed_both, share(attended_cols)), shard)
    token_both = share_columns(token_rows)
    qkv_total = scatter(weight_grad(token_both, share(qkv_low)), shard)

    low_planes = planes // 2

    def hidden_whole(total):
        blocks = total.reshape(shard, 4, 2, low_planes * part)
        theirs = swap_half(pick(blocks, 1 - half, 2).astype(BF)).astype(F32)
        mine = pick(blocks, half, 2)
        stacked = jnp.where(
            half == 0, jnp.stack([mine, theirs], axis=2), jnp.stack([theirs, mine], axis=2)
        )
        blocks = stacked.reshape(shard, 2, 2, 2, low_planes, part)
        return jnp.transpose(blocks, (0, 4, 2, 1, 3, 5)).reshape(shard, -1)

    up_out = hidden_whole(up_gate_total[:, :hidden_width])
    gate_out = hidden_whole(up_gate_total[:, hidden_width:])
    down_cols = down_total.reshape(part, 2, half_width)
    mine = pick(down_cols, half, 1)
    theirs = swap_half(pick(down_cols, 1 - half, 1).astype(BF)).astype(F32)
    down_out = jnp.where(
        half == 0, jnp.concatenate([mine, theirs]), jnp.concatenate([theirs, mine])
    )

    def hidden_spread(grad):
        blocks = jnp.transpose(grad.reshape(2, 2, planes, part), (2, 1, 0, 3))
        blank = jnp.zeros_like(blocks)
        both_halves = jnp.where(
            half == 0, jnp.stack([blocks, blank], axis=3), jnp.stack([blank, blocks], axis=3)
        )
        return both_halves.reshape(size, hidden_shard)

    scoring_spread = jnp.where(
        half == 0,
        jnp.concatenate([scoring_grad, jnp.zeros_like(scoring_grad)]),
        jnp.concatenate([jnp.zeros_like(scoring_grad), scoring_grad]),
    )
    small = jnp.concatenate(
        [
            scoring_spread.reshape(size, shard),
            attention_grad.reshape(size, shard),
            feed_grad.reshape(size, shard),
            hidden_spread(upscale_grad),
            hidden_spread(gatescale_grad),
        ],
        axis=1,
    ).reshape(planes, 2, 2, -1)
    small = pick(small, core, 2) + swap_core(pick(small, 1 - core, 2))
    small = pick(small, side, 1) + swap_side(pick(small, 1 - side, 1))
    total = pick(small, order[0], 0)
    for k in range(1, planes):
        total = pick(small, order[k], 0) + next_plane(total)
    total = total + swap_half(total)

    return (
        returned[0],
        returned[1],
        qkv_total[:, :half_width],
        qkv_total[:, half_width : 2 * half_width],
        qkv_total[:, 2 * half_width :],
        out_total,
        up_out,
        gate_out,
        down_out,
        total[:shard],
        total[3 * shard : 3 * shard + hidden_shard],
        total[3 * shard + hidden_shard :],
        total[shard : 2 * shard],
        total[2 * shard : 3 * shard],
    )


def solution(mesh):
    rows = P("grp", "fsdp", None)
    group = P("grp", None)
    matrix = P("fsdp", None)
    vector = P("fsdp")
    split = P("fsdp", "grp")
    return jax.shard_map(
        per_device,
        mesh=mesh,
        in_specs=(rows, rows, group, group) + (matrix,) * 7 + (vector,) * 5,
        out_specs=(rows, rows) + (split,) * 7 + (vector,) * 5,
        check_vma=False,
    )
```

```python
import math

import jax
import jax.numpy as jnp
from jax import lax
from jax.experimental import pallas as pl
from jax.experimental.pallas import tpu as pltpu
from jax.sharding import PartitionSpec as P

H = 20
DK = 64
BF = jnp.bfloat16
F32 = jnp.float32


def rms_norm(vector):
    return vector * lax.rsqrt(jnp.mean(vector * vector, axis=-1, keepdims=True) + 1e-06)


def residual_mix(base_rows, branch_rows, blending):
    return rms_norm(base_rows + blending * (rms_norm(branch_rows) - base_rows))


def swiglu(up_proj, gate_proj, upscale, gatescale):
    scaled = gatescale * gate_proj
    return scaled * jax.nn.sigmoid(scaled) * (upscale * up_proj)


def matmul(left_side, right_side):
    return jnp.dot(left_side, right_side, preferred_element_type=F32)


def weight_grad(left_side, right_side):
    return lax.dot_general(
        left_side, right_side, (((0,), (0,)), ((), ())), preferred_element_type=F32
    )


def back_matmul(grad_rows, weight_rows):
    return lax.dot_general(
        grad_rows, weight_rows, (((1,), (1,)), ((), ())), preferred_element_type=F32
    )


def after(value, *earlier):
    return lax.optimization_barrier((value, *earlier))[0]


def head_inverse(vector, low_head):
    squares = vector * vector
    low_sum = jnp.sum(jnp.where(low_head, squares, 0.0), axis=-1, keepdims=True)
    high_sum = jnp.sum(jnp.where(low_head, 0.0, squares), axis=-1, keepdims=True)
    return jnp.where(low_head, lax.rsqrt(low_sum + 1e-06), lax.rsqrt(high_sum + 1e-06))


def head_probs(query_head, key_unit, seq_len):
    scores = back_matmul(query_head, key_unit) * math.sqrt(DK)
    query_row = lax.broadcasted_iota(jnp.int32, scores.shape, 0)
    key_row = lax.broadcasted_iota(jnp.int32, scores.shape, 1)
    start = query_row - lax.rem(query_row, seq_len)
    scores = jnp.where((key_row <= query_row) & (key_row >= start), scores, -1e30)
    exp_scores = jnp.exp(scores - jnp.max(scores, axis=-1, keepdims=True))
    return exp_scores / jnp.sum(exp_scores, axis=-1, keepdims=True)


def only(mask, values):
    return jnp.where(mask, values.astype(F32), 0.0).astype(BF)


def attention_forward(qkv, scoring, seq_len):
    rows = qkv.shape[0]
    width = qkv.shape[1] // 3
    pairs = width // 128

    def body(q_ref, k_ref, v_ref, scoring_ref, qu_ref, ku_ref, vl_ref, mixed_ref):
        low_head = lax.broadcasted_iota(jnp.int32, (rows, 128), 1) < DK
        queries = q_ref[...]
        key_rows = k_ref[...]
        scaling = scoring_ref[...]
        query_unit = queries * head_inverse(queries, low_head) * scaling
        key_unit = (key_rows * head_inverse(key_rows, low_head) * scaling).astype(BF)
        value_low = v_ref[...].astype(BF)
        mixed = None
        for mask in (low_head, ~low_head):
            probs = head_probs(only(mask, query_unit), key_unit, seq_len)
            head = matmul(probs.astype(BF), value_low)
            mixed = head if mixed is None else jnp.where(low_head, mixed, head)
        qu_ref[...] = query_unit.astype(BF)
        ku_ref[...] = key_unit
        vl_ref[...] = value_low
        mixed_ref[...] = mixed.astype(BF)

    def block(part):
        return pl.BlockSpec((rows, 128), lambda i: (0, part * pairs + i))

    return pl.pallas_call(
        body,
        grid=(pairs,),
        out_shape=[jax.ShapeDtypeStruct((rows, width), BF)] * 4,
        in_specs=[block(0), block(1), block(2), pl.BlockSpec((1, 128), lambda i: (0, i))],
        out_specs=[block(0)] * 4,
        compiler_params=pltpu.CompilerParams(vmem_limit_bytes=48 * 2**20),
        cost_estimate=pl.CostEstimate(
            flops=8 * rows * rows * width, bytes_accessed=20 * rows * width, transcendentals=rows * rows * pairs * 2
        ),
        name="attention_forward",
    )(qkv, qkv, qkv, scoring.reshape(1, width))


def attention_backward(grad_mixed, qkv, query_unit, key_unit, value_low, scoring, seq_len):
    rows, width = grad_mixed.shape
    pairs = width // 128

    def body(gm_ref, q_ref, k_ref, qu_ref, ku_ref, vl_ref, scoring_ref, grads_ref, scoring_grad_ref):
        low_head = lax.broadcasted_iota(jnp.int32, (rows, 128), 1) < DK
        query_unit = qu_ref[...]
        key_unit = ku_ref[...]
        value_low = vl_ref[...]
        scaling = scoring_ref[...]
        grad_value = grad_qunit = grad_kunit = None
        for mask in (low_head, ~low_head):
            probs = head_probs(only(mask, query_unit), key_unit, seq_len)
            grad_head = only(mask, gm_ref[...])
            value_part = weight_grad(probs.astype(BF), grad_head)
            grad_probs = back_matmul(grad_head, value_low)
            grad_scores = (
                probs * (grad_probs - jnp.sum(grad_probs * probs, axis=-1, keepdims=True))
            ).astype(BF)
            query_part = matmul(grad_scores, key_unit)
            key_part = weight_grad(grad_scores, query_unit)
            if grad_value is None:
                grad_value, grad_qunit, grad_kunit = value_part, query_part, key_part
            else:
                grad_value = grad_value + value_part
                grad_qunit = jnp.where(low_head, grad_qunit, query_part)
                grad_kunit = jnp.where(low_head, grad_kunit, key_part)
        scoring_grad = None
        for place, raw, grad in ((0, q_ref[...], grad_qunit), (1, k_ref[...], grad_kunit)):
            grad = grad * math.sqrt(DK)
            inverse = head_inverse(raw, low_head)
            unit = raw * inverse
            term = jnp.sum(grad * unit, axis=0, keepdims=True)
            scoring_grad = term if scoring_grad is None else scoring_grad + term
            grad = grad * scaling
            along = grad * unit
            low_sum = jnp.sum(jnp.where(low_head, along, 0.0), axis=-1, keepdims=True)
            high_sum = jnp.sum(jnp.where(low_head, 0.0, along), axis=-1, keepdims=True)
            grads_ref[place] = (
                inverse * (grad - unit * jnp.where(low_head, low_sum, high_sum))
            ).astype(BF)
        grads_ref[2] = grad_value.astype(BF)
        scoring_grad_ref[...] = scoring_grad

    def block(part):
        return pl.BlockSpec((rows, 128), lambda i: (0, part * pairs + i))

    vector = pl.BlockSpec((1, 128), lambda i: (0, i))
    return pl.pallas_call(
        body,
        grid=(pairs,),
        out_shape=[
            jax.ShapeDtypeStruct((3, rows, width), BF),
            jax.ShapeDtypeStruct((1, width), F32),
        ],
        in_specs=[block(0), block(0), block(1), block(0), block(0), block(0), vector],
        out_specs=[pl.BlockSpec((3, rows, 128), lambda i: (0, 0, i)), vector],
        compiler_params=pltpu.CompilerParams(vmem_limit_bytes=48 * 2**20),
        cost_estimate=pl.CostEstimate(
            flops=16 * rows * rows * width, bytes_accessed=22 * rows * width, transcendentals=rows * rows * pairs * 2
        ),
        name="attention_backward",
    )(grad_mixed, qkv, qkv, query_unit, key_unit, value_low, scoring.reshape(1, width))


def per_device(
    tokens,
    cotangent,
    lengths,
    placement,
    query_weight,
    key_weight,
    value_weight,
    out_weight,
    up_weight,
    gate_weight,
    down_weight,
    scoring,
    upscale,
    gatescale,
    attention_rate,
    feedforward_rate,
):
    size = lax.axis_size("fsdp")
    planes = size // 4
    half = lax.axis_index("grp")
    me = lax.axis_index("fsdp")
    core = me % 2
    side = (me // 2) % 2
    plane = me // 4
    local_seqs = tokens.shape[0] // size
    seq_len = tokens.shape[1] * size
    width = tokens.shape[2]
    own_rows = local_seqs * seq_len
    shard = query_weight.shape[0]
    hidden_shard = down_weight.shape[0]
    part = hidden_shard // 2
    half_width = width // 2

    def swap_core(array):
        return lax.ppermute(array, "fsdp", [(i, i ^ 1) for i in range(size)])

    def swap_side(array):
        return lax.ppermute(array, "fsdp", [(i, i ^ 2) for i in range(size)])

    def next_plane(array):
        return lax.ppermute(array, "fsdp", [(i, (i + 4) % size) for i in range(size)])

    def swap_half(array):
        return lax.ppermute(array, "grp", [(0, 1), (1, 0)])

    def pick(array, index, axis):
        return lax.dynamic_index_in_dim(array, index, axis, keepdims=False)

    def column_half(weight):
        return pick(weight.reshape(shard, 2, half_width), half, 1)

    def hidden_half(weight):
        blocks = weight.reshape(shard, planes, 2, 2, 2, part)
        mine = pick(blocks, half, 4)
        return jnp.transpose(mine, (0, 3, 2, 1, 4)).reshape(shard, -1)

    per_row = hidden_shard // shard
    scales = jnp.concatenate(
        [
            scoring.reshape(shard, 1),
            attention_rate.reshape(shard, 1),
            feedforward_rate.reshape(shard, 1),
            upscale.reshape(shard, per_row),
            gatescale.reshape(shard, per_row),
        ],
        axis=1,
    )
    scales = jnp.pad(scales, ((0, 0), (0, 128 - scales.shape[1])))
    first_group = jnp.concatenate(
        [
            column_half(query_weight),
            column_half(key_weight),
            column_half(value_weight),
            out_weight,
            scales,
        ],
        axis=1,
    )
    up_half = hidden_half(up_weight)
    gate_half = hidden_half(gate_weight)
    hidden_width = up_half.shape[1]
    core_width = hidden_width // 2
    second_group = jnp.concatenate(
        [
            up_half[:, :core_width],
            up_half[:, core_width:],
            gate_half[:, :core_width],
            gate_half[:, core_width:],
            pick(down_weight.reshape(2, part, width), half, 0),
        ]
    )
    cols = 3 * half_width
    first_whole = lax.all_gather(first_group, "fsdp", axis=0, tiled=True)
    qkv_weight = first_whole[:, :cols]
    out_full = first_whole[:, cols : cols + width]
    scale_full = first_whole[:, cols + width :]
    second_whole = lax.all_gather(after(second_group, first_whole), "fsdp", axis=0)

    def hidden_matrix(low, high):
        return jnp.concatenate(
            [
                second_whole[:, i * shard : (i + 1) * shard].reshape(width, core_width)
                for i in range(low, high)
            ],
            axis=1,
        )

    up_gate = hidden_matrix(0, 4)
    down_blocks = second_whole[:, 4 * shard :].reshape(planes, 2, 2, part, width)
    down_full = jnp.transpose(down_blocks, (2, 1, 0, 3, 4)).reshape(hidden_width, width)

    scale_float = scale_full.astype(F32)
    scoring_half = lax.dynamic_slice_in_dim(scale_float[:, 0], half * half_width, half_width)
    attention_mix = scale_float[:, 1]
    feed_mix = scale_float[:, 2]

    def hidden_scale(columns):
        blocks = columns.reshape(planes, 2, 2, 2, part)
        return jnp.transpose(pick(blocks, half, 3), (2, 1, 0, 3)).reshape(-1)

    up_scale = hidden_scale(scale_float[:, 3 : 3 + per_row])
    gate_scale = hidden_scale(scale_float[:, 3 + per_row : 3 + 2 * per_row])

    both = jnp.stack([tokens, cotangent])
    arrived = lax.all_to_all(both, "fsdp", split_axis=1, concat_axis=2, tiled=True)
    group_order = placement[0]
    own_slots = lax.dynamic_slice_in_dim(group_order, me * local_seqs, local_seqs)
    own_lengths = jnp.take(lengths[0], own_slots)
    valid = (jnp.arange(seq_len, dtype=jnp.int32)[None, :] < own_lengths[:, None]).reshape(
        own_rows, 1
    )
    own_tokens = arrived[0].reshape(own_rows, width)
    own_cot = jnp.where(valid, arrived[1].reshape(own_rows, width), jnp.zeros((), BF))
    token_rows = jnp.concatenate([own_tokens, swap_half(own_tokens)])
    cot_rows = jnp.concatenate([own_cot, swap_half(own_cot)])

    def turned(array):
        return jnp.concatenate([array[own_rows:], array[:own_rows]])

    def whole_sum(partial):
        return partial + swap_half(turned(partial).astype(BF)).astype(F32)

    token_float = token_rows.astype(F32)
    qkv = matmul(token_rows, qkv_weight)
    query_unit, key_unit, value_low, mixed_half = attention_forward(qkv, scoring_half, seq_len)
    mixed_other = swap_half(turned(mixed_half))
    mixed_low = jnp.where(
        half == 0,
        jnp.concatenate([mixed_half, mixed_other], axis=1),
        jnp.concatenate([mixed_other, mixed_half], axis=1),
    )
    attended = matmul(mixed_low, out_full)
    first_state = residual_mix(token_float, attended, attention_mix)
    first_low = first_state.astype(BF)
    up_gate_proj = matmul(first_low, up_gate)
    up_proj = up_gate_proj[:, :hidden_width]
    gate_proj = up_gate_proj[:, hidden_width:]
    hidden_low = swiglu(up_proj, gate_proj, up_scale, gate_scale).astype(BF)
    down_proj = whole_sum(matmul(hidden_low, down_full))

    order = [(plane - 1 - k) % planes for k in range(planes)]
    feature = jnp.arange(width, dtype=jnp.int32)
    block = []
    for b in range(2):
        for a in range(2):
            for k in range(planes):
                there_core = core if b == 0 else 1 - core
                there_side = 1 - side if a == 0 else side
                block.append((order[k] * 2 + there_side) * 2 + there_core)
    block = jnp.stack(block).astype(jnp.int32)
    wanted = (block[:, None] * shard + jnp.arange(shard, dtype=jnp.int32)[None, :]).reshape(-1)
    chooser = (feature[:, None] == wanted[None, :]).astype(BF)

    def share(array, axis=0):
        return jnp.concatenate([array, swap_core(array)], axis=axis)

    def share_columns(array):
        chosen = matmul(array, chooser).astype(BF)
        return jnp.concatenate([chosen[:, :half_width], swap_core(chosen[:, half_width:])])

    side_line = []

    def scatter(sent, kept):
        total = None
        for k in range(planes):
            ready = sent(k)
            if len(side_line) > 1:
                ready = after(ready, side_line[-2])
            arrived_block = swap_side(ready)
            side_line.append(arrived_block)
            total_here = kept(k).astype(F32) + arrived_block.astype(F32)
            if total is not None:
                total_here = total_here + next_plane(total.astype(BF)).astype(F32)
            total = total_here
        return total

    def scatter_rows(grads):
        blocks = grads.reshape(2, planes, grads.shape[0] // (2 * planes), -1)
        return scatter(lambda k: blocks[0, k], lambda k: blocks[1, k])

    feed_rows = jnp.broadcast_to(feed_mix, down_proj.shape)
    second, pullback = jax.vjp(residual_mix, first_state, down_proj, feed_rows)
    layer_own = jnp.where(valid, second[:own_rows], 0.0).astype(BF)
    grad_first, grad_down, feed_grad = pullback(cot_rows.astype(F32))
    feed_grad = jnp.sum(feed_grad[:own_rows], axis=0)
    down_low = grad_down.astype(BF)
    grad_hidden = back_matmul(down_low, down_full)
    hidden_blocks = hidden_low.reshape(hidden_low.shape[0], 2, core_width)
    hidden_both = jnp.concatenate(
        [pick(hidden_blocks, core, 1), swap_core(pick(hidden_blocks, 1 - core, 1))]
    )
    down_wgrad = weight_grad(hidden_both, share(down_low)).astype(BF)
    grad_hidden, down_wgrad = lax.optimization_barrier((grad_hidden, down_wgrad))
    down_wgrad = down_wgrad.reshape(2, planes, part, width)
    down_total = scatter(
        lambda k: pick(pick(down_wgrad, 1 - side, 0), order[k], 0),
        lambda k: pick(pick(down_wgrad, side, 0), order[k], 0),
    )
    _, pullback = jax.vjp(swiglu, up_proj, gate_proj, up_scale, gate_scale)
    grad_up, grad_gate, upscale_grad, gatescale_grad = pullback(grad_hidden)
    up_gate_low = jnp.concatenate([grad_up.astype(BF), grad_gate.astype(BF)], axis=1)
    first_both = share_columns(first_low)
    up_gate_both = share(up_gate_low)
    partial = back_matmul(up_gate_low, up_gate)
    partial_other = swap_half(turned(partial).astype(BF))
    up_gate_wgrad = weight_grad(first_both, up_gate_both).astype(BF)
    partial_other, up_gate_wgrad = lax.optimization_barrier((partial_other, up_gate_wgrad))
    up_gate_total = scatter_rows(up_gate_wgrad)
    grad_first = grad_first + partial + partial_other.astype(F32)
    attention_rows = jnp.broadcast_to(attention_mix, attended.shape)
    _, pullback = jax.vjp(residual_mix, token_float, attended, attention_rows)
    grad_tokens, grad_attended, attention_grad = pullback(grad_first)
    attention_grad = jnp.sum(attention_grad[:own_rows], axis=0)
    attended_low = grad_attended.astype(BF)
    out_half = pick(out_full.reshape(2, half_width, width), half, 0)
    grad_mixed = back_matmul(attended_low, out_half).astype(BF)
    mixed_both = share_columns(mixed_low)
    attended_cols = pick(attended_low.reshape(-1, 2, half_width), half, 1)
    out_wgrad = weight_grad(mixed_both, share(attended_cols)).astype(BF)
    grad_mixed, out_wgrad = lax.optimization_barrier((grad_mixed, out_wgrad))
    out_total = scatter_rows(out_wgrad)
    qkv_low, scoring_grad = attention_backward(
        grad_mixed, qkv, query_unit, key_unit, value_low, scoring_half, seq_len
    )
    scoring_grad = scoring_grad[0]
    qkv_both = share(qkv_low, 1)
    token_partial = sum(
        back_matmul(qkv_low[j], qkv_weight[:, j * half_width : (j + 1) * half_width])
        for j in range(3)
    )
    input_other = swap_half(token_partial[own_rows:].astype(BF))
    token_both = share_columns(token_rows)
    qkv_wgrad = jnp.concatenate(
        [weight_grad(token_both, qkv_both[j]).astype(BF) for j in range(3)], axis=1
    )
    input_other, qkv_wgrad = lax.optimization_barrier((input_other, qkv_wgrad))
    qkv_total = scatter_rows(qkv_wgrad)
    input_own = (
        grad_tokens[:own_rows] + token_partial[:own_rows] + input_other.astype(F32)
    ).astype(BF)
    outgoing = jnp.stack([layer_own, input_own]).reshape(2, local_seqs, seq_len, width)
    returned = lax.all_to_all(outgoing, "fsdp", split_axis=2, concat_axis=1, tiled=True)

    low_planes = planes // 2

    def hidden_whole(total):
        blocks = total.reshape(shard, 4, 2, low_planes * part)
        theirs = swap_half(pick(blocks, 1 - half, 2).astype(BF)).astype(F32)
        mine = pick(blocks, half, 2)
        stacked = jnp.where(
            half == 0, jnp.stack([mine, theirs], axis=2), jnp.stack([theirs, mine], axis=2)
        )
        blocks = stacked.reshape(shard, 2, 2, 2, low_planes, part)
        return jnp.transpose(blocks, (0, 4, 2, 1, 3, 5)).reshape(shard, -1)

    up_out = hidden_whole(up_gate_total[:, :hidden_width])
    gate_out = hidden_whole(up_gate_total[:, hidden_width:])
    down_cols = down_total.reshape(part, 2, half_width)
    mine = pick(down_cols, half, 1)
    theirs = swap_half(pick(down_cols, 1 - half, 1).astype(BF)).astype(F32)
    down_out = jnp.where(
        half == 0, jnp.concatenate([mine, theirs]), jnp.concatenate([theirs, mine])
    )

    def hidden_spread(grad):
        blocks = jnp.transpose(grad.reshape(2, 2, planes, part), (2, 1, 0, 3))
        blank = jnp.zeros_like(blocks)
        both_halves = jnp.where(
            half == 0, jnp.stack([blocks, blank], axis=3), jnp.stack([blank, blocks], axis=3)
        )
        return both_halves.reshape(size, hidden_shard)

    scoring_spread = jnp.where(
        half == 0,
        jnp.concatenate([scoring_grad, jnp.zeros_like(scoring_grad)]),
        jnp.concatenate([jnp.zeros_like(scoring_grad), scoring_grad]),
    )
    small = jnp.concatenate(
        [
            scoring_spread.reshape(size, shard),
            attention_grad.reshape(size, shard),
            feed_grad.reshape(size, shard),
            hidden_spread(upscale_grad),
            hidden_spread(gatescale_grad),
        ],
        axis=1,
    ).reshape(planes, 2, 2, -1)
    small = pick(small, core, 2) + swap_core(pick(small, 1 - core, 2))
    small = pick(small, side, 1) + swap_side(pick(small, 1 - side, 1))
    total = pick(small, order[0], 0)
    for k in range(1, planes):
        total = pick(small, order[k], 0) + next_plane(total)
    total = total + swap_half(total)

    return (
        returned[0],
        returned[1],
        qkv_total[:, :half_width],
        qkv_total[:, half_width : 2 * half_width],
        qkv_total[:, 2 * half_width :],
        out_total,
        up_out,
        gate_out,
        down_out,
        total[:shard],
        total[3 * shard : 3 * shard + hidden_shard],
        total[3 * shard + hidden_shard :],
        total[shard : 2 * shard],
        total[2 * shard : 3 * shard],
    )


def solution(mesh):
    rows = P("grp", "fsdp", None)
    group = P("grp", None)
    matrix = P("fsdp", None)
    vector = P("fsdp")
    split = P("fsdp", "grp")
    return jax.shard_map(
        per_device,
        mesh=mesh,
        in_specs=(rows, rows, group, group) + (matrix,) * 7 + (vector,) * 5,
        out_specs=(rows, rows) + (split,) * 7 + (vector,) * 5,
        check_vma=False,
    )
```

```python
import math

import jax
import jax.numpy as jnp
from jax import lax
from jax.experimental import pallas as pl
from jax.experimental.pallas import tpu as pltpu
from jax.sharding import PartitionSpec as P

H = 20
DK = 64
BF = jnp.bfloat16
F32 = jnp.float32


def rms_norm(vector):
    return vector * lax.rsqrt(jnp.mean(vector * vector, axis=-1, keepdims=True) + 1e-06)


def residual_mix(base_rows, branch_rows, blending):
    return rms_norm(base_rows + blending * (rms_norm(branch_rows) - base_rows))


def swiglu(up_proj, gate_proj, upscale, gatescale):
    scaled = gatescale * gate_proj
    return scaled * jax.nn.sigmoid(scaled) * (upscale * up_proj)


def matmul(left_side, right_side):
    return jnp.dot(left_side, right_side, preferred_element_type=F32)


def weight_grad(left_side, right_side):
    return lax.dot_general(
        left_side, right_side, (((0,), (0,)), ((), ())), preferred_element_type=F32
    )


def back_matmul(grad_rows, weight_rows):
    return lax.dot_general(
        grad_rows, weight_rows, (((1,), (1,)), ((), ())), preferred_element_type=F32
    )


def after(value, *earlier):
    return lax.optimization_barrier((value, *earlier))[0]


def head_inverse(vector, low_head):
    squares = vector * vector
    low_sum = jnp.sum(jnp.where(low_head, squares, 0.0), axis=-1, keepdims=True)
    high_sum = jnp.sum(jnp.where(low_head, 0.0, squares), axis=-1, keepdims=True)
    return jnp.where(low_head, lax.rsqrt(low_sum + 1e-06), lax.rsqrt(high_sum + 1e-06))


def head_probs(query_head, key_unit, seq_len):
    scores = back_matmul(query_head, key_unit) * math.sqrt(DK)
    query_row = lax.broadcasted_iota(jnp.int32, scores.shape, 0)
    key_row = lax.broadcasted_iota(jnp.int32, scores.shape, 1)
    start = query_row - lax.rem(query_row, seq_len)
    scores = jnp.where((key_row <= query_row) & (key_row >= start), scores, -1e30)
    exp_scores = jnp.exp(scores - jnp.max(scores, axis=-1, keepdims=True))
    return exp_scores / jnp.sum(exp_scores, axis=-1, keepdims=True)


def only(mask, values):
    return jnp.where(mask, values.astype(F32), 0.0).astype(BF)


def attention_forward(qkv, scoring, seq_len):
    rows = qkv.shape[0]
    width = qkv.shape[1] // 3
    pairs = width // 128

    def body(q_ref, k_ref, v_ref, scoring_ref, qu_ref, ku_ref, vl_ref, mixed_ref):
        low_head = lax.broadcasted_iota(jnp.int32, (rows, 128), 1) < DK
        queries = q_ref[...]
        key_rows = k_ref[...]
        scaling = scoring_ref[...]
        query_unit = queries * head_inverse(queries, low_head) * scaling
        key_unit = (key_rows * head_inverse(key_rows, low_head) * scaling).astype(BF)
        value_low = v_ref[...].astype(BF)
        mixed = None
        for mask in (low_head, ~low_head):
            probs = head_probs(only(mask, query_unit), key_unit, seq_len)
            head = matmul(probs.astype(BF), value_low)
            mixed = head if mixed is None else jnp.where(low_head, mixed, head)
        qu_ref[...] = query_unit.astype(BF)
        ku_ref[...] = key_unit
        vl_ref[...] = value_low
        mixed_ref[...] = mixed.astype(BF)

    def block(part):
        return pl.BlockSpec((rows, 128), lambda i: (0, part * pairs + i))

    return pl.pallas_call(
        body,
        grid=(pairs,),
        out_shape=[jax.ShapeDtypeStruct((rows, width), BF)] * 4,
        in_specs=[block(0), block(1), block(2), pl.BlockSpec((1, 128), lambda i: (0, i))],
        out_specs=[block(0)] * 4,
        compiler_params=pltpu.CompilerParams(vmem_limit_bytes=48 * 2**20),
        cost_estimate=pl.CostEstimate(
            flops=8 * rows * rows * width, bytes_accessed=20 * rows * width, transcendentals=rows * rows * pairs * 2
        ),
        name="attention_forward",
    )(qkv, qkv, qkv, scoring.reshape(1, width))


def attention_backward(grad_mixed, qkv, query_unit, key_unit, value_low, scoring, seq_len):
    rows, width = grad_mixed.shape
    pairs = width // 128

    def body(gm_ref, q_ref, k_ref, qu_ref, ku_ref, vl_ref, scoring_ref, grads_ref, scoring_grad_ref):
        low_head = lax.broadcasted_iota(jnp.int32, (rows, 128), 1) < DK
        query_unit = qu_ref[...]
        key_unit = ku_ref[...]
        value_low = vl_ref[...]
        scaling = scoring_ref[...]
        grad_value = grad_qunit = grad_kunit = None
        for mask in (low_head, ~low_head):
            probs = head_probs(only(mask, query_unit), key_unit, seq_len)
            grad_head = only(mask, gm_ref[...])
            value_part = weight_grad(probs.astype(BF), grad_head)
            grad_probs = back_matmul(grad_head, value_low)
            grad_scores = (
                probs * (grad_probs - jnp.sum(grad_probs * probs, axis=-1, keepdims=True))
            ).astype(BF)
            query_part = matmul(grad_scores, key_unit)
            key_part = weight_grad(grad_scores, query_unit)
            if grad_value is None:
                grad_value, grad_qunit, grad_kunit = value_part, query_part, key_part
            else:
                grad_value = grad_value + value_part
                grad_qunit = jnp.where(low_head, grad_qunit, query_part)
                grad_kunit = jnp.where(low_head, grad_kunit, key_part)
        scoring_grad = None
        for place, raw, grad in ((0, q_ref[...], grad_qunit), (1, k_ref[...], grad_kunit)):
            grad = grad * math.sqrt(DK)
            inverse = head_inverse(raw, low_head)
            unit = raw * inverse
            term = jnp.sum(grad * unit, axis=0, keepdims=True)
            scoring_grad = term if scoring_grad is None else scoring_grad + term
            grad = grad * scaling
            along = grad * unit
            low_sum = jnp.sum(jnp.where(low_head, along, 0.0), axis=-1, keepdims=True)
            high_sum = jnp.sum(jnp.where(low_head, 0.0, along), axis=-1, keepdims=True)
            grads_ref[place] = (
                inverse * (grad - unit * jnp.where(low_head, low_sum, high_sum))
            ).astype(BF)
        grads_ref[2] = grad_value.astype(BF)
        scoring_grad_ref[...] = scoring_grad

    def block(part):
        return pl.BlockSpec((rows, 128), lambda i: (0, part * pairs + i))

    vector = pl.BlockSpec((1, 128), lambda i: (0, i))
    return pl.pallas_call(
        body,
        grid=(pairs,),
        out_shape=[
            jax.ShapeDtypeStruct((3, rows, width), BF),
            jax.ShapeDtypeStruct((1, width), F32),
        ],
        in_specs=[block(0), block(0), block(1), block(0), block(0), block(0), vector],
        out_specs=[pl.BlockSpec((3, rows, 128), lambda i: (0, 0, i)), vector],
        compiler_params=pltpu.CompilerParams(vmem_limit_bytes=48 * 2**20),
        cost_estimate=pl.CostEstimate(
            flops=16 * rows * rows * width, bytes_accessed=22 * rows * width, transcendentals=rows * rows * pairs * 2
        ),
        name="attention_backward",
    )(grad_mixed, qkv, qkv, query_unit, key_unit, value_low, scoring.reshape(1, width))


class HiddenWeights:
    def __init__(self, gathered, planes, shard, part):
        width = gathered.shape[2]
        units = 2 * planes * part
        self.direct = shard % 16 == 0 and part % 16 == 0
        self.width, self.units, self.shard, self.part = width, units, shard, part
        if self.direct:
            self.arrays = [gathered.reshape(planes, 2, 2, -1, width)]
            self.matrix = (planes, 2, 2, shard, units)
            self.down = (planes, part, width)
        else:
            blocks = gathered[:, 4 * shard :].reshape(planes, 2, 2, part, width)
            self.arrays = [
                jnp.stack(
                    [gathered[:, i * shard : (i + 1) * shard].reshape(width, width) for i in range(4)]
                ),
                jnp.transpose(blocks, (2, 1, 0, 3, 4)).reshape(2, 2, planes * part, width),
            ]
            self.matrix = (width, units)
            self.down = (planes * part, width)

    def scratch(self):
        return [
            pltpu.VMEM((4,) + self.matrix, BF),
            pltpu.VMEM((2, 2) + self.down, BF),
            pltpu.SemaphoreType.DMA((8,)),
        ]

    def specs(self):
        return [pl.BlockSpec(memory_space=pl.ANY)] * len(self.arrays)

    def matrix_copy(self, sources, wide, sems, i):
        if self.direct:
            source = sources[0].at[:, :, :, pl.ds(i * self.shard, self.shard), :]
        else:
            source = sources[0].at[i]
        return pltpu.make_async_copy(source, wide.at[i], sems.at[i])

    def down_copy(self, sources, tall, sems, core, side):
        if self.direct:
            source = sources[0].at[:, side, core, pl.ds(4 * self.shard, self.part), :]
        else:
            source = sources[1].at[core, side]
        return pltpu.make_async_copy(source, tall.at[core, side], sems.at[4 + core * 2 + side])

    def matrix_value(self, wide, i, columns):
        if self.direct:
            return wide[i, :, :, :, :, columns].reshape(self.width, -1)
        return wide[i, :, columns]

    def matrix_rows(self, wide, i, j, parts):
        if self.direct:
            step = self.matrix[0] // parts
            return wide[i, pl.ds(j * step, step)].reshape(self.width // parts, -1)
        step = self.width // parts
        return wide[i, pl.ds(j * step, step)]

    def down_value(self, tall, core, side, columns):
        if self.direct:
            return tall[core, side, :, :, columns].reshape(-1, columns.size)
        return tall[core, side, :, columns]

    def down_rows(self, tall, core, side):
        return tall[core, side].reshape(-1, self.width)


def hidden_forward(first_low, weights, up_scale, gate_scale, own_rows):
    rows, width = first_low.shape
    units = weights.units
    block = units // 2
    step = 256

    def body(first_ref, up_scale_ref, gate_scale_ref, *refs):
        sources = refs[: len(weights.arrays)]
        hidden_ref, up_ref, gate_ref, partial_ref, turned_ref, wide, tall, sems = refs[
            len(weights.arrays) :
        ]
        copies = [weights.matrix_copy(sources, wide, sems, i) for i in (0, 2, 1, 3)]
        down_copies = [
            weights.down_copy(sources, tall, sems, i, j) for i in range(2) for j in range(2)
        ]
        for copy in copies + down_copies:
            copy.start()
        first = first_ref[...]
        for core in range(2):
            copies[2 * core].wait()
            copies[2 * core + 1].wait()

            for begin in range(0, units, step):
                columns = pl.ds(begin, step)
                here = pl.ds(core * units + begin, step)
                up = matmul(first, weights.matrix_value(wide, core, columns))
                gate = matmul(first, weights.matrix_value(wide, 2 + core, columns))
                up_ref[:, here] = up
                gate_ref[:, here] = gate
                hidden = swiglu(up, gate, up_scale_ref[:, here], gate_scale_ref[:, here])
                hidden_ref[core, :, columns] = hidden.astype(BF)
        for copy in down_copies:
            copy.wait()

        for begin in range(0, width, step):
            columns = pl.ds(begin, step)
            total = None
            for core in range(2):
                for side in range(2):
                    term = matmul(
                        hidden_ref[core, :, pl.ds(side * block, block)],
                        weights.down_value(tall, core, side, columns),
                    )
                    total = term if total is None else total + term
            partial_ref[:, columns] = total
            turned_ref[pl.ds(0, own_rows), columns] = total[own_rows:].astype(BF)
            turned_ref[pl.ds(own_rows, own_rows), columns] = total[:own_rows].astype(BF)

    whole = pl.BlockSpec(memory_space=pltpu.VMEM)
    return pl.pallas_call(
        body,
        out_shape=[
            jax.ShapeDtypeStruct((2, rows, units), BF),
            jax.ShapeDtypeStruct((rows, 2 * units), F32),
            jax.ShapeDtypeStruct((rows, 2 * units), F32),
            jax.ShapeDtypeStruct((rows, width), F32),
            jax.ShapeDtypeStruct((rows, width), BF),
        ],
        in_specs=[whole] * 3 + weights.specs(),
        out_specs=[whole] * 5,
        scratch_shapes=weights.scratch(),
        compiler_params=pltpu.CompilerParams(vmem_limit_bytes=56 * 2**20),
        cost_estimate=pl.CostEstimate(
            flops=12 * rows * width * units, bytes_accessed=12 * width * units, transcendentals=rows * units * 2
        ),
        name="hidden_forward",
    )(first_low, up_scale.reshape(1, -1), gate_scale.reshape(1, -1), *weights.arrays)


def hidden_backward(down_low, up_proj, gate_proj, weights, up_scale, gate_scale, own_rows):
    rows, width = down_low.shape
    units = weights.units
    block = units // 2

    def body(down_ref, up_ref, gate_ref, up_scale_ref, gate_scale_ref, *refs):
        sources = refs[: len(weights.arrays)]
        low_ref, up_grad_ref, gate_grad_ref, partial_ref, turned_ref, wide, tall, sems = refs[
            len(weights.arrays) :
        ]
        down_copies = [
            weights.down_copy(sources, tall, sems, i, j) for i in range(2) for j in range(2)
        ]
        copies = [weights.matrix_copy(sources, wide, sems, i) for i in range(4)]
        for copy in down_copies + copies:
            copy.start()
        down = down_ref[...]
        for core in range(2):
            for side in range(2):
                down_copies[core * 2 + side].wait()
                here = pl.ds((core * 2 + side) * block, block)
                grad_hidden = back_matmul(down, weights.down_rows(tall, core, side))
                up_scaling = up_scale_ref[:, here]
                gate_scaling = gate_scale_ref[:, here]
                up = up_ref[:, here]
                gate = gate_ref[:, here]
                scaled = gate_scaling * gate
                sigmoid = jax.nn.sigmoid(scaled)
                silu = scaled * sigmoid
                grad_scaled_up = grad_hidden * silu
                grad_scaled = grad_hidden * (up_scaling * up) * (sigmoid + silu * (1.0 - sigmoid))
                low_ref[0, :, here] = (grad_scaled_up * up_scaling).astype(BF)
                low_ref[1, :, here] = (grad_scaled * gate_scaling).astype(BF)
                up_grad_ref[:, here] = jnp.sum(grad_scaled_up * up, axis=0, keepdims=True)
                gate_grad_ref[:, here] = jnp.sum(grad_scaled * gate, axis=0, keepdims=True)
        for copy in copies:
            copy.wait()
        pieces = 2
        piece = width // pieces
        for j in range(pieces):
            total = None
            for i in range(4):
                term = back_matmul(
                    low_ref[i // 2, :, pl.ds((i % 2) * units, units)],
                    weights.matrix_rows(wide, i, j, pieces),
                )
                total = term if total is None else total + term
            columns = pl.ds(j * piece, piece)
            partial_ref[:, columns] = total
            turned_ref[pl.ds(0, own_rows), columns] = total[own_rows:].astype(BF)
            turned_ref[pl.ds(own_rows, own_rows), columns] = total[:own_rows].astype(BF)

    whole = pl.BlockSpec(memory_space=pltpu.VMEM)
    return pl.pallas_call(
        body,
        out_shape=[
            jax.ShapeDtypeStruct((2, rows, 2 * units), BF),
            jax.ShapeDtypeStruct((1, 2 * units), F32),
            jax.ShapeDtypeStruct((1, 2 * units), F32),
            jax.ShapeDtypeStruct((rows, width), F32),
            jax.ShapeDtypeStruct((rows, width), BF),
        ],
        in_specs=[whole] * 5 + weights.specs(),
        out_specs=[whole] * 5,
        scratch_shapes=weights.scratch(),
        compiler_params=pltpu.CompilerParams(vmem_limit_bytes=56 * 2**20),
        cost_estimate=pl.CostEstimate(
            flops=12 * rows * width * units, bytes_accessed=12 * width * units, transcendentals=rows * units * 2
        ),
        name="hidden_backward",
    )(
        down_low,
        up_proj,
        gate_proj,
        up_scale.reshape(1, -1),
        gate_scale.reshape(1, -1),
        *weights.arrays,
    )


def per_device(
    tokens,
    cotangent,
    lengths,
    placement,
    query_weight,
    key_weight,
    value_weight,
    out_weight,
    up_weight,
    gate_weight,
    down_weight,
    scoring,
    upscale,
    gatescale,
    attention_rate,
    feedforward_rate,
):
    size = lax.axis_size("fsdp")
    planes = size // 4
    half = lax.axis_index("grp")
    me = lax.axis_index("fsdp")
    core = me % 2
    side = (me // 2) % 2
    plane = me // 4
    local_seqs = tokens.shape[0] // size
    seq_len = tokens.shape[1] * size
    width = tokens.shape[2]
    own_rows = local_seqs * seq_len
    shard = query_weight.shape[0]
    hidden_shard = down_weight.shape[0]
    part = hidden_shard // 2
    half_width = width // 2

    def swap_core(array):
        return lax.ppermute(array, "fsdp", [(i, i ^ 1) for i in range(size)])

    def swap_side(array):
        return lax.ppermute(array, "fsdp", [(i, i ^ 2) for i in range(size)])

    def next_plane(array):
        return lax.ppermute(array, "fsdp", [(i, (i + 4) % size) for i in range(size)])

    def swap_half(array):
        return lax.ppermute(array, "grp", [(0, 1), (1, 0)])

    def pick(array, index, axis):
        return lax.dynamic_index_in_dim(array, index, axis, keepdims=False)

    def column_half(weight):
        return pick(weight.reshape(shard, 2, half_width), half, 1)

    def hidden_half(weight):
        blocks = weight.reshape(shard, planes, 2, 2, 2, part)
        mine = pick(blocks, half, 4)
        return jnp.transpose(mine, (0, 3, 2, 1, 4)).reshape(shard, -1)

    first_group = jnp.concatenate(
        [column_half(query_weight), column_half(key_weight), column_half(value_weight), out_weight],
        axis=1,
    )
    up_half = hidden_half(up_weight)
    gate_half = hidden_half(gate_weight)
    hidden_width = up_half.shape[1]
    core_width = hidden_width // 2
    second_group = jnp.concatenate(
        [
            up_half[:, :core_width],
            up_half[:, core_width:],
            gate_half[:, :core_width],
            gate_half[:, core_width:],
            pick(down_weight.reshape(2, part, width), half, 0),
        ]
    )
    cols = 3 * half_width
    held = [first_group]
    for _ in range(planes - 1):
        held.append(next_plane(held[-1]))
    held = held + [swap_side(array) for array in held]
    second_whole = lax.all_gather(after(second_group, *held), "fsdp", axis=0)
    held = held + [swap_core(array) for array in held]
    qkv_weight = jnp.zeros((size, shard, cols), BF)
    out_full = jnp.zeros((size, shard, width), BF)
    for i, array in enumerate(held):
        there_core = 1 - core if i >= 2 * planes else core
        there_side = 1 - side if i // planes % 2 else side
        there = ((plane - i) % planes * 2 + there_side) * 2 + there_core
        qkv_weight = lax.dynamic_update_index_in_dim(qkv_weight, array[:, :cols], there, 0)
        out_full = lax.dynamic_update_index_in_dim(out_full, array[:, cols:], there, 0)
    qkv_weight = qkv_weight.reshape(width, cols)
    out_full = out_full.reshape(width, width)

    local_len = tokens.shape[1]
    small = jnp.concatenate([scoring, attention_rate, feedforward_rate, upscale, gatescale])
    small = jnp.pad(small, (0, width - small.shape[0] % width))
    small_rows = small.shape[0] // width
    spread = jnp.zeros((tokens.shape[0], local_len, width), BF)
    spread = spread + jnp.pad(
        small.reshape(1, small_rows, width), ((0, 0), (0, local_len - small_rows), (0, 0))
    )
    both = jnp.stack([tokens, cotangent, spread])
    arrived = lax.all_to_all(both, "fsdp", split_axis=1, concat_axis=2, tiled=True)
    scale_float = arrived[2, 0].reshape(size, local_len * width).astype(F32)
    starts = [0, shard, 2 * shard, 3 * shard, 3 * shard + hidden_shard, 3 * shard + 2 * hidden_shard]
    scale_parts = [scale_float[:, starts[i] : starts[i + 1]].reshape(-1) for i in range(5)]
    scoring_half = lax.dynamic_slice_in_dim(scale_parts[0], half * half_width, half_width)
    attention_mix = scale_parts[1]
    feed_mix = scale_parts[2]

    def hidden_scale(columns):
        blocks = columns.reshape(planes, 2, 2, 2, part)
        return jnp.transpose(pick(blocks, half, 3), (2, 1, 0, 3)).reshape(-1)

    up_scale = hidden_scale(scale_parts[3])
    gate_scale = hidden_scale(scale_parts[4])

    group_order = placement[0]
    own_slots = lax.dynamic_slice_in_dim(group_order, me * local_seqs, local_seqs)
    own_lengths = jnp.take(lengths[0], own_slots)
    valid = (jnp.arange(seq_len, dtype=jnp.int32)[None, :] < own_lengths[:, None]).reshape(
        own_rows, 1
    )
    own_tokens = arrived[0].reshape(own_rows, width)
    own_cot = jnp.where(valid, arrived[1].reshape(own_rows, width), jnp.zeros((), BF))
    token_rows = jnp.concatenate([own_tokens, swap_half(own_tokens)])
    cot_rows = jnp.concatenate([own_cot, swap_half(own_cot)])

    def turned(array):
        return jnp.concatenate([array[own_rows:], array[:own_rows]])

    token_float = token_rows.astype(F32)
    qkv = matmul(token_rows, qkv_weight)
    query_unit, key_unit, value_low, mixed_half = attention_forward(qkv, scoring_half, seq_len)
    mixed_other = swap_half(turned(mixed_half))
    mixed_low = jnp.where(
        half == 0,
        jnp.concatenate([mixed_half, mixed_other], axis=1),
        jnp.concatenate([mixed_other, mixed_half], axis=1),
    )
    attended = matmul(mixed_low, out_full)
    first_state = residual_mix(token_float, attended, attention_mix)
    first_low = first_state.astype(BF)
    feature = jnp.arange(width, dtype=jnp.int32)
    block = []
    for b in range(2):
        for a in range(2):
            for k in range(planes):
                there_core = core if b == 0 else 1 - core
                there_side = 1 - side if a == 0 else side
                block.append((k * 2 + there_side) * 2 + there_core)
    block = jnp.stack(block).astype(jnp.int32)
    wanted = (block[:, None] * shard + jnp.arange(shard, dtype=jnp.int32)[None, :]).reshape(-1)
    chooser = (feature[:, None] == wanted[None, :]).astype(BF)

    def share(array, axis=0):
        return jnp.concatenate([array, swap_core(array)], axis=axis)

    def share_columns(array):
        chosen = matmul(array, chooser).astype(BF)
        both_cores = jnp.concatenate([chosen[:, :half_width], swap_core(chosen[:, half_width:])])
        return both_cores[:, : half_width // 2], both_cores[:, half_width // 2 :]

    def scatter(kept, arrived_blocks):
        total = (kept.astype(F32) + arrived_blocks.astype(F32)).astype(BF)
        return lax.psum_scatter(
            total.reshape(planes, kept.shape[0] // planes, kept.shape[1]),
            "fsdp",
            scatter_dimension=0,
            axis_index_groups=[[k * 4 + j for k in range(planes)] for j in range(4)],
        ).astype(F32)

    def grads(sides, columns):
        return [weight_grad(one, columns).astype(BF) for one in sides]

    token_sides = share_columns(token_rows)
    mixed_sides = share_columns(mixed_low)
    first_sides = share_columns(first_low)
    hidden_weights = HiddenWeights(
        after(second_whole, *token_sides, *mixed_sides, *first_sides), planes, shard, part
    )
    hidden_low, up_proj, gate_proj, partial, partial_turned = hidden_forward(
        first_low, hidden_weights, up_scale, gate_scale, own_rows
    )
    down_proj = partial + swap_half(partial_turned).astype(F32)

    feed_rows = jnp.broadcast_to(feed_mix, down_proj.shape)
    second, pullback = jax.vjp(residual_mix, first_state, down_proj, feed_rows)
    layer_own = jnp.where(valid, second[:own_rows], 0.0).astype(BF)
    grad_first, grad_down, feed_grad = pullback(cot_rows.astype(F32))
    feed_grad = jnp.sum(feed_grad[:own_rows], axis=0)
    down_low = grad_down.astype(BF)
    hidden_both = jnp.concatenate(
        [pick(hidden_low, core, 0), swap_core(pick(hidden_low, 1 - core, 0))]
    ).reshape(-1, 2, core_width // 2)
    down_sent, down_kept = grads(
        (pick(hidden_both, 1 - side, 1), pick(hidden_both, side, 1)), share(down_low)
    )
    down_arrived = swap_side(down_sent)
    down_low = after(down_low, down_sent)
    up_gate_low, upscale_grad, gatescale_grad, partial, partial_turned = hidden_backward(
        down_low, up_proj, gate_proj, hidden_weights, up_scale, gate_scale, own_rows
    )
    up_gate_both = share(up_gate_low, 1)
    partial_other = swap_half(partial_turned)
    up_sent, up_kept = grads(first_sides, up_gate_both[0])
    gate_sent, gate_kept = grads(first_sides, up_gate_both[1])
    partial_other, up_sent, gate_sent = lax.optimization_barrier(
        (partial_other, up_sent, gate_sent)
    )
    up_arrived = swap_side(after(up_sent, down_arrived))
    gate_arrived = swap_side(after(gate_sent, up_arrived))
    grad_first = grad_first + partial + partial_other.astype(F32)
    attention_rows = jnp.broadcast_to(attention_mix, attended.shape)
    _, pullback = jax.vjp(residual_mix, token_float, attended, attention_rows)
    grad_tokens, grad_attended, attention_grad = pullback(grad_first)
    attention_grad = jnp.sum(attention_grad[:own_rows], axis=0)
    attended_low = grad_attended.astype(BF)
    out_half = pick(out_full.reshape(2, half_width, width), half, 0)
    grad_mixed = back_matmul(attended_low, out_half).astype(BF)
    attended_cols = pick(attended_low.reshape(-1, 2, half_width), half, 1)
    out_sent, out_kept = grads(mixed_sides, share(attended_cols))
    grad_mixed, out_sent = lax.optimization_barrier((grad_mixed, out_sent))
    out_arrived = swap_side(after(out_sent, up_arrived))
    qkv_low, scoring_grad = attention_backward(
        grad_mixed, qkv, query_unit, key_unit, value_low, scoring_half, seq_len
    )
    scoring_grad = scoring_grad[0]
    qkv_both = share(qkv_low, 1)
    token_partial = sum(
        back_matmul(qkv_low[j], qkv_weight[:, j * half_width : (j + 1) * half_width])
        for j in range(3)
    )
    input_other = swap_half(token_partial[own_rows:].astype(BF))
    qkv_pairs = [grads(token_sides, qkv_both[j]) for j in range(3)]
    qkv_sent = jnp.concatenate([pair[0] for pair in qkv_pairs], axis=1)
    qkv_kept = jnp.concatenate([pair[1] for pair in qkv_pairs], axis=1)
    input_other, qkv_sent = lax.optimization_barrier((input_other, qkv_sent))
    qkv_arrived = swap_side(after(qkv_sent, gate_arrived))
    input_own = (
        grad_tokens[:own_rows] + token_partial[:own_rows] + input_other.astype(F32)
    ).astype(BF)
    outgoing = jnp.stack([layer_own, input_own]).reshape(2, local_seqs, seq_len, width)
    returned = lax.all_to_all(outgoing, "fsdp", split_axis=2, concat_axis=1, tiled=True)
    down_total = scatter(down_kept, after(down_arrived, partial_other))
    up_total = scatter(up_kept, after(up_arrived, qkv_low))
    gate_total = scatter(gate_kept, after(gate_arrived, qkv_sent))
    out_total = scatter(out_kept, out_arrived)
    qkv_total = scatter(qkv_kept, qkv_arrived)

    low_planes = planes // 2

    def hidden_whole(total):
        blocks = total.reshape(shard, 4, 2, low_planes * part)
        theirs = swap_half(pick(blocks, 1 - half, 2).astype(BF)).astype(F32)
        mine = pick(blocks, half, 2)
        stacked = jnp.where(
            half == 0, jnp.stack([mine, theirs], axis=2), jnp.stack([theirs, mine], axis=2)
        )
        blocks = stacked.reshape(shard, 2, 2, 2, low_planes, part)
        return jnp.transpose(blocks, (0, 4, 2, 1, 3, 5)).reshape(shard, -1)

    up_out = hidden_whole(up_total)
    gate_out = hidden_whole(gate_total)
    down_cols = down_total.reshape(part, 2, half_width)
    mine = pick(down_cols, half, 1)
    theirs = swap_half(pick(down_cols, 1 - half, 1).astype(BF)).astype(F32)
    down_out = jnp.where(
        half == 0, jnp.concatenate([mine, theirs]), jnp.concatenate([theirs, mine])
    )

    def hidden_spread(grad):
        blocks = jnp.transpose(grad.reshape(2, 2, planes, part), (2, 1, 0, 3))
        blank = jnp.zeros_like(blocks)
        both_halves = jnp.where(
            half == 0, jnp.stack([blocks, blank], axis=3), jnp.stack([blank, blocks], axis=3)
        )
        return both_halves.reshape(size, hidden_shard)

    scoring_spread = jnp.where(
        half == 0,
        jnp.concatenate([scoring_grad, jnp.zeros_like(scoring_grad)]),
        jnp.concatenate([jnp.zeros_like(scoring_grad), scoring_grad]),
    )
    small = jnp.concatenate(
        [
            scoring_spread.reshape(size, shard),
            attention_grad.reshape(size, shard),
            feed_grad.reshape(size, shard),
            hidden_spread(upscale_grad[0]),
            hidden_spread(gatescale_grad[0]),
        ],
        axis=1,
    ).reshape(planes, 2, 2, -1)
    small = pick(small, core, 2) + swap_core(pick(small, 1 - core, 2))
    small = pick(small, side, 1) + swap_side(pick(small, 1 - side, 1))
    order = [(plane - 1 - k) % planes for k in range(planes)]
    total = pick(small, order[0], 0)
    for k in range(1, planes):
        total = pick(small, order[k], 0) + next_plane(total)
    total = total + swap_half(total)

    return (
        returned[0],
        returned[1],
        qkv_total[:, :half_width],
        qkv_total[:, half_width : 2 * half_width],
        qkv_total[:, 2 * half_width :],
        out_total,
        up_out,
        gate_out,
        down_out,
        total[:shard],
        total[3 * shard : 3 * shard + hidden_shard],
        total[3 * shard + hidden_shard :],
        total[shard : 2 * shard],
        total[2 * shard : 3 * shard],
    )


def solution(mesh):
    rows = P("grp", "fsdp", None)
    group = P("grp", None)
    matrix = P("fsdp", None)
    vector = P("fsdp")
    split = P("fsdp", "grp")
    return jax.shard_map(
        per_device,
        mesh=mesh,
        in_specs=(rows, rows, group, group) + (matrix,) * 7 + (vector,) * 5,
        out_specs=(rows, rows) + (split,) * 7 + (vector,) * 5,
        check_vma=False,
    )
```

```python
import math

import jax
import jax.numpy as jnp
from jax import lax
from jax.experimental import pallas as pl
from jax.experimental.pallas import tpu as pltpu
from jax.sharding import PartitionSpec as P

H = 20
DK = 64
BF = jnp.bfloat16
F32 = jnp.float32
COST = pl.CostEstimate(flops=1000, bytes_accessed=1000, transcendentals=0)


def swiglu(up_proj, gate_proj, upscale, gatescale):
    scaled = gatescale * gate_proj
    return scaled * jax.nn.sigmoid(scaled) * (upscale * up_proj)


def matmul(left_side, right_side):
    return jnp.dot(left_side, right_side, preferred_element_type=F32)


def weight_grad(left_side, right_side):
    return lax.dot_general(
        left_side, right_side, (((0,), (0,)), ((), ())), preferred_element_type=F32
    )


def back_matmul(grad_rows, weight_rows):
    return lax.dot_general(
        grad_rows, weight_rows, (((1,), (1,)), ((), ())), preferred_element_type=F32
    )


def after(value, *earlier):
    return lax.optimization_barrier((value, *earlier))[0]


def like(*shape, dtype=BF):
    return jax.ShapeDtypeStruct(shape, dtype)


def call(name, body, outs, scalars=(), arrays=(), remote=(), scratch=(), earlier=()):
    counts = (len(scalars), len(arrays), len(remote), len(earlier), len(outs))

    def kernel(*refs):
        groups = []
        at = 0
        for count in counts:
            groups.append(refs[at : at + count])
            at += count
        body(*groups[0], *groups[1], groups[2], *groups[4], *refs[at:])

    whole = pl.BlockSpec(memory_space=pltpu.VMEM)
    kept = pl.BlockSpec(memory_space=pl.ANY)
    return pl.pallas_call(
        kernel,
        out_shape=list(outs),
        in_specs=[pl.BlockSpec(memory_space=pltpu.SMEM)] * counts[0]
        + [whole] * counts[1]
        + [kept] * (counts[2] + counts[3]),
        out_specs=[whole] * counts[4],
        scratch_shapes=list(scratch),
        compiler_params=pltpu.CompilerParams(vmem_limit_bytes=56 * 2**20),
        cost_estimate=COST,
        name=name,
    )(*scalars, *arrays, *remote, *earlier)


class Shards:
    def __init__(self, arrays, places):
        self.direct = arrays[0].shape[0] % 16 == 0
        if self.direct:
            self.arrays, self.places = list(arrays), places
        else:
            whole = jnp.zeros((len(arrays),) + arrays[0].shape, BF)
            for i, array in enumerate(arrays):
                whole = lax.dynamic_update_index_in_dim(whole, array, places[i], 0)
            self.arrays = [whole.reshape(-1, arrays[0].shape[1])]
            self.places = jnp.zeros((1,), jnp.int32)
        self.count = len(self.arrays)
        self.height = self.arrays[0].shape[0]

    def scratch(self, width):
        return [
            pltpu.VMEM((self.count, self.height, width), BF),
            pltpu.SemaphoreType.DMA((self.count,)),
        ]

    def copies(self, places, sources, target, sems, begin, width):
        return [
            pltpu.make_async_copy(
                sources[i].at[:, pl.ds(begin, width)], target.at[places[i]], sems.at[i]
            )
            for i in range(self.count)
        ]

    def columns(self, target, begin, width):
        return target[:, :, pl.ds(begin, width)].reshape(self.count * self.height, width)

    def rows(self, target, index, parts, begin, width):
        if self.direct:
            step = self.count // parts
            rows = target[pl.ds(index * step, step), :, pl.ds(begin, width)]
        else:
            step = self.height // parts
            rows = target[:, pl.ds(pl.multiple_of(index * step, step), step), pl.ds(begin, width)]
        return rows.reshape(-1, width)


def inverse_rms(vector):
    return lax.rsqrt(jnp.mean(vector * vector, axis=-1, keepdims=True) + 1e-06)


def head_sums(values, low_head):
    low_sum = jnp.sum(jnp.where(low_head, values, 0.0), axis=-1, keepdims=True)
    high_sum = jnp.sum(jnp.where(low_head, 0.0, values), axis=-1, keepdims=True)
    return low_sum, high_sum


def head_inverse(vector, low_head):
    low_sum, high_sum = head_sums(vector * vector, low_head)
    return jnp.where(low_head, lax.rsqrt(low_sum + 1e-06), lax.rsqrt(high_sum + 1e-06))


def head_probs(query_head, key_unit, seq_len):
    scores = back_matmul(query_head, key_unit) * math.sqrt(DK)
    query_row = lax.broadcasted_iota(jnp.int32, scores.shape, 0)
    key_row = lax.broadcasted_iota(jnp.int32, scores.shape, 1)
    start = query_row - lax.rem(query_row, seq_len)
    scores = jnp.where((key_row <= query_row) & (key_row >= start), scores, -1e30)
    exp_scores = jnp.exp(scores - jnp.max(scores, axis=-1, keepdims=True))
    return exp_scores / jnp.sum(exp_scores, axis=-1, keepdims=True)


def only(mask, values):
    return jnp.where(mask, values.astype(F32), 0.0).astype(BF)


def turn(ref, rows, columns, value):
    ref[pl.ds(0, rows), columns] = value[rows:].astype(BF)
    ref[pl.ds(rows, rows), columns] = value[:rows].astype(BF)


def attention_forward(half, token_rows, shards, seq_len):
    rows, width = token_rows.shape
    half_width = width // 2
    pairs = half_width // 128
    cols = 3 * half_width + 128

    def body(
        places, half_ref, x_ref, sources, qkv_ref, qu_ref, ku_ref, vl_ref, mixed_ref, turned_ref, scale_ref, w_ref, sems
    ):
        copies = shards.copies(places, sources, w_ref, sems, 0, cols)
        for copy in copies:
            copy.start()
        for copy in copies:
            copy.wait()
        scale_ref[...] = jnp.transpose(
            shards.columns(w_ref, 3 * half_width, 128).astype(F32)
        )[:16]
        x = x_ref[...]
        step = 384
        for begin in range(0, 3 * half_width, step):
            qkv_ref[:, pl.ds(begin, step)] = matmul(x, shards.columns(w_ref, begin, step))
        low_head = lax.broadcasted_iota(jnp.int32, (rows, 128), 1) < DK
        later = half_ref[0] == 1

        def pair(i, carry):
            at = pl.multiple_of(i * 128, 128)
            here = pl.ds(at, 128)
            queries = qkv_ref[:, here]
            key_rows = qkv_ref[:, pl.ds(half_width + at, 128)]
            value_low = qkv_ref[:, pl.ds(2 * half_width + at, 128)].astype(BF)
            scaling = jnp.where(
                later, scale_ref[0:1, pl.ds(half_width + at, 128)], scale_ref[0:1, here]
            )
            query_unit = queries * head_inverse(queries, low_head) * scaling
            key_unit = (key_rows * head_inverse(key_rows, low_head) * scaling).astype(BF)
            mixed = None
            for mask in (low_head, ~low_head):
                probs = head_probs(only(mask, query_unit), key_unit, seq_len)
                head = matmul(probs.astype(BF), value_low)
                mixed = head if mixed is None else jnp.where(low_head, mixed, head)
            qu_ref[:, here] = query_unit.astype(BF)
            ku_ref[:, here] = key_unit
            vl_ref[:, here] = value_low
            mixed_ref[:, here] = mixed.astype(BF)
            turn(turned_ref, rows // 2, here, mixed)
            return carry

        lax.fori_loop(0, pairs, pair, 0)

    return call(
        "attention_forward",
        body,
        [like(rows, 3 * half_width, dtype=F32)] + [like(rows, half_width)] * 5 + [like(16, width, dtype=F32)],
        scalars=[shards.places, half],
        arrays=[token_rows],
        remote=shards.arrays,
        scratch=shards.scratch(cols),
    )


def place_halves(half_ref, target, own, other):
    width = own.shape[1]

    @pl.when(half_ref[0] == 0)
    def _():
        target[:, pl.ds(0, width)] = own[...]
        target[:, pl.ds(width, width)] = other[...]

    @pl.when(half_ref[0] != 0)
    def _():
        target[:, pl.ds(0, width)] = other[...]
        target[:, pl.ds(width, width)] = own[...]


def first_forward(half, mixed, mixed_other, token_rows, attention_mix, shards, skip):
    rows, width = token_rows.shape

    def body(
        places, half_ref, own_ref, other_ref, x_ref, mix_ref, sources, mixed_ref, attended_ref, first_ref, low_ref, w_ref, sems
    ):
        copies = shards.copies(places, sources, w_ref, sems, skip, width)
        for copy in copies:
            copy.start()
        place_halves(half_ref, mixed_ref, own_ref, other_ref)
        for copy in copies:
            copy.wait()
        for begin in range(0, width, 256):
            attended_ref[:, pl.ds(begin, 256)] = matmul(
                mixed_ref[...], shards.columns(w_ref, begin, 256)
            )
        x = x_ref[...].astype(F32)
        attended = attended_ref[...]
        mix = x + mix_ref[...] * (attended * inverse_rms(attended) - x)
        first = mix * inverse_rms(mix)
        first_ref[...] = first
        low_ref[...] = first.astype(BF)

    return call(
        "first_forward",
        body,
        [like(rows, width)] + [like(rows, width, dtype=F32)] * 2 + [like(rows, width)],
        scalars=[shards.places, half],
        arrays=[mixed, mixed_other, token_rows, attention_mix],
        remote=shards.arrays,
        scratch=shards.scratch(width),
    )


def mix_backward(base, branch, rate, grad):
    branch_inverse = inverse_rms(branch)
    branch_unit = branch * branch_inverse
    mix = base + rate * (branch_unit - base)
    inverse = inverse_rms(mix)
    value = mix * inverse
    grad_mix = inverse * (grad - value * jnp.mean(grad * value, axis=-1, keepdims=True))
    grad_unit = grad_mix * rate
    grad_branch = branch_inverse * (
        grad_unit - branch_unit * jnp.mean(grad_unit * branch_unit, axis=-1, keepdims=True)
    )
    return value, grad_mix - grad_unit, grad_branch, grad_mix * (branch_unit - base)


def second_backward(partial, partial_other, first_state, cot, cot_other, valid, feed_mix):
    rows, width = partial.shape
    own = rows // 2

    def body(partial_ref, other_ref, first_ref, cot_ref, cot_other_ref, valid_ref, mix_ref, _, layer_ref, grad_ref, low_ref, rate_ref):
        for begin in (0, own):
            here = pl.ds(begin, own)
            down = partial_ref[here, :] + other_ref[here, :].astype(F32)
            grad = (cot_ref if begin == 0 else cot_other_ref)[...].astype(F32)
            value, grad_first, grad_down, grad_rate = mix_backward(
                first_ref[here, :], down, mix_ref[...], grad
            )
            grad_ref[here, :] = grad_first
            low_ref[here, :] = grad_down.astype(BF)
            if begin == 0:
                layer_ref[...] = (value * valid_ref[...]).astype(BF)
                rate_ref[...] = jnp.sum(grad_rate, axis=0, keepdims=True)

    return call(
        "second_backward",
        body,
        [like(own, width), like(rows, width, dtype=F32), like(rows, width), like(1, width, dtype=F32)],
        arrays=[partial, partial_other, first_state, cot, cot_other, valid, feed_mix],
    )


def first_backward(half, grad_first, partial, partial_other, token_rows, attended, attention_mix, shards, skip, earlier):
    rows, width = partial.shape
    own = rows // 2
    half_width = width // 2

    def body(
        places, half_ref, grad_ref, partial_ref, other_ref, x_ref, attended_ref, mix_ref, sources, cols_ref, mixed_ref, token_ref, rate_ref, low_ref, w_ref, sems
    ):
        copies = shards.copies(places, sources, w_ref, sems, skip, width)
        for copy in copies:
            copy.start()
        for begin in (0, own):
            here = pl.ds(begin, own)
            grad = grad_ref[here, :] + partial_ref[here, :] + other_ref[here, :].astype(F32)
            _, grad_token, grad_attended, grad_rate = mix_backward(
                x_ref[here, :].astype(F32), attended_ref[here, :], mix_ref[...], grad
            )
            low_ref[here, :] = grad_attended.astype(BF)
            if begin == 0:
                token_ref[...] = grad_token
                rate_ref[...] = jnp.sum(grad_rate, axis=0, keepdims=True)
        at = pl.multiple_of(half_ref[0] * half_width, 128)
        cols_ref[...] = low_ref[:, pl.ds(at, half_width)]
        for copy in copies:
            copy.wait()
        mixed_ref[...] = back_matmul(
            low_ref[...], shards.rows(w_ref, half_ref[0], 2, 0, width)
        ).astype(BF)

    return call(
        "first_backward",
        body,
        [like(rows, half_width)] * 2 + [like(own, width, dtype=F32), like(1, width, dtype=F32)],
        scalars=[shards.places, half],
        arrays=[grad_first, partial, partial_other, token_rows, attended, attention_mix],
        remote=shards.arrays,
        scratch=[pltpu.VMEM((rows, width), BF)] + shards.scratch(width),
        earlier=earlier,
    )


def attention_backward(half, grad_mixed, qkv, query_unit, key_unit, value_low, scales, shards, seq_len, earlier):
    rows, half_width = grad_mixed.shape
    width = 2 * half_width
    pairs = half_width // 128
    own = rows // 2

    def body(
        places, half_ref, gm_ref, qkv_ref, qu_ref, ku_ref, vl_ref, scale_ref, sources, grads_ref, scoring_ref, own_ref, other_ref, w_ref, sems
    ):
        copies = shards.copies(places, sources, w_ref, sems, 0, 3 * half_width)
        for copy in copies:
            copy.start()
        low_head = lax.broadcasted_iota(jnp.int32, (rows, 128), 1) < DK
        later = half_ref[0] == 1

        def pair(i, carry):
            at = pl.multiple_of(i * 128, 128)
            here = pl.ds(at, 128)
            query_unit = qu_ref[:, here]
            key_unit = ku_ref[:, here]
            value_low = vl_ref[:, here]
            scaling = jnp.where(
                later, scale_ref[0:1, pl.ds(half_width + at, 128)], scale_ref[0:1, here]
            )
            grad_value = grad_qunit = grad_kunit = None
            for mask in (low_head, ~low_head):
                probs = head_probs(only(mask, query_unit), key_unit, seq_len)
                grad_head = only(mask, gm_ref[:, here])
                value_part = weight_grad(probs.astype(BF), grad_head)
                grad_probs = back_matmul(grad_head, value_low)
                grad_scores = (
                    probs * (grad_probs - jnp.sum(grad_probs * probs, axis=-1, keepdims=True))
                ).astype(BF)
                query_part = matmul(grad_scores, key_unit)
                key_part = weight_grad(grad_scores, query_unit)
                if grad_value is None:
                    grad_value, grad_qunit, grad_kunit = value_part, query_part, key_part
                else:
                    grad_value = grad_value + value_part
                    grad_qunit = jnp.where(low_head, grad_qunit, query_part)
                    grad_kunit = jnp.where(low_head, grad_kunit, key_part)
            scoring_grad = None
            for place, grad in ((0, grad_qunit), (1, grad_kunit)):
                raw = qkv_ref[:, pl.ds(place * half_width + at, 128)]
                grad = grad * math.sqrt(DK)
                inverse = head_inverse(raw, low_head)
                unit = raw * inverse
                term = jnp.sum(grad * unit, axis=0, keepdims=True)
                scoring_grad = term if scoring_grad is None else scoring_grad + term
                grad = grad * scaling
                low_sum, high_sum = head_sums(grad * unit, low_head)
                grads_ref[place, :, here] = (
                    inverse * (grad - unit * jnp.where(low_head, low_sum, high_sum))
                ).astype(BF)
            grads_ref[2, :, here] = grad_value.astype(BF)
            scoring_ref[:, here] = scoring_grad
            return carry

        lax.fori_loop(0, pairs, pair, 0)
        for copy in copies:
            copy.wait()
        for piece in range(2):
            total = None
            for j in range(3):
                term = back_matmul(
                    grads_ref[j], shards.rows(w_ref, piece, 2, j * half_width, half_width)
                )
                total = term if total is None else total + term
            columns = pl.ds(piece * half_width, half_width)
            own_ref[:, columns] = total[:own]
            other_ref[:, columns] = total[own:].astype(BF)

    return call(
        "attention_backward",
        body,
        [
            like(3, rows, half_width),
            like(1, half_width, dtype=F32),
            like(own, width, dtype=F32),
            like(own, width),
        ],
        scalars=[shards.places, half],
        arrays=[grad_mixed, qkv, query_unit, key_unit, value_low, scales],
        remote=shards.arrays,
        scratch=shards.scratch(3 * half_width),
        earlier=earlier,
    )


def down_grads(which, hidden, hidden_other, down, down_other, kept, earlier):
    rows, units = hidden_other.shape
    width = down.shape[1]
    block = units // 2

    def body(which_ref, hidden_ref, hidden_other_ref, down_ref, down_other_ref, _, *out_refs):
        side = which_ref[1] if kept else 1 - which_ref[1]
        columns = pl.ds(pl.multiple_of(side * block, 128), block)
        own = hidden_ref[which_ref[0], :, columns]
        other = hidden_other_ref[:, columns]
        for begin in range(0, width, 256):
            here = pl.ds(begin, 256)
            total = weight_grad(own, down_ref[:, here]) + weight_grad(other, down_other_ref[:, here])
            if kept:
                out_refs[0][:, here] = total
            else:
                for i, out_ref in enumerate(out_refs):
                    out_ref[:, here] = total[i * (block // 2) : (i + 1) * (block // 2)].astype(BF)

    return call(
        "down_kept" if kept else "down_sent",
        body,
        [like(block, width, dtype=F32)] if kept else [like(block // 2, width)] * 2,
        scalars=[which],
        arrays=[hidden, hidden_other, down, down_other],
        earlier=earlier,
    )


def side_grads(name, lefts, rights, kept, earlier):
    block = lefts[0][0].shape[1] // 2
    number = len(lefts)
    total_width = sum(right[0].shape[-1] * len(right[2] or (0,)) for right in rights)

    def body(*refs):
        refs = [ref for ref in refs if not isinstance(ref, tuple)]
        out_ref = refs[-1]
        begin = 0
        for i in range(number):
            own_ref, other_ref, right_ref, right_other_ref = refs[4 * i : 4 * i + 4]
            columns = pl.ds(block if kept else 0, block)
            own = own_ref[:, columns]
            other = other_ref[:, columns]
            for index in rights[i][2] or (None,):
                for at in range(0, right_ref.shape[-1], 640):
                    here = (slice(None), pl.ds(at, 640))
                    if index is not None:
                        here = (index, *here)
                    total = weight_grad(own, right_ref[here]) + weight_grad(other, right_other_ref[here])
                    out_ref[:, pl.ds(begin, 640)] = total.astype(out_ref.dtype)
                    begin += 640

    arrays = []
    for left, right in zip(lefts, rights):
        arrays += [*left, *right[:2]]
    return call(
        name,
        body,
        [like(block, total_width, dtype=F32 if kept else BF)],
        arrays=arrays,
        earlier=earlier,
    )[0]


def join(name, kept, arrived, by_rows, earlier):
    rows, width = kept.shape

    def body(kept_ref, *refs):
        out_ref = refs[-1]
        begin = 0
        for ref in refs[:-1]:
            if isinstance(ref, tuple):
                continue
            step = ref.shape[0] if by_rows else ref.shape[1]
            here = (pl.ds(begin, step), slice(None)) if by_rows else (slice(None), pl.ds(begin, step))
            out_ref[here] = (kept_ref[here] + ref[...].astype(F32)).astype(BF)
            begin += step

    return call(name, body, [like(rows, width)], arrays=[kept, *arrived], earlier=earlier)[0]


def lay_first(half, query_weight, key_weight, value_weight, out_weight, scales):
    shard, width = query_weight.shape
    half_width = width // 2

    def body(half_ref, q_ref, k_ref, v_ref, out_ref, *refs):
        target, square = refs[-2:]
        for i, ref in enumerate((q_ref, k_ref, v_ref)):
            place = pl.ds(i * half_width, half_width)

            @pl.when(half_ref[0] == 0)
            def _():
                target[:, place] = ref[:, pl.ds(0, half_width)]

            @pl.when(half_ref[0] != 0)
            def _():
                target[:, place] = ref[:, pl.ds(half_width, half_width)]

        square[...] = jnp.zeros_like(square)
        row = 0
        for ref in refs[: len(scales)]:
            values = ref[...].astype(F32)
            for begin in range(0, values.shape[1], shard):
                square[pl.ds(row, 1), pl.ds(0, shard)] = values[:, begin : begin + shard]
                row += 1
        target[:, pl.ds(3 * half_width, 128)] = jnp.transpose(square[...])[:shard].astype(BF)
        target[:, pl.ds(3 * half_width + 128, width)] = out_ref[...]

    return call(
        "lay_first",
        body,
        [like(shard, 3 * half_width + 128 + width)],
        scalars=[half],
        arrays=[query_weight, key_weight, value_weight, out_weight]
        + [scale.reshape(1, -1) for scale in scales],
        scratch=[pltpu.VMEM((128, 128), F32)],
    )[0]


def split_hidden(half, totals, planes, part):
    shard, width = totals[0].shape
    run = planes // 2 * part

    def body(half_ref, *refs):
        for source, target in zip(refs[: len(totals)], refs[-len(totals) :]):
            for i in range(4):
                begin = 2 * i * run
                first, later = source[:, begin : begin + run], source[:, begin + run : begin + 2 * run]
                target[:, i * run : (i + 1) * run] = jnp.where(
                    half_ref[0] == 0, later.astype(F32), first.astype(F32)
                ).astype(BF)

    return call(
        "split_hidden",
        body,
        [like(shard, width // 2)] * len(totals),
        scalars=[half],
        arrays=totals,
    )


def merge_hidden(half, totals, others, planes, part):
    shard, width = totals[0].shape
    run = planes // 2 * part

    def body(half_ref, *refs):
        number = len(totals)
        upper = half_ref[0] != 0
        for own_ref, other_ref, target in zip(refs[:number], refs[number : 2 * number], refs[-number:]):
            for plane in range(planes // 2):
                for side in range(2):
                    for core in range(2):
                        i = core * 2 + side
                        begin = 2 * i * run + plane * part
                        own = jnp.where(
                            upper,
                            own_ref[:, begin + run : begin + run + part].astype(F32),
                            own_ref[:, begin : begin + part].astype(F32),
                        )
                        begin = i * run + plane * part
                        other = other_ref[:, begin : begin + part].astype(F32)
                        begin = ((plane * 2 + side) * 2 + core) * 2 * part
                        target[:, begin : begin + part] = jnp.where(upper, other, own)
                        target[:, begin + part : begin + 2 * part] = jnp.where(upper, own, other)

    return call(
        "merge_hidden",
        body,
        [like(shard, width, dtype=F32)] * len(totals),
        scalars=[half],
        arrays=[*totals, *others],
    )


class HiddenWeights:
    def __init__(self, gathered, planes, shard, part):
        width = gathered.shape[2]
        units = 2 * planes * part
        self.direct = shard % 16 == 0 and part % 16 == 0
        self.width, self.units, self.shard, self.part = width, units, shard, part
        if self.direct:
            self.arrays = [gathered.reshape(planes, 2, 2, -1, width)]
            self.matrix = (planes, 2, 2, shard, units)
            self.down = (planes, part, width)
        else:
            blocks = gathered[:, 4 * shard :].reshape(planes, 2, 2, part, width)
            self.arrays = [
                jnp.stack(
                    [gathered[:, i * shard : (i + 1) * shard].reshape(width, width) for i in range(4)]
                ),
                jnp.transpose(blocks, (2, 1, 0, 3, 4)).reshape(2, 2, planes * part, width),
            ]
            self.matrix = (width, units)
            self.down = (planes * part, width)

    def scratch(self):
        return [
            pltpu.VMEM((4,) + self.matrix, BF),
            pltpu.VMEM((2, 2) + self.down, BF),
            pltpu.SemaphoreType.DMA((8,)),
        ]

    def specs(self):
        return [pl.BlockSpec(memory_space=pl.ANY)] * len(self.arrays)

    def matrix_copy(self, sources, wide, sems, i):
        if self.direct:
            source = sources[0].at[:, :, :, pl.ds(i * self.shard, self.shard), :]
        else:
            source = sources[0].at[i]
        return pltpu.make_async_copy(source, wide.at[i], sems.at[i])

    def down_copy(self, sources, tall, sems, core, side):
        if self.direct:
            source = sources[0].at[:, side, core, pl.ds(4 * self.shard, self.part), :]
        else:
            source = sources[1].at[core, side]
        return pltpu.make_async_copy(source, tall.at[core, side], sems.at[4 + core * 2 + side])

    def matrix_value(self, wide, i, columns):
        if self.direct:
            return wide[i, :, :, :, :, columns].reshape(self.width, -1)
        return wide[i, :, columns]

    def matrix_rows(self, wide, i, j, parts):
        if self.direct:
            step = self.matrix[0] // parts
            return wide[i, pl.ds(j * step, step)].reshape(self.width // parts, -1)
        step = self.width // parts
        return wide[i, pl.ds(j * step, step)]

    def down_value(self, tall, core, side, columns):
        if self.direct:
            return tall[core, side, :, :, columns].reshape(-1, columns.size)
        return tall[core, side, :, columns]

    def down_rows(self, tall, core, side):
        return tall[core, side].reshape(-1, self.width)


def hidden_forward(first_low, weights, up_scale, gate_scale, own_rows):
    rows, width = first_low.shape
    units = weights.units
    block = units // 2
    step = 256

    def body(first_ref, up_scale_ref, gate_scale_ref, *refs):
        sources = refs[: len(weights.arrays)]
        hidden_ref, up_ref, gate_ref, partial_ref, turned_ref, wide, tall, sems = refs[
            len(weights.arrays) :
        ]
        copies = [weights.matrix_copy(sources, wide, sems, i) for i in (0, 2, 1, 3)]
        down_copies = [
            weights.down_copy(sources, tall, sems, i, j) for i in range(2) for j in range(2)
        ]
        for copy in copies + down_copies:
            copy.start()
        first = first_ref[...]
        for core in range(2):
            copies[2 * core].wait()
            copies[2 * core + 1].wait()

            for begin in range(0, units, step):
                columns = pl.ds(begin, step)
                here = pl.ds(core * units + begin, step)
                up = matmul(first, weights.matrix_value(wide, core, columns))
                gate = matmul(first, weights.matrix_value(wide, 2 + core, columns))
                up_ref[:, here] = up
                gate_ref[:, here] = gate
                hidden = swiglu(up, gate, up_scale_ref[:, here], gate_scale_ref[:, here])
                hidden_ref[core, :, columns] = hidden.astype(BF)
        for copy in down_copies:
            copy.wait()

        for begin in range(0, width, step):
            columns = pl.ds(begin, step)
            total = None
            for core in range(2):
                for side in range(2):
                    term = matmul(
                        hidden_ref[core, :, pl.ds(side * block, block)],
                        weights.down_value(tall, core, side, columns),
                    )
                    total = term if total is None else total + term
            partial_ref[:, columns] = total
            turned_ref[pl.ds(0, own_rows), columns] = total[own_rows:].astype(BF)
            turned_ref[pl.ds(own_rows, own_rows), columns] = total[:own_rows].astype(BF)

    whole = pl.BlockSpec(memory_space=pltpu.VMEM)
    return pl.pallas_call(
        body,
        out_shape=[
            jax.ShapeDtypeStruct((2, rows, units), BF),
            jax.ShapeDtypeStruct((rows, 2 * units), F32),
            jax.ShapeDtypeStruct((rows, 2 * units), F32),
            jax.ShapeDtypeStruct((rows, width), F32),
            jax.ShapeDtypeStruct((rows, width), BF),
        ],
        in_specs=[whole] * 3 + weights.specs(),
        out_specs=[whole] * 5,
        scratch_shapes=weights.scratch(),
        compiler_params=pltpu.CompilerParams(vmem_limit_bytes=56 * 2**20),
        cost_estimate=COST,
        name="hidden_forward",
    )(first_low, up_scale.reshape(1, -1), gate_scale.reshape(1, -1), *weights.arrays)


def hidden_backward(down_low, up_proj, gate_proj, weights, up_scale, gate_scale, own_rows, earlier):
    rows, width = down_low.shape
    units = weights.units
    block = units // 2

    def body(down_ref, up_ref, gate_ref, up_scale_ref, gate_scale_ref, *refs):
        sources = refs[: len(weights.arrays)]
        low_ref, up_grad_ref, gate_grad_ref, partial_ref, turned_ref, wide, tall, sems = refs[
            len(weights.arrays) + len(earlier) :
        ]
        down_copies = [
            weights.down_copy(sources, tall, sems, i, j) for i in range(2) for j in range(2)
        ]
        copies = [weights.matrix_copy(sources, wide, sems, i) for i in range(4)]
        for copy in down_copies + copies:
            copy.start()
        down = down_ref[...]
        for core in range(2):
            for side in range(2):
                down_copies[core * 2 + side].wait()
                here = pl.ds((core * 2 + side) * block, block)
                grad_hidden = back_matmul(down, weights.down_rows(tall, core, side))
                up_scaling = up_scale_ref[:, here]
                gate_scaling = gate_scale_ref[:, here]
                up = up_ref[:, here]
                gate = gate_ref[:, here]
                scaled = gate_scaling * gate
                sigmoid = jax.nn.sigmoid(scaled)
                silu = scaled * sigmoid
                grad_scaled_up = grad_hidden * silu
                grad_scaled = grad_hidden * (up_scaling * up) * (sigmoid + silu * (1.0 - sigmoid))
                low_ref[0, :, here] = (grad_scaled_up * up_scaling).astype(BF)
                low_ref[1, :, here] = (grad_scaled * gate_scaling).astype(BF)
                up_grad_ref[:, here] = jnp.sum(grad_scaled_up * up, axis=0, keepdims=True)
                gate_grad_ref[:, here] = jnp.sum(grad_scaled * gate, axis=0, keepdims=True)
        for copy in copies:
            copy.wait()
        pieces = 2
        piece = width // pieces
        for j in range(pieces):
            total = None
            for i in range(4):
                term = back_matmul(
                    low_ref[i // 2, :, pl.ds((i % 2) * units, units)],
                    weights.matrix_rows(wide, i, j, pieces),
                )
                total = term if total is None else total + term
            columns = pl.ds(j * piece, piece)
            partial_ref[:, columns] = total
            turned_ref[pl.ds(0, own_rows), columns] = total[own_rows:].astype(BF)
            turned_ref[pl.ds(own_rows, own_rows), columns] = total[:own_rows].astype(BF)

    whole = pl.BlockSpec(memory_space=pltpu.VMEM)
    return pl.pallas_call(
        body,
        out_shape=[
            jax.ShapeDtypeStruct((2, rows, 2 * units), BF),
            jax.ShapeDtypeStruct((1, 2 * units), F32),
            jax.ShapeDtypeStruct((1, 2 * units), F32),
            jax.ShapeDtypeStruct((rows, width), F32),
            jax.ShapeDtypeStruct((rows, width), BF),
        ],
        in_specs=[whole] * 5
        + weights.specs()
        + [pl.BlockSpec(memory_space=pl.ANY)] * len(earlier),
        out_specs=[whole] * 5,
        scratch_shapes=weights.scratch(),
        compiler_params=pltpu.CompilerParams(vmem_limit_bytes=56 * 2**20),
        cost_estimate=COST,
        name="hidden_backward",
    )(
        down_low,
        up_proj,
        gate_proj,
        up_scale.reshape(1, -1),
        gate_scale.reshape(1, -1),
        *weights.arrays,
        *earlier,
    )


def per_device(
    tokens,
    cotangent,
    lengths,
    placement,
    query_weight,
    key_weight,
    value_weight,
    out_weight,
    up_weight,
    gate_weight,
    down_weight,
    scoring,
    upscale,
    gatescale,
    attention_rate,
    feedforward_rate,
):
    size = lax.axis_size("fsdp")
    planes = size // 4
    half = lax.axis_index("grp")
    me = lax.axis_index("fsdp")
    core = me % 2
    side = (me // 2) % 2
    plane = me // 4
    half_scalar = half.reshape(1).astype(jnp.int32)
    which = jnp.stack([core, side]).astype(jnp.int32)
    local_seqs = tokens.shape[0] // size
    seq_len = tokens.shape[1] * size
    width = tokens.shape[2]
    own_rows = local_seqs * seq_len
    shard = query_weight.shape[0]
    hidden_shard = down_weight.shape[0]
    part = hidden_shard // 2
    per_row = hidden_shard // shard
    half_width = width // 2

    def swap_core(array):
        return lax.ppermute(array, "fsdp", [(i, i ^ 1) for i in range(size)])

    def swap_side(array):
        return lax.ppermute(array, "fsdp", [(i, i ^ 2) for i in range(size)])

    def next_plane(array):
        return lax.ppermute(array, "fsdp", [(i, (i + 4) % size) for i in range(size)])

    def swap_half(array):
        return lax.ppermute(array, "grp", [(0, 1), (1, 0)])

    def pick(array, index, axis):
        return lax.dynamic_index_in_dim(array, index, axis, keepdims=False)

    both = jnp.stack([tokens, cotangent])
    arrived = lax.all_to_all(both, "fsdp", split_axis=1, concat_axis=2, tiled=True)

    first_group = lay_first(
        half_scalar,
        query_weight,
        key_weight,
        value_weight,
        out_weight,
        [scoring, attention_rate, feedforward_rate, upscale, gatescale],
    )
    held = [first_group]
    for i in range(planes - 1):
        held.append(next_plane(after(held[-1], arrived) if i == 1 else held[-1]))
    for i in range(planes):
        held.append(swap_side(after(held[i], held[-2]) if i > 1 else held[i]))

    def hidden_half(weight):
        blocks = weight.reshape(shard, planes, 2, 2, 2, part)
        mine = pick(blocks, half, 4)
        return jnp.transpose(mine, (0, 3, 2, 1, 4)).reshape(shard, -1)

    up_half = hidden_half(up_weight)
    gate_half = hidden_half(gate_weight)
    hidden_width = up_half.shape[1]
    core_width = hidden_width // 2
    second_group = jnp.concatenate(
        [
            up_half[:, :core_width],
            up_half[:, core_width:],
            gate_half[:, :core_width],
            gate_half[:, core_width:],
            pick(down_weight.reshape(2, part, width), half, 0),
        ]
    )
    second_whole = lax.all_gather(after(second_group, *held), "fsdp", axis=0)
    held = held + [swap_core(array) for array in held]
    places = []
    for i in range(4 * planes):
        there_core = 1 - core if i >= 2 * planes else core
        there_side = 1 - side if i // planes % 2 else side
        places.append(((plane - i) % planes * 2 + there_side) * 2 + there_core)
    shards = Shards(held, jnp.stack(places).astype(jnp.int32))

    group_order = placement[0]
    own_slots = lax.dynamic_slice_in_dim(group_order, me * local_seqs, local_seqs)
    own_lengths = jnp.take(lengths[0], own_slots)
    valid = (jnp.arange(seq_len, dtype=jnp.int32)[None, :] < own_lengths[:, None]).reshape(
        own_rows, 1
    )
    own_tokens = arrived[0].reshape(own_rows, width)
    own_cot = jnp.where(valid, arrived[1].reshape(own_rows, width), jnp.zeros((), BF))
    token_rows = jnp.concatenate([own_tokens, swap_half(own_tokens)])
    other_cot = swap_half(own_cot)

    qkv, query_unit, key_unit, value_low, mixed_half, mixed_turned, scale_float = attention_forward(
        half_scalar, token_rows, shards, seq_len
    )
    attention_mix = scale_float[1:2]
    feed_mix = scale_float[2:3]

    def hidden_scale(begin):
        rows = scale_float[begin : begin + per_row].reshape(2, per_row // 2, planes, 2, 2, shard)
        return jnp.transpose(pick(rows, half, 0), (3, 2, 1, 0, 4)).reshape(-1)

    up_scale = hidden_scale(3)
    gate_scale = hidden_scale(3 + per_row)
    skip = 3 * half_width + 128
    mixed_low, attended, first_state, first_low = first_forward(
        half_scalar, mixed_half, swap_half(mixed_turned), token_rows, attention_mix, shards, skip
    )

    feature = jnp.arange(width, dtype=jnp.int32)
    block = []
    for b in range(2):
        for a in range(2):
            for k in range(planes):
                there_core = core if b == 0 else 1 - core
                there_side = 1 - side if a == 0 else side
                block.append((k * 2 + there_side) * 2 + there_core)
    block = jnp.stack(block).astype(jnp.int32)
    wanted = (block[:, None] * shard + jnp.arange(shard, dtype=jnp.int32)[None, :]).reshape(-1)
    chooser = (feature[:, None] == wanted[None, :]).astype(BF)

    def share_columns(array):
        chosen = matmul(array, chooser).astype(BF)
        return chosen[:, :half_width], swap_core(chosen[:, half_width:])

    def share(array):
        return array, swap_core(array)

    def over_planes(total):
        return lax.psum_scatter(
            total.reshape(planes, total.shape[0] // planes, total.shape[1]),
            "fsdp",
            scatter_dimension=0,
            axis_index_groups=[[k * 4 + j for k in range(planes)] for j in range(4)],
        )

    token_sides = share_columns(token_rows)
    mixed_sides = share_columns(mixed_low)
    first_sides = share_columns(first_low)
    hidden_weights = HiddenWeights(
        after(second_whole, *token_sides, *mixed_sides, *first_sides, other_cot), planes, shard, part
    )
    hidden_low, up_proj, gate_proj, partial, partial_turned = hidden_forward(
        first_low, hidden_weights, up_scale, gate_scale, own_rows
    )
    hidden_other = swap_core(pick(hidden_low, 1 - core, 0))

    layer_own, grad_first, down_low, feed_grad = second_backward(
        partial,
        swap_half(partial_turned),
        first_state,
        own_cot,
        other_cot,
        valid.astype(F32),
        feed_mix,
    )
    down_other = swap_core(down_low)
    down_args = (which, hidden_low, hidden_other, down_low, down_other)
    down_sent = down_grads(*down_args, False, [])
    down_first = swap_side(down_sent[0])
    up_gate_low, upscale_grad, gatescale_grad, partial, partial_turned = hidden_backward(
        down_low, up_proj, gate_proj, hidden_weights, up_scale, gate_scale, own_rows, down_sent
    )
    up_gate_other = swap_core(after(up_gate_low, down_first))
    partial_other = swap_half(after(partial_turned, down_first))
    down_later = swap_side(after(down_sent[1], down_first))
    (down_kept,) = down_grads(*down_args, True, [down_first])
    up_side = [(up_gate_low, up_gate_other, (0,))]
    gate_side = [(up_gate_low, up_gate_other, (1,))]
    up_sent = side_grads("up_sent", [first_sides], up_side, False, [down_kept])
    gate_sent = side_grads("gate_sent", [first_sides], gate_side, False, [up_sent, partial_other])
    up_arrived = swap_side(after(up_sent, down_later, gate_sent))
    down_joined = join("down_join", down_kept, [down_first, down_later], True, [gate_sent])
    down_total = over_planes(down_joined)
    attended_cols, grad_mixed, grad_tokens, attention_grad = first_backward(
        half_scalar,
        grad_first,
        partial,
        partial_other,
        token_rows,
        attended,
        attention_mix,
        shards,
        skip,
        [down_joined],
    )
    qkv_low, scoring_grad, token_own, token_sent = attention_backward(
        half_scalar, grad_mixed, qkv, query_unit, key_unit, value_low, scale_float, shards, seq_len, []
    )
    up_kept = side_grads("up_kept", [first_sides], up_side, True, [qkv_low])
    gate_arrived = swap_side(after(gate_sent, up_arrived))
    attended_other = swap_core(after(attended_cols, up_arrived))
    qkv_other = swap_core(after(qkv_low, up_arrived))
    token_other = swap_half(after(token_sent, up_arrived))
    up_joined = join("up_join", up_kept, [up_arrived], False, [down_total])
    up_total = over_planes(up_joined)
    last_args = (
        [mixed_sides, token_sides],
        [(attended_cols, attended_other, None), (qkv_low, qkv_other, (0, 1, 2))],
    )
    last_sent = side_grads("last_sent", *last_args, False, [up_joined])
    gate_kept = side_grads("gate_kept", [first_sides], gate_side, True, [last_sent])
    last_kept = side_grads("last_kept", *last_args, True, [gate_kept])
    input_own = (grad_tokens + token_own + token_other.astype(F32)).astype(BF)
    last_arrived = swap_side(after(last_sent, gate_arrived))
    gate_joined = join("gate_join", gate_kept, [gate_arrived], False, [up_total, last_kept])
    gate_total = over_planes(gate_joined)
    last_joined = join("last_join", last_kept, [last_arrived], False, [gate_total])
    last_total = over_planes(last_joined)
    layer_own = after(layer_own, last_joined)
    outgoing = jnp.stack([layer_own, input_own]).reshape(2, local_seqs, seq_len, width)
    returned = lax.all_to_all(outgoing, "fsdp", split_axis=2, concat_axis=1, tiled=True)
    down_total = down_total.astype(F32)
    last_total = last_total.astype(F32)
    out_total = last_total[:, :half_width]
    qkv_total = last_total[:, half_width:]

    up_out, gate_out = merge_hidden(
        half_scalar,
        [up_total, gate_total],
        [swap_half(array) for array in split_hidden(half_scalar, [up_total], planes, part)]
        + [swap_half(array) for array in split_hidden(half_scalar, [gate_total], planes, part)],
        planes,
        part,
    )
    down_cols = down_total.reshape(part, 2, half_width)
    mine = pick(down_cols, half, 1)
    theirs = swap_half(pick(down_cols, 1 - half, 1).astype(BF)).astype(F32)
    down_out = jnp.where(
        half == 0, jnp.concatenate([mine, theirs]), jnp.concatenate([theirs, mine])
    )

    def hidden_spread(grad):
        blocks = jnp.transpose(grad.reshape(2, 2, planes, part), (2, 1, 0, 3))
        blank = jnp.zeros_like(blocks)
        both_halves = jnp.where(
            half == 0, jnp.stack([blocks, blank], axis=3), jnp.stack([blank, blocks], axis=3)
        )
        return both_halves.reshape(size, hidden_shard)

    blank = jnp.zeros_like(scoring_grad)
    scoring_spread = jnp.where(
        half == 0,
        jnp.concatenate([scoring_grad, blank], axis=1),
        jnp.concatenate([blank, scoring_grad], axis=1),
    )
    small = jnp.concatenate(
        [
            scoring_spread.reshape(size, shard),
            attention_grad.reshape(size, shard),
            feed_grad.reshape(size, shard),
            hidden_spread(upscale_grad),
            hidden_spread(gatescale_grad),
        ],
        axis=1,
    )
    small = lax.all_to_all(small, "fsdp", split_axis=0, concat_axis=0, tiled=True)
    total = jnp.sum(small, axis=0)
    total = total + swap_half(total)

    return (
        returned[0],
        returned[1],
        qkv_total[:, :half_width],
        qkv_total[:, half_width : 2 * half_width],
        qkv_total[:, 2 * half_width :],
        out_total,
        up_out,
        gate_out,
        down_out,
        total[:shard],
        total[3 * shard : 3 * shard + hidden_shard],
        total[3 * shard + hidden_shard :],
        total[shard : 2 * shard],
        total[2 * shard : 3 * shard],
    )


def solution(mesh):
    rows = P("grp", "fsdp", None)
    group = P("grp", None)
    matrix = P("fsdp", None)
    vector = P("fsdp")
    split = P("fsdp", "grp")
    return jax.shard_map(
        per_device,
        mesh=mesh,
        in_specs=(rows, rows, group, group) + (matrix,) * 7 + (vector,) * 5,
        out_specs=(rows, rows) + (split,) * 7 + (vector,) * 5,
        check_vma=False,
    )
```

```python
import math

import jax
import jax.numpy as jnp
from jax import lax
from jax.experimental import pallas as pl
from jax.experimental.pallas import tpu as pltpu
from jax.sharding import PartitionSpec as P

H = 20
DK = 64
BF = jnp.bfloat16
F32 = jnp.float32
COST = pl.CostEstimate(flops=1000, bytes_accessed=1000, transcendentals=0)


def swiglu(up_proj, gate_proj, upscale, gatescale):
    scaled = gatescale * gate_proj
    return scaled * jax.nn.sigmoid(scaled) * (upscale * up_proj)


def matmul(left_side, right_side):
    return jnp.dot(left_side, right_side, preferred_element_type=F32)


def weight_grad(left_side, right_side):
    return lax.dot_general(
        left_side, right_side, (((0,), (0,)), ((), ())), preferred_element_type=F32
    )


def back_matmul(grad_rows, weight_rows):
    return lax.dot_general(
        grad_rows, weight_rows, (((1,), (1,)), ((), ())), preferred_element_type=F32
    )


def after(value, *earlier):
    return lax.optimization_barrier((value, *earlier))[0]


def like(*shape, dtype=BF):
    return jax.ShapeDtypeStruct(shape, dtype)


def call(name, body, outs, scalars=(), arrays=(), remote=(), scratch=(), earlier=()):
    counts = (len(scalars), len(arrays), len(remote), len(earlier), len(outs))

    def kernel(*refs):
        groups = []
        at = 0
        for count in counts:
            groups.append(refs[at : at + count])
            at += count
        body(*groups[0], *groups[1], groups[2], *groups[4], *refs[at:])

    whole = pl.BlockSpec(memory_space=pltpu.VMEM)
    kept = pl.BlockSpec(memory_space=pl.ANY)
    return pl.pallas_call(
        kernel,
        out_shape=list(outs),
        in_specs=[pl.BlockSpec(memory_space=pltpu.SMEM)] * counts[0]
        + [whole] * counts[1]
        + [kept] * (counts[2] + counts[3]),
        out_specs=[whole] * counts[4],
        scratch_shapes=list(scratch),
        compiler_params=pltpu.CompilerParams(vmem_limit_bytes=56 * 2**20),
        cost_estimate=COST,
        name=name,
    )(*scalars, *arrays, *remote, *earlier)


class Shards:
    def __init__(self, arrays, places):
        self.direct = arrays[0].shape[0] % 16 == 0
        if self.direct:
            self.arrays, self.places = list(arrays), places
        else:
            whole = jnp.zeros((len(arrays),) + arrays[0].shape, BF)
            for i, array in enumerate(arrays):
                whole = lax.dynamic_update_index_in_dim(whole, array, places[i], 0)
            self.arrays = [whole.reshape(-1, arrays[0].shape[1])]
            self.places = jnp.zeros((1,), jnp.int32)
        self.count = len(self.arrays)
        self.height = self.arrays[0].shape[0]

    def scratch(self, width):
        return [
            pltpu.VMEM((self.count, self.height, width), BF),
            pltpu.SemaphoreType.DMA((self.count,)),
        ]

    def copies(self, places, sources, target, sems, begin, width):
        return [
            pltpu.make_async_copy(
                sources[i].at[:, pl.ds(begin, width)], target.at[places[i]], sems.at[i]
            )
            for i in range(self.count)
        ]

    def columns(self, target, begin, width):
        return target[:, :, pl.ds(begin, width)].reshape(self.count * self.height, width)

    def rows(self, target, index, parts, begin, width):
        if self.direct:
            step = self.count // parts
            rows = target[pl.ds(index * step, step), :, pl.ds(begin, width)]
        else:
            step = self.height // parts
            rows = target[:, pl.ds(pl.multiple_of(index * step, step), step), pl.ds(begin, width)]
        return rows.reshape(-1, width)


def inverse_rms(vector):
    return lax.rsqrt(jnp.mean(vector * vector, axis=-1, keepdims=True) + 1e-06)


def head_sums(values, low_head):
    low_sum = jnp.sum(jnp.where(low_head, values, 0.0), axis=-1, keepdims=True)
    high_sum = jnp.sum(jnp.where(low_head, 0.0, values), axis=-1, keepdims=True)
    return low_sum, high_sum


def head_inverse(vector, low_head):
    low_sum, high_sum = head_sums(vector * vector, low_head)
    return jnp.where(low_head, lax.rsqrt(low_sum + 1e-06), lax.rsqrt(high_sum + 1e-06))


def head_probs(query_head, key_unit, seq_len):
    scores = back_matmul(query_head, key_unit) * math.sqrt(DK)
    query_row = lax.broadcasted_iota(jnp.int32, scores.shape, 0)
    key_row = lax.broadcasted_iota(jnp.int32, scores.shape, 1)
    start = query_row - lax.rem(query_row, seq_len)
    scores = jnp.where((key_row <= query_row) & (key_row >= start), scores, -1e30)
    exp_scores = jnp.exp(scores - jnp.max(scores, axis=-1, keepdims=True))
    return exp_scores / jnp.sum(exp_scores, axis=-1, keepdims=True)


def only(mask, values):
    return jnp.where(mask, values.astype(F32), 0.0).astype(BF)


def turn(ref, rows, columns, value):
    ref[pl.ds(0, rows), columns] = value[rows:].astype(BF)
    ref[pl.ds(rows, rows), columns] = value[:rows].astype(BF)


def attention_forward(half, token_rows, shards, seq_len):
    rows, width = token_rows.shape
    half_width = width // 2
    pairs = half_width // 128
    cols = 3 * half_width + 128

    def body(
        places, half_ref, x_ref, sources, qkv_ref, qu_ref, ku_ref, vl_ref, mixed_ref, turned_ref, scale_ref, w_ref, sems
    ):
        copies = shards.copies(places, sources, w_ref, sems, 0, cols)
        for copy in copies:
            copy.start()
        for copy in copies:
            copy.wait()
        scale_ref[...] = jnp.transpose(
            shards.columns(w_ref, 3 * half_width, 128).astype(F32)
        )[:16]
        x = x_ref[...]
        step = 384
        for begin in range(0, 3 * half_width, step):
            qkv_ref[:, pl.ds(begin, step)] = matmul(x, shards.columns(w_ref, begin, step))
        low_head = lax.broadcasted_iota(jnp.int32, (rows, 128), 1) < DK
        later = half_ref[0] == 1

        def pair(i, carry):
            at = pl.multiple_of(i * 128, 128)
            here = pl.ds(at, 128)
            queries = qkv_ref[:, here]
            key_rows = qkv_ref[:, pl.ds(half_width + at, 128)]
            value_low = qkv_ref[:, pl.ds(2 * half_width + at, 128)].astype(BF)
            scaling = jnp.where(
                later, scale_ref[0:1, pl.ds(half_width + at, 128)], scale_ref[0:1, here]
            )
            query_unit = queries * head_inverse(queries, low_head) * scaling
            key_unit = (key_rows * head_inverse(key_rows, low_head) * scaling).astype(BF)
            mixed = None
            for mask in (low_head, ~low_head):
                probs = head_probs(only(mask, query_unit), key_unit, seq_len)
                head = matmul(probs.astype(BF), value_low)
                mixed = head if mixed is None else jnp.where(low_head, mixed, head)
            qu_ref[:, here] = query_unit.astype(BF)
            ku_ref[:, here] = key_unit
            vl_ref[:, here] = value_low
            mixed_ref[:, here] = mixed.astype(BF)
            turn(turned_ref, rows // 2, here, mixed)
            return carry

        lax.fori_loop(0, pairs, pair, 0)

    return call(
        "attention_forward",
        body,
        [like(rows, 3 * half_width, dtype=F32)] + [like(rows, half_width)] * 5 + [like(16, width, dtype=F32)],
        scalars=[shards.places, half],
        arrays=[token_rows],
        remote=shards.arrays,
        scratch=shards.scratch(cols),
    )


def place_halves(half_ref, target, own, other):
    width = own.shape[1]

    @pl.when(half_ref[0] == 0)
    def _():
        target[:, pl.ds(0, width)] = own[...]
        target[:, pl.ds(width, width)] = other[...]

    @pl.when(half_ref[0] != 0)
    def _():
        target[:, pl.ds(0, width)] = other[...]
        target[:, pl.ds(width, width)] = own[...]


def first_forward(half, mixed, mixed_other, token_rows, attention_mix, shards, skip):
    rows, width = token_rows.shape

    def body(
        places, half_ref, own_ref, other_ref, x_ref, mix_ref, sources, mixed_ref, attended_ref, first_ref, low_ref, w_ref, sems
    ):
        copies = shards.copies(places, sources, w_ref, sems, skip, width)
        for copy in copies:
            copy.start()
        place_halves(half_ref, mixed_ref, own_ref, other_ref)
        for copy in copies:
            copy.wait()
        for begin in range(0, width, 256):
            attended_ref[:, pl.ds(begin, 256)] = matmul(
                mixed_ref[...], shards.columns(w_ref, begin, 256)
            )
        x = x_ref[...].astype(F32)
        attended = attended_ref[...]
        mix = x + mix_ref[...] * (attended * inverse_rms(attended) - x)
        first = mix * inverse_rms(mix)
        first_ref[...] = first
        low_ref[...] = first.astype(BF)

    return call(
        "first_forward",
        body,
        [like(rows, width)] + [like(rows, width, dtype=F32)] * 2 + [like(rows, width)],
        scalars=[shards.places, half],
        arrays=[mixed, mixed_other, token_rows, attention_mix],
        remote=shards.arrays,
        scratch=shards.scratch(width),
    )


def mix_backward(base, branch, rate, grad):
    branch_inverse = inverse_rms(branch)
    branch_unit = branch * branch_inverse
    mix = base + rate * (branch_unit - base)
    inverse = inverse_rms(mix)
    value = mix * inverse
    grad_mix = inverse * (grad - value * jnp.mean(grad * value, axis=-1, keepdims=True))
    grad_unit = grad_mix * rate
    grad_branch = branch_inverse * (
        grad_unit - branch_unit * jnp.mean(grad_unit * branch_unit, axis=-1, keepdims=True)
    )
    return value, grad_mix - grad_unit, grad_branch, grad_mix * (branch_unit - base)


def second_backward(partial, partial_other, first_state, cot, cot_other, valid, feed_mix):
    rows, width = partial.shape
    own = rows // 2

    def body(partial_ref, other_ref, first_ref, cot_ref, cot_other_ref, valid_ref, mix_ref, _, layer_ref, grad_ref, low_ref, rate_ref):
        for begin in (0, own):
            here = pl.ds(begin, own)
            down = partial_ref[here, :] + other_ref[here, :].astype(F32)
            grad = (cot_ref if begin == 0 else cot_other_ref)[...].astype(F32)
            value, grad_first, grad_down, grad_rate = mix_backward(
                first_ref[here, :], down, mix_ref[...], grad
            )
            grad_ref[here, :] = grad_first
            low_ref[here, :] = grad_down.astype(BF)
            if begin == 0:
                layer_ref[...] = (value * valid_ref[...]).astype(BF)
                rate_ref[...] = jnp.sum(grad_rate, axis=0, keepdims=True)

    return call(
        "second_backward",
        body,
        [like(own, width), like(rows, width, dtype=F32), like(rows, width), like(1, width, dtype=F32)],
        arrays=[partial, partial_other, first_state, cot, cot_other, valid, feed_mix],
    )


def first_backward(half, grad_first, partial, partial_other, token_rows, attended, attention_mix, shards, skip, earlier):
    rows, width = partial.shape
    own = rows // 2
    half_width = width // 2

    def body(
        places, half_ref, grad_ref, partial_ref, other_ref, x_ref, attended_ref, mix_ref, sources, cols_ref, mixed_ref, token_ref, rate_ref, low_ref, w_ref, sems
    ):
        copies = shards.copies(places, sources, w_ref, sems, skip, width)
        for copy in copies:
            copy.start()
        for begin in (0, own):
            here = pl.ds(begin, own)
            grad = grad_ref[here, :] + partial_ref[here, :] + other_ref[here, :].astype(F32)
            _, grad_token, grad_attended, grad_rate = mix_backward(
                x_ref[here, :].astype(F32), attended_ref[here, :], mix_ref[...], grad
            )
            low_ref[here, :] = grad_attended.astype(BF)
            if begin == 0:
                token_ref[...] = grad_token
                rate_ref[...] = jnp.sum(grad_rate, axis=0, keepdims=True)
        at = pl.multiple_of(half_ref[0] * half_width, 128)
        cols_ref[...] = low_ref[:, pl.ds(at, half_width)]
        for copy in copies:
            copy.wait()
        mixed_ref[...] = back_matmul(
            low_ref[...], shards.rows(w_ref, half_ref[0], 2, 0, width)
        ).astype(BF)

    return call(
        "first_backward",
        body,
        [like(rows, half_width)] * 2 + [like(own, width, dtype=F32), like(1, width, dtype=F32)],
        scalars=[shards.places, half],
        arrays=[grad_first, partial, partial_other, token_rows, attended, attention_mix],
        remote=shards.arrays,
        scratch=[pltpu.VMEM((rows, width), BF)] + shards.scratch(width),
        earlier=earlier,
    )


def attention_backward(half, grad_mixed, qkv, query_unit, key_unit, value_low, scales, shards, seq_len, earlier):
    rows, half_width = grad_mixed.shape
    width = 2 * half_width
    pairs = half_width // 128
    own = rows // 2

    def body(
        places, half_ref, gm_ref, qkv_ref, qu_ref, ku_ref, vl_ref, scale_ref, sources, grads_ref, scoring_ref, own_ref, other_ref, w_ref, sems
    ):
        copies = shards.copies(places, sources, w_ref, sems, 0, 3 * half_width)
        for copy in copies:
            copy.start()
        low_head = lax.broadcasted_iota(jnp.int32, (rows, 128), 1) < DK
        later = half_ref[0] == 1

        def pair(i, carry):
            at = pl.multiple_of(i * 128, 128)
            here = pl.ds(at, 128)
            query_unit = qu_ref[:, here]
            key_unit = ku_ref[:, here]
            value_low = vl_ref[:, here]
            scaling = jnp.where(
                later, scale_ref[0:1, pl.ds(half_width + at, 128)], scale_ref[0:1, here]
            )
            grad_value = grad_qunit = grad_kunit = None
            for mask in (low_head, ~low_head):
                probs = head_probs(only(mask, query_unit), key_unit, seq_len)
                grad_head = only(mask, gm_ref[:, here])
                value_part = weight_grad(probs.astype(BF), grad_head)
                grad_probs = back_matmul(grad_head, value_low)
                grad_scores = (
                    probs * (grad_probs - jnp.sum(grad_probs * probs, axis=-1, keepdims=True))
                ).astype(BF)
                query_part = matmul(grad_scores, key_unit)
                key_part = weight_grad(grad_scores, query_unit)
                if grad_value is None:
                    grad_value, grad_qunit, grad_kunit = value_part, query_part, key_part
                else:
                    grad_value = grad_value + value_part
                    grad_qunit = jnp.where(low_head, grad_qunit, query_part)
                    grad_kunit = jnp.where(low_head, grad_kunit, key_part)
            scoring_grad = None
            for place, grad in ((0, grad_qunit), (1, grad_kunit)):
                raw = qkv_ref[:, pl.ds(place * half_width + at, 128)]
                grad = grad * math.sqrt(DK)
                inverse = head_inverse(raw, low_head)
                unit = raw * inverse
                term = jnp.sum(grad * unit, axis=0, keepdims=True)
                scoring_grad = term if scoring_grad is None else scoring_grad + term
                grad = grad * scaling
                low_sum, high_sum = head_sums(grad * unit, low_head)
                grads_ref[place, :, here] = (
                    inverse * (grad - unit * jnp.where(low_head, low_sum, high_sum))
                ).astype(BF)
            grads_ref[2, :, here] = grad_value.astype(BF)
            scoring_ref[:, here] = scoring_grad
            return carry

        lax.fori_loop(0, pairs, pair, 0)
        for copy in copies:
            copy.wait()
        for piece in range(2):
            total = None
            for j in range(3):
                term = back_matmul(
                    grads_ref[j], shards.rows(w_ref, piece, 2, j * half_width, half_width)
                )
                total = term if total is None else total + term
            columns = pl.ds(piece * half_width, half_width)
            own_ref[:, columns] = total[:own]
            other_ref[:, columns] = total[own:].astype(BF)

    return call(
        "attention_backward",
        body,
        [
            like(3, rows, half_width),
            like(1, half_width, dtype=F32),
            like(own, width, dtype=F32),
            like(own, width),
        ],
        scalars=[shards.places, half],
        arrays=[grad_mixed, qkv, query_unit, key_unit, value_low, scales],
        remote=shards.arrays,
        scratch=shards.scratch(3 * half_width),
        earlier=earlier,
    )


def down_grads(which, hidden, hidden_other, down, down_other, kept, earlier):
    rows, units = hidden_other.shape
    width = down.shape[1]
    block = units // 2

    def body(which_ref, hidden_ref, hidden_other_ref, down_ref, down_other_ref, _, *out_refs):
        side = which_ref[1] if kept else 1 - which_ref[1]
        columns = pl.ds(pl.multiple_of(side * block, 128), block)
        own = hidden_ref[which_ref[0], :, columns]
        other = hidden_other_ref[:, columns]
        for begin in range(0, width, 256):
            here = pl.ds(begin, 256)
            total = weight_grad(own, down_ref[:, here]) + weight_grad(other, down_other_ref[:, here])
            if kept:
                out_refs[0][:, here] = total
            else:
                for i, out_ref in enumerate(out_refs):
                    out_ref[:, here] = total[i * (block // 2) : (i + 1) * (block // 2)].astype(BF)

    return call(
        "down_kept" if kept else "down_sent",
        body,
        [like(block, width, dtype=F32)] if kept else [like(block // 2, width)] * 2,
        scalars=[which],
        arrays=[hidden, hidden_other, down, down_other],
        earlier=earlier,
    )


def side_grads(name, lefts, rights, kept, earlier):
    block = lefts[0][0].shape[1] // 2
    number = len(lefts)
    total_width = sum(right[0].shape[-1] * len(right[2] or (0,)) for right in rights)

    def body(*refs):
        refs = [ref for ref in refs if not isinstance(ref, tuple)]
        out_ref = refs[-1]
        begin = 0
        for i in range(number):
            own_ref, other_ref, right_ref, right_other_ref = refs[4 * i : 4 * i + 4]
            columns = pl.ds(block if kept else 0, block)
            own = own_ref[:, columns]
            other = other_ref[:, columns]
            for index in rights[i][2] or (None,):
                for at in range(0, right_ref.shape[-1], 640):
                    here = (slice(None), pl.ds(at, 640))
                    if index is not None:
                        here = (index, *here)
                    total = weight_grad(own, right_ref[here]) + weight_grad(other, right_other_ref[here])
                    out_ref[:, pl.ds(begin, 640)] = total.astype(out_ref.dtype)
                    begin += 640

    arrays = []
    for left, right in zip(lefts, rights):
        arrays += [*left, *right[:2]]
    return call(
        name,
        body,
        [like(block, total_width, dtype=F32 if kept else BF)],
        arrays=arrays,
        earlier=earlier,
    )[0]


def join(name, kept, arrived, by_rows, earlier):
    rows, width = kept.shape
    pieces = 4
    if by_rows:
        block, places = (rows // pieces, width), lambda i: (i, 0)
    else:
        block, places = (rows, width // pieces), lambda i: (0, i)
    each = pieces // len(arrived)

    def body(kept_ref, *refs):
        out_ref = refs[-1]
        for j in range(len(arrived)):

            @pl.when(pl.program_id(0) // each == j)
            def _():
                out_ref[...] = (kept_ref[...] + refs[j][...].astype(F32)).astype(BF)

    def part(j):
        if len(arrived) == 1:
            return places
        return lambda i: places(jnp.clip(i - j * each, 0, each - 1))

    return pl.pallas_call(
        body,
        grid=(pieces,),
        out_shape=like(rows, width),
        in_specs=[pl.BlockSpec(block, places)]
        + [pl.BlockSpec(block, part(j)) for j in range(len(arrived))]
        + [pl.BlockSpec(memory_space=pl.ANY)] * len(earlier),
        out_specs=pl.BlockSpec(block, places),
        compiler_params=pltpu.CompilerParams(vmem_limit_bytes=56 * 2**20),
        cost_estimate=COST,
        name=name,
    )(kept, *arrived, *earlier)


def lay_first(half, query_weight, key_weight, value_weight, out_weight, scales, tokens, cotangent):
    shard, width = query_weight.shape
    half_width = width // 2

    def body(half_ref, q_ref, k_ref, v_ref, out_ref, token_ref, cot_ref, *refs):
        target, both, square = refs[-3:]
        both[0] = token_ref[...]
        both[1] = cot_ref[...]
        for i, ref in enumerate((q_ref, k_ref, v_ref)):
            place = pl.ds(i * half_width, half_width)

            @pl.when(half_ref[0] == 0)
            def _():
                target[:, place] = ref[:, pl.ds(0, half_width)]

            @pl.when(half_ref[0] != 0)
            def _():
                target[:, place] = ref[:, pl.ds(half_width, half_width)]

        square[...] = jnp.zeros_like(square)
        row = 0
        for ref in refs[: len(scales)]:
            values = ref[...].astype(F32)
            for begin in range(0, values.shape[1], shard):
                square[pl.ds(row, 1), pl.ds(0, shard)] = values[:, begin : begin + shard]
                row += 1
        target[:, pl.ds(3 * half_width, 128)] = jnp.transpose(square[...])[:shard].astype(BF)
        target[:, pl.ds(3 * half_width + 128, width)] = out_ref[...]

    return call(
        "lay_first",
        body,
        [like(shard, 3 * half_width + 128 + width), like(2, *tokens.shape)],
        scalars=[half],
        arrays=[query_weight, key_weight, value_weight, out_weight, tokens, cotangent]
        + [scale.reshape(1, -1) for scale in scales],
        scratch=[pltpu.VMEM((128, 128), F32)],
    )


def lay_second(half, up_weight, gate_weight, down_weight, planes):
    shard = up_weight.shape[0]
    part = down_weight.shape[0] // 2
    width = down_weight.shape[1]

    def body(half_ref, up_ref, gate_ref, down_ref, _, target):
        upper = half_ref[0] != 0
        for i, ref in enumerate((up_ref, gate_ref)):
            for core in range(2):
                rows = slice((2 * i + core) * shard, (2 * i + core + 1) * shard)
                for side in range(2):
                    for plane in range(planes):
                        begin = ((plane * 2 + side) * 2 + core) * 2 * part
                        place = (side * planes + plane) * part
                        target[rows, place : place + part] = jnp.where(
                            upper,
                            ref[:, begin + part : begin + 2 * part].astype(F32),
                            ref[:, begin : begin + part].astype(F32),
                        ).astype(BF)

        @pl.when(jnp.logical_not(upper))
        def _():
            target[pl.ds(4 * shard, part), :] = down_ref[pl.ds(0, part), :]

        @pl.when(upper)
        def _():
            target[pl.ds(4 * shard, part), :] = down_ref[pl.ds(part, part), :]

    return call(
        "lay_second",
        body,
        [like(4 * shard + part, width)],
        scalars=[half],
        arrays=[up_weight, gate_weight, down_weight],
    )[0]


def split_hidden(half, totals, planes, part):
    shard, width = totals[0].shape
    run = planes // 2 * part

    def body(half_ref, *refs):
        for source, target in zip(refs[: len(totals)], refs[-len(totals) :]):
            for i in range(4):
                begin = 2 * i * run
                first, later = source[:, begin : begin + run], source[:, begin + run : begin + 2 * run]
                target[:, i * run : (i + 1) * run] = jnp.where(
                    half_ref[0] == 0, later.astype(F32), first.astype(F32)
                ).astype(BF)

    return call(
        "split_hidden",
        body,
        [like(shard, width // 2)] * len(totals),
        scalars=[half],
        arrays=totals,
    )


def merge_hidden(half, totals, others, planes, part):
    shard, width = totals[0].shape
    run = planes // 2 * part

    def body(half_ref, *refs):
        number = len(totals)
        upper = half_ref[0] != 0
        for own_ref, other_ref, target in zip(refs[:number], refs[number : 2 * number], refs[-number:]):
            for plane in range(planes // 2):
                for side in range(2):
                    for core in range(2):
                        i = core * 2 + side
                        begin = 2 * i * run + plane * part
                        own = jnp.where(
                            upper,
                            own_ref[:, begin + run : begin + run + part].astype(F32),
                            own_ref[:, begin : begin + part].astype(F32),
                        )
                        begin = i * run + plane * part
                        other = other_ref[:, begin : begin + part].astype(F32)
                        begin = ((plane * 2 + side) * 2 + core) * 2 * part
                        target[:, begin : begin + part] = jnp.where(upper, other, own)
                        target[:, begin + part : begin + 2 * part] = jnp.where(upper, own, other)

    return call(
        "merge_hidden",
        body,
        [like(shard, width, dtype=F32)] * len(totals),
        scalars=[half],
        arrays=[*totals, *others],
    )


class HiddenWeights:
    def __init__(self, gathered, planes, shard, part):
        width = gathered.shape[2]
        units = 2 * planes * part
        self.direct = shard % 16 == 0 and part % 16 == 0
        self.width, self.units, self.shard, self.part = width, units, shard, part
        if self.direct:
            self.arrays = [gathered.reshape(planes, 2, 2, -1, width)]
            self.matrix = (planes, 2, 2, shard, units)
            self.down = (planes, part, width)
        else:
            blocks = gathered[:, 4 * shard :].reshape(planes, 2, 2, part, width)
            self.arrays = [
                jnp.stack(
                    [gathered[:, i * shard : (i + 1) * shard].reshape(width, width) for i in range(4)]
                ),
                jnp.transpose(blocks, (2, 1, 0, 3, 4)).reshape(2, 2, planes * part, width),
            ]
            self.matrix = (width, units)
            self.down = (planes * part, width)

    def scratch(self):
        return [
            pltpu.VMEM((4,) + self.matrix, BF),
            pltpu.VMEM((2, 2) + self.down, BF),
            pltpu.SemaphoreType.DMA((8,)),
        ]

    def specs(self):
        return [pl.BlockSpec(memory_space=pl.ANY)] * len(self.arrays)

    def matrix_copy(self, sources, wide, sems, i):
        if self.direct:
            source = sources[0].at[:, :, :, pl.ds(i * self.shard, self.shard), :]
        else:
            source = sources[0].at[i]
        return pltpu.make_async_copy(source, wide.at[i], sems.at[i])

    def down_copy(self, sources, tall, sems, core, side):
        if self.direct:
            source = sources[0].at[:, side, core, pl.ds(4 * self.shard, self.part), :]
        else:
            source = sources[1].at[core, side]
        return pltpu.make_async_copy(source, tall.at[core, side], sems.at[4 + core * 2 + side])

    def matrix_value(self, wide, i, columns):
        if self.direct:
            return wide[i, :, :, :, :, columns].reshape(self.width, -1)
        return wide[i, :, columns]

    def matrix_rows(self, wide, i, j, parts):
        if self.direct:
            step = self.matrix[0] // parts
            return wide[i, pl.ds(j * step, step)].reshape(self.width // parts, -1)
        step = self.width // parts
        return wide[i, pl.ds(j * step, step)]

    def down_value(self, tall, core, side, columns):
        if self.direct:
            return tall[core, side, :, :, columns].reshape(-1, columns.size)
        return tall[core, side, :, columns]

    def down_rows(self, tall, core, side):
        return tall[core, side].reshape(-1, self.width)


def hidden_forward(first_low, weights, up_scale, gate_scale, own_rows):
    rows, width = first_low.shape
    units = weights.units
    block = units // 2
    step = 256

    def body(first_ref, up_scale_ref, gate_scale_ref, *refs):
        sources = refs[: len(weights.arrays)]
        hidden_ref, up_ref, gate_ref, partial_ref, turned_ref, wide, tall, sems = refs[
            len(weights.arrays) :
        ]
        copies = [weights.matrix_copy(sources, wide, sems, i) for i in (0, 2, 1, 3)]
        down_copies = [
            weights.down_copy(sources, tall, sems, i, j) for i in range(2) for j in range(2)
        ]
        for copy in copies + down_copies:
            copy.start()
        first = first_ref[...]
        for core in range(2):
            copies[2 * core].wait()
            copies[2 * core + 1].wait()

            for begin in range(0, units, step):
                columns = pl.ds(begin, step)
                here = pl.ds(core * units + begin, step)
                up = matmul(first, weights.matrix_value(wide, core, columns))
                gate = matmul(first, weights.matrix_value(wide, 2 + core, columns))
                up_ref[:, here] = up
                gate_ref[:, here] = gate
                hidden = swiglu(up, gate, up_scale_ref[:, here], gate_scale_ref[:, here])
                hidden_ref[core, :, columns] = hidden.astype(BF)
        for copy in down_copies:
            copy.wait()

        for begin in range(0, width, step):
            columns = pl.ds(begin, step)
            total = None
            for core in range(2):
                for side in range(2):
                    term = matmul(
                        hidden_ref[core, :, pl.ds(side * block, block)],
                        weights.down_value(tall, core, side, columns),
                    )
                    total = term if total is None else total + term
            partial_ref[:, columns] = total
            turned_ref[pl.ds(0, own_rows), columns] = total[own_rows:].astype(BF)
            turned_ref[pl.ds(own_rows, own_rows), columns] = total[:own_rows].astype(BF)

    whole = pl.BlockSpec(memory_space=pltpu.VMEM)
    return pl.pallas_call(
        body,
        out_shape=[
            jax.ShapeDtypeStruct((2, rows, units), BF),
            jax.ShapeDtypeStruct((rows, 2 * units), F32),
            jax.ShapeDtypeStruct((rows, 2 * units), F32),
            jax.ShapeDtypeStruct((rows, width), F32),
            jax.ShapeDtypeStruct((rows, width), BF),
        ],
        in_specs=[whole] * 3 + weights.specs(),
        out_specs=[whole] * 5,
        scratch_shapes=weights.scratch(),
        compiler_params=pltpu.CompilerParams(vmem_limit_bytes=56 * 2**20),
        cost_estimate=COST,
        name="hidden_forward",
    )(first_low, up_scale.reshape(1, -1), gate_scale.reshape(1, -1), *weights.arrays)


def hidden_backward(down_low, up_proj, gate_proj, weights, up_scale, gate_scale, own_rows, earlier):
    rows, width = down_low.shape
    units = weights.units
    block = units // 2

    def body(down_ref, up_ref, gate_ref, up_scale_ref, gate_scale_ref, *refs):
        sources = refs[: len(weights.arrays)]
        low_ref, up_grad_ref, gate_grad_ref, partial_ref, turned_ref, wide, tall, sems = refs[
            len(weights.arrays) + len(earlier) :
        ]
        down_copies = [
            weights.down_copy(sources, tall, sems, i, j) for i in range(2) for j in range(2)
        ]
        copies = [weights.matrix_copy(sources, wide, sems, i) for i in range(4)]
        for copy in down_copies + copies:
            copy.start()
        down = down_ref[...]
        for core in range(2):
            for side in range(2):
                down_copies[core * 2 + side].wait()
                here = pl.ds((core * 2 + side) * block, block)
                grad_hidden = back_matmul(down, weights.down_rows(tall, core, side))
                up_scaling = up_scale_ref[:, here]
                gate_scaling = gate_scale_ref[:, here]
                up = up_ref[:, here]
                gate = gate_ref[:, here]
                scaled = gate_scaling * gate
                sigmoid = jax.nn.sigmoid(scaled)
                silu = scaled * sigmoid
                grad_scaled_up = grad_hidden * silu
                grad_scaled = grad_hidden * (up_scaling * up) * (sigmoid + silu * (1.0 - sigmoid))
                low_ref[0, :, here] = (grad_scaled_up * up_scaling).astype(BF)
                low_ref[1, :, here] = (grad_scaled * gate_scaling).astype(BF)
                up_grad_ref[:, here] = jnp.sum(grad_scaled_up * up, axis=0, keepdims=True)
                gate_grad_ref[:, here] = jnp.sum(grad_scaled * gate, axis=0, keepdims=True)
        for copy in copies:
            copy.wait()
        pieces = 2
        piece = width // pieces
        for j in range(pieces):
            total = None
            for i in range(4):
                term = back_matmul(
                    low_ref[i // 2, :, pl.ds((i % 2) * units, units)],
                    weights.matrix_rows(wide, i, j, pieces),
                )
                total = term if total is None else total + term
            columns = pl.ds(j * piece, piece)
            partial_ref[:, columns] = total
            turned_ref[pl.ds(0, own_rows), columns] = total[own_rows:].astype(BF)
            turned_ref[pl.ds(own_rows, own_rows), columns] = total[:own_rows].astype(BF)

    whole = pl.BlockSpec(memory_space=pltpu.VMEM)
    return pl.pallas_call(
        body,
        out_shape=[
            jax.ShapeDtypeStruct((2, rows, 2 * units), BF),
            jax.ShapeDtypeStruct((1, 2 * units), F32),
            jax.ShapeDtypeStruct((1, 2 * units), F32),
            jax.ShapeDtypeStruct((rows, width), F32),
            jax.ShapeDtypeStruct((rows, width), BF),
        ],
        in_specs=[whole] * 5
        + weights.specs()
        + [pl.BlockSpec(memory_space=pl.ANY)] * len(earlier),
        out_specs=[whole] * 5,
        scratch_shapes=weights.scratch(),
        compiler_params=pltpu.CompilerParams(vmem_limit_bytes=56 * 2**20),
        cost_estimate=COST,
        name="hidden_backward",
    )(
        down_low,
        up_proj,
        gate_proj,
        up_scale.reshape(1, -1),
        gate_scale.reshape(1, -1),
        *weights.arrays,
        *earlier,
    )


def per_device(
    tokens,
    cotangent,
    lengths,
    placement,
    query_weight,
    key_weight,
    value_weight,
    out_weight,
    up_weight,
    gate_weight,
    down_weight,
    scoring,
    upscale,
    gatescale,
    attention_rate,
    feedforward_rate,
):
    size = lax.axis_size("fsdp")
    planes = size // 4
    half = lax.axis_index("grp")
    me = lax.axis_index("fsdp")
    core = me % 2
    side = (me // 2) % 2
    plane = me // 4
    half_scalar = half.reshape(1).astype(jnp.int32)
    which = jnp.stack([core, side]).astype(jnp.int32)
    local_seqs = tokens.shape[0] // size
    seq_len = tokens.shape[1] * size
    width = tokens.shape[2]
    own_rows = local_seqs * seq_len
    shard = query_weight.shape[0]
    hidden_shard = down_weight.shape[0]
    part = hidden_shard // 2
    per_row = hidden_shard // shard
    half_width = width // 2

    def swap_core(array):
        return lax.ppermute(array, "fsdp", [(i, i ^ 1) for i in range(size)])

    def swap_side(array):
        return lax.ppermute(array, "fsdp", [(i, i ^ 2) for i in range(size)])

    def next_plane(array):
        return lax.ppermute(array, "fsdp", [(i, (i + 4) % size) for i in range(size)])

    def swap_half(array):
        return lax.ppermute(array, "grp", [(0, 1), (1, 0)])

    def pick(array, index, axis):
        return lax.dynamic_index_in_dim(array, index, axis, keepdims=False)

    first_group, both = lay_first(
        half_scalar,
        query_weight,
        key_weight,
        value_weight,
        out_weight,
        [scoring, attention_rate, feedforward_rate, upscale, gatescale],
        tokens,
        cotangent,
    )
    arrived = lax.all_to_all(both, "fsdp", split_axis=1, concat_axis=2, tiled=True)
    second_group = lay_second(half_scalar, up_weight, gate_weight, down_weight, planes)
    hidden_width = planes * 4 * part
    core_width = hidden_width // 2
    own_tokens = arrived[0].reshape(own_rows, width)
    other_tokens = swap_half(own_tokens)

    held = [first_group]
    crossed = []
    for i in range(planes):
        here = after(held[-1], *crossed[-1:]) if crossed else held[-1]
        if i < planes - 1:
            held.append(next_plane(here))
        crossed.append(swap_side(here))
    held = held + crossed
    second_whole = lax.all_gather(after(second_group, *held), "fsdp", axis=0)
    held = held + [swap_core(array) for array in held]
    places = []
    for i in range(4 * planes):
        there_core = 1 - core if i >= 2 * planes else core
        there_side = 1 - side if i // planes % 2 else side
        places.append(((plane - i) % planes * 2 + there_side) * 2 + there_core)
    shards = Shards(held, jnp.stack(places).astype(jnp.int32))

    group_order = placement[0]
    own_slots = lax.dynamic_slice_in_dim(group_order, me * local_seqs, local_seqs)
    own_lengths = jnp.take(lengths[0], own_slots)
    valid = (jnp.arange(seq_len, dtype=jnp.int32)[None, :] < own_lengths[:, None]).reshape(
        own_rows, 1
    )
    own_cot = jnp.where(valid, arrived[1].reshape(own_rows, width), jnp.zeros((), BF))
    token_rows = jnp.concatenate([own_tokens, other_tokens])
    other_cot = swap_half(own_cot)

    qkv, query_unit, key_unit, value_low, mixed_half, mixed_turned, scale_float = attention_forward(
        half_scalar, token_rows, shards, seq_len
    )
    attention_mix = scale_float[1:2]
    feed_mix = scale_float[2:3]

    def hidden_scale(begin):
        rows = scale_float[begin : begin + per_row].reshape(2, per_row // 2, planes, 2, 2, shard)
        return jnp.transpose(pick(rows, half, 0), (3, 2, 1, 0, 4)).reshape(-1)

    up_scale = hidden_scale(3)
    gate_scale = hidden_scale(3 + per_row)
    skip = 3 * half_width + 128
    mixed_low, attended, first_state, first_low = first_forward(
        half_scalar, mixed_half, swap_half(mixed_turned), token_rows, attention_mix, shards, skip
    )

    feature = jnp.arange(width, dtype=jnp.int32)
    block = []
    for b in range(2):
        for a in range(2):
            for k in range(planes):
                there_core = core if b == 0 else 1 - core
                there_side = 1 - side if a == 0 else side
                block.append((k * 2 + there_side) * 2 + there_core)
    block = jnp.stack(block).astype(jnp.int32)
    wanted = (block[:, None] * shard + jnp.arange(shard, dtype=jnp.int32)[None, :]).reshape(-1)
    chooser = (feature[:, None] == wanted[None, :]).astype(BF)

    def share_columns(array):
        chosen = matmul(array, chooser).astype(BF)
        return chosen[:, :half_width], swap_core(chosen[:, half_width:])

    def share(array):
        return array, swap_core(array)

    def over_planes(total):
        return lax.psum_scatter(
            total.reshape(planes, total.shape[0] // planes, total.shape[1]),
            "fsdp",
            scatter_dimension=0,
            axis_index_groups=[[k * 4 + j for k in range(planes)] for j in range(4)],
        )

    token_sides = share_columns(token_rows)
    mixed_sides = share_columns(mixed_low)
    first_sides = share_columns(first_low)
    hidden_weights = HiddenWeights(
        after(second_whole, *token_sides, *mixed_sides, *first_sides, other_cot), planes, shard, part
    )
    hidden_low, up_proj, gate_proj, partial, partial_turned = hidden_forward(
        first_low, hidden_weights, up_scale, gate_scale, own_rows
    )
    hidden_other = swap_core(pick(hidden_low, 1 - core, 0))

    layer_own, grad_first, down_low, feed_grad = second_backward(
        partial,
        swap_half(partial_turned),
        first_state,
        own_cot,
        other_cot,
        valid.astype(F32),
        feed_mix,
    )
    down_other = swap_core(down_low)
    down_args = (which, hidden_low, hidden_other, down_low, down_other)
    down_sent = down_grads(*down_args, False, [])
    down_first = swap_side(down_sent[0])
    up_gate_low, upscale_grad, gatescale_grad, partial, partial_turned = hidden_backward(
        down_low, up_proj, gate_proj, hidden_weights, up_scale, gate_scale, own_rows, down_sent
    )
    (down_kept,) = down_grads(*down_args, True, [up_gate_low])
    up_gate_other = swap_core(after(up_gate_low, down_first, down_kept))
    partial_other = swap_half(after(partial_turned, down_first, down_kept))
    down_later = swap_side(after(down_sent[1], down_first, down_kept))
    up_side = [(up_gate_low, up_gate_other, (0,))]
    gate_side = [(up_gate_low, up_gate_other, (1,))]
    up_sent = side_grads("up_sent", [first_sides], up_side, False, [down_kept])
    up_arrived = swap_side(after(up_sent, down_later, partial_other))
    down_joined = join("down_join", down_kept, [down_first, down_later], True, [up_sent, partial_other])
    down_total = over_planes(down_joined)
    gate_sent = side_grads("gate_sent", [first_sides], gate_side, False, [down_joined])
    attended_cols, grad_mixed, grad_tokens, attention_grad = first_backward(
        half_scalar,
        grad_first,
        partial,
        partial_other,
        token_rows,
        attended,
        attention_mix,
        shards,
        skip,
        [gate_sent],
    )
    qkv_low, scoring_grad, token_own, token_sent = attention_backward(
        half_scalar, grad_mixed, qkv, query_unit, key_unit, value_low, scale_float, shards, seq_len, []
    )
    up_kept = side_grads("up_kept", [first_sides], up_side, True, [qkv_low])
    gate_arrived = swap_side(after(gate_sent, up_arrived))
    attended_other = swap_core(after(attended_cols, up_arrived))
    qkv_other = swap_core(after(qkv_low, up_arrived))
    token_other = swap_half(after(token_sent, up_arrived))
    up_joined = join("up_join", up_kept, [up_arrived], False, [down_total])
    up_total = over_planes(up_joined)
    last_args = (
        [mixed_sides, token_sides],
        [(attended_cols, attended_other, None), (qkv_low, qkv_other, (0, 1, 2))],
    )
    last_sent = side_grads("last_sent", *last_args, False, [up_joined])
    gate_kept = side_grads("gate_kept", [first_sides], gate_side, True, [last_sent])
    last_kept = side_grads("last_kept", *last_args, True, [gate_kept])
    input_own = (grad_tokens + token_own + token_other.astype(F32)).astype(BF)
    last_arrived = swap_side(after(last_sent, gate_arrived))
    gate_joined = join("gate_join", gate_kept, [gate_arrived], False, [up_total, last_kept])
    gate_total = over_planes(gate_joined)
    def hidden_spread(grad):
        blocks = jnp.transpose(grad.reshape(2, 2, planes, part), (2, 1, 0, 3))
        blank = jnp.zeros_like(blocks)
        both_halves = jnp.where(
            half == 0, jnp.stack([blocks, blank], axis=3), jnp.stack([blank, blocks], axis=3)
        )
        return both_halves.reshape(size, hidden_shard)

    blank = jnp.zeros_like(scoring_grad)
    scoring_spread = jnp.where(
        half == 0,
        jnp.concatenate([scoring_grad, blank], axis=1),
        jnp.concatenate([blank, scoring_grad], axis=1),
    )
    small = jnp.concatenate(
        [
            scoring_spread.reshape(size, shard),
            attention_grad.reshape(size, shard),
            feed_grad.reshape(size, shard),
            hidden_spread(upscale_grad),
            hidden_spread(gatescale_grad),
        ],
        axis=1,
    )
    small = lax.all_to_all(small, "fsdp", split_axis=0, concat_axis=0, tiled=True)
    outgoing = jnp.stack([layer_own, input_own]).reshape(2, local_seqs, seq_len, width)
    returned = lax.all_to_all(outgoing, "fsdp", split_axis=2, concat_axis=1, tiled=True)
    last_joined = join(
        "last_join", last_kept, [last_arrived], False, [gate_total, returned, small]
    )
    last_total = over_planes(last_joined).astype(F32)
    total = jnp.sum(small, axis=0)
    total = total + swap_half(total)

    def hidden_whole(total):
        (sent,) = split_hidden(half_scalar, [total], planes, part)
        return merge_hidden(half_scalar, [total], [swap_half(sent)], planes, part)[0]

    up_out = hidden_whole(up_total)
    down_total = down_total.astype(F32)
    down_cols = down_total.reshape(part, 2, half_width)
    mine = pick(down_cols, half, 1)
    theirs = swap_half(pick(down_cols, 1 - half, 1).astype(BF)).astype(F32)
    down_out = jnp.where(
        half == 0, jnp.concatenate([mine, theirs]), jnp.concatenate([theirs, mine])
    )
    gate_out = hidden_whole(gate_total)
    out_total = last_total[:, :half_width]
    qkv_total = last_total[:, half_width:]

    return (
        returned[0],
        returned[1],
        qkv_total[:, :half_width],
        qkv_total[:, half_width : 2 * half_width],
        qkv_total[:, 2 * half_width :],
        out_total,
        up_out,
        gate_out,
        down_out,
        total[:shard],
        total[3 * shard : 3 * shard + hidden_shard],
        total[3 * shard + hidden_shard :],
        total[shard : 2 * shard],
        total[2 * shard : 3 * shard],
    )


def solution(mesh):
    rows = P("grp", "fsdp", None)
    group = P("grp", None)
    matrix = P("fsdp", None)
    vector = P("fsdp")
    split = P("fsdp", "grp")
    return jax.shard_map(
        per_device,
        mesh=mesh,
        in_specs=(rows, rows, group, group) + (matrix,) * 7 + (vector,) * 5,
        out_specs=(rows, rows) + (split,) * 7 + (vector,) * 5,
        check_vma=False,
    )
```

```python
import math

import jax
import jax.numpy as jnp
from jax import lax
from jax.experimental import pallas as pl
from jax.experimental.pallas import tpu as pltpu
from jax.sharding import PartitionSpec as P

H = 20
DK = 64
BF = jnp.bfloat16
F32 = jnp.float32
COST = pl.CostEstimate(flops=1000, bytes_accessed=1000, transcendentals=0)


def swiglu(up_proj, gate_proj, upscale, gatescale):
    scaled = gatescale * gate_proj
    return scaled * jax.nn.sigmoid(scaled) * (upscale * up_proj)


def matmul(left_side, right_side):
    return jnp.dot(left_side, right_side, preferred_element_type=F32)


def weight_grad(left_side, right_side):
    return lax.dot_general(
        left_side, right_side, (((0,), (0,)), ((), ())), preferred_element_type=F32
    )


def back_matmul(grad_rows, weight_rows):
    return lax.dot_general(
        grad_rows, weight_rows, (((1,), (1,)), ((), ())), preferred_element_type=F32
    )


def after(value, *earlier):
    return lax.optimization_barrier((value, *earlier))[0]


def like(*shape, dtype=BF):
    return jax.ShapeDtypeStruct(shape, dtype)


def call(name, body, outs, scalars=(), arrays=(), remote=(), scratch=(), earlier=(), limit=16):
    counts = (len(scalars), len(arrays), len(remote), len(earlier), len(outs))

    def kernel(*refs):
        groups = []
        at = 0
        for count in counts:
            groups.append(refs[at : at + count])
            at += count
        body(*groups[0], *groups[1], groups[2], *groups[4], *refs[at:])

    whole = pl.BlockSpec(memory_space=pltpu.VMEM)
    kept = pl.BlockSpec(memory_space=pl.ANY)
    placed = pl.BlockSpec(memory_space=pltpu.HBM)
    return pl.pallas_call(
        kernel,
        out_shape=list(outs),
        in_specs=[pl.BlockSpec(memory_space=pltpu.SMEM)] * counts[0]
        + [whole] * counts[1]
        + [placed] * counts[2]
        + [kept] * counts[3],
        out_specs=[whole] * counts[4],
        scratch_shapes=list(scratch),
        compiler_params=pltpu.CompilerParams(vmem_limit_bytes=limit * 2**20),
        cost_estimate=COST,
        name=name,
    )(*scalars, *arrays, *remote, *earlier)


class Shards:
    def __init__(self, arrays, places):
        self.direct = arrays[0].shape[0] % 16 == 0
        if self.direct:
            self.arrays, self.places = list(arrays), places
        else:
            whole = jnp.zeros((len(arrays),) + arrays[0].shape, BF)
            for i, array in enumerate(arrays):
                whole = lax.dynamic_update_index_in_dim(whole, array, places[i], 0)
            self.arrays = [whole.reshape(-1, arrays[0].shape[1])]
            self.places = jnp.zeros((1,), jnp.int32)
        self.count = len(self.arrays)
        self.height = self.arrays[0].shape[0]

    def scratch(self, width):
        return [
            pltpu.VMEM((self.count, self.height, width), BF),
            pltpu.SemaphoreType.DMA((self.count,)),
        ]

    def copies(self, places, sources, target, sems, begin, width):
        return [
            pltpu.make_async_copy(
                sources[i].at[:, pl.ds(begin, width)], target.at[places[i]], sems.at[i]
            )
            for i in range(self.count)
        ]

    def columns(self, target, begin, width):
        return target[:, :, pl.ds(begin, width)].reshape(self.count * self.height, width)

    def rows(self, target, index, parts, begin, width):
        if self.direct:
            step = self.count // parts
            rows = target[pl.ds(index * step, step), :, pl.ds(begin, width)]
        else:
            step = self.height // parts
            rows = target[:, pl.ds(pl.multiple_of(index * step, step), step), pl.ds(begin, width)]
        return rows.reshape(-1, width)


def inverse_rms(vector):
    return lax.rsqrt(jnp.mean(vector * vector, axis=-1, keepdims=True) + 1e-06)


def head_sums(values, low_head):
    low_sum = jnp.sum(jnp.where(low_head, values, 0.0), axis=-1, keepdims=True)
    high_sum = jnp.sum(jnp.where(low_head, 0.0, values), axis=-1, keepdims=True)
    return low_sum, high_sum


def head_inverse(vector, low_head):
    low_sum, high_sum = head_sums(vector * vector, low_head)
    return jnp.where(low_head, lax.rsqrt(low_sum + 1e-06), lax.rsqrt(high_sum + 1e-06))


def head_probs(query_head, key_unit, seq_len):
    scores = back_matmul(query_head, key_unit) * math.sqrt(DK)
    query_row = lax.broadcasted_iota(jnp.int32, scores.shape, 0)
    key_row = lax.broadcasted_iota(jnp.int32, scores.shape, 1)
    start = query_row - lax.rem(query_row, seq_len)
    scores = jnp.where((key_row <= query_row) & (key_row >= start), scores, -1e30)
    exp_scores = jnp.exp(scores - jnp.max(scores, axis=-1, keepdims=True))
    return exp_scores / jnp.sum(exp_scores, axis=-1, keepdims=True)


def only(mask, values):
    return jnp.where(mask, values.astype(F32), 0.0).astype(BF)


def turn(ref, rows, columns, value):
    ref[pl.ds(0, rows), columns] = value[rows:].astype(BF)
    ref[pl.ds(rows, rows), columns] = value[:rows].astype(BF)


def attention_forward(half, token_rows, shards, seq_len):
    rows, width = token_rows.shape
    half_width = width // 2
    pairs = half_width // 128
    cols = 3 * half_width + 128

    def body(
        places, half_ref, x_ref, sources, qkv_ref, qu_ref, ku_ref, vl_ref, mixed_ref, turned_ref, scale_ref, w_ref, sems
    ):
        copies = shards.copies(places, sources, w_ref, sems, 0, cols)
        for copy in copies:
            copy.start()
        for copy in copies:
            copy.wait()
        scale_ref[...] = jnp.transpose(
            shards.columns(w_ref, 3 * half_width, 128).astype(F32)
        )[:16]
        x = x_ref[...]
        step = 384
        for begin in range(0, 3 * half_width, step):
            qkv_ref[:, pl.ds(begin, step)] = matmul(x, shards.columns(w_ref, begin, step))
        low_head = lax.broadcasted_iota(jnp.int32, (rows, 128), 1) < DK
        later = half_ref[0] == 1

        def pair(i, carry):
            at = pl.multiple_of(i * 128, 128)
            here = pl.ds(at, 128)
            queries = qkv_ref[:, here]
            key_rows = qkv_ref[:, pl.ds(half_width + at, 128)]
            value_low = qkv_ref[:, pl.ds(2 * half_width + at, 128)].astype(BF)
            scaling = jnp.where(
                later, scale_ref[0:1, pl.ds(half_width + at, 128)], scale_ref[0:1, here]
            )
            query_unit = queries * head_inverse(queries, low_head) * scaling
            key_unit = (key_rows * head_inverse(key_rows, low_head) * scaling).astype(BF)
            mixed = None
            for mask in (low_head, ~low_head):
                probs = head_probs(only(mask, query_unit), key_unit, seq_len)
                head = matmul(probs.astype(BF), value_low)
                mixed = head if mixed is None else jnp.where(low_head, mixed, head)
            qu_ref[:, here] = query_unit.astype(BF)
            ku_ref[:, here] = key_unit
            vl_ref[:, here] = value_low
            mixed_ref[:, here] = mixed.astype(BF)
            turn(turned_ref, rows // 2, here, mixed)
            return carry

        lax.fori_loop(0, pairs, pair, 0)

    return call(
        "attention_forward",
        body,
        [like(rows, 3 * half_width, dtype=F32)] + [like(rows, half_width)] * 5 + [like(16, width, dtype=F32)],
        scalars=[shards.places, half],
        arrays=[token_rows],
        remote=shards.arrays,
        limit=24,
        scratch=shards.scratch(cols),
    )


def place_whole(source, _, target):
    target[...] = source[...]


def place_pair(first, later, _, target):
    target[0] = first[...]
    target[1] = later[...]


def sum_whole(source, _, target):
    target[...] = jnp.sum(source[...], axis=0, keepdims=True)


def place_halves(half_ref, target, own, other):
    width = own.shape[1]

    @pl.when(half_ref[0] == 0)
    def _():
        target[:, pl.ds(0, width)] = own[...]
        target[:, pl.ds(width, width)] = other[...]

    @pl.when(half_ref[0] != 0)
    def _():
        target[:, pl.ds(0, width)] = other[...]
        target[:, pl.ds(width, width)] = own[...]


def first_forward(half, mixed, mixed_other, token_rows, attention_mix, shards, skip):
    rows, width = token_rows.shape

    def body(
        places, half_ref, own_ref, other_ref, x_ref, mix_ref, sources, mixed_ref, attended_ref, first_ref, low_ref, w_ref, sems
    ):
        copies = shards.copies(places, sources, w_ref, sems, skip, width)
        for copy in copies:
            copy.start()
        place_halves(half_ref, mixed_ref, own_ref, other_ref)
        for copy in copies:
            copy.wait()
        for begin in range(0, width, 256):
            attended_ref[:, pl.ds(begin, 256)] = matmul(
                mixed_ref[...], shards.columns(w_ref, begin, 256)
            )
        x = x_ref[...].astype(F32)
        attended = attended_ref[...]
        mix = x + mix_ref[...] * (attended * inverse_rms(attended) - x)
        first = mix * inverse_rms(mix)
        first_ref[...] = first
        low_ref[...] = first.astype(BF)

    return call(
        "first_forward",
        body,
        [like(rows, width)] + [like(rows, width, dtype=F32)] * 2 + [like(rows, width)],
        scalars=[shards.places, half],
        arrays=[mixed, mixed_other, token_rows, attention_mix],
        remote=shards.arrays,
        limit=20,
        scratch=shards.scratch(width),
    )


def mix_backward(base, branch, rate, grad):
    branch_inverse = inverse_rms(branch)
    branch_unit = branch * branch_inverse
    mix = base + rate * (branch_unit - base)
    inverse = inverse_rms(mix)
    value = mix * inverse
    grad_mix = inverse * (grad - value * jnp.mean(grad * value, axis=-1, keepdims=True))
    grad_unit = grad_mix * rate
    grad_branch = branch_inverse * (
        grad_unit - branch_unit * jnp.mean(grad_unit * branch_unit, axis=-1, keepdims=True)
    )
    return value, grad_mix - grad_unit, grad_branch, grad_mix * (branch_unit - base)


def second_backward(partial, partial_other, first_state, cot, cot_other, valid, feed_mix):
    rows, width = partial.shape
    own = rows // 2

    def body(partial_ref, other_ref, first_ref, cot_ref, cot_other_ref, valid_ref, mix_ref, _, layer_ref, grad_ref, low_ref, rate_ref):
        for begin in (0, own):
            here = pl.ds(begin, own)
            down = partial_ref[here, :] + other_ref[here, :].astype(F32)
            grad = (cot_ref if begin == 0 else cot_other_ref)[...].astype(F32)
            value, grad_first, grad_down, grad_rate = mix_backward(
                first_ref[here, :], down, mix_ref[...], grad
            )
            grad_ref[here, :] = grad_first
            low_ref[here, :] = grad_down.astype(BF)
            if begin == 0:
                layer_ref[...] = (value * valid_ref[...]).astype(BF)
                rate_ref[...] = jnp.sum(grad_rate, axis=0, keepdims=True)

    return call(
        "second_backward",
        body,
        [like(own, width), like(rows, width, dtype=F32), like(rows, width), like(1, width, dtype=F32)],
        limit=18,
        arrays=[partial, partial_other, first_state, cot, cot_other, valid, feed_mix],
    )


def first_backward(half, grad_first, partial, partial_other, token_rows, attended, attention_mix, shards, skip, earlier):
    rows, width = partial.shape
    own = rows // 2
    half_width = width // 2

    def body(
        places, half_ref, grad_ref, partial_ref, other_ref, x_ref, attended_ref, mix_ref, sources, cols_ref, mixed_ref, token_ref, rate_ref, low_ref, w_ref, sems
    ):
        copies = shards.copies(places, sources, w_ref, sems, skip, width)
        for copy in copies:
            copy.start()
        for begin in (0, own):
            here = pl.ds(begin, own)
            grad = grad_ref[here, :] + partial_ref[here, :] + other_ref[here, :].astype(F32)
            _, grad_token, grad_attended, grad_rate = mix_backward(
                x_ref[here, :].astype(F32), attended_ref[here, :], mix_ref[...], grad
            )
            low_ref[here, :] = grad_attended.astype(BF)
            if begin == 0:
                token_ref[...] = grad_token
                rate_ref[...] = jnp.sum(grad_rate, axis=0, keepdims=True)
        at = pl.multiple_of(half_ref[0] * half_width, 128)
        cols_ref[...] = low_ref[:, pl.ds(at, half_width)]
        for copy in copies:
            copy.wait()
        mixed_ref[...] = back_matmul(
            low_ref[...], shards.rows(w_ref, half_ref[0], 2, 0, width)
        ).astype(BF)

    return call(
        "first_backward",
        body,
        [like(rows, half_width)] * 2 + [like(own, width, dtype=F32), like(1, width, dtype=F32)],
        scalars=[shards.places, half],
        arrays=[grad_first, partial, partial_other, token_rows, attended, attention_mix],
        remote=shards.arrays,
        limit=20,
        scratch=[pltpu.VMEM((rows, width), BF)] + shards.scratch(width),
        earlier=earlier,
    )


def attention_backward(half, grad_mixed, qkv, query_unit, key_unit, value_low, scales, shards, seq_len, earlier):
    rows, half_width = grad_mixed.shape
    width = 2 * half_width
    pairs = half_width // 128
    own = rows // 2

    def body(
        places, half_ref, gm_ref, qkv_ref, qu_ref, ku_ref, vl_ref, scale_ref, sources, grads_ref, scoring_ref, own_ref, other_ref, w_ref, sems
    ):
        copies = shards.copies(places, sources, w_ref, sems, 0, 3 * half_width)
        for copy in copies:
            copy.start()
        low_head = lax.broadcasted_iota(jnp.int32, (rows, 128), 1) < DK
        later = half_ref[0] == 1

        def pair(i, carry):
            at = pl.multiple_of(i * 128, 128)
            here = pl.ds(at, 128)
            query_unit = qu_ref[:, here]
            key_unit = ku_ref[:, here]
            value_low = vl_ref[:, here]
            scaling = jnp.where(
                later, scale_ref[0:1, pl.ds(half_width + at, 128)], scale_ref[0:1, here]
            )
            grad_value = grad_qunit = grad_kunit = None
            for mask in (low_head, ~low_head):
                probs = head_probs(only(mask, query_unit), key_unit, seq_len)
                grad_head = only(mask, gm_ref[:, here])
                value_part = weight_grad(probs.astype(BF), grad_head)
                grad_probs = back_matmul(grad_head, value_low)
                grad_scores = (
                    probs * (grad_probs - jnp.sum(grad_probs * probs, axis=-1, keepdims=True))
                ).astype(BF)
                query_part = matmul(grad_scores, key_unit)
                key_part = weight_grad(grad_scores, query_unit)
                if grad_value is None:
                    grad_value, grad_qunit, grad_kunit = value_part, query_part, key_part
                else:
                    grad_value = grad_value + value_part
                    grad_qunit = jnp.where(low_head, grad_qunit, query_part)
                    grad_kunit = jnp.where(low_head, grad_kunit, key_part)
            scoring_grad = None
            for place, grad in ((0, grad_qunit), (1, grad_kunit)):
                raw = qkv_ref[:, pl.ds(place * half_width + at, 128)]
                grad = grad * math.sqrt(DK)
                inverse = head_inverse(raw, low_head)
                unit = raw * inverse
                term = jnp.sum(grad * unit, axis=0, keepdims=True)
                scoring_grad = term if scoring_grad is None else scoring_grad + term
                grad = grad * scaling
                low_sum, high_sum = head_sums(grad * unit, low_head)
                grads_ref[place, :, here] = (
                    inverse * (grad - unit * jnp.where(low_head, low_sum, high_sum))
                ).astype(BF)
            grads_ref[2, :, here] = grad_value.astype(BF)
            scoring_ref[:, here] = scoring_grad
            return carry

        lax.fori_loop(0, pairs, pair, 0)
        for copy in copies:
            copy.wait()
        for piece in range(2):
            total = None
            for j in range(3):
                term = back_matmul(
                    grads_ref[j], shards.rows(w_ref, piece, 2, j * half_width, half_width)
                )
                total = term if total is None else total + term
            columns = pl.ds(piece * half_width, half_width)
            own_ref[:, columns] = total[:own]
            other_ref[:, columns] = total[own:].astype(BF)

    return call(
        "attention_backward",
        body,
        [
            like(3, rows, half_width),
            like(1, half_width, dtype=F32),
            like(own, width, dtype=F32),
            like(own, width),
        ],
        scalars=[shards.places, half],
        arrays=[grad_mixed, qkv, query_unit, key_unit, value_low, scales],
        remote=shards.arrays,
        limit=56,
        scratch=shards.scratch(3 * half_width),
        earlier=earlier,
    )


def down_grads(name, which, hidden, hidden_other, down, down_other, pieces, earlier):
    rows, units = hidden_other.shape
    block = units // 2

    def body(which_ref, hidden_ref, hidden_other_ref, down_ref, down_other_ref, _, *out_refs):
        for out_ref, parts in zip(out_refs, pieces):
            place = 0
            for kept, begin, width in parts:
                side = which_ref[1] if kept else 1 - which_ref[1]
                columns = pl.ds(pl.multiple_of(side * block, 128), block)
                own = hidden_ref[which_ref[0], :, columns]
                other = hidden_other_ref[:, columns]
                for at in range(0, width, 256):
                    here = pl.ds(begin + at, 256)
                    total = weight_grad(own, down_ref[:, here])
                    total = total + weight_grad(other, down_other_ref[:, here])
                    out_ref[:, pl.ds(place + at, 256)] = total.astype(BF)
                place += width

    return call(
        name,
        body,
        [like(block, sum(width for _, _, width in parts)) for parts in pieces],
        scalars=[which],
        arrays=[hidden, hidden_other, down, down_other],
        earlier=earlier,
    )


def side_grads(name, lefts, rights, kept, earlier):
    block = lefts[0][0].shape[1] // 2
    number = len(lefts)
    total_width = sum(right[0].shape[-1] * len(right[2] or (0,)) for right in rights)

    def body(*refs):
        refs = [ref for ref in refs if not isinstance(ref, tuple)]
        out_ref = refs[-1]
        begin = 0
        for i in range(number):
            own_ref, other_ref, right_ref, right_other_ref = refs[4 * i : 4 * i + 4]
            columns = pl.ds(block if kept else 0, block)
            own = own_ref[:, columns]
            other = other_ref[:, columns]
            for index in rights[i][2] or (None,):
                for at in range(0, right_ref.shape[-1], 640):
                    here = (slice(None), pl.ds(at, 640))
                    if index is not None:
                        here = (index, *here)
                    total = weight_grad(own, right_ref[here]) + weight_grad(other, right_other_ref[here])
                    out_ref[:, pl.ds(begin, 640)] = total.astype(out_ref.dtype)
                    begin += 640

    arrays = []
    for left, right in zip(lefts, rights):
        arrays += [*left, *right[:2]]
    return call(
        name,
        body,
        [like(block, total_width)],
        limit=20,
        arrays=arrays,
        earlier=earlier,
    )[0]


def lay_first(half, query_weight, key_weight, value_weight, out_weight, scales, tokens, cotangent):
    shard, width = query_weight.shape
    half_width = width // 2

    def body(half_ref, q_ref, k_ref, v_ref, out_ref, token_ref, cot_ref, *refs):
        target, both, square = refs[-3:]
        both[0] = token_ref[...]
        both[1] = cot_ref[...]
        for i, ref in enumerate((q_ref, k_ref, v_ref)):
            place = pl.ds(i * half_width, half_width)

            @pl.when(half_ref[0] == 0)
            def _():
                target[:, place] = ref[:, pl.ds(0, half_width)]

            @pl.when(half_ref[0] != 0)
            def _():
                target[:, place] = ref[:, pl.ds(half_width, half_width)]

        square[...] = jnp.zeros_like(square)
        row = 0
        for ref in refs[: len(scales)]:
            values = ref[...].astype(F32)
            for begin in range(0, values.shape[1], shard):
                square[pl.ds(row, 1), pl.ds(0, shard)] = values[:, begin : begin + shard]
                row += 1
        target[:, pl.ds(3 * half_width, 128)] = jnp.transpose(square[...])[:shard].astype(BF)
        target[:, pl.ds(3 * half_width + 128, width)] = out_ref[...]

    return call(
        "lay_first",
        body,
        [like(shard, 3 * half_width + 128 + width), like(2, *tokens.shape)],
        limit=56,
        scalars=[half],
        arrays=[query_weight, key_weight, value_weight, out_weight, tokens, cotangent]
        + [scale.reshape(1, -1) for scale in scales],
        scratch=[pltpu.VMEM((128, 128), F32)],
    )


def lay_second(half, up_weight, gate_weight, down_weight, planes):
    shard = up_weight.shape[0]
    part = down_weight.shape[0] // 2
    width = down_weight.shape[1]

    def body(half_ref, up_ref, gate_ref, down_ref, _, target):
        upper = half_ref[0] != 0
        for i, ref in enumerate((up_ref, gate_ref)):
            for core in range(2):
                rows = slice((2 * i + core) * shard, (2 * i + core + 1) * shard)
                for side in range(2):
                    for plane in range(planes):
                        begin = ((plane * 2 + side) * 2 + core) * 2 * part
                        place = (side * planes + plane) * part
                        target[rows, place : place + part] = jnp.where(
                            upper,
                            ref[:, begin + part : begin + 2 * part].astype(F32),
                            ref[:, begin : begin + part].astype(F32),
                        ).astype(BF)

        @pl.when(jnp.logical_not(upper))
        def _():
            target[pl.ds(4 * shard, part), :] = down_ref[pl.ds(0, part), :]

        @pl.when(upper)
        def _():
            target[pl.ds(4 * shard, part), :] = down_ref[pl.ds(part, part), :]

    return call(
        "lay_second",
        body,
        [like(4 * shard + part, width)],
        limit=56,
        scalars=[half],
        arrays=[up_weight, gate_weight, down_weight],
    )[0]


def split_hidden(half, totals, planes, part):
    shard, width = totals[0].shape
    run = planes // 2 * part

    def body(half_ref, *refs):
        for source, target in zip(refs[: len(totals)], refs[-len(totals) :]):
            for i in range(4):
                begin = 2 * i * run
                first, later = source[:, begin : begin + run], source[:, begin + run : begin + 2 * run]
                target[:, i * run : (i + 1) * run] = jnp.where(
                    half_ref[0] == 0, later.astype(F32), first.astype(F32)
                ).astype(BF)

    return call(
        "split_hidden",
        body,
        [like(shard, width // 2)] * len(totals),
        scalars=[half],
        arrays=totals,
    )


def merge_hidden(half, totals, others, planes, part, earlier):
    shard, width = totals[0].shape
    run = planes // 2 * part

    def body(half_ref, *refs):
        number = len(totals)
        upper = half_ref[0] != 0
        for own_ref, other_ref, target in zip(refs[:number], refs[number : 2 * number], refs[-number:]):
            for plane in range(planes // 2):
                for side in range(2):
                    for core in range(2):
                        i = core * 2 + side
                        begin = 2 * i * run + plane * part
                        own = jnp.where(
                            upper,
                            own_ref[:, begin + run : begin + run + part].astype(F32),
                            own_ref[:, begin : begin + part].astype(F32),
                        )
                        begin = i * run + plane * part
                        other = other_ref[:, begin : begin + part].astype(F32)
                        begin = ((plane * 2 + side) * 2 + core) * 2 * part
                        target[:, begin : begin + part] = jnp.where(upper, other, own)
                        target[:, begin + part : begin + 2 * part] = jnp.where(upper, own, other)

    return call(
        "merge_hidden",
        body,
        [like(shard, width, dtype=F32)] * len(totals),
        scalars=[half],
        arrays=[*totals, *others],
        earlier=earlier,
    )


class HiddenWeights:
    def __init__(self, gathered, planes, shard, part):
        width = gathered.shape[2]
        units = 2 * planes * part
        self.direct = shard % 16 == 0 and part % 16 == 0
        self.width, self.units, self.shard, self.part = width, units, shard, part
        if self.direct:
            self.arrays = [gathered.reshape(planes, 2, 2, -1, width)]
            self.matrix = (planes, 2, 2, shard, units)
            self.down = (planes, part, width)
        else:
            blocks = gathered[:, 4 * shard :].reshape(planes, 2, 2, part, width)
            self.arrays = [
                jnp.stack(
                    [gathered[:, i * shard : (i + 1) * shard].reshape(width, width) for i in range(4)]
                ),
                jnp.transpose(blocks, (2, 1, 0, 3, 4)).reshape(2, 2, planes * part, width),
            ]
            self.matrix = (width, units)
            self.down = (planes * part, width)

    def scratch(self):
        return [
            pltpu.VMEM((4,) + self.matrix, BF),
            pltpu.VMEM((2, 2) + self.down, BF),
            pltpu.SemaphoreType.DMA((8,)),
        ]

    def specs(self):
        return [pl.BlockSpec(memory_space=pltpu.HBM)] * len(self.arrays)

    def matrix_copy(self, sources, wide, sems, i):
        if self.direct:
            source = sources[0].at[:, :, :, pl.ds(i * self.shard, self.shard), :]
        else:
            source = sources[0].at[i]
        return pltpu.make_async_copy(source, wide.at[i], sems.at[i])

    def down_copy(self, sources, tall, sems, core, side):
        if self.direct:
            source = sources[0].at[:, side, core, pl.ds(4 * self.shard, self.part), :]
        else:
            source = sources[1].at[core, side]
        return pltpu.make_async_copy(source, tall.at[core, side], sems.at[4 + core * 2 + side])

    def matrix_value(self, wide, i, columns):
        if self.direct:
            return wide[i, :, :, :, :, columns].reshape(self.width, -1)
        return wide[i, :, columns]

    def matrix_rows(self, wide, i, j, parts):
        if self.direct:
            step = self.matrix[0] // parts
            return wide[i, pl.ds(j * step, step)].reshape(self.width // parts, -1)
        step = self.width // parts
        return wide[i, pl.ds(j * step, step)]

    def down_value(self, tall, core, side, columns):
        if self.direct:
            return tall[core, side, :, :, columns].reshape(-1, columns.size)
        return tall[core, side, :, columns]

    def down_rows(self, tall, core, side):
        return tall[core, side].reshape(-1, self.width)


def hidden_forward(first_low, weights, up_scale, gate_scale, own_rows):
    rows, width = first_low.shape
    units = weights.units
    block = units // 2
    step = 256

    def body(first_ref, up_scale_ref, gate_scale_ref, *refs):
        sources = refs[: len(weights.arrays)]
        hidden_ref, up_ref, gate_ref, partial_ref, turned_ref, wide, tall, sems = refs[
            len(weights.arrays) :
        ]
        copies = [weights.matrix_copy(sources, wide, sems, i) for i in (0, 2, 1, 3)]
        down_copies = [
            weights.down_copy(sources, tall, sems, i, j) for i in range(2) for j in range(2)
        ]
        for copy in copies + down_copies:
            copy.start()
        first = first_ref[...]
        for core in range(2):
            copies[2 * core].wait()
            copies[2 * core + 1].wait()

            for begin in range(0, units, step):
                columns = pl.ds(begin, step)
                here = pl.ds(core * units + begin, step)
                up = matmul(first, weights.matrix_value(wide, core, columns))
                gate = matmul(first, weights.matrix_value(wide, 2 + core, columns))
                up_ref[:, here] = up
                gate_ref[:, here] = gate
                hidden = swiglu(up, gate, up_scale_ref[:, here], gate_scale_ref[:, here])
                hidden_ref[core, :, columns] = hidden.astype(BF)
        for copy in down_copies:
            copy.wait()

        for begin in range(0, width, step):
            columns = pl.ds(begin, step)
            total = None
            for core in range(2):
                for side in range(2):
                    term = matmul(
                        hidden_ref[core, :, pl.ds(side * block, block)],
                        weights.down_value(tall, core, side, columns),
                    )
                    total = term if total is None else total + term
            partial_ref[:, columns] = total
            turned_ref[pl.ds(0, own_rows), columns] = total[own_rows:].astype(BF)
            turned_ref[pl.ds(own_rows, own_rows), columns] = total[:own_rows].astype(BF)

    whole = pl.BlockSpec(memory_space=pltpu.VMEM)
    return pl.pallas_call(
        body,
        out_shape=[
            jax.ShapeDtypeStruct((2, rows, units), BF),
            jax.ShapeDtypeStruct((rows, 2 * units), F32),
            jax.ShapeDtypeStruct((rows, 2 * units), F32),
            jax.ShapeDtypeStruct((rows, width), F32),
            jax.ShapeDtypeStruct((rows, width), BF),
        ],
        in_specs=[whole] * 3 + weights.specs(),
        out_specs=[whole] * 5,
        scratch_shapes=weights.scratch(),
        compiler_params=pltpu.CompilerParams(vmem_limit_bytes=56 * 2**20),
        cost_estimate=COST,
        name="hidden_forward",
    )(first_low, up_scale.reshape(1, -1), gate_scale.reshape(1, -1), *weights.arrays)


def hidden_backward(down_low, up_proj, gate_proj, weights, up_scale, gate_scale, own_rows, earlier):
    rows, width = down_low.shape
    units = weights.units
    block = units // 2

    def body(down_ref, up_ref, gate_ref, up_scale_ref, gate_scale_ref, *refs):
        sources = refs[: len(weights.arrays)]
        low_ref, up_grad_ref, gate_grad_ref, partial_ref, turned_ref, wide, tall, sems = refs[
            len(weights.arrays) + len(earlier) :
        ]
        down_copies = [
            weights.down_copy(sources, tall, sems, i, j) for i in range(2) for j in range(2)
        ]
        copies = [weights.matrix_copy(sources, wide, sems, i) for i in range(4)]
        for copy in down_copies + copies:
            copy.start()
        down = down_ref[...]
        for core in range(2):
            for side in range(2):
                down_copies[core * 2 + side].wait()
                here = pl.ds((core * 2 + side) * block, block)
                grad_hidden = back_matmul(down, weights.down_rows(tall, core, side))
                up_scaling = up_scale_ref[:, here]
                gate_scaling = gate_scale_ref[:, here]
                up = up_ref[:, here]
                gate = gate_ref[:, here]
                scaled = gate_scaling * gate
                sigmoid = jax.nn.sigmoid(scaled)
                silu = scaled * sigmoid
                grad_scaled_up = grad_hidden * silu
                grad_scaled = grad_hidden * (up_scaling * up) * (sigmoid + silu * (1.0 - sigmoid))
                low_ref[0, :, here] = (grad_scaled_up * up_scaling).astype(BF)
                low_ref[1, :, here] = (grad_scaled * gate_scaling).astype(BF)
                up_grad_ref[:, here] = jnp.sum(grad_scaled_up * up, axis=0, keepdims=True)
                gate_grad_ref[:, here] = jnp.sum(grad_scaled * gate, axis=0, keepdims=True)
        for copy in copies:
            copy.wait()
        pieces = 2
        piece = width // pieces
        for j in range(pieces):
            total = None
            for i in range(4):
                term = back_matmul(
                    low_ref[i // 2, :, pl.ds((i % 2) * units, units)],
                    weights.matrix_rows(wide, i, j, pieces),
                )
                total = term if total is None else total + term
            columns = pl.ds(j * piece, piece)
            partial_ref[:, columns] = total
            turned_ref[pl.ds(0, own_rows), columns] = total[own_rows:].astype(BF)
            turned_ref[pl.ds(own_rows, own_rows), columns] = total[:own_rows].astype(BF)

    whole = pl.BlockSpec(memory_space=pltpu.VMEM)
    return pl.pallas_call(
        body,
        out_shape=[
            jax.ShapeDtypeStruct((2, rows, 2 * units), BF),
            jax.ShapeDtypeStruct((1, 2 * units), F32),
            jax.ShapeDtypeStruct((1, 2 * units), F32),
            jax.ShapeDtypeStruct((rows, width), F32),
            jax.ShapeDtypeStruct((rows, width), BF),
        ],
        in_specs=[whole] * 5
        + weights.specs()
        + [pl.BlockSpec(memory_space=pl.ANY)] * len(earlier),
        out_specs=[whole] * 5,
        scratch_shapes=weights.scratch(),
        compiler_params=pltpu.CompilerParams(vmem_limit_bytes=42 * 2**20),
        cost_estimate=COST,
        name="hidden_backward",
    )(
        down_low,
        up_proj,
        gate_proj,
        up_scale.reshape(1, -1),
        gate_scale.reshape(1, -1),
        *weights.arrays,
        *earlier,
    )


def per_device(
    tokens,
    cotangent,
    lengths,
    placement,
    query_weight,
    key_weight,
    value_weight,
    out_weight,
    up_weight,
    gate_weight,
    down_weight,
    scoring,
    upscale,
    gatescale,
    attention_rate,
    feedforward_rate,
):
    size = lax.axis_size("fsdp")
    planes = size // 4
    half = lax.axis_index("grp")
    me = lax.axis_index("fsdp")
    core = me % 2
    side = (me // 2) % 2
    plane = me // 4
    half_scalar = half.reshape(1).astype(jnp.int32)
    which = jnp.stack([core, side]).astype(jnp.int32)
    local_seqs = tokens.shape[0] // size
    seq_len = tokens.shape[1] * size
    width = tokens.shape[2]
    own_rows = local_seqs * seq_len
    shard = query_weight.shape[0]
    hidden_shard = down_weight.shape[0]
    part = hidden_shard // 2
    per_row = hidden_shard // shard
    half_width = width // 2

    def swap_core(array):
        return lax.ppermute(array, "fsdp", [(i, i ^ 1) for i in range(size)])

    def swap_side(array):
        return lax.ppermute(array, "fsdp", [(i, i ^ 2) for i in range(size)])

    def next_plane(array):
        return lax.ppermute(array, "fsdp", [(i, (i + 4) % size) for i in range(size)])

    def swap_half(array):
        return lax.ppermute(array, "grp", [(0, 1), (1, 0)])

    def pick(array, index, axis):
        return lax.dynamic_index_in_dim(array, index, axis, keepdims=False)

    first_group, both = lay_first(
        half_scalar,
        query_weight,
        key_weight,
        value_weight,
        out_weight,
        [scoring, attention_rate, feedforward_rate, upscale, gatescale],
        tokens,
        cotangent,
    )
    arrived = lax.all_to_all(both, "fsdp", split_axis=1, concat_axis=2, tiled=True)
    second_group = lay_second(half_scalar, up_weight, gate_weight, down_weight, planes)
    hidden_width = planes * 4 * part
    core_width = hidden_width // 2
    own_tokens = arrived[0].reshape(own_rows, width)
    other_tokens = swap_half(own_tokens)

    held = [first_group]
    crossed = []
    for i in range(planes):
        here = after(held[-1], *crossed[-1:]) if crossed else held[-1]
        if i < planes - 1:
            held.append(next_plane(here))
        crossed.append(swap_side(here))
    held = held + crossed
    second_whole = lax.all_gather(after(second_group, *held), "fsdp", axis=0)
    held = held + [swap_core(array) for array in held]
    places = []
    for i in range(4 * planes):
        there_core = 1 - core if i >= 2 * planes else core
        there_side = 1 - side if i // planes % 2 else side
        places.append(((plane - i) % planes * 2 + there_side) * 2 + there_core)
    shards = Shards(held, jnp.stack(places).astype(jnp.int32))

    group_order = placement[0]
    own_slots = lax.dynamic_slice_in_dim(group_order, me * local_seqs, local_seqs)
    own_lengths = jnp.take(lengths[0], own_slots)
    valid = (jnp.arange(seq_len, dtype=jnp.int32)[None, :] < own_lengths[:, None]).reshape(
        own_rows, 1
    )
    own_cot = jnp.where(valid, arrived[1].reshape(own_rows, width), jnp.zeros((), BF))
    token_rows = jnp.concatenate([own_tokens, other_tokens])
    other_cot = swap_half(own_cot)

    qkv, query_unit, key_unit, value_low, mixed_half, mixed_turned, scale_float = attention_forward(
        half_scalar, token_rows, shards, seq_len
    )
    attention_mix = scale_float[1:2]
    feed_mix = scale_float[2:3]

    def hidden_scale(begin):
        rows = scale_float[begin : begin + per_row].reshape(2, per_row // 2, planes, 2, 2, shard)
        return jnp.transpose(pick(rows, half, 0), (3, 2, 1, 0, 4)).reshape(-1)

    up_scale = hidden_scale(3)
    gate_scale = hidden_scale(3 + per_row)
    skip = 3 * half_width + 128
    mixed_low, attended, first_state, first_low = first_forward(
        half_scalar, mixed_half, swap_half(mixed_turned), token_rows, attention_mix, shards, skip
    )

    feature = jnp.arange(width, dtype=jnp.int32)
    block = []
    for b in range(2):
        for a in range(2):
            for k in range(planes):
                there_core = core if b == 0 else 1 - core
                there_side = 1 - side if a == 0 else side
                block.append((k * 2 + there_side) * 2 + there_core)
    block = jnp.stack(block).astype(jnp.int32)
    wanted = (block[:, None] * shard + jnp.arange(shard, dtype=jnp.int32)[None, :]).reshape(-1)
    chooser = (feature[:, None] == wanted[None, :]).astype(BF)

    def share_columns(array):
        chosen = matmul(array, chooser).astype(BF)
        return chosen[:, :half_width], swap_core(chosen[:, half_width:])

    def share(array):
        return array, swap_core(array)

    def over_planes(total):
        return lax.psum_scatter(
            total.reshape(planes, total.shape[0] // planes, total.shape[1]),
            "fsdp",
            scatter_dimension=0,
            axis_index_groups=[[k * 4 + j for k in range(planes)] for j in range(4)],
        )

    def joined(kept, arrived_part):
        return (kept.astype(F32) + arrived_part.astype(F32)).astype(BF)

    token_sides = share_columns(token_rows)
    mixed_sides = share_columns(mixed_low)
    first_sides = share_columns(first_low)
    hidden_weights = HiddenWeights(
        after(second_whole, *token_sides, *mixed_sides, *first_sides, other_cot), planes, shard, part
    )
    hidden_low, up_proj, gate_proj, partial, partial_turned = hidden_forward(
        first_low, hidden_weights, up_scale, gate_scale, own_rows
    )
    hidden_other = swap_core(pick(hidden_low, 1 - core, 0))

    layer_own, grad_first, down_low, feed_grad = second_backward(
        partial,
        swap_half(partial_turned),
        first_state,
        own_cot,
        other_cot,
        valid.astype(F32),
        feed_mix,
    )
    down_other = swap_core(down_low)
    down_args = (which, hidden_low, hidden_other, down_low, down_other)
    early = 3 * width // 5
    down_early, down_sent = down_grads(
        "down_sent",
        *down_args,
        [((False, 0, early), (True, 0, early)), ((False, early, width - early),)],
        [],
    )
    down_early = over_planes(down_early)
    down_arrived = swap_side(down_sent)
    up_gate_low, upscale_grad, gatescale_grad, partial, partial_turned = hidden_backward(
        down_low, up_proj, gate_proj, hidden_weights, up_scale, gate_scale, own_rows, [down_sent]
    )
    (down_kept,) = down_grads(
        "down_kept", *down_args, [((True, early, width - early),)], [up_gate_low]
    )
    up_gate_other = swap_core(after(up_gate_low, down_arrived, down_kept))
    partial_other = swap_half(after(partial_turned, down_arrived, down_kept))
    up_side = [(up_gate_low, up_gate_other, (0,))]
    gate_side = [(up_gate_low, up_gate_other, (1,))]
    up_sent = side_grads("up_sent", [first_sides], up_side, False, [])
    up_arrived = swap_side(after(up_sent, down_arrived))
    down_joined = joined(down_kept, after(down_arrived, up_sent))
    down_total = over_planes(down_joined)
    gate_sent = side_grads("gate_sent", [first_sides], gate_side, False, [up_sent])
    attended_cols, grad_mixed, grad_tokens, attention_grad = first_backward(
        half_scalar,
        grad_first,
        partial,
        partial_other,
        token_rows,
        attended,
        attention_mix,
        shards,
        skip,
        [gate_sent],
    )
    qkv_low, scoring_grad, token_own, token_sent = attention_backward(
        half_scalar, grad_mixed, qkv, query_unit, key_unit, value_low, scale_float, shards, seq_len, [down_early]
    )
    up_kept = side_grads("up_kept", [first_sides], up_side, True, [qkv_low])
    early_sent = down_early[:, :early]
    gate_arrived = swap_side(after(gate_sent, up_arrived))
    attended_other = swap_core(after(attended_cols, up_arrived))
    qkv_other = swap_core(after(qkv_low, up_arrived))
    token_other = swap_half(after(token_sent, up_arrived))
    up_joined = joined(up_kept, up_arrived)
    up_total = over_planes(up_joined)
    last_args = (
        [mixed_sides, token_sides],
        [(attended_cols, attended_other, None), (qkv_low, qkv_other, (0, 1, 2))],
    )
    last_sent = side_grads("last_sent", *last_args, False, [up_joined, down_total])
    gate_kept = side_grads("gate_kept", [first_sides], gate_side, True, [last_sent])
    input_own = (grad_tokens + token_own + token_other.astype(F32)).astype(BF)
    last_kept = side_grads("last_kept", *last_args, True, [gate_kept])
    last_arrived = swap_side(after(last_sent, gate_arrived))
    gate_joined = joined(gate_kept, after(gate_arrived, last_kept))
    gate_total = over_planes(gate_joined)
    def hidden_spread(grad):
        blocks = jnp.transpose(grad.reshape(2, 2, planes, part), (2, 1, 0, 3))
        blank = jnp.zeros_like(blocks)
        both_halves = jnp.where(
            half == 0, jnp.stack([blocks, blank], axis=3), jnp.stack([blank, blocks], axis=3)
        )
        return both_halves.reshape(size, hidden_shard)

    blank = jnp.zeros_like(scoring_grad)
    scoring_spread = jnp.where(
        half == 0,
        jnp.concatenate([scoring_grad, blank], axis=1),
        jnp.concatenate([blank, scoring_grad], axis=1),
    )
    small = jnp.concatenate(
        [
            scoring_spread.reshape(size, shard),
            attention_grad.reshape(size, shard),
            feed_grad.reshape(size, shard),
            hidden_spread(upscale_grad),
            hidden_spread(gatescale_grad),
        ],
        axis=1,
    )
    (up_part,) = split_hidden(half_scalar, [up_total], planes, part)
    up_other = swap_half(up_part)
    (outgoing,) = call(
        "outgoing", place_pair, [like(2, own_rows, width)], arrays=[layer_own, input_own], earlier=[up_other]
    )
    returned = lax.all_to_all(
        outgoing.reshape(2, local_seqs, seq_len, width), "fsdp", split_axis=2, concat_axis=1, tiled=True
    )
    (up_out,) = merge_hidden(half_scalar, [up_total], [up_other], planes, part, [returned])
    last_joined = joined(last_kept, after(last_arrived, up_out))
    last_total = over_planes(last_joined).astype(F32)
    early_arrived = swap_side(after(early_sent, last_joined))
    down_total = jnp.concatenate(
        [down_early[:, early:].astype(F32) + early_arrived.astype(F32), down_total.astype(F32)], axis=1
    )
    down_cols = down_total.reshape(part, 2, half_width)
    mine = pick(down_cols, half, 1)
    theirs = swap_half(pick(down_cols, 1 - half, 1).astype(BF)).astype(F32)
    down_out = jnp.where(
        half == 0, jnp.concatenate([mine, theirs]), jnp.concatenate([theirs, mine])
    )
    (small,) = call(
        "pass", place_whole, [like(*small.shape, dtype=F32)], arrays=[small], earlier=[last_joined]
    )
    small = lax.all_to_all(small, "fsdp", split_axis=0, concat_axis=0, tiled=True)
    (total,) = call("add", sum_whole, [like(1, small.shape[1], dtype=F32)], arrays=[small])
    total = total[0]
    total = total + swap_half(total)

    (gate_part,) = split_hidden(half_scalar, [gate_total], planes, part)
    (gate_out,) = merge_hidden(half_scalar, [gate_total], [swap_half(gate_part)], planes, part, [])
    out_total = last_total[:, :half_width]
    qkv_total = last_total[:, half_width:]

    return (
        returned[0],
        returned[1],
        qkv_total[:, :half_width],
        qkv_total[:, half_width : 2 * half_width],
        qkv_total[:, 2 * half_width :],
        out_total,
        up_out,
        gate_out,
        down_out,
        total[:shard],
        total[3 * shard : 3 * shard + hidden_shard],
        total[3 * shard + hidden_shard :],
        total[shard : 2 * shard],
        total[2 * shard : 3 * shard],
    )


def solution(mesh):
    rows = P("grp", "fsdp", None)
    group = P("grp", None)
    matrix = P("fsdp", None)
    vector = P("fsdp")
    split = P("fsdp", "grp")
    return jax.shard_map(
        per_device,
        mesh=mesh,
        in_specs=(rows, rows, group, group) + (matrix,) * 7 + (vector,) * 5,
        out_specs=(rows, rows) + (split,) * 7 + (vector,) * 5,
        check_vma=False,
    )
```

```python
import math

import jax
import jax.numpy as jnp
from jax import lax
from jax.experimental import pallas as pl
from jax.experimental.pallas import tpu as pltpu
from jax.sharding import PartitionSpec as P

H = 20
DK = 64
BF = jnp.bfloat16
F32 = jnp.float32
COST = pl.CostEstimate(flops=1000, bytes_accessed=1000, transcendentals=0)


def swiglu(up_proj, gate_proj, upscale, gatescale):
    scaled = gatescale * gate_proj
    return scaled * jax.nn.sigmoid(scaled) * (upscale * up_proj)


def matmul(left_side, right_side):
    return jnp.dot(left_side, right_side, preferred_element_type=F32)


def weight_grad(left_side, right_side):
    return lax.dot_general(
        left_side, right_side, (((0,), (0,)), ((), ())), preferred_element_type=F32
    )


def back_matmul(grad_rows, weight_rows):
    return lax.dot_general(
        grad_rows, weight_rows, (((1,), (1,)), ((), ())), preferred_element_type=F32
    )


def after(value, *earlier):
    return lax.optimization_barrier((value, *earlier))[0]


def like(*shape, dtype=BF):
    return jax.ShapeDtypeStruct(shape, dtype)


def call(name, body, outs, scalars=(), arrays=(), remote=(), scratch=(), earlier=(), limit=16):
    counts = (len(scalars), len(arrays), len(remote), len(earlier), len(outs))

    def kernel(*refs):
        groups = []
        at = 0
        for count in counts:
            groups.append(refs[at : at + count])
            at += count
        body(*groups[0], *groups[1], groups[2], *groups[4], *refs[at:])

    whole = pl.BlockSpec(memory_space=pltpu.VMEM)
    kept = pl.BlockSpec(memory_space=pl.ANY)
    placed = pl.BlockSpec(memory_space=pltpu.HBM)
    return pl.pallas_call(
        kernel,
        out_shape=list(outs),
        in_specs=[pl.BlockSpec(memory_space=pltpu.SMEM)] * counts[0]
        + [whole] * counts[1]
        + [placed] * counts[2]
        + [kept] * counts[3],
        out_specs=[whole] * counts[4],
        scratch_shapes=list(scratch),
        compiler_params=pltpu.CompilerParams(vmem_limit_bytes=limit * 2**20),
        cost_estimate=COST,
        name=name,
    )(*scalars, *arrays, *remote, *earlier)


class Shards:
    def __init__(self, arrays, places):
        self.direct = arrays[0].shape[0] % 16 == 0
        if self.direct:
            self.arrays, self.places = list(arrays), places
        else:
            whole = jnp.zeros((len(arrays),) + arrays[0].shape, BF)
            for i, array in enumerate(arrays):
                whole = lax.dynamic_update_index_in_dim(whole, array, places[i], 0)
            self.arrays = [whole.reshape(-1, arrays[0].shape[1])]
            self.places = jnp.zeros((1,), jnp.int32)
        self.count = len(self.arrays)
        self.height = self.arrays[0].shape[0]

    def scratch(self, width):
        return [
            pltpu.VMEM((self.count, self.height, width), BF),
            pltpu.SemaphoreType.DMA((self.count,)),
        ]

    def copies(self, places, sources, target, sems, begin, width):
        return [
            pltpu.make_async_copy(
                sources[i].at[:, pl.ds(begin, width)], target.at[places[i]], sems.at[i]
            )
            for i in range(self.count)
        ]

    def columns(self, target, begin, width):
        return target[:, :, pl.ds(begin, width)].reshape(self.count * self.height, width)

    def rows(self, target, index, parts, begin, width):
        if self.direct:
            step = self.count // parts
            rows = target[pl.ds(index * step, step), :, pl.ds(begin, width)]
        else:
            step = self.height // parts
            rows = target[:, pl.ds(pl.multiple_of(index * step, step), step), pl.ds(begin, width)]
        return rows.reshape(-1, width)


def inverse_rms(vector):
    return lax.rsqrt(jnp.mean(vector * vector, axis=-1, keepdims=True) + 1e-06)


def head_sums(values, low_head):
    low_sum = jnp.sum(jnp.where(low_head, values, 0.0), axis=-1, keepdims=True)
    high_sum = jnp.sum(jnp.where(low_head, 0.0, values), axis=-1, keepdims=True)
    return low_sum, high_sum


def head_inverse(vector, low_head):
    low_sum, high_sum = head_sums(vector * vector, low_head)
    return jnp.where(low_head, lax.rsqrt(low_sum + 1e-06), lax.rsqrt(high_sum + 1e-06))


def head_probs(query_head, key_unit, seq_len):
    scores = back_matmul(query_head, key_unit) * math.sqrt(DK)
    query_row = lax.broadcasted_iota(jnp.int32, scores.shape, 0)
    key_row = lax.broadcasted_iota(jnp.int32, scores.shape, 1)
    start = query_row - lax.rem(query_row, seq_len)
    scores = jnp.where((key_row <= query_row) & (key_row >= start), scores, -1e30)
    exp_scores = jnp.exp(scores - jnp.max(scores, axis=-1, keepdims=True))
    return exp_scores / jnp.sum(exp_scores, axis=-1, keepdims=True)


def only(mask, values):
    return jnp.where(mask, values.astype(F32), 0.0).astype(BF)


def turn(ref, rows, columns, value):
    ref[pl.ds(0, rows), columns] = value[rows:].astype(BF)
    ref[pl.ds(rows, rows), columns] = value[:rows].astype(BF)


def attention_forward(half, token_rows, shards, seq_len):
    rows, width = token_rows.shape
    half_width = width // 2
    pairs = half_width // 128
    cols = 3 * half_width + 128

    def body(
        places, half_ref, x_ref, sources, qkv_ref, qu_ref, ku_ref, vl_ref, mixed_ref, turned_ref, scale_ref, w_ref, sems
    ):
        copies = shards.copies(places, sources, w_ref, sems, 0, cols)
        for copy in copies:
            copy.start()
        for copy in copies:
            copy.wait()
        scale_ref[...] = jnp.transpose(
            shards.columns(w_ref, 3 * half_width, 128).astype(F32)
        )[:16]
        x = x_ref[...]
        step = 384
        for begin in range(0, 3 * half_width, step):
            qkv_ref[:, pl.ds(begin, step)] = matmul(x, shards.columns(w_ref, begin, step))
        low_head = lax.broadcasted_iota(jnp.int32, (rows, 128), 1) < DK
        later = half_ref[0] == 1

        def pair(i, carry):
            at = pl.multiple_of(i * 128, 128)
            here = pl.ds(at, 128)
            queries = qkv_ref[:, here]
            key_rows = qkv_ref[:, pl.ds(half_width + at, 128)]
            value_low = qkv_ref[:, pl.ds(2 * half_width + at, 128)].astype(BF)
            scaling = jnp.where(
                later, scale_ref[0:1, pl.ds(half_width + at, 128)], scale_ref[0:1, here]
            )
            query_unit = queries * head_inverse(queries, low_head) * scaling
            key_unit = (key_rows * head_inverse(key_rows, low_head) * scaling).astype(BF)
            mixed = None
            for mask in (low_head, ~low_head):
                probs = head_probs(only(mask, query_unit), key_unit, seq_len)
                head = matmul(probs.astype(BF), value_low)
                mixed = head if mixed is None else jnp.where(low_head, mixed, head)
            qu_ref[:, here] = query_unit.astype(BF)
            ku_ref[:, here] = key_unit
            vl_ref[:, here] = value_low
            mixed_ref[:, here] = mixed.astype(BF)
            turn(turned_ref, rows // 2, here, mixed)
            return carry

        lax.fori_loop(0, pairs, pair, 0)

    return call(
        "attention_forward",
        body,
        [like(rows, 3 * half_width, dtype=F32)] + [like(rows, half_width)] * 5 + [like(16, width, dtype=F32)],
        scalars=[shards.places, half],
        arrays=[token_rows],
        remote=shards.arrays,
        limit=24,
        scratch=shards.scratch(cols),
    )


def place_whole(source, _, target):
    target[...] = source[...]


def place_pair(first, later, _, target):
    target[0] = first[...]
    target[1] = later[...]


def sum_whole(source, _, target):
    target[...] = jnp.sum(source[...], axis=0, keepdims=True)


def place_halves(half_ref, target, own, other):
    width = own.shape[1]

    @pl.when(half_ref[0] == 0)
    def _():
        target[:, pl.ds(0, width)] = own[...]
        target[:, pl.ds(width, width)] = other[...]

    @pl.when(half_ref[0] != 0)
    def _():
        target[:, pl.ds(0, width)] = other[...]
        target[:, pl.ds(width, width)] = own[...]


def first_forward(half, mixed, mixed_other, token_rows, attention_mix, shards, skip):
    rows, width = token_rows.shape

    def body(
        places, half_ref, own_ref, other_ref, x_ref, mix_ref, sources, mixed_ref, attended_ref, first_ref, low_ref, w_ref, sems
    ):
        copies = shards.copies(places, sources, w_ref, sems, skip, width)
        for copy in copies:
            copy.start()
        place_halves(half_ref, mixed_ref, own_ref, other_ref)
        for copy in copies:
            copy.wait()
        for begin in range(0, width, 256):
            attended_ref[:, pl.ds(begin, 256)] = matmul(
                mixed_ref[...], shards.columns(w_ref, begin, 256)
            )
        x = x_ref[...].astype(F32)
        attended = attended_ref[...]
        mix = x + mix_ref[...] * (attended * inverse_rms(attended) - x)
        first = mix * inverse_rms(mix)
        first_ref[...] = first
        low_ref[...] = first.astype(BF)

    return call(
        "first_forward",
        body,
        [like(rows, width)] + [like(rows, width, dtype=F32)] * 2 + [like(rows, width)],
        scalars=[shards.places, half],
        arrays=[mixed, mixed_other, token_rows, attention_mix],
        remote=shards.arrays,
        limit=20,
        scratch=shards.scratch(width),
    )


def mix_backward(base, branch, rate, grad):
    branch_inverse = inverse_rms(branch)
    branch_unit = branch * branch_inverse
    mix = base + rate * (branch_unit - base)
    inverse = inverse_rms(mix)
    value = mix * inverse
    grad_mix = inverse * (grad - value * jnp.mean(grad * value, axis=-1, keepdims=True))
    grad_unit = grad_mix * rate
    grad_branch = branch_inverse * (
        grad_unit - branch_unit * jnp.mean(grad_unit * branch_unit, axis=-1, keepdims=True)
    )
    return value, grad_mix - grad_unit, grad_branch, grad_mix * (branch_unit - base)


def second_backward(partial, partial_other, first_state, cot, cot_other, valid, feed_mix):
    rows, width = partial.shape
    own = rows // 2

    def body(partial_ref, other_ref, first_ref, cot_ref, cot_other_ref, valid_ref, mix_ref, _, layer_ref, grad_ref, low_ref, rate_ref):
        for begin in (0, own):
            here = pl.ds(begin, own)
            down = partial_ref[here, :] + other_ref[here, :].astype(F32)
            grad = (cot_ref if begin == 0 else cot_other_ref)[...].astype(F32)
            value, grad_first, grad_down, grad_rate = mix_backward(
                first_ref[here, :], down, mix_ref[...], grad
            )
            grad_ref[here, :] = grad_first
            low_ref[here, :] = grad_down.astype(BF)
            if begin == 0:
                layer_ref[...] = (value * valid_ref[...]).astype(BF)
                rate_ref[...] = jnp.sum(grad_rate, axis=0, keepdims=True)

    return call(
        "second_backward",
        body,
        [like(own, width), like(rows, width, dtype=F32), like(rows, width), like(1, width, dtype=F32)],
        limit=18,
        arrays=[partial, partial_other, first_state, cot, cot_other, valid, feed_mix],
    )


def first_backward(half, grad_first, partial, partial_other, token_rows, attended, attention_mix, shards, skip, earlier):
    rows, width = partial.shape
    own = rows // 2
    half_width = width // 2

    def body(
        places, half_ref, grad_ref, partial_ref, other_ref, x_ref, attended_ref, mix_ref, sources, cols_ref, mixed_ref, token_ref, rate_ref, low_ref, w_ref, sems
    ):
        copies = shards.copies(places, sources, w_ref, sems, skip, width)
        for copy in copies:
            copy.start()
        for begin in (0, own):
            here = pl.ds(begin, own)
            grad = grad_ref[here, :] + partial_ref[here, :] + other_ref[here, :].astype(F32)
            _, grad_token, grad_attended, grad_rate = mix_backward(
                x_ref[here, :].astype(F32), attended_ref[here, :], mix_ref[...], grad
            )
            low_ref[here, :] = grad_attended.astype(BF)
            if begin == 0:
                token_ref[...] = grad_token
                rate_ref[...] = jnp.sum(grad_rate, axis=0, keepdims=True)
        at = pl.multiple_of(half_ref[0] * half_width, 128)
        cols_ref[...] = low_ref[:, pl.ds(at, half_width)]
        for copy in copies:
            copy.wait()
        mixed_ref[...] = back_matmul(
            low_ref[...], shards.rows(w_ref, half_ref[0], 2, 0, width)
        ).astype(BF)

    return call(
        "first_backward",
        body,
        [like(rows, half_width)] * 2 + [like(own, width, dtype=F32), like(1, width, dtype=F32)],
        scalars=[shards.places, half],
        arrays=[grad_first, partial, partial_other, token_rows, attended, attention_mix],
        remote=shards.arrays,
        limit=20,
        scratch=[pltpu.VMEM((rows, width), BF)] + shards.scratch(width),
        earlier=earlier,
    )


def attention_backward(half, grad_mixed, qkv, query_unit, key_unit, value_low, scales, shards, seq_len, earlier):
    rows, half_width = grad_mixed.shape
    width = 2 * half_width
    pairs = half_width // 128
    own = rows // 2

    def body(
        places, half_ref, gm_ref, qkv_ref, qu_ref, ku_ref, vl_ref, scale_ref, sources, grads_ref, scoring_ref, own_ref, other_ref, w_ref, sems
    ):
        copies = shards.copies(places, sources, w_ref, sems, 0, 3 * half_width)
        for copy in copies:
            copy.start()
        low_head = lax.broadcasted_iota(jnp.int32, (rows, 128), 1) < DK
        later = half_ref[0] == 1

        def pair(i, carry):
            at = pl.multiple_of(i * 128, 128)
            here = pl.ds(at, 128)
            query_unit = qu_ref[:, here]
            key_unit = ku_ref[:, here]
            value_low = vl_ref[:, here]
            scaling = jnp.where(
                later, scale_ref[0:1, pl.ds(half_width + at, 128)], scale_ref[0:1, here]
            )
            grad_value = grad_qunit = grad_kunit = None
            for mask in (low_head, ~low_head):
                probs = head_probs(only(mask, query_unit), key_unit, seq_len)
                grad_head = only(mask, gm_ref[:, here])
                value_part = weight_grad(probs.astype(BF), grad_head)
                grad_probs = back_matmul(grad_head, value_low)
                grad_scores = (
                    probs * (grad_probs - jnp.sum(grad_probs * probs, axis=-1, keepdims=True))
                ).astype(BF)
                query_part = matmul(grad_scores, key_unit)
                key_part = weight_grad(grad_scores, query_unit)
                if grad_value is None:
                    grad_value, grad_qunit, grad_kunit = value_part, query_part, key_part
                else:
                    grad_value = grad_value + value_part
                    grad_qunit = jnp.where(low_head, grad_qunit, query_part)
                    grad_kunit = jnp.where(low_head, grad_kunit, key_part)
            scoring_grad = None
            for place, grad in ((0, grad_qunit), (1, grad_kunit)):
                raw = qkv_ref[:, pl.ds(place * half_width + at, 128)]
                grad = grad * math.sqrt(DK)
                inverse = head_inverse(raw, low_head)
                unit = raw * inverse
                term = jnp.sum(grad * unit, axis=0, keepdims=True)
                scoring_grad = term if scoring_grad is None else scoring_grad + term
                grad = grad * scaling
                low_sum, high_sum = head_sums(grad * unit, low_head)
                grads_ref[place, :, here] = (
                    inverse * (grad - unit * jnp.where(low_head, low_sum, high_sum))
                ).astype(BF)
            grads_ref[2, :, here] = grad_value.astype(BF)
            scoring_ref[:, here] = scoring_grad
            return carry

        lax.fori_loop(0, pairs, pair, 0)
        for copy in copies:
            copy.wait()
        for piece in range(2):
            total = None
            for j in range(3):
                term = back_matmul(
                    grads_ref[j], shards.rows(w_ref, piece, 2, j * half_width, half_width)
                )
                total = term if total is None else total + term
            columns = pl.ds(piece * half_width, half_width)
            own_ref[:, columns] = total[:own]
            other_ref[:, columns] = total[own:].astype(BF)

    return call(
        "attention_backward",
        body,
        [
            like(3, rows, half_width),
            like(1, half_width, dtype=F32),
            like(own, width, dtype=F32),
            like(own, width),
        ],
        scalars=[shards.places, half],
        arrays=[grad_mixed, qkv, query_unit, key_unit, value_low, scales],
        remote=shards.arrays,
        limit=56,
        scratch=shards.scratch(3 * half_width),
        earlier=earlier,
    )


def down_grads(name, which, hidden, hidden_other, down, down_other, pieces, earlier):
    rows, units = hidden_other.shape
    block = units // 2

    def body(which_ref, hidden_ref, hidden_other_ref, down_ref, down_other_ref, _, *out_refs):
        for out_ref, parts in zip(out_refs, pieces):
            place = 0
            for kept, begin, width in parts:
                side = which_ref[1] if kept else 1 - which_ref[1]
                columns = pl.ds(pl.multiple_of(side * block, 128), block)
                own = hidden_ref[which_ref[0], :, columns]
                other = hidden_other_ref[:, columns]


                def piece(i, carry, own=own, other=other, begin=begin, place=place, out_ref=out_ref):
                    at = pl.multiple_of(i * 256, 256)
                    here = pl.ds(begin + at, 256)
                    total = weight_grad(own, down_ref[:, here])
                    total = total + weight_grad(other, down_other_ref[:, here])
                    out_ref[:, pl.ds(place + at, 256)] = total.astype(BF)
                    return carry

                lax.fori_loop(0, width // 256, piece, 0)
                place += width

    return call(
        name,
        body,
        [like(block, sum(width for _, _, width in parts)) for parts in pieces],
        scalars=[which],
        arrays=[hidden, hidden_other, down, down_other],
        earlier=earlier,
    )


def side_grads(name, lefts, rights, kept, earlier):
    block = lefts[0][0].shape[1] // 2
    number = len(lefts)
    total_width = sum(right[0].shape[-1] * len(right[2] or (0,)) for right in rights)

    def body(*refs):
        refs = [ref for ref in refs if not isinstance(ref, tuple)]
        out_ref = refs[-1]
        begin = 0
        for i in range(number):
            own_ref, other_ref, right_ref, right_other_ref = refs[4 * i : 4 * i + 4]
            columns = pl.ds(block if kept else 0, block)
            own = own_ref[:, columns]
            other = other_ref[:, columns]
            for index in rights[i][2] or (None,):
                for at in range(0, right_ref.shape[-1], 640):
                    here = (slice(None), pl.ds(at, 640))
                    if index is not None:
                        here = (index, *here)
                    total = weight_grad(own, right_ref[here]) + weight_grad(other, right_other_ref[here])
                    out_ref[:, pl.ds(begin, 640)] = total.astype(out_ref.dtype)
                    begin += 640

    arrays = []
    for left, right in zip(lefts, rights):
        arrays += [*left, *right[:2]]
    return call(
        name,
        body,
        [like(block, total_width)],
        limit=20,
        arrays=arrays,
        earlier=earlier,
    )[0]


def lay_first(half, query_weight, key_weight, value_weight, out_weight, scales, tokens, cotangent):
    shard, width = query_weight.shape
    half_width = width // 2

    def body(half_ref, q_ref, k_ref, v_ref, out_ref, token_ref, cot_ref, *refs):
        target, both, square = refs[-3:]
        both[0] = token_ref[...]
        both[1] = cot_ref[...]
        for i, ref in enumerate((q_ref, k_ref, v_ref)):
            place = pl.ds(i * half_width, half_width)

            @pl.when(half_ref[0] == 0)
            def _():
                target[:, place] = ref[:, pl.ds(0, half_width)]

            @pl.when(half_ref[0] != 0)
            def _():
                target[:, place] = ref[:, pl.ds(half_width, half_width)]

        square[...] = jnp.zeros_like(square)
        row = 0
        for ref in refs[: len(scales)]:
            values = ref[...].astype(F32)
            for begin in range(0, values.shape[1], shard):
                square[pl.ds(row, 1), pl.ds(0, shard)] = values[:, begin : begin + shard]
                row += 1
        target[:, pl.ds(3 * half_width, 128)] = jnp.transpose(square[...])[:shard].astype(BF)
        target[:, pl.ds(3 * half_width + 128, width)] = out_ref[...]

    return call(
        "lay_first",
        body,
        [like(shard, 3 * half_width + 128 + width), like(2, *tokens.shape)],
        limit=56,
        scalars=[half],
        arrays=[query_weight, key_weight, value_weight, out_weight, tokens, cotangent]
        + [scale.reshape(1, -1) for scale in scales],
        scratch=[pltpu.VMEM((128, 128), F32)],
    )


def lay_second(half, up_weight, gate_weight, down_weight, planes):
    shard = up_weight.shape[0]
    part = down_weight.shape[0] // 2
    width = down_weight.shape[1]

    def body(half_ref, up_ref, gate_ref, down_ref, _, target):
        upper = half_ref[0] != 0
        for i, ref in enumerate((up_ref, gate_ref)):
            for core in range(2):
                rows = slice((2 * i + core) * shard, (2 * i + core + 1) * shard)
                for side in range(2):
                    for plane in range(planes):
                        begin = ((plane * 2 + side) * 2 + core) * 2 * part
                        place = (side * planes + plane) * part
                        target[rows, place : place + part] = jnp.where(
                            upper,
                            ref[:, begin + part : begin + 2 * part].astype(F32),
                            ref[:, begin : begin + part].astype(F32),
                        ).astype(BF)

        @pl.when(jnp.logical_not(upper))
        def _():
            target[pl.ds(4 * shard, part), :] = down_ref[pl.ds(0, part), :]

        @pl.when(upper)
        def _():
            target[pl.ds(4 * shard, part), :] = down_ref[pl.ds(part, part), :]

    return call(
        "lay_second",
        body,
        [like(4 * shard + part, width)],
        limit=56,
        scalars=[half],
        arrays=[up_weight, gate_weight, down_weight],
    )[0]


def split_hidden(half, totals, planes, part):
    shard, width = totals[0].shape
    run = planes // 2 * part

    def body(half_ref, *refs):
        for source, target in zip(refs[: len(totals)], refs[-len(totals) :]):
            for i in range(4):
                begin = 2 * i * run
                first, later = source[:, begin : begin + run], source[:, begin + run : begin + 2 * run]
                target[:, i * run : (i + 1) * run] = jnp.where(
                    half_ref[0] == 0, later.astype(F32), first.astype(F32)
                ).astype(BF)

    return call(
        "split_hidden",
        body,
        [like(shard, width // 2)] * len(totals),
        scalars=[half],
        arrays=totals,
    )


def merge_hidden(half, totals, others, planes, part, earlier):
    shard, width = totals[0].shape
    run = planes // 2 * part

    def body(half_ref, *refs):
        number = len(totals)
        upper = half_ref[0] != 0
        for own_ref, other_ref, target in zip(refs[:number], refs[number : 2 * number], refs[-number:]):
            for plane in range(planes // 2):
                for side in range(2):
                    for core in range(2):
                        i = core * 2 + side
                        begin = 2 * i * run + plane * part
                        own = jnp.where(
                            upper,
                            own_ref[:, begin + run : begin + run + part].astype(F32),
                            own_ref[:, begin : begin + part].astype(F32),
                        )
                        begin = i * run + plane * part
                        other = other_ref[:, begin : begin + part].astype(F32)
                        begin = ((plane * 2 + side) * 2 + core) * 2 * part
                        target[:, begin : begin + part] = jnp.where(upper, other, own)
                        target[:, begin + part : begin + 2 * part] = jnp.where(upper, own, other)

    return call(
        "merge_hidden",
        body,
        [like(shard, width, dtype=F32)] * len(totals),
        scalars=[half],
        arrays=[*totals, *others],
        earlier=earlier,
    )


class HiddenWeights:
    def __init__(self, gathered, planes, shard, part):
        width = gathered.shape[2]
        units = 2 * planes * part
        self.direct = shard % 16 == 0 and part % 16 == 0
        self.width, self.units, self.shard, self.part = width, units, shard, part
        if self.direct:
            self.arrays = [gathered.reshape(planes, 2, 2, -1, width)]
            self.matrix = (planes, 2, 2, shard, units)
            self.down = (planes, part, width)
        else:
            blocks = gathered[:, 4 * shard :].reshape(planes, 2, 2, part, width)
            self.arrays = [
                jnp.stack(
                    [gathered[:, i * shard : (i + 1) * shard].reshape(width, width) for i in range(4)]
                ),
                jnp.transpose(blocks, (2, 1, 0, 3, 4)).reshape(2, 2, planes * part, width),
            ]
            self.matrix = (width, units)
            self.down = (planes * part, width)

    def scratch(self):
        return [
            pltpu.VMEM((4,) + self.matrix, BF),
            pltpu.VMEM((2, 2) + self.down, BF),
            pltpu.SemaphoreType.DMA((8,)),
        ]

    def specs(self):
        return [pl.BlockSpec(memory_space=pltpu.HBM)] * len(self.arrays)

    def matrix_copy(self, sources, wide, sems, i):
        if self.direct:
            source = sources[0].at[:, :, :, pl.ds(i * self.shard, self.shard), :]
        else:
            source = sources[0].at[i]
        return pltpu.make_async_copy(source, wide.at[i], sems.at[i])

    def down_copy(self, sources, tall, sems, core, side):
        if self.direct:
            source = sources[0].at[:, side, core, pl.ds(4 * self.shard, self.part), :]
        else:
            source = sources[1].at[core, side]
        return pltpu.make_async_copy(source, tall.at[core, side], sems.at[4 + core * 2 + side])

    def matrix_value(self, wide, i, columns):
        if self.direct:
            return wide[i, :, :, :, :, columns].reshape(self.width, -1)
        return wide[i, :, columns]

    def matrix_rows(self, wide, i, j, parts):
        if self.direct:
            step = self.matrix[0] // parts
            return wide[i, pl.ds(j * step, step)].reshape(self.width // parts, -1)
        step = self.width // parts
        return wide[i, pl.ds(j * step, step)]

    def down_value(self, tall, core, side, columns):
        if self.direct:
            return tall[core, side, :, :, columns].reshape(-1, columns.size)
        return tall[core, side, :, columns]

    def down_rows(self, tall, core, side):
        return tall[core, side].reshape(-1, self.width)


def hidden_forward(first_low, weights, up_scale, gate_scale, own_rows):
    rows, width = first_low.shape
    units = weights.units
    block = units // 2
    step = 256

    def body(first_ref, up_scale_ref, gate_scale_ref, *refs):
        sources = refs[: len(weights.arrays)]
        hidden_ref, up_ref, gate_ref, partial_ref, turned_ref, wide, tall, sems = refs[
            len(weights.arrays) :
        ]
        copies = [weights.matrix_copy(sources, wide, sems, i) for i in (0, 2, 1, 3)]
        down_copies = [
            weights.down_copy(sources, tall, sems, i, j) for i in range(2) for j in range(2)
        ]
        for copy in copies + down_copies:
            copy.start()
        first = first_ref[...]
        for core in range(2):
            copies[2 * core].wait()
            copies[2 * core + 1].wait()

            for begin in range(0, units, step):
                columns = pl.ds(begin, step)
                here = pl.ds(core * units + begin, step)
                up = matmul(first, weights.matrix_value(wide, core, columns))
                gate = matmul(first, weights.matrix_value(wide, 2 + core, columns))
                up_ref[:, here] = up.astype(BF)
                gate_ref[:, here] = gate.astype(BF)
                hidden = swiglu(up, gate, up_scale_ref[:, here], gate_scale_ref[:, here])
                hidden_ref[core, :, columns] = hidden.astype(BF)
        for copy in down_copies:
            copy.wait()

        for begin in range(0, width, step):
            columns = pl.ds(begin, step)
            total = None
            for core in range(2):
                for side in range(2):
                    term = matmul(
                        hidden_ref[core, :, pl.ds(side * block, block)],
                        weights.down_value(tall, core, side, columns),
                    )
                    total = term if total is None else total + term
            partial_ref[:, columns] = total
            turned_ref[pl.ds(0, own_rows), columns] = total[own_rows:].astype(BF)
            turned_ref[pl.ds(own_rows, own_rows), columns] = total[:own_rows].astype(BF)

    whole = pl.BlockSpec(memory_space=pltpu.VMEM)
    return pl.pallas_call(
        body,
        out_shape=[
            jax.ShapeDtypeStruct((2, rows, units), BF),
            jax.ShapeDtypeStruct((rows, 2 * units), BF),
            jax.ShapeDtypeStruct((rows, 2 * units), BF),
            jax.ShapeDtypeStruct((rows, width), F32),
            jax.ShapeDtypeStruct((rows, width), BF),
        ],
        in_specs=[whole] * 3 + weights.specs(),
        out_specs=[whole] * 5,
        scratch_shapes=weights.scratch(),
        compiler_params=pltpu.CompilerParams(vmem_limit_bytes=56 * 2**20),
        cost_estimate=COST,
        name="hidden_forward",
    )(first_low, up_scale.reshape(1, -1), gate_scale.reshape(1, -1), *weights.arrays)


def hidden_backward(down_low, up_proj, gate_proj, weights, up_scale, gate_scale, own_rows, earlier):
    rows, width = down_low.shape
    units = weights.units
    block = units // 2

    def body(down_ref, up_ref, gate_ref, up_scale_ref, gate_scale_ref, *refs):
        sources = refs[: len(weights.arrays)]
        low_ref, gate_low_ref, up_grad_ref, gate_grad_ref, partial_ref, turned_ref, wide, tall, sems = refs[
            len(weights.arrays) + len(earlier) :
        ]
        down_copies = [
            weights.down_copy(sources, tall, sems, i, j) for i in range(2) for j in range(2)
        ]
        copies = [weights.matrix_copy(sources, wide, sems, i) for i in range(4)]
        for copy in down_copies + copies:
            copy.start()
        down = down_ref[...]
        for core in range(2):
            for side in range(2):
                down_copies[core * 2 + side].wait()
                here = pl.ds((core * 2 + side) * block, block)
                grad_hidden = back_matmul(down, weights.down_rows(tall, core, side))
                up_scaling = up_scale_ref[:, here]
                gate_scaling = gate_scale_ref[:, here]
                up = up_ref[:, here].astype(F32)
                gate = gate_ref[:, here].astype(F32)
                scaled = gate_scaling * gate
                sigmoid = jax.nn.sigmoid(scaled)
                silu = scaled * sigmoid
                grad_scaled_up = grad_hidden * silu
                grad_scaled = grad_hidden * (up_scaling * up) * (sigmoid + silu * (1.0 - sigmoid))
                low_ref[:, here] = (grad_scaled_up * up_scaling).astype(BF)
                gate_low_ref[:, here] = (grad_scaled * gate_scaling).astype(BF)
                up_grad_ref[:, here] = jnp.sum(grad_scaled_up * up, axis=0, keepdims=True)
                gate_grad_ref[:, here] = jnp.sum(grad_scaled * gate, axis=0, keepdims=True)
        for copy in copies:
            copy.wait()
        pieces = 2
        piece = width // pieces
        for j in range(pieces):
            total = None
            for i in range(4):
                term = back_matmul(
                    (low_ref, gate_low_ref)[i // 2][:, pl.ds((i % 2) * units, units)],
                    weights.matrix_rows(wide, i, j, pieces),
                )
                total = term if total is None else total + term
            columns = pl.ds(j * piece, piece)
            partial_ref[:, columns] = total
            turned_ref[pl.ds(0, own_rows), columns] = total[own_rows:].astype(BF)
            turned_ref[pl.ds(own_rows, own_rows), columns] = total[:own_rows].astype(BF)

    whole = pl.BlockSpec(memory_space=pltpu.VMEM)
    return pl.pallas_call(
        body,
        out_shape=[
            jax.ShapeDtypeStruct((rows, 2 * units), BF),
            jax.ShapeDtypeStruct((rows, 2 * units), BF),
            jax.ShapeDtypeStruct((1, 2 * units), F32),
            jax.ShapeDtypeStruct((1, 2 * units), F32),
            jax.ShapeDtypeStruct((rows, width), F32),
            jax.ShapeDtypeStruct((rows, width), BF),
        ],
        in_specs=[whole] * 5
        + weights.specs()
        + [pl.BlockSpec(memory_space=pl.ANY)] * len(earlier),
        out_specs=[whole] * 6,
        scratch_shapes=weights.scratch(),
        compiler_params=pltpu.CompilerParams(vmem_limit_bytes=56 * 2**20),
        cost_estimate=COST,
        name="hidden_backward",
    )(
        down_low,
        up_proj,
        gate_proj,
        up_scale.reshape(1, -1),
        gate_scale.reshape(1, -1),
        *weights.arrays,
        *earlier,
    )


def per_device(
    tokens,
    cotangent,
    lengths,
    placement,
    query_weight,
    key_weight,
    value_weight,
    out_weight,
    up_weight,
    gate_weight,
    down_weight,
    scoring,
    upscale,
    gatescale,
    attention_rate,
    feedforward_rate,
):
    size = lax.axis_size("fsdp")
    planes = size // 4
    half = lax.axis_index("grp")
    me = lax.axis_index("fsdp")
    core = me % 2
    side = (me // 2) % 2
    plane = me // 4
    half_scalar = half.reshape(1).astype(jnp.int32)
    which = jnp.stack([core, side]).astype(jnp.int32)
    local_seqs = tokens.shape[0] // size
    seq_len = tokens.shape[1] * size
    width = tokens.shape[2]
    own_rows = local_seqs * seq_len
    shard = query_weight.shape[0]
    hidden_shard = down_weight.shape[0]
    part = hidden_shard // 2
    per_row = hidden_shard // shard
    half_width = width // 2

    def swap_core(array):
        return lax.ppermute(array, "fsdp", [(i, i ^ 1) for i in range(size)])

    def swap_side(array):
        return lax.ppermute(array, "fsdp", [(i, i ^ 2) for i in range(size)])

    def next_plane(array):
        return lax.ppermute(array, "fsdp", [(i, (i + 4) % size) for i in range(size)])

    def swap_half(array):
        return lax.ppermute(array, "grp", [(0, 1), (1, 0)])

    def pick(array, index, axis):
        return lax.dynamic_index_in_dim(array, index, axis, keepdims=False)

    first_group, both = lay_first(
        half_scalar,
        query_weight,
        key_weight,
        value_weight,
        out_weight,
        [scoring, attention_rate, feedforward_rate, upscale, gatescale],
        tokens,
        cotangent,
    )
    arrived = lax.all_to_all(both, "fsdp", split_axis=1, concat_axis=2, tiled=True)
    second_group = lay_second(half_scalar, up_weight, gate_weight, down_weight, planes)
    hidden_width = planes * 4 * part
    core_width = hidden_width // 2
    own_tokens = arrived[0].reshape(own_rows, width)
    other_tokens = swap_half(own_tokens)

    held = [first_group]
    crossed = []
    for i in range(planes):
        here = after(held[-1], *crossed[-1:]) if crossed else held[-1]
        if i < planes - 1:
            held.append(next_plane(here))
        crossed.append(swap_side(here))
    held = held + crossed
    second_whole = lax.all_gather(after(second_group, *held[:planes], *crossed[:-1]), "fsdp", axis=0)
    held = held + [swap_core(array) for array in held]
    places = []
    for i in range(4 * planes):
        there_core = 1 - core if i >= 2 * planes else core
        there_side = 1 - side if i // planes % 2 else side
        places.append(((plane - i) % planes * 2 + there_side) * 2 + there_core)
    shards = Shards(held, jnp.stack(places).astype(jnp.int32))

    group_order = placement[0]
    own_slots = lax.dynamic_slice_in_dim(group_order, me * local_seqs, local_seqs)
    own_lengths = jnp.take(lengths[0], own_slots)
    valid = (jnp.arange(seq_len, dtype=jnp.int32)[None, :] < own_lengths[:, None]).reshape(
        own_rows, 1
    )
    own_cot = jnp.where(valid, arrived[1].reshape(own_rows, width), jnp.zeros((), BF))
    token_rows = jnp.concatenate([own_tokens, other_tokens])
    other_cot = swap_half(own_cot)

    qkv, query_unit, key_unit, value_low, mixed_half, mixed_turned, scale_float = attention_forward(
        half_scalar, token_rows, shards, seq_len
    )
    attention_mix = scale_float[1:2]
    feed_mix = scale_float[2:3]

    def hidden_scale(begin):
        rows = scale_float[begin : begin + per_row].reshape(2, per_row // 2, planes, 2, 2, shard)
        return jnp.transpose(pick(rows, half, 0), (3, 2, 1, 0, 4)).reshape(-1)

    up_scale = hidden_scale(3)
    gate_scale = hidden_scale(3 + per_row)
    skip = 3 * half_width + 128
    mixed_low, attended, first_state, first_low = first_forward(
        half_scalar, mixed_half, swap_half(mixed_turned), token_rows, attention_mix, shards, skip
    )

    feature = jnp.arange(width, dtype=jnp.int32)
    block = []
    for b in range(2):
        for a in range(2):
            for k in range(planes):
                there_core = core if b == 0 else 1 - core
                there_side = 1 - side if a == 0 else side
                block.append((k * 2 + there_side) * 2 + there_core)
    block = jnp.stack(block).astype(jnp.int32)
    wanted = (block[:, None] * shard + jnp.arange(shard, dtype=jnp.int32)[None, :]).reshape(-1)
    chooser = (feature[:, None] == wanted[None, :]).astype(BF)

    def share_columns(array):
        chosen = matmul(array, chooser).astype(BF)
        return chosen[:, :half_width], swap_core(chosen[:, half_width:])

    def share(array):
        return array, swap_core(array)

    def over_planes(total):
        return lax.psum_scatter(
            total.reshape(planes, total.shape[0] // planes, total.shape[1]),
            "fsdp",
            scatter_dimension=0,
            axis_index_groups=[[k * 4 + j for k in range(planes)] for j in range(4)],
        )

    def joined(kept, arrived_part):
        return (kept.astype(F32) + arrived_part.astype(F32)).astype(BF)

    token_sides = share_columns(token_rows)
    mixed_sides = share_columns(mixed_low)
    first_sides = share_columns(first_low)
    hidden_weights = HiddenWeights(
        after(second_whole, *token_sides, *mixed_sides, *first_sides, other_cot), planes, shard, part
    )
    hidden_low, up_proj, gate_proj, partial, partial_turned = hidden_forward(
        first_low, hidden_weights, up_scale, gate_scale, own_rows
    )
    hidden_other = swap_core(pick(hidden_low, 1 - core, 0))

    layer_own, grad_first, down_low, feed_grad = second_backward(
        partial,
        swap_half(partial_turned),
        first_state,
        own_cot,
        other_cot,
        valid.astype(F32),
        feed_mix,
    )
    down_other = swap_core(down_low)
    down_args = (which, hidden_low, hidden_other, down_low, down_other)
    early = 3 * width // 5
    down_early, down_sent = down_grads(
        "down_sent",
        *down_args,
        [((False, 0, early), (True, 0, early)), ((False, early, width - early),)],
        [],
    )
    down_early = over_planes(down_early)
    down_arrived = swap_side(down_sent)
    up_low, gate_low, upscale_grad, gatescale_grad, partial, partial_turned = hidden_backward(
        down_low, up_proj, gate_proj, hidden_weights, up_scale, gate_scale, own_rows, [down_sent]
    )
    (down_kept,) = down_grads(
        "down_kept", *down_args, [((True, early, width - early),)], [up_low]
    )
    up_other = swap_core(after(up_low, down_arrived, down_kept))
    gate_other = swap_core(after(gate_low, down_arrived, down_kept))
    partial_other = swap_half(after(partial_turned, down_arrived, down_kept))
    up_side = [(up_low, up_other, None)]
    gate_side = [(gate_low, gate_other, None)]
    up_sent = side_grads("up_sent", [first_sides], up_side, False, [])
    up_arrived = swap_side(after(up_sent, down_arrived))
    down_joined = joined(down_kept, after(down_arrived, up_sent))
    down_total = over_planes(down_joined)
    gate_sent = side_grads("gate_sent", [first_sides], gate_side, False, [up_sent])
    attended_cols, grad_mixed, grad_tokens, attention_grad = first_backward(
        half_scalar,
        grad_first,
        partial,
        partial_other,
        token_rows,
        attended,
        attention_mix,
        shards,
        skip,
        [gate_sent],
    )
    qkv_low, scoring_grad, token_own, token_sent = attention_backward(
        half_scalar, grad_mixed, qkv, query_unit, key_unit, value_low, scale_float, shards, seq_len, [down_early]
    )
    up_kept = side_grads("up_kept", [first_sides], up_side, True, [qkv_low])
    early_sent = down_early[:, :early]
    gate_arrived = swap_side(after(gate_sent, up_arrived))
    attended_other = swap_core(after(attended_cols, up_arrived))
    qkv_other = swap_core(after(qkv_low, up_arrived))
    token_other = swap_half(after(token_sent, up_arrived))
    up_joined = joined(up_kept, up_arrived)
    up_total = over_planes(up_joined)
    last_args = (
        [mixed_sides, token_sides],
        [(attended_cols, attended_other, None), (qkv_low, qkv_other, (0, 1, 2))],
    )
    last_sent = side_grads("last_sent", *last_args, False, [up_joined, down_total])
    gate_kept = side_grads("gate_kept", [first_sides], gate_side, True, [last_sent])
    input_own = (grad_tokens + token_own + token_other.astype(F32)).astype(BF)
    last_kept = side_grads("last_kept", *last_args, True, [gate_kept])
    last_arrived = swap_side(after(last_sent, gate_arrived))
    gate_joined = joined(gate_kept, after(gate_arrived, last_kept))
    gate_total = over_planes(gate_joined)
    def hidden_spread(grad):
        blocks = jnp.transpose(grad.reshape(2, 2, planes, part), (2, 1, 0, 3))
        blank = jnp.zeros_like(blocks)
        both_halves = jnp.where(
            half == 0, jnp.stack([blocks, blank], axis=3), jnp.stack([blank, blocks], axis=3)
        )
        return both_halves.reshape(size, hidden_shard)

    blank = jnp.zeros_like(scoring_grad)
    scoring_spread = jnp.where(
        half == 0,
        jnp.concatenate([scoring_grad, blank], axis=1),
        jnp.concatenate([blank, scoring_grad], axis=1),
    )
    small = jnp.concatenate(
        [
            scoring_spread.reshape(size, shard),
            attention_grad.reshape(size, shard),
            feed_grad.reshape(size, shard),
            hidden_spread(upscale_grad),
            hidden_spread(gatescale_grad),
        ],
        axis=1,
    )
    (up_part,) = split_hidden(half_scalar, [up_total], planes, part)
    up_swapped = swap_half(up_part)
    (outgoing,) = call(
        "outgoing", place_pair, [like(2, own_rows, width)], arrays=[layer_own, input_own], earlier=[up_swapped]
    )
    returned = lax.all_to_all(
        outgoing.reshape(2, local_seqs, seq_len, width), "fsdp", split_axis=2, concat_axis=1, tiled=True
    )
    (up_out,) = merge_hidden(half_scalar, [up_total], [up_swapped], planes, part, [returned])
    last_joined = joined(last_kept, after(last_arrived, up_out))
    last_total = over_planes(last_joined).astype(F32)
    early_arrived = swap_side(after(early_sent, last_joined))
    down_total = jnp.concatenate(
        [down_early[:, early:].astype(F32) + early_arrived.astype(F32), down_total.astype(F32)], axis=1
    )
    down_cols = down_total.reshape(part, 2, half_width)
    mine = pick(down_cols, half, 1)
    theirs = swap_half(pick(down_cols, 1 - half, 1).astype(BF)).astype(F32)
    down_out = jnp.where(
        half == 0, jnp.concatenate([mine, theirs]), jnp.concatenate([theirs, mine])
    )
    (small,) = call(
        "pass", place_whole, [like(*small.shape, dtype=F32)], arrays=[small], earlier=[last_joined]
    )
    small = lax.all_to_all(small, "fsdp", split_axis=0, concat_axis=0, tiled=True)
    (total,) = call("add", sum_whole, [like(1, small.shape[1], dtype=F32)], arrays=[small])
    total = total[0]
    total = total + swap_half(total)

    (gate_part,) = split_hidden(half_scalar, [gate_total], planes, part)
    (gate_out,) = merge_hidden(half_scalar, [gate_total], [swap_half(gate_part)], planes, part, [])
    out_total = last_total[:, :half_width]
    qkv_total = last_total[:, half_width:]

    return (
        returned[0],
        returned[1],
        qkv_total[:, :half_width],
        qkv_total[:, half_width : 2 * half_width],
        qkv_total[:, 2 * half_width :],
        out_total,
        up_out,
        gate_out,
        down_out,
        total[:shard],
        total[3 * shard : 3 * shard + hidden_shard],
        total[3 * shard + hidden_shard :],
        total[shard : 2 * shard],
        total[2 * shard : 3 * shard],
    )


def solution(mesh):
    rows = P("grp", "fsdp", None)
    group = P("grp", None)
    matrix = P("fsdp", None)
    vector = P("fsdp")
    split = P("fsdp", "grp")
    return jax.shard_map(
        per_device,
        mesh=mesh,
        in_specs=(rows, rows, group, group) + (matrix,) * 7 + (vector,) * 5,
        out_specs=(rows, rows) + (split,) * 7 + (vector,) * 5,
        check_vma=False,
    )
```

```python
import math

import jax
import jax.numpy as jnp
from jax import lax
from jax.experimental import pallas as pl
from jax.experimental.pallas import tpu as pltpu
from jax.sharding import PartitionSpec as P

H = 20
DK = 64
BF = jnp.bfloat16
F32 = jnp.float32
GATE = 2
COST = pl.CostEstimate(flops=1000, bytes_accessed=1000, transcendentals=0)


def swiglu(up_proj, gate_proj, upscale, gatescale):
    scaled = gatescale * gate_proj
    return scaled * jax.nn.sigmoid(scaled) * (upscale * up_proj)


def matmul(left_side, right_side):
    return jnp.dot(left_side, right_side, preferred_element_type=F32)


def weight_grad(left_side, right_side):
    return lax.dot_general(
        left_side, right_side, (((0,), (0,)), ((), ())), preferred_element_type=F32
    )


def back_matmul(grad_rows, weight_rows):
    return lax.dot_general(
        grad_rows, weight_rows, (((1,), (1,)), ((), ())), preferred_element_type=F32
    )


def after(value, *earlier):
    return lax.optimization_barrier((value, *earlier))[0]


def like(*shape, dtype=BF):
    return jax.ShapeDtypeStruct(shape, dtype)


def call(name, body, outs, scalars=(), arrays=(), remote=(), scratch=(), earlier=(), limit=16):
    counts = (len(scalars), len(arrays), len(remote), len(earlier), len(outs))

    def kernel(*refs):
        groups = []
        at = 0
        for count in counts:
            groups.append(refs[at : at + count])
            at += count
        body(*groups[0], *groups[1], groups[2], *groups[4], *refs[at:])

    whole = pl.BlockSpec(memory_space=pltpu.VMEM)
    kept = pl.BlockSpec(memory_space=pl.ANY)
    placed = pl.BlockSpec(memory_space=pltpu.HBM)
    return pl.pallas_call(
        kernel,
        out_shape=list(outs),
        in_specs=[pl.BlockSpec(memory_space=pltpu.SMEM)] * counts[0]
        + [whole] * counts[1]
        + [placed] * counts[2]
        + [kept] * counts[3],
        out_specs=[whole] * counts[4],
        scratch_shapes=list(scratch),
        compiler_params=pltpu.CompilerParams(vmem_limit_bytes=limit * 2**20),
        cost_estimate=COST,
        name=name,
    )(*scalars, *arrays, *remote, *earlier)


class Shards:
    def __init__(self, arrays, places):
        self.direct = arrays[0].shape[0] % 16 == 0
        if self.direct:
            self.arrays, self.places = list(arrays), places
        else:
            whole = jnp.zeros((len(arrays),) + arrays[0].shape, BF)
            for i, array in enumerate(arrays):
                whole = lax.dynamic_update_index_in_dim(whole, array, places[i], 0)
            self.arrays = [whole.reshape(-1, arrays[0].shape[1])]
            self.places = jnp.zeros((1,), jnp.int32)
        self.count = len(self.arrays)
        self.height = self.arrays[0].shape[0]

    def scratch(self, width):
        return [
            pltpu.VMEM((self.count, self.height, width), BF),
            pltpu.SemaphoreType.DMA((self.count,)),
        ]

    def copies(self, places, sources, target, sems, begin, width):
        return [
            pltpu.make_async_copy(
                sources[i].at[:, pl.ds(begin, width)], target.at[places[i]], sems.at[i]
            )
            for i in range(self.count)
        ]

    def columns(self, target, begin, width):
        return target[:, :, pl.ds(begin, width)].reshape(self.count * self.height, width)

    def rows(self, target, index, parts, begin, width):
        if self.direct:
            step = self.count // parts
            rows = target[pl.ds(index * step, step), :, pl.ds(begin, width)]
        else:
            step = self.height // parts
            rows = target[:, pl.ds(pl.multiple_of(index * step, step), step), pl.ds(begin, width)]
        return rows.reshape(-1, width)


def inverse_rms(vector):
    return lax.rsqrt(jnp.mean(vector * vector, axis=-1, keepdims=True) + 1e-06)


def head_sums(values, low_head):
    low_sum = jnp.sum(jnp.where(low_head, values, 0.0), axis=-1, keepdims=True)
    high_sum = jnp.sum(jnp.where(low_head, 0.0, values), axis=-1, keepdims=True)
    return low_sum, high_sum


def head_inverse(vector, low_head):
    low_sum, high_sum = head_sums(vector * vector, low_head)
    return jnp.where(low_head, lax.rsqrt(low_sum + 1e-06), lax.rsqrt(high_sum + 1e-06))


def head_probs(query_head, key_unit, seq_len):
    scores = back_matmul(query_head, key_unit) * math.sqrt(DK)
    query_row = lax.broadcasted_iota(jnp.int32, scores.shape, 0)
    key_row = lax.broadcasted_iota(jnp.int32, scores.shape, 1)
    start = query_row - lax.rem(query_row, seq_len)
    scores = jnp.where((key_row <= query_row) & (key_row >= start), scores, -1e30)
    exp_scores = jnp.exp(scores - jnp.max(scores, axis=-1, keepdims=True))
    return exp_scores / jnp.sum(exp_scores, axis=-1, keepdims=True)


def only(mask, values):
    return jnp.where(mask, values.astype(F32), 0.0).astype(BF)


def turn(ref, rows, columns, value):
    ref[pl.ds(0, rows), columns] = value[rows:].astype(BF)
    ref[pl.ds(rows, rows), columns] = value[:rows].astype(BF)


def attention_forward(half, token_rows, shards, seq_len):
    rows, width = token_rows.shape
    half_width = width // 2
    pairs = half_width // 128
    cols = 3 * half_width + 128

    def body(
        places, half_ref, x_ref, sources, qkv_ref, qu_ref, ku_ref, vl_ref, mixed_ref, turned_ref, scale_ref, w_ref, sems
    ):
        copies = shards.copies(places, sources, w_ref, sems, 0, cols)
        for copy in copies:
            copy.start()
        for copy in copies:
            copy.wait()
        scale_ref[...] = jnp.transpose(
            shards.columns(w_ref, 3 * half_width, 128).astype(F32)
        )[:16]
        x = x_ref[...]
        step = 384
        for begin in range(0, 3 * half_width, step):
            qkv_ref[:, pl.ds(begin, step)] = matmul(x, shards.columns(w_ref, begin, step))
        low_head = lax.broadcasted_iota(jnp.int32, (rows, 128), 1) < DK
        later = half_ref[0] == 1

        def pair(i, carry):
            at = pl.multiple_of(i * 128, 128)
            here = pl.ds(at, 128)
            queries = qkv_ref[:, here]
            key_rows = qkv_ref[:, pl.ds(half_width + at, 128)]
            value_low = qkv_ref[:, pl.ds(2 * half_width + at, 128)].astype(BF)
            scaling = jnp.where(
                later, scale_ref[0:1, pl.ds(half_width + at, 128)], scale_ref[0:1, here]
            )
            query_unit = queries * head_inverse(queries, low_head) * scaling
            key_unit = (key_rows * head_inverse(key_rows, low_head) * scaling).astype(BF)
            mixed = None
            for mask in (low_head, ~low_head):
                probs = head_probs(only(mask, query_unit), key_unit, seq_len)
                head = matmul(probs.astype(BF), value_low)
                mixed = head if mixed is None else jnp.where(low_head, mixed, head)
            qu_ref[:, here] = query_unit.astype(BF)
            ku_ref[:, here] = key_unit
            vl_ref[:, here] = value_low
            mixed_ref[:, here] = mixed.astype(BF)
            turn(turned_ref, rows // 2, here, mixed)
            return carry

        lax.fori_loop(0, pairs, pair, 0)

    return call(
        "attention_forward",
        body,
        [like(rows, 3 * half_width, dtype=F32)] + [like(rows, half_width)] * 5 + [like(16, width, dtype=F32)],
        scalars=[shards.places, half],
        arrays=[token_rows],
        remote=shards.arrays,
        limit=24,
        scratch=shards.scratch(cols),
    )


def place_whole(source, _, target):
    target[...] = source[...]


def place_pair(first, later, _, target):
    target[0] = first[...]
    target[1] = later[...]


def sum_whole(source, _, target):
    target[...] = jnp.sum(source[...], axis=0, keepdims=True)


def place_halves(half_ref, target, own, other):
    width = own.shape[1]

    @pl.when(half_ref[0] == 0)
    def _():
        target[:, pl.ds(0, width)] = own[...]
        target[:, pl.ds(width, width)] = other[...]

    @pl.when(half_ref[0] != 0)
    def _():
        target[:, pl.ds(0, width)] = other[...]
        target[:, pl.ds(width, width)] = own[...]


def first_forward(half, mixed, mixed_other, token_rows, attention_mix, shards, skip):
    rows, width = token_rows.shape

    def body(
        places, half_ref, own_ref, other_ref, x_ref, mix_ref, sources, mixed_ref, attended_ref, first_ref, low_ref, w_ref, sems
    ):
        copies = shards.copies(places, sources, w_ref, sems, skip, width)
        for copy in copies:
            copy.start()
        place_halves(half_ref, mixed_ref, own_ref, other_ref)
        for copy in copies:
            copy.wait()
        for begin in range(0, width, 256):
            attended_ref[:, pl.ds(begin, 256)] = matmul(
                mixed_ref[...], shards.columns(w_ref, begin, 256)
            )
        x = x_ref[...].astype(F32)
        attended = attended_ref[...]
        mix = x + mix_ref[...] * (attended * inverse_rms(attended) - x)
        first = mix * inverse_rms(mix)
        first_ref[...] = first
        low_ref[...] = first.astype(BF)

    return call(
        "first_forward",
        body,
        [like(rows, width)] + [like(rows, width, dtype=F32)] * 2 + [like(rows, width)],
        scalars=[shards.places, half],
        arrays=[mixed, mixed_other, token_rows, attention_mix],
        remote=shards.arrays,
        limit=20,
        scratch=shards.scratch(width),
    )


def mix_backward(base, branch, rate, grad):
    branch_inverse = inverse_rms(branch)
    branch_unit = branch * branch_inverse
    mix = base + rate * (branch_unit - base)
    inverse = inverse_rms(mix)
    value = mix * inverse
    grad_mix = inverse * (grad - value * jnp.mean(grad * value, axis=-1, keepdims=True))
    grad_unit = grad_mix * rate
    grad_branch = branch_inverse * (
        grad_unit - branch_unit * jnp.mean(grad_unit * branch_unit, axis=-1, keepdims=True)
    )
    return value, grad_mix - grad_unit, grad_branch, grad_mix * (branch_unit - base)


def second_backward(partial, partial_other, first_state, cot, cot_other, valid, feed_mix):
    rows, width = partial.shape
    own = rows // 2

    def body(partial_ref, other_ref, first_ref, cot_ref, cot_other_ref, valid_ref, mix_ref, _, layer_ref, grad_ref, low_ref, rate_ref):
        for begin in (0, own):
            here = pl.ds(begin, own)
            down = partial_ref[here, :] + other_ref[here, :].astype(F32)
            grad = (cot_ref if begin == 0 else cot_other_ref)[...].astype(F32)
            value, grad_first, grad_down, grad_rate = mix_backward(
                first_ref[here, :], down, mix_ref[...], grad
            )
            grad_ref[here, :] = grad_first
            low_ref[here, :] = grad_down.astype(BF)
            if begin == 0:
                layer_ref[...] = (value * valid_ref[...]).astype(BF)
                rate_ref[...] = jnp.sum(grad_rate, axis=0, keepdims=True)

    return call(
        "second_backward",
        body,
        [like(own, width), like(rows, width, dtype=F32), like(rows, width), like(1, width, dtype=F32)],
        limit=18,
        arrays=[partial, partial_other, first_state, cot, cot_other, valid, feed_mix],
    )


def first_backward(half, grad_first, partial, partial_other, token_rows, attended, attention_mix, shards, skip, earlier):
    rows, width = partial.shape
    own = rows // 2
    half_width = width // 2

    def body(
        places, half_ref, grad_ref, partial_ref, other_ref, x_ref, attended_ref, mix_ref, sources, cols_ref, mixed_ref, token_ref, rate_ref, low_ref, w_ref, sems
    ):
        copies = shards.copies(places, sources, w_ref, sems, skip, width)
        for copy in copies:
            copy.start()
        for begin in (0, own):
            here = pl.ds(begin, own)
            grad = grad_ref[here, :] + partial_ref[here, :] + other_ref[here, :].astype(F32)
            _, grad_token, grad_attended, grad_rate = mix_backward(
                x_ref[here, :].astype(F32), attended_ref[here, :], mix_ref[...], grad
            )
            low_ref[here, :] = grad_attended.astype(BF)
            if begin == 0:
                token_ref[...] = grad_token
                rate_ref[...] = jnp.sum(grad_rate, axis=0, keepdims=True)
        at = pl.multiple_of(half_ref[0] * half_width, 128)
        cols_ref[...] = low_ref[:, pl.ds(at, half_width)]
        for copy in copies:
            copy.wait()
        mixed_ref[...] = back_matmul(
            low_ref[...], shards.rows(w_ref, half_ref[0], 2, 0, width)
        ).astype(BF)

    return call(
        "first_backward",
        body,
        [like(rows, half_width)] * 2 + [like(own, width, dtype=F32), like(1, width, dtype=F32)],
        scalars=[shards.places, half],
        arrays=[grad_first, partial, partial_other, token_rows, attended, attention_mix],
        remote=shards.arrays,
        limit=20,
        scratch=[pltpu.VMEM((rows, width), BF)] + shards.scratch(width),
        earlier=earlier,
    )


def attention_backward(half, grad_mixed, qkv, query_unit, key_unit, value_low, scales, shards, seq_len, earlier):
    rows, half_width = grad_mixed.shape
    width = 2 * half_width
    pairs = half_width // 128
    own = rows // 2

    def body(
        places, half_ref, gm_ref, qkv_ref, qu_ref, ku_ref, vl_ref, scale_ref, sources, grads_ref, scoring_ref, own_ref, other_ref, w_ref, sems
    ):
        copies = shards.copies(places, sources, w_ref, sems, 0, 3 * half_width)
        for copy in copies:
            copy.start()
        low_head = lax.broadcasted_iota(jnp.int32, (rows, 128), 1) < DK
        later = half_ref[0] == 1

        def pair(i, carry):
            at = pl.multiple_of(i * 128, 128)
            here = pl.ds(at, 128)
            query_unit = qu_ref[:, here]
            key_unit = ku_ref[:, here]
            value_low = vl_ref[:, here]
            scaling = jnp.where(
                later, scale_ref[0:1, pl.ds(half_width + at, 128)], scale_ref[0:1, here]
            )
            grad_value = grad_qunit = grad_kunit = None
            for mask in (low_head, ~low_head):
                probs = head_probs(only(mask, query_unit), key_unit, seq_len)
                grad_head = only(mask, gm_ref[:, here])
                value_part = weight_grad(probs.astype(BF), grad_head)
                grad_probs = back_matmul(grad_head, value_low)
                grad_scores = (
                    probs * (grad_probs - jnp.sum(grad_probs * probs, axis=-1, keepdims=True))
                ).astype(BF)
                query_part = matmul(grad_scores, key_unit)
                key_part = weight_grad(grad_scores, query_unit)
                if grad_value is None:
                    grad_value, grad_qunit, grad_kunit = value_part, query_part, key_part
                else:
                    grad_value = grad_value + value_part
                    grad_qunit = jnp.where(low_head, grad_qunit, query_part)
                    grad_kunit = jnp.where(low_head, grad_kunit, key_part)
            scoring_grad = None
            for place, grad in ((0, grad_qunit), (1, grad_kunit)):
                raw = qkv_ref[:, pl.ds(place * half_width + at, 128)]
                grad = grad * math.sqrt(DK)
                inverse = head_inverse(raw, low_head)
                unit = raw * inverse
                term = jnp.sum(grad * unit, axis=0, keepdims=True)
                scoring_grad = term if scoring_grad is None else scoring_grad + term
                grad = grad * scaling
                low_sum, high_sum = head_sums(grad * unit, low_head)
                grads_ref[place, :, here] = (
                    inverse * (grad - unit * jnp.where(low_head, low_sum, high_sum))
                ).astype(BF)
            grads_ref[2, :, here] = grad_value.astype(BF)
            scoring_ref[:, here] = scoring_grad
            return carry

        lax.fori_loop(0, pairs, pair, 0)
        for copy in copies:
            copy.wait()
        for piece in range(2):
            total = None
            for j in range(3):
                term = back_matmul(
                    grads_ref[j], shards.rows(w_ref, piece, 2, j * half_width, half_width)
                )
                total = term if total is None else total + term
            columns = pl.ds(piece * half_width, half_width)
            own_ref[:, columns] = total[:own]
            other_ref[:, columns] = total[own:].astype(BF)

    return call(
        "attention_backward",
        body,
        [
            like(3, rows, half_width),
            like(1, half_width, dtype=F32),
            like(own, width, dtype=F32),
            like(own, width),
        ],
        scalars=[shards.places, half],
        arrays=[grad_mixed, qkv, query_unit, key_unit, value_low, scales],
        remote=shards.arrays,
        limit=56,
        scratch=shards.scratch(3 * half_width),
        earlier=earlier,
    )


def down_grads(which, hidden, hidden_other, down, down_other):
    units = hidden_other.shape[1]
    width = down.shape[1]
    block = units // 2

    def body(which_ref, hidden_ref, hidden_other_ref, down_ref, down_other_ref, _, out_ref):
        for kept in range(2):
            side = which_ref[1] if kept else 1 - which_ref[1]
            columns = pl.ds(pl.multiple_of(side * block, 128), block)
            own = hidden_ref[which_ref[0], :, columns]
            other = hidden_other_ref[:, columns]
            for begin in range(0, width, 640):
                here = pl.ds(begin, 640)
                total = weight_grad(own, down_ref[:, here]) + weight_grad(other, down_other_ref[:, here])
                out_ref[:, pl.ds(kept * width + begin, 640)] = total.astype(BF)

    return call(
        "down_grads",
        body,
        [like(block, 2 * width)],
        scalars=[which],
        arrays=[hidden, hidden_other, down, down_other],
    )[0]


def side_grads(name, lefts, rights, kept, earlier):
    block = lefts[0][0].shape[1] // 2
    number = len(lefts)
    total_width = sum(right[0].shape[-1] * len(right[2] or (0,)) for right in rights)

    def body(*refs):
        refs = [ref for ref in refs if not isinstance(ref, tuple)]
        out_ref = refs[-1]
        begin = 0
        for i in range(number):
            own_ref, other_ref, right_ref, right_other_ref = refs[4 * i : 4 * i + 4]
            columns = pl.ds(block if kept else 0, block)
            own = own_ref[:, columns]
            other = other_ref[:, columns]
            for index in rights[i][2] or (None,):
                for at in range(0, right_ref.shape[-1], 640):
                    here = (slice(None), pl.ds(at, 640))
                    if index is not None:
                        here = (index, *here)
                    total = weight_grad(own, right_ref[here]) + weight_grad(other, right_other_ref[here])
                    out_ref[:, pl.ds(begin, 640)] = total.astype(out_ref.dtype)
                    begin += 640

    arrays = []
    for left, right in zip(lefts, rights):
        arrays += [*left, *right[:2]]
    return call(
        name,
        body,
        [like(block, total_width)],
        limit=20,
        arrays=arrays,
        earlier=earlier,
    )[0]


def lay_first(half, query_weight, key_weight, value_weight, out_weight, scales):
    shard, width = query_weight.shape
    half_width = width // 2

    def body(half_ref, q_ref, k_ref, v_ref, out_ref, *refs):
        target, square = refs[-2:]
        for i, ref in enumerate((q_ref, k_ref, v_ref)):
            place = pl.ds(i * half_width, half_width)

            @pl.when(half_ref[0] == 0)
            def _():
                target[:, place] = ref[:, pl.ds(0, half_width)]

            @pl.when(half_ref[0] != 0)
            def _():
                target[:, place] = ref[:, pl.ds(half_width, half_width)]

        square[...] = jnp.zeros_like(square)
        row = 0
        for ref in refs[: len(scales)]:
            values = ref[...].astype(F32)
            for begin in range(0, values.shape[1], shard):
                square[pl.ds(row, 1), pl.ds(0, shard)] = values[:, begin : begin + shard]
                row += 1
        target[:, pl.ds(3 * half_width, 128)] = jnp.transpose(square[...])[:shard].astype(BF)
        target[:, pl.ds(3 * half_width + 128, width)] = out_ref[...]

    return call(
        "lay_first",
        body,
        [like(shard, 3 * half_width + 128 + width)],
        limit=56,
        scalars=[half],
        arrays=[query_weight, key_weight, value_weight, out_weight]
        + [scale.reshape(1, -1) for scale in scales],
        scratch=[pltpu.VMEM((128, 128), F32)],
    )[0]


def lay_second(half, up_weight, gate_weight, down_weight, planes):
    shard = up_weight.shape[0]
    part = down_weight.shape[0] // 2
    width = down_weight.shape[1]

    def body(half_ref, up_ref, gate_ref, down_ref, _, target):
        upper = half_ref[0] != 0
        for i, ref in enumerate((up_ref, gate_ref)):
            for core in range(2):
                rows = slice((2 * i + core) * shard, (2 * i + core + 1) * shard)
                for side in range(2):
                    for plane in range(planes):
                        begin = ((plane * 2 + side) * 2 + core) * 2 * part
                        place = (side * planes + plane) * part
                        target[rows, place : place + part] = jnp.where(
                            upper,
                            ref[:, begin + part : begin + 2 * part].astype(F32),
                            ref[:, begin : begin + part].astype(F32),
                        ).astype(BF)

        @pl.when(jnp.logical_not(upper))
        def _():
            target[pl.ds(4 * shard, part), :] = down_ref[pl.ds(0, part), :]

        @pl.when(upper)
        def _():
            target[pl.ds(4 * shard, part), :] = down_ref[pl.ds(part, part), :]

    return call(
        "lay_second",
        body,
        [like(4 * shard + part, width)],
        limit=56,
        scalars=[half],
        arrays=[up_weight, gate_weight, down_weight],
    )[0]


def split_hidden(half, totals, planes, part):
    shard, width = totals[0].shape
    run = planes // 2 * part

    def body(half_ref, *refs):
        for source, target in zip(refs[: len(totals)], refs[-len(totals) :]):
            for i in range(4):
                begin = 2 * i * run
                first, later = source[:, begin : begin + run], source[:, begin + run : begin + 2 * run]
                target[:, i * run : (i + 1) * run] = jnp.where(
                    half_ref[0] == 0, later.astype(F32), first.astype(F32)
                ).astype(BF)

    return call(
        "split_hidden",
        body,
        [like(shard, width // 2)] * len(totals),
        scalars=[half],
        arrays=totals,
    )


def merge_hidden(half, totals, others, planes, part, earlier):
    shard, width = totals[0].shape
    run = planes // 2 * part

    def body(half_ref, *refs):
        number = len(totals)
        upper = half_ref[0] != 0
        for own_ref, other_ref, target in zip(refs[:number], refs[number : 2 * number], refs[-number:]):
            for plane in range(planes // 2):
                for side in range(2):
                    for core in range(2):
                        i = core * 2 + side
                        begin = 2 * i * run + plane * part
                        own = jnp.where(
                            upper,
                            own_ref[:, begin + run : begin + run + part].astype(F32),
                            own_ref[:, begin : begin + part].astype(F32),
                        )
                        begin = i * run + plane * part
                        other = other_ref[:, begin : begin + part].astype(F32)
                        begin = ((plane * 2 + side) * 2 + core) * 2 * part
                        target[:, begin : begin + part] = jnp.where(upper, other, own)
                        target[:, begin + part : begin + 2 * part] = jnp.where(upper, own, other)

    return call(
        "merge_hidden",
        body,
        [like(shard, width, dtype=F32)] * len(totals),
        scalars=[half],
        arrays=[*totals, *others],
        earlier=earlier,
    )


class HiddenWeights:
    def __init__(self, gathered, planes, shard, part):
        width = gathered.shape[2]
        units = 2 * planes * part
        self.direct = shard % 16 == 0 and part % 16 == 0
        self.width, self.units, self.shard, self.part = width, units, shard, part
        if self.direct:
            self.arrays = [gathered.reshape(planes, 2, 2, -1, width)]
            self.matrix = (planes, 2, 2, shard, units)
            self.down = (planes, part, width)
        else:
            blocks = gathered[:, 4 * shard :].reshape(planes, 2, 2, part, width)
            self.arrays = [
                jnp.stack(
                    [gathered[:, i * shard : (i + 1) * shard].reshape(width, width) for i in range(4)]
                ),
                jnp.transpose(blocks, (2, 1, 0, 3, 4)).reshape(2, 2, planes * part, width),
            ]
            self.matrix = (width, units)
            self.down = (planes * part, width)

    def scratch(self):
        return [
            pltpu.VMEM((4,) + self.matrix, BF),
            pltpu.VMEM((2, 2) + self.down, BF),
            pltpu.SemaphoreType.DMA((8,)),
        ]

    def specs(self):
        return [pl.BlockSpec(memory_space=pltpu.HBM)] * len(self.arrays)

    def matrix_copy(self, sources, wide, sems, i):
        if self.direct:
            source = sources[0].at[:, :, :, pl.ds(i * self.shard, self.shard), :]
        else:
            source = sources[0].at[i]
        return pltpu.make_async_copy(source, wide.at[i], sems.at[i])

    def down_copy(self, sources, tall, sems, core, side):
        if self.direct:
            source = sources[0].at[:, side, core, pl.ds(4 * self.shard, self.part), :]
        else:
            source = sources[1].at[core, side]
        return pltpu.make_async_copy(source, tall.at[core, side], sems.at[4 + core * 2 + side])

    def matrix_value(self, wide, i, columns):
        if self.direct:
            return wide[i, :, :, :, :, columns].reshape(self.width, -1)
        return wide[i, :, columns]

    def matrix_rows(self, wide, i, j, parts):
        if self.direct:
            step = self.matrix[0] // parts
            return wide[i, pl.ds(j * step, step)].reshape(self.width // parts, -1)
        step = self.width // parts
        return wide[i, pl.ds(j * step, step)]

    def down_value(self, tall, core, side, columns):
        if self.direct:
            return tall[core, side, :, :, columns].reshape(-1, columns.size)
        return tall[core, side, :, columns]

    def down_rows(self, tall, core, side):
        return tall[core, side].reshape(-1, self.width)


def hidden_forward(first_low, weights, up_scale, gate_scale, own_rows):
    rows, width = first_low.shape
    units = weights.units
    block = units // 2
    step = 256

    def body(first_ref, up_scale_ref, gate_scale_ref, *refs):
        sources = refs[: len(weights.arrays)]
        hidden_ref, up_ref, gate_ref, partial_ref, turned_ref, wide, tall, sems = refs[
            len(weights.arrays) :
        ]
        copies = [weights.matrix_copy(sources, wide, sems, i) for i in (0, 2, 1, 3)]
        down_copies = [
            weights.down_copy(sources, tall, sems, i, j) for i in range(2) for j in range(2)
        ]
        for copy in copies + down_copies:
            copy.start()
        first = first_ref[...]
        for core in range(2):
            copies[2 * core].wait()
            copies[2 * core + 1].wait()

            for begin in range(0, units, step):
                columns = pl.ds(begin, step)
                here = pl.ds(core * units + begin, step)
                up = matmul(first, weights.matrix_value(wide, core, columns))
                gate = matmul(first, weights.matrix_value(wide, 2 + core, columns))
                up_ref[:, here] = up.astype(BF)
                gate_ref[:, here] = gate.astype(BF)
                hidden = swiglu(up, gate, up_scale_ref[:, here], gate_scale_ref[:, here])
                hidden_ref[core, :, columns] = hidden.astype(BF)
        for copy in down_copies:
            copy.wait()

        for begin in range(0, width, step):
            columns = pl.ds(begin, step)
            total = None
            for core in range(2):
                for side in range(2):
                    term = matmul(
                        hidden_ref[core, :, pl.ds(side * block, block)],
                        weights.down_value(tall, core, side, columns),
                    )
                    total = term if total is None else total + term
            partial_ref[:, columns] = total
            turned_ref[pl.ds(0, own_rows), columns] = total[own_rows:].astype(BF)
            turned_ref[pl.ds(own_rows, own_rows), columns] = total[:own_rows].astype(BF)

    whole = pl.BlockSpec(memory_space=pltpu.VMEM)
    return pl.pallas_call(
        body,
        out_shape=[
            jax.ShapeDtypeStruct((2, rows, units), BF),
            jax.ShapeDtypeStruct((rows, 2 * units), BF),
            jax.ShapeDtypeStruct((rows, 2 * units), BF),
            jax.ShapeDtypeStruct((rows, width), F32),
            jax.ShapeDtypeStruct((rows, width), BF),
        ],
        in_specs=[whole] * 3 + weights.specs(),
        out_specs=[whole] * 5,
        scratch_shapes=weights.scratch(),
        compiler_params=pltpu.CompilerParams(vmem_limit_bytes=56 * 2**20),
        cost_estimate=COST,
        name="hidden_forward",
    )(first_low, up_scale.reshape(1, -1), gate_scale.reshape(1, -1), *weights.arrays)


def hidden_backward(down_low, up_proj, gate_proj, weights, up_scale, gate_scale, own_rows, earlier):
    rows, width = down_low.shape
    units = weights.units
    block = units // 2

    def body(down_ref, up_ref, gate_ref, up_scale_ref, gate_scale_ref, *refs):
        sources = refs[: len(weights.arrays)]
        low_ref, gate_low_ref, up_grad_ref, gate_grad_ref, partial_ref, turned_ref, wide, tall, sems = refs[
            len(weights.arrays) + len(earlier) :
        ]
        down_copies = [
            weights.down_copy(sources, tall, sems, i, j) for i in range(2) for j in range(2)
        ]
        copies = [weights.matrix_copy(sources, wide, sems, i) for i in range(4)]
        for copy in down_copies + copies:
            copy.start()
        down = down_ref[...]
        for core in range(2):
            for side in range(2):
                down_copies[core * 2 + side].wait()
                here = pl.ds((core * 2 + side) * block, block)
                grad_hidden = back_matmul(down, weights.down_rows(tall, core, side))
                up_scaling = up_scale_ref[:, here]
                gate_scaling = gate_scale_ref[:, here]
                up = up_ref[:, here].astype(F32)
                gate = gate_ref[:, here].astype(F32)
                scaled = gate_scaling * gate
                sigmoid = jax.nn.sigmoid(scaled)
                silu = scaled * sigmoid
                grad_scaled_up = grad_hidden * silu
                grad_scaled = grad_hidden * (up_scaling * up) * (sigmoid + silu * (1.0 - sigmoid))
                low_ref[:, here] = (grad_scaled_up * up_scaling).astype(BF)
                gate_low_ref[:, here] = (grad_scaled * gate_scaling).astype(BF)
                up_grad_ref[:, here] = jnp.sum(grad_scaled_up * up, axis=0, keepdims=True)
                gate_grad_ref[:, here] = jnp.sum(grad_scaled * gate, axis=0, keepdims=True)
        for copy in copies:
            copy.wait()
        pieces = 2
        piece = width // pieces
        for j in range(pieces):
            total = None
            for i in range(4):
                term = back_matmul(
                    (low_ref, gate_low_ref)[i // 2][:, pl.ds((i % 2) * units, units)],
                    weights.matrix_rows(wide, i, j, pieces),
                )
                total = term if total is None else total + term
            columns = pl.ds(j * piece, piece)
            partial_ref[:, columns] = total
            turned_ref[pl.ds(0, own_rows), columns] = total[own_rows:].astype(BF)
            turned_ref[pl.ds(own_rows, own_rows), columns] = total[:own_rows].astype(BF)

    whole = pl.BlockSpec(memory_space=pltpu.VMEM)
    return pl.pallas_call(
        body,
        out_shape=[
            jax.ShapeDtypeStruct((rows, 2 * units), BF),
            jax.ShapeDtypeStruct((rows, 2 * units), BF),
            jax.ShapeDtypeStruct((1, 2 * units), F32),
            jax.ShapeDtypeStruct((1, 2 * units), F32),
            jax.ShapeDtypeStruct((rows, width), F32),
            jax.ShapeDtypeStruct((rows, width), BF),
        ],
        in_specs=[whole] * 5
        + weights.specs()
        + [pl.BlockSpec(memory_space=pl.ANY)] * len(earlier),
        out_specs=[whole] * 6,
        scratch_shapes=weights.scratch(),
        compiler_params=pltpu.CompilerParams(vmem_limit_bytes=56 * 2**20),
        cost_estimate=COST,
        name="hidden_backward",
    )(
        down_low,
        up_proj,
        gate_proj,
        up_scale.reshape(1, -1),
        gate_scale.reshape(1, -1),
        *weights.arrays,
        *earlier,
    )


def per_device(
    tokens,
    cotangent,
    lengths,
    placement,
    query_weight,
    key_weight,
    value_weight,
    out_weight,
    up_weight,
    gate_weight,
    down_weight,
    scoring,
    upscale,
    gatescale,
    attention_rate,
    feedforward_rate,
):
    size = lax.axis_size("fsdp")
    planes = size // 4
    half = lax.axis_index("grp")
    me = lax.axis_index("fsdp")
    core = me % 2
    side = (me // 2) % 2
    plane = me // 4
    half_scalar = half.reshape(1).astype(jnp.int32)
    which = jnp.stack([core, side]).astype(jnp.int32)
    local_seqs = tokens.shape[0] // size
    seq_len = tokens.shape[1] * size
    width = tokens.shape[2]
    own_rows = local_seqs * seq_len
    shard = query_weight.shape[0]
    hidden_shard = down_weight.shape[0]
    part = hidden_shard // 2
    per_row = hidden_shard // shard
    half_width = width // 2

    def swap_core(array):
        return lax.ppermute(array, "fsdp", [(i, i ^ 1) for i in range(size)])

    def swap_side(array):
        return lax.ppermute(array, "fsdp", [(i, i ^ 2) for i in range(size)])

    def next_plane(array):
        return lax.ppermute(array, "fsdp", [(i, (i + 4) % size) for i in range(size)])

    def swap_half(array):
        return lax.ppermute(array, "grp", [(0, 1), (1, 0)])

    def pick(array, index, axis):
        return lax.dynamic_index_in_dim(array, index, axis, keepdims=False)

    first_group = lay_first(
        half_scalar,
        query_weight,
        key_weight,
        value_weight,
        out_weight,
        [scoring, attention_rate, feedforward_rate, upscale, gatescale],
    )
    second_group = lay_second(half_scalar, up_weight, gate_weight, down_weight, planes)
    hidden_width = planes * 4 * part
    core_width = hidden_width // 2
    held = [first_group]
    crossed = []
    for i in range(planes):
        here = after(held[-1], *crossed[-1:]) if crossed else held[-1]
        if i < planes - 1:
            held.append(next_plane(here))
        crossed.append(swap_side(here))
    second_whole = lax.all_gather(
        after(second_group, *held[: GATE + 1], *crossed[:GATE]), "fsdp", axis=0
    )
    (both,) = call(
        "rows",
        place_pair,
        [like(2, *tokens.shape)],
        arrays=[tokens, cotangent],
        earlier=[held[-1], crossed[-2]],
        limit=56,
    )
    arrived = lax.all_to_all(both, "fsdp", split_axis=1, concat_axis=2, tiled=True)
    own_tokens = arrived[0].reshape(own_rows, width)
    other_tokens = swap_half(own_tokens)
    held = held + crossed
    held = held + [swap_core(array) for array in held]
    places = []
    for i in range(4 * planes):
        there_core = 1 - core if i >= 2 * planes else core
        there_side = 1 - side if i // planes % 2 else side
        places.append(((plane - i) % planes * 2 + there_side) * 2 + there_core)
    shards = Shards(held, jnp.stack(places).astype(jnp.int32))

    group_order = placement[0]
    own_slots = lax.dynamic_slice_in_dim(group_order, me * local_seqs, local_seqs)
    own_lengths = jnp.take(lengths[0], own_slots)
    valid = (jnp.arange(seq_len, dtype=jnp.int32)[None, :] < own_lengths[:, None]).reshape(
        own_rows, 1
    )
    own_cot = jnp.where(valid, arrived[1].reshape(own_rows, width), jnp.zeros((), BF))
    token_rows = jnp.concatenate([own_tokens, other_tokens])
    other_cot = swap_half(own_cot)

    qkv, query_unit, key_unit, value_low, mixed_half, mixed_turned, scale_float = attention_forward(
        half_scalar, token_rows, shards, seq_len
    )
    attention_mix = scale_float[1:2]
    feed_mix = scale_float[2:3]

    def hidden_scale(begin):
        rows = scale_float[begin : begin + per_row].reshape(2, per_row // 2, planes, 2, 2, shard)
        return jnp.transpose(pick(rows, half, 0), (3, 2, 1, 0, 4)).reshape(-1)

    up_scale = hidden_scale(3)
    gate_scale = hidden_scale(3 + per_row)
    skip = 3 * half_width + 128
    mixed_low, attended, first_state, first_low = first_forward(
        half_scalar, mixed_half, swap_half(mixed_turned), token_rows, attention_mix, shards, skip
    )

    feature = jnp.arange(width, dtype=jnp.int32)
    block = []
    for b in range(2):
        for a in range(2):
            for k in range(planes):
                there_core = core if b == 0 else 1 - core
                there_side = 1 - side if a == 0 else side
                block.append((k * 2 + there_side) * 2 + there_core)
    block = jnp.stack(block).astype(jnp.int32)
    wanted = (block[:, None] * shard + jnp.arange(shard, dtype=jnp.int32)[None, :]).reshape(-1)
    chooser = (feature[:, None] == wanted[None, :]).astype(BF)

    def share_columns(array):
        chosen = matmul(array, chooser).astype(BF)
        return chosen[:, :half_width], swap_core(chosen[:, half_width:])

    def share(array):
        return array, swap_core(array)

    def over_planes(total):
        return lax.psum_scatter(
            total.reshape(planes, total.shape[0] // planes, total.shape[1]),
            "fsdp",
            scatter_dimension=0,
            axis_index_groups=[[k * 4 + j for k in range(planes)] for j in range(4)],
        )

    def joined(kept, arrived_part):
        return (kept.astype(F32) + arrived_part.astype(F32)).astype(BF)

    token_sides = share_columns(token_rows)
    mixed_sides = share_columns(mixed_low)
    first_sides = share_columns(first_low)
    hidden_weights = HiddenWeights(
        after(second_whole, *token_sides, *mixed_sides, *first_sides, other_cot), planes, shard, part
    )
    hidden_low, up_proj, gate_proj, partial, partial_turned = hidden_forward(
        first_low, hidden_weights, up_scale, gate_scale, own_rows
    )
    hidden_other = swap_core(pick(hidden_low, 1 - core, 0))

    layer_own, grad_first, down_low, feed_grad = second_backward(
        partial,
        swap_half(partial_turned),
        first_state,
        own_cot,
        other_cot,
        valid.astype(F32),
        feed_mix,
    )
    down_other = swap_core(down_low)
    down_args = (which, hidden_low, hidden_other, down_low, down_other)
    down_both = down_grads(*down_args)
    down_sum = over_planes(down_both)
    up_low, gate_low, upscale_grad, gatescale_grad, partial, partial_turned = hidden_backward(
        down_low, up_proj, gate_proj, hidden_weights, up_scale, gate_scale, own_rows, [down_both]
    )
    up_other = swap_core(up_low)
    partial_other = swap_half(partial_turned)
    gate_other = swap_core(gate_low)
    up_side = [(up_low, up_other, None)]
    gate_side = [(gate_low, gate_other, None)]
    up_sent = side_grads("up_sent", [first_sides], up_side, False, [])
    up_arrived = swap_side(up_sent)
    gate_sent = side_grads("gate_sent", [first_sides], gate_side, False, [up_sent])
    attended_cols, grad_mixed, grad_tokens, attention_grad = first_backward(
        half_scalar,
        grad_first,
        partial,
        partial_other,
        token_rows,
        attended,
        attention_mix,
        shards,
        skip,
        [gate_sent],
    )
    qkv_low, scoring_grad, token_own, token_sent = attention_backward(
        half_scalar, grad_mixed, qkv, query_unit, key_unit, value_low, scale_float, shards, seq_len, []
    )
    up_kept = side_grads("up_kept", [first_sides], up_side, True, [qkv_low])
    gate_arrived = swap_side(after(gate_sent, up_arrived))
    attended_other = swap_core(after(attended_cols, up_arrived))
    qkv_other = swap_core(after(qkv_low, up_arrived))
    token_other = swap_half(after(token_sent, up_arrived))
    up_joined = joined(up_kept, up_arrived)
    up_total = over_planes(up_joined)
    last_args = (
        [mixed_sides, token_sides],
        [(attended_cols, attended_other, None), (qkv_low, qkv_other, (0, 1, 2))],
    )
    last_sent = side_grads("last_sent", *last_args, False, [up_joined, down_sum])
    gate_kept = side_grads("gate_kept", [first_sides], gate_side, True, [last_sent])
    input_own = (grad_tokens + token_own + token_other.astype(F32)).astype(BF)
    last_kept = side_grads("last_kept", *last_args, True, [gate_kept])
    last_arrived = swap_side(after(last_sent, gate_arrived))
    gate_joined = joined(gate_kept, after(gate_arrived, last_kept))
    gate_total = over_planes(gate_joined)
    def hidden_spread(grad):
        blocks = jnp.transpose(grad.reshape(2, 2, planes, part), (2, 1, 0, 3))
        blank = jnp.zeros_like(blocks)
        both_halves = jnp.where(
            half == 0, jnp.stack([blocks, blank], axis=3), jnp.stack([blank, blocks], axis=3)
        )
        return both_halves.reshape(size, hidden_shard)

    blank = jnp.zeros_like(scoring_grad)
    scoring_spread = jnp.where(
        half == 0,
        jnp.concatenate([scoring_grad, blank], axis=1),
        jnp.concatenate([blank, scoring_grad], axis=1),
    )
    small = jnp.concatenate(
        [
            scoring_spread.reshape(size, shard),
            attention_grad.reshape(size, shard),
            feed_grad.reshape(size, shard),
            hidden_spread(upscale_grad),
            hidden_spread(gatescale_grad),
        ],
        axis=1,
    )
    (up_part,) = split_hidden(half_scalar, [up_total], planes, part)
    up_swapped = swap_half(up_part)
    (outgoing,) = call(
        "outgoing", place_pair, [like(2, own_rows, width)], arrays=[layer_own, input_own], earlier=[up_swapped]
    )
    returned = lax.all_to_all(
        outgoing.reshape(2, local_seqs, seq_len, width), "fsdp", split_axis=2, concat_axis=1, tiled=True
    )
    (up_out,) = merge_hidden(half_scalar, [up_total], [up_swapped], planes, part, [returned])
    last_joined = joined(last_kept, after(last_arrived, up_out))
    last_total = over_planes(last_joined).astype(F32)
    down_total = down_sum[:, width:].astype(F32) + swap_side(
        after(down_sum[:, :width], last_joined)
    ).astype(F32)
    down_cols = down_total.reshape(part, 2, half_width)
    mine = pick(down_cols, half, 1)
    theirs = swap_half(pick(down_cols, 1 - half, 1).astype(BF)).astype(F32)
    down_out = jnp.where(
        half == 0, jnp.concatenate([mine, theirs]), jnp.concatenate([theirs, mine])
    )
    (small,) = call(
        "pass", place_whole, [like(*small.shape, dtype=F32)], arrays=[small], earlier=[last_joined]
    )
    small = lax.all_to_all(small, "fsdp", split_axis=0, concat_axis=0, tiled=True)
    (total,) = call("add", sum_whole, [like(1, small.shape[1], dtype=F32)], arrays=[small])
    total = total[0]
    total = total + swap_half(total)

    (gate_part,) = split_hidden(half_scalar, [gate_total], planes, part)
    (gate_out,) = merge_hidden(half_scalar, [gate_total], [swap_half(gate_part)], planes, part, [])
    out_total = last_total[:, :half_width]
    qkv_total = last_total[:, half_width:]

    return (
        returned[0],
        returned[1],
        qkv_total[:, :half_width],
        qkv_total[:, half_width : 2 * half_width],
        qkv_total[:, 2 * half_width :],
        out_total,
        up_out,
        gate_out,
        down_out,
        total[:shard],
        total[3 * shard : 3 * shard + hidden_shard],
        total[3 * shard + hidden_shard :],
        total[shard : 2 * shard],
        total[2 * shard : 3 * shard],
    )


def solution(mesh):
    rows = P("grp", "fsdp", None)
    group = P("grp", None)
    matrix = P("fsdp", None)
    vector = P("fsdp")
    split = P("fsdp", "grp")
    return jax.shard_map(
        per_device,
        mesh=mesh,
        in_specs=(rows, rows, group, group) + (matrix,) * 7 + (vector,) * 5,
        out_specs=(rows, rows) + (split,) * 7 + (vector,) * 5,
        check_vma=False,
    )
```

```python
import math

import jax
import jax.numpy as jnp
from jax import lax
from jax.experimental import pallas as pl
from jax.experimental.pallas import tpu as pltpu
from jax.sharding import PartitionSpec as P

H = 20
DK = 64
BF = jnp.bfloat16
F32 = jnp.float32
GATE = 1
COST = pl.CostEstimate(flops=1000, bytes_accessed=1000, transcendentals=0)


def swiglu(up_proj, gate_proj, upscale, gatescale):
    scaled = gatescale * gate_proj
    return scaled * jax.nn.sigmoid(scaled) * (upscale * up_proj)


def matmul(left_side, right_side):
    return jnp.dot(left_side, right_side, preferred_element_type=F32)


def weight_grad(left_side, right_side):
    return lax.dot_general(
        left_side, right_side, (((0,), (0,)), ((), ())), preferred_element_type=F32
    )


def back_matmul(grad_rows, weight_rows):
    return lax.dot_general(
        grad_rows, weight_rows, (((1,), (1,)), ((), ())), preferred_element_type=F32
    )


def after(value, *earlier):
    return lax.optimization_barrier((value, *earlier))[0]


def like(*shape, dtype=BF):
    return jax.ShapeDtypeStruct(shape, dtype)


def call(name, body, outs, scalars=(), arrays=(), remote=(), scratch=(), earlier=(), limit=16):
    counts = (len(scalars), len(arrays), len(remote), len(earlier), len(outs))

    def kernel(*refs):
        groups = []
        at = 0
        for count in counts:
            groups.append(refs[at : at + count])
            at += count
        body(*groups[0], *groups[1], groups[2], *groups[4], *refs[at:])

    whole = pl.BlockSpec(memory_space=pltpu.VMEM)
    kept = pl.BlockSpec(memory_space=pl.ANY)
    placed = pl.BlockSpec(memory_space=pltpu.HBM)
    return pl.pallas_call(
        kernel,
        out_shape=list(outs),
        in_specs=[pl.BlockSpec(memory_space=pltpu.SMEM)] * counts[0]
        + [whole] * counts[1]
        + [placed] * counts[2]
        + [kept] * counts[3],
        out_specs=[whole] * counts[4],
        scratch_shapes=list(scratch),
        compiler_params=pltpu.CompilerParams(vmem_limit_bytes=limit * 2**20),
        cost_estimate=COST,
        name=name,
    )(*scalars, *arrays, *remote, *earlier)


class Shards:
    def __init__(self, arrays, places):
        self.direct = arrays[0].shape[0] % 16 == 0
        if self.direct:
            self.arrays, self.places = list(arrays), places
        else:
            whole = jnp.zeros((len(arrays),) + arrays[0].shape, BF)
            for i, array in enumerate(arrays):
                whole = lax.dynamic_update_index_in_dim(whole, array, places[i], 0)
            self.arrays = [whole.reshape(-1, arrays[0].shape[1])]
            self.places = jnp.zeros((1,), jnp.int32)
        self.count = len(self.arrays)
        self.height = self.arrays[0].shape[0]

    def scratch(self, width):
        return [
            pltpu.VMEM((self.count, self.height, width), BF),
            pltpu.SemaphoreType.DMA((self.count,)),
        ]

    def copies(self, places, sources, target, sems, begin, width):
        return [
            pltpu.make_async_copy(
                sources[i].at[:, pl.ds(begin, width)], target.at[places[i]], sems.at[i]
            )
            for i in range(self.count)
        ]

    def columns(self, target, begin, width):
        return target[:, :, pl.ds(begin, width)].reshape(self.count * self.height, width)

    def rows(self, target, index, parts, begin, width):
        if self.direct:
            step = self.count // parts
            rows = target[pl.ds(index * step, step), :, pl.ds(begin, width)]
        else:
            step = self.height // parts
            rows = target[:, pl.ds(pl.multiple_of(index * step, step), step), pl.ds(begin, width)]
        return rows.reshape(-1, width)


def inverse_rms(vector):
    return lax.rsqrt(jnp.mean(vector * vector, axis=-1, keepdims=True) + 1e-06)


def head_sums(values, low_head):
    low_sum = jnp.sum(jnp.where(low_head, values, 0.0), axis=-1, keepdims=True)
    high_sum = jnp.sum(jnp.where(low_head, 0.0, values), axis=-1, keepdims=True)
    return low_sum, high_sum


def head_inverse(vector, low_head):
    low_sum, high_sum = head_sums(vector * vector, low_head)
    return jnp.where(low_head, lax.rsqrt(low_sum + 1e-06), lax.rsqrt(high_sum + 1e-06))


def head_probs(query_head, key_unit, seq_len):
    scores = back_matmul(query_head, key_unit) * math.sqrt(DK)
    query_row = lax.broadcasted_iota(jnp.int32, scores.shape, 0)
    key_row = lax.broadcasted_iota(jnp.int32, scores.shape, 1)
    start = query_row - lax.rem(query_row, seq_len)
    scores = jnp.where((key_row <= query_row) & (key_row >= start), scores, -1e30)
    exp_scores = jnp.exp(scores - jnp.max(scores, axis=-1, keepdims=True))
    return exp_scores / jnp.sum(exp_scores, axis=-1, keepdims=True)


def only(mask, values):
    return jnp.where(mask, values.astype(F32), 0.0).astype(BF)


def turn(ref, rows, columns, value):
    ref[pl.ds(0, rows), columns] = value[rows:].astype(BF)
    ref[pl.ds(rows, rows), columns] = value[:rows].astype(BF)


def attention_forward(half, token_rows, shards, seq_len):
    rows, width = token_rows.shape
    half_width = width // 2
    pairs = half_width // 128
    cols = 3 * half_width + 128

    def body(
        places, half_ref, x_ref, sources, qkv_ref, qu_ref, ku_ref, vl_ref, mixed_ref, turned_ref, scale_ref, w_ref, sems
    ):
        copies = shards.copies(places, sources, w_ref, sems, 0, cols)
        for copy in copies:
            copy.start()
        for copy in copies:
            copy.wait()
        scale_ref[...] = jnp.transpose(
            shards.columns(w_ref, 3 * half_width, 128).astype(F32)
        )[:16]
        x = x_ref[...]
        step = 384
        for begin in range(0, 3 * half_width, step):
            qkv_ref[:, pl.ds(begin, step)] = matmul(x, shards.columns(w_ref, begin, step))
        low_head = lax.broadcasted_iota(jnp.int32, (rows, 128), 1) < DK
        later = half_ref[0] == 1

        def pair(i, carry):
            at = pl.multiple_of(i * 128, 128)
            here = pl.ds(at, 128)
            queries = qkv_ref[:, here]
            key_rows = qkv_ref[:, pl.ds(half_width + at, 128)]
            value_low = qkv_ref[:, pl.ds(2 * half_width + at, 128)].astype(BF)
            scaling = jnp.where(
                later, scale_ref[0:1, pl.ds(half_width + at, 128)], scale_ref[0:1, here]
            )
            query_unit = queries * head_inverse(queries, low_head) * scaling
            key_unit = (key_rows * head_inverse(key_rows, low_head) * scaling).astype(BF)
            mixed = None
            for mask in (low_head, ~low_head):
                probs = head_probs(only(mask, query_unit), key_unit, seq_len)
                head = matmul(probs.astype(BF), value_low)
                mixed = head if mixed is None else jnp.where(low_head, mixed, head)
            qu_ref[:, here] = query_unit.astype(BF)
            ku_ref[:, here] = key_unit
            vl_ref[:, here] = value_low
            mixed_ref[:, here] = mixed.astype(BF)
            turn(turned_ref, rows // 2, here, mixed)
            return carry

        lax.fori_loop(0, pairs, pair, 0)

    return call(
        "attention_forward",
        body,
        [like(rows, 3 * half_width, dtype=F32)] + [like(rows, half_width)] * 5 + [like(16, width, dtype=F32)],
        scalars=[shards.places, half],
        arrays=[token_rows],
        remote=shards.arrays,
        limit=24,
        scratch=shards.scratch(cols),
    )


def place_whole(source, _, target):
    target[...] = source[...]


def place_pair(first, later, _, target):
    target[0] = first[...]
    target[1] = later[...]


def place_outgoing(layer, mix, own, other, _, target):
    target[0] = layer[...]
    target[1] = (mix[...] + own[...] + other[...].astype(F32)).astype(BF)


def sum_whole(source, _, target):
    target[...] = jnp.sum(source[...], axis=0, keepdims=True)


def hidden_scales(half, scales, per_row, planes, shard):
    pieces = per_row // 2

    def body(half_ref, scale_ref, _, *targets):
        later = half_ref[0] != 0
        for i, target in enumerate(targets):
            for piece in range(pieces):
                row = 3 + i * per_row + piece
                values = jnp.where(
                    later, scale_ref[row + pieces : row + pieces + 1, :], scale_ref[row : row + 1, :]
                )
                for core in range(2):
                    for side in range(2):
                        for plane in range(planes):
                            begin = ((plane * 2 + side) * 2 + core) * shard
                            place = (((core * 2 + side) * planes + plane) * pieces + piece) * shard
                            target[:, place : place + shard] = values[:, begin : begin + shard]

    width = 4 * planes * pieces * shard
    return call(
        "hidden_scales",
        body,
        [like(1, width, dtype=F32)] * 2,
        scalars=[half],
        arrays=[scales],
    )


def place_halves(half_ref, target, own, other):
    width = own.shape[1]

    @pl.when(half_ref[0] == 0)
    def _():
        target[:, pl.ds(0, width)] = own[...]
        target[:, pl.ds(width, width)] = other[...]

    @pl.when(half_ref[0] != 0)
    def _():
        target[:, pl.ds(0, width)] = other[...]
        target[:, pl.ds(width, width)] = own[...]


def first_forward(half, mixed, mixed_other, token_rows, attention_mix, shards, skip):
    rows, width = token_rows.shape

    def body(
        places, half_ref, own_ref, other_ref, x_ref, mix_ref, sources, mixed_ref, attended_ref, first_ref, low_ref, w_ref, sems
    ):
        copies = shards.copies(places, sources, w_ref, sems, skip, width)
        for copy in copies:
            copy.start()
        place_halves(half_ref, mixed_ref, own_ref, other_ref)
        for copy in copies:
            copy.wait()
        for begin in range(0, width, 256):
            attended_ref[:, pl.ds(begin, 256)] = matmul(
                mixed_ref[...], shards.columns(w_ref, begin, 256)
            )
        x = x_ref[...].astype(F32)
        attended = attended_ref[...]
        mix = x + mix_ref[...] * (attended * inverse_rms(attended) - x)
        first = mix * inverse_rms(mix)
        first_ref[...] = first
        low_ref[...] = first.astype(BF)

    return call(
        "first_forward",
        body,
        [like(rows, width)] + [like(rows, width, dtype=F32)] * 2 + [like(rows, width)],
        scalars=[shards.places, half],
        arrays=[mixed, mixed_other, token_rows, attention_mix],
        remote=shards.arrays,
        limit=20,
        scratch=shards.scratch(width),
    )


def mix_backward(base, branch, rate, grad):
    branch_inverse = inverse_rms(branch)
    branch_unit = branch * branch_inverse
    mix = base + rate * (branch_unit - base)
    inverse = inverse_rms(mix)
    value = mix * inverse
    grad_mix = inverse * (grad - value * jnp.mean(grad * value, axis=-1, keepdims=True))
    grad_unit = grad_mix * rate
    grad_branch = branch_inverse * (
        grad_unit - branch_unit * jnp.mean(grad_unit * branch_unit, axis=-1, keepdims=True)
    )
    return value, grad_mix - grad_unit, grad_branch, grad_mix * (branch_unit - base)


def second_backward(partial, partial_other, first_state, cot, cot_other, valid, feed_mix):
    rows, width = partial.shape
    own = rows // 2

    def body(partial_ref, other_ref, first_ref, cot_ref, cot_other_ref, valid_ref, mix_ref, _, layer_ref, grad_ref, low_ref, rate_ref):
        for begin in (0, own):
            here = pl.ds(begin, own)
            down = partial_ref[here, :] + other_ref[here, :].astype(F32)
            grad = (cot_ref if begin == 0 else cot_other_ref)[...].astype(F32)
            value, grad_first, grad_down, grad_rate = mix_backward(
                first_ref[here, :], down, mix_ref[...], grad
            )
            grad_ref[here, :] = grad_first
            low_ref[here, :] = grad_down.astype(BF)
            if begin == 0:
                layer_ref[...] = (value * valid_ref[...]).astype(BF)
                rate_ref[...] = jnp.sum(grad_rate, axis=0, keepdims=True)

    return call(
        "second_backward",
        body,
        [like(own, width), like(rows, width, dtype=F32), like(rows, width), like(1, width, dtype=F32)],
        limit=18,
        arrays=[partial, partial_other, first_state, cot, cot_other, valid, feed_mix],
    )


def first_backward(half, grad_first, partial, partial_other, token_rows, attended, attention_mix, shards, skip, earlier):
    rows, width = partial.shape
    own = rows // 2
    half_width = width // 2

    def body(
        places, half_ref, grad_ref, partial_ref, other_ref, x_ref, attended_ref, mix_ref, sources, cols_ref, mixed_ref, token_ref, rate_ref, low_ref, w_ref, sems
    ):
        copies = shards.copies(places, sources, w_ref, sems, skip, width)
        for copy in copies:
            copy.start()
        for begin in (0, own):
            here = pl.ds(begin, own)
            grad = grad_ref[here, :] + partial_ref[here, :] + other_ref[here, :].astype(F32)
            _, grad_token, grad_attended, grad_rate = mix_backward(
                x_ref[here, :].astype(F32), attended_ref[here, :], mix_ref[...], grad
            )
            low_ref[here, :] = grad_attended.astype(BF)
            if begin == 0:
                token_ref[...] = grad_token
                rate_ref[...] = jnp.sum(grad_rate, axis=0, keepdims=True)
        at = pl.multiple_of(half_ref[0] * half_width, 128)
        cols_ref[...] = low_ref[:, pl.ds(at, half_width)]
        for copy in copies:
            copy.wait()
        mixed_ref[...] = back_matmul(
            low_ref[...], shards.rows(w_ref, half_ref[0], 2, 0, width)
        ).astype(BF)

    return call(
        "first_backward",
        body,
        [like(rows, half_width)] * 2 + [like(own, width, dtype=F32), like(1, width, dtype=F32)],
        scalars=[shards.places, half],
        arrays=[grad_first, partial, partial_other, token_rows, attended, attention_mix],
        remote=shards.arrays,
        limit=20,
        scratch=[pltpu.VMEM((rows, width), BF)] + shards.scratch(width),
        earlier=earlier,
    )


def attention_backward(half, grad_mixed, qkv, query_unit, key_unit, value_low, scales, shards, seq_len, earlier):
    rows, half_width = grad_mixed.shape
    width = 2 * half_width
    pairs = half_width // 128
    own = rows // 2

    def body(
        places, half_ref, gm_ref, qkv_ref, qu_ref, ku_ref, vl_ref, scale_ref, sources, grads_ref, scoring_ref, own_ref, other_ref, w_ref, sems
    ):
        copies = shards.copies(places, sources, w_ref, sems, 0, 3 * half_width)
        for copy in copies:
            copy.start()
        low_head = lax.broadcasted_iota(jnp.int32, (rows, 128), 1) < DK
        later = half_ref[0] == 1

        def pair(i, carry):
            at = pl.multiple_of(i * 128, 128)
            here = pl.ds(at, 128)
            query_unit = qu_ref[:, here]
            key_unit = ku_ref[:, here]
            value_low = vl_ref[:, here]
            scaling = jnp.where(
                later, scale_ref[0:1, pl.ds(half_width + at, 128)], scale_ref[0:1, here]
            )
            grad_value = grad_qunit = grad_kunit = None
            for mask in (low_head, ~low_head):
                probs = head_probs(only(mask, query_unit), key_unit, seq_len)
                grad_head = only(mask, gm_ref[:, here])
                value_part = weight_grad(probs.astype(BF), grad_head)
                grad_probs = back_matmul(grad_head, value_low)
                grad_scores = (
                    probs * (grad_probs - jnp.sum(grad_probs * probs, axis=-1, keepdims=True))
                ).astype(BF)
                query_part = matmul(grad_scores, key_unit)
                key_part = weight_grad(grad_scores, query_unit)
                if grad_value is None:
                    grad_value, grad_qunit, grad_kunit = value_part, query_part, key_part
                else:
                    grad_value = grad_value + value_part
                    grad_qunit = jnp.where(low_head, grad_qunit, query_part)
                    grad_kunit = jnp.where(low_head, grad_kunit, key_part)
            scoring_grad = None
            for place, grad in ((0, grad_qunit), (1, grad_kunit)):
                raw = qkv_ref[:, pl.ds(place * half_width + at, 128)]
                grad = grad * math.sqrt(DK)
                inverse = head_inverse(raw, low_head)
                unit = raw * inverse
                term = jnp.sum(grad * unit, axis=0, keepdims=True)
                scoring_grad = term if scoring_grad is None else scoring_grad + term
                grad = grad * scaling
                low_sum, high_sum = head_sums(grad * unit, low_head)
                grads_ref[place, :, here] = (
                    inverse * (grad - unit * jnp.where(low_head, low_sum, high_sum))
                ).astype(BF)
            grads_ref[2, :, here] = grad_value.astype(BF)
            scoring_ref[:, here] = scoring_grad
            return carry

        lax.fori_loop(0, pairs, pair, 0)
        for copy in copies:
            copy.wait()
        for piece in range(2):
            total = None
            for j in range(3):
                term = back_matmul(
                    grads_ref[j], shards.rows(w_ref, piece, 2, j * half_width, half_width)
                )
                total = term if total is None else total + term
            columns = pl.ds(piece * half_width, half_width)
            own_ref[:, columns] = total[:own]
            other_ref[:, columns] = total[own:].astype(BF)

    return call(
        "attention_backward",
        body,
        [
            like(3, rows, half_width),
            like(1, half_width, dtype=F32),
            like(own, width, dtype=F32),
            like(own, width),
        ],
        scalars=[shards.places, half],
        arrays=[grad_mixed, qkv, query_unit, key_unit, value_low, scales],
        remote=shards.arrays,
        limit=56,
        scratch=shards.scratch(3 * half_width),
        earlier=earlier,
    )


def down_grads(which, hidden, hidden_other, down, down_other, earlier):
    units = hidden_other.shape[1]
    width = down.shape[1]
    block = units // 2

    def body(which_ref, hidden_ref, hidden_other_ref, down_ref, down_other_ref, _, out_ref):
        def piece(i, carry):
            kept = i // 2
            side = jnp.where(kept == 1, which_ref[1], 1 - which_ref[1])
            columns = pl.ds(pl.multiple_of(side * block, 128), block)
            here = pl.ds(pl.multiple_of(i % 2 * 640, 128), 640)
            total = weight_grad(hidden_ref[which_ref[0], :, columns], down_ref[:, here])
            total = total + weight_grad(hidden_other_ref[:, columns], down_other_ref[:, here])
            out_ref[:, pl.ds(pl.multiple_of(i * 640, 128), 640)] = total.astype(BF)
            return carry

        lax.fori_loop(0, 2 * width // 640, piece, 0)

    return call(
        "down_grads",
        body,
        [like(block, 2 * width)],
        scalars=[which],
        arrays=[hidden, hidden_other, down, down_other],
        earlier=earlier,
    )[0]


def side_grads(name, lefts, rights, kept, earlier):
    block = lefts[0][0].shape[1] // 2
    number = len(lefts)
    total_width = sum(right[0].shape[-1] * len(right[2] or (0,)) for right in rights)

    def body(*refs):
        refs = [ref for ref in refs if not isinstance(ref, tuple)]
        out_ref = refs[-1]
        begin = 0
        for i in range(number):
            own_ref, other_ref, right_ref, right_other_ref = refs[4 * i : 4 * i + 4]
            columns = pl.ds(block if kept else 0, block)
            own = own_ref[:, columns]
            other = other_ref[:, columns]
            for index in rights[i][2] or (None,):
                def piece(j, carry, own=own, other=other, right=right_ref, right_other=right_other_ref, index=index, begin=begin):
                    at = pl.multiple_of(j * 640, 128)
                    here = (slice(None), pl.ds(at, 640))
                    if index is not None:
                        here = (index, *here)
                    total = weight_grad(own, right[here]) + weight_grad(other, right_other[here])
                    out_ref[:, pl.ds(begin + at, 640)] = total.astype(out_ref.dtype)
                    return carry

                count = right_ref.shape[-1] // 640
                lax.fori_loop(0, count, piece, 0)
                begin += 640 * count

    arrays = []
    for left, right in zip(lefts, rights):
        arrays += [*left, *right[:2]]
    return call(
        name,
        body,
        [like(block, total_width)],
        limit=20,
        arrays=arrays,
        earlier=earlier,
    )[0]


def lay_first(half, query_weight, key_weight, value_weight, out_weight, scales):
    shard, width = query_weight.shape
    half_width = width // 2

    def body(half_ref, q_ref, k_ref, v_ref, out_ref, *refs):
        target, square = refs[-2:]
        for i, ref in enumerate((q_ref, k_ref, v_ref)):
            place = pl.ds(i * half_width, half_width)

            @pl.when(half_ref[0] == 0)
            def _():
                target[:, place] = ref[:, pl.ds(0, half_width)]

            @pl.when(half_ref[0] != 0)
            def _():
                target[:, place] = ref[:, pl.ds(half_width, half_width)]

        square[...] = jnp.zeros_like(square)
        row = 0
        for ref in refs[: len(scales)]:
            values = ref[...].astype(F32)
            for begin in range(0, values.shape[1], shard):
                square[pl.ds(row, 1), pl.ds(0, shard)] = values[:, begin : begin + shard]
                row += 1
        target[:, pl.ds(3 * half_width, 128)] = jnp.transpose(square[...])[:shard].astype(BF)
        target[:, pl.ds(3 * half_width + 128, width)] = out_ref[...]

    return call(
        "lay_first",
        body,
        [like(shard, 3 * half_width + 128 + width)],
        limit=56,
        scalars=[half],
        arrays=[query_weight, key_weight, value_weight, out_weight]
        + [scale.reshape(1, -1) for scale in scales],
        scratch=[pltpu.VMEM((128, 128), F32)],
    )[0]


def lay_second(half, up_weight, gate_weight, down_weight, planes):
    shard = up_weight.shape[0]
    part = down_weight.shape[0] // 2
    width = down_weight.shape[1]

    def body(half_ref, up_ref, gate_ref, down_ref, _, target):
        upper = half_ref[0] != 0
        for i, ref in enumerate((up_ref, gate_ref)):
            for core in range(2):
                rows = slice((2 * i + core) * shard, (2 * i + core + 1) * shard)
                for side in range(2):
                    for plane in range(planes):
                        begin = ((plane * 2 + side) * 2 + core) * 2 * part
                        place = (side * planes + plane) * part
                        target[rows, place : place + part] = jnp.where(
                            upper,
                            ref[:, begin + part : begin + 2 * part].astype(F32),
                            ref[:, begin : begin + part].astype(F32),
                        ).astype(BF)

        @pl.when(jnp.logical_not(upper))
        def _():
            target[pl.ds(4 * shard, part), :] = down_ref[pl.ds(0, part), :]

        @pl.when(upper)
        def _():
            target[pl.ds(4 * shard, part), :] = down_ref[pl.ds(part, part), :]

    return call(
        "lay_second",
        body,
        [like(4 * shard + part, width)],
        limit=56,
        scalars=[half],
        arrays=[up_weight, gate_weight, down_weight],
    )[0]


def split_hidden(half, totals, planes, part):
    shard, width = totals[0].shape
    run = planes // 2 * part

    def body(half_ref, *refs):
        for source, target in zip(refs[: len(totals)], refs[-len(totals) :]):
            for i in range(4):
                begin = 2 * i * run
                first, later = source[:, begin : begin + run], source[:, begin + run : begin + 2 * run]
                target[:, i * run : (i + 1) * run] = jnp.where(
                    half_ref[0] == 0, later.astype(F32), first.astype(F32)
                ).astype(BF)

    return call(
        "split_hidden",
        body,
        [like(shard, width // 2)] * len(totals),
        scalars=[half],
        arrays=totals,
    )


def merge_hidden(half, totals, others, planes, part, earlier):
    shard, width = totals[0].shape
    run = planes // 2 * part

    def body(half_ref, *refs):
        number = len(totals)
        upper = half_ref[0] != 0
        for own_ref, other_ref, target in zip(refs[:number], refs[number : 2 * number], refs[-number:]):
            for plane in range(planes // 2):
                for side in range(2):
                    for core in range(2):
                        i = core * 2 + side
                        begin = 2 * i * run + plane * part
                        own = jnp.where(
                            upper,
                            own_ref[:, begin + run : begin + run + part].astype(F32),
                            own_ref[:, begin : begin + part].astype(F32),
                        )
                        begin = i * run + plane * part
                        other = other_ref[:, begin : begin + part].astype(F32)
                        begin = ((plane * 2 + side) * 2 + core) * 2 * part
                        target[:, begin : begin + part] = jnp.where(upper, other, own)
                        target[:, begin + part : begin + 2 * part] = jnp.where(upper, own, other)

    return call(
        "merge_hidden",
        body,
        [like(shard, width, dtype=F32)] * len(totals),
        scalars=[half],
        arrays=[*totals, *others],
        earlier=earlier,
    )


class HiddenWeights:
    def __init__(self, gathered, planes, shard, part):
        width = gathered.shape[2]
        units = 2 * planes * part
        self.direct = shard % 16 == 0 and part % 16 == 0
        self.width, self.units, self.shard, self.part = width, units, shard, part
        if self.direct:
            self.arrays = [gathered.reshape(planes, 2, 2, -1, width)]
            self.matrix = (planes, 2, 2, shard, units)
            self.down = (planes, part, width)
        else:
            blocks = gathered[:, 4 * shard :].reshape(planes, 2, 2, part, width)
            self.arrays = [
                jnp.stack(
                    [gathered[:, i * shard : (i + 1) * shard].reshape(width, width) for i in range(4)]
                ),
                jnp.transpose(blocks, (2, 1, 0, 3, 4)).reshape(2, 2, planes * part, width),
            ]
            self.matrix = (width, units)
            self.down = (planes * part, width)

    def scratch(self):
        return [
            pltpu.VMEM((4,) + self.matrix, BF),
            pltpu.VMEM((2, 2) + self.down, BF),
            pltpu.SemaphoreType.DMA((8,)),
        ]

    def specs(self):
        return [pl.BlockSpec(memory_space=pltpu.HBM)] * len(self.arrays)

    def matrix_copy(self, sources, wide, sems, i):
        if self.direct:
            source = sources[0].at[:, :, :, pl.ds(i * self.shard, self.shard), :]
        else:
            source = sources[0].at[i]
        return pltpu.make_async_copy(source, wide.at[i], sems.at[i])

    def down_copy(self, sources, tall, sems, core, side):
        if self.direct:
            source = sources[0].at[:, side, core, pl.ds(4 * self.shard, self.part), :]
        else:
            source = sources[1].at[core, side]
        return pltpu.make_async_copy(source, tall.at[core, side], sems.at[4 + core * 2 + side])

    def matrix_value(self, wide, i, columns):
        if self.direct:
            return wide[i, :, :, :, :, columns].reshape(self.width, -1)
        return wide[i, :, columns]

    def matrix_rows(self, wide, i, j, parts):
        if self.direct:
            step = self.matrix[0] // parts
            return wide[i, pl.ds(j * step, step)].reshape(self.width // parts, -1)
        step = self.width // parts
        return wide[i, pl.ds(j * step, step)]

    def down_value(self, tall, core, side, columns):
        if self.direct:
            return tall[core, side, :, :, columns].reshape(-1, columns.size)
        return tall[core, side, :, columns]

    def down_rows(self, tall, core, side):
        return tall[core, side].reshape(-1, self.width)


def hidden_forward(first_low, weights, up_scale, gate_scale, own_rows):
    rows, width = first_low.shape
    units = weights.units
    block = units // 2
    step = 256

    def body(first_ref, up_scale_ref, gate_scale_ref, *refs):
        sources = refs[: len(weights.arrays)]
        hidden_ref, up_ref, gate_ref, partial_ref, turned_ref, wide, tall, sems = refs[
            len(weights.arrays) :
        ]
        copies = [weights.matrix_copy(sources, wide, sems, i) for i in (0, 2, 1, 3)]
        down_copies = [
            weights.down_copy(sources, tall, sems, i, j) for i in range(2) for j in range(2)
        ]
        for copy in copies + down_copies:
            copy.start()
        first = first_ref[...]
        for core in range(2):
            copies[2 * core].wait()
            copies[2 * core + 1].wait()

            for begin in range(0, units, step):
                columns = pl.ds(begin, step)
                here = pl.ds(core * units + begin, step)
                up = matmul(first, weights.matrix_value(wide, core, columns))
                gate = matmul(first, weights.matrix_value(wide, 2 + core, columns))
                up_ref[:, here] = up.astype(BF)
                gate_ref[:, here] = gate.astype(BF)
                hidden = swiglu(up, gate, up_scale_ref[:, here], gate_scale_ref[:, here])
                hidden_ref[core, :, columns] = hidden.astype(BF)
        for copy in down_copies:
            copy.wait()

        for begin in range(0, width, step):
            columns = pl.ds(begin, step)
            total = None
            for core in range(2):
                for side in range(2):
                    term = matmul(
                        hidden_ref[core, :, pl.ds(side * block, block)],
                        weights.down_value(tall, core, side, columns),
                    )
                    total = term if total is None else total + term
            partial_ref[:, columns] = total
            turned_ref[pl.ds(0, own_rows), columns] = total[own_rows:].astype(BF)
            turned_ref[pl.ds(own_rows, own_rows), columns] = total[:own_rows].astype(BF)

    whole = pl.BlockSpec(memory_space=pltpu.VMEM)
    return pl.pallas_call(
        body,
        out_shape=[
            jax.ShapeDtypeStruct((2, rows, units), BF),
            jax.ShapeDtypeStruct((rows, 2 * units), BF),
            jax.ShapeDtypeStruct((rows, 2 * units), BF),
            jax.ShapeDtypeStruct((rows, width), F32),
            jax.ShapeDtypeStruct((rows, width), BF),
        ],
        in_specs=[whole] * 3 + weights.specs(),
        out_specs=[whole] * 5,
        scratch_shapes=weights.scratch(),
        compiler_params=pltpu.CompilerParams(vmem_limit_bytes=56 * 2**20),
        cost_estimate=COST,
        name="hidden_forward",
    )(first_low, up_scale.reshape(1, -1), gate_scale.reshape(1, -1), *weights.arrays)


def hidden_backward(down_low, up_proj, gate_proj, weights, up_scale, gate_scale, own_rows, earlier):
    rows, width = down_low.shape
    units = weights.units
    block = units // 2

    def body(down_ref, up_ref, gate_ref, up_scale_ref, gate_scale_ref, *refs):
        sources = refs[: len(weights.arrays)]
        low_ref, gate_low_ref, up_grad_ref, gate_grad_ref, partial_ref, turned_ref, wide, tall, sems = refs[
            len(weights.arrays) + len(earlier) :
        ]
        down_copies = [
            weights.down_copy(sources, tall, sems, i, j) for i in range(2) for j in range(2)
        ]
        copies = [weights.matrix_copy(sources, wide, sems, i) for i in range(4)]
        for copy in down_copies + copies:
            copy.start()
        down = down_ref[...]
        for core in range(2):
            for side in range(2):
                down_copies[core * 2 + side].wait()
                here = pl.ds((core * 2 + side) * block, block)
                grad_hidden = back_matmul(down, weights.down_rows(tall, core, side))
                up_scaling = up_scale_ref[:, here]
                gate_scaling = gate_scale_ref[:, here]
                up = up_ref[:, here].astype(F32)
                gate = gate_ref[:, here].astype(F32)
                scaled = gate_scaling * gate
                sigmoid = jax.nn.sigmoid(scaled)
                silu = scaled * sigmoid
                grad_scaled_up = grad_hidden * silu
                grad_scaled = grad_hidden * (up_scaling * up) * (sigmoid + silu * (1.0 - sigmoid))
                low_ref[:, here] = (grad_scaled_up * up_scaling).astype(BF)
                gate_low_ref[:, here] = (grad_scaled * gate_scaling).astype(BF)
                up_grad_ref[:, here] = jnp.sum(grad_scaled_up * up, axis=0, keepdims=True)
                gate_grad_ref[:, here] = jnp.sum(grad_scaled * gate, axis=0, keepdims=True)
        for copy in copies:
            copy.wait()
        pieces = 2
        piece = width // pieces
        for j in range(pieces):
            total = None
            for i in range(4):
                term = back_matmul(
                    (low_ref, gate_low_ref)[i // 2][:, pl.ds((i % 2) * units, units)],
                    weights.matrix_rows(wide, i, j, pieces),
                )
                total = term if total is None else total + term
            columns = pl.ds(j * piece, piece)
            partial_ref[:, columns] = total
            turned_ref[pl.ds(0, own_rows), columns] = total[own_rows:].astype(BF)
            turned_ref[pl.ds(own_rows, own_rows), columns] = total[:own_rows].astype(BF)

    whole = pl.BlockSpec(memory_space=pltpu.VMEM)
    return pl.pallas_call(
        body,
        out_shape=[
            jax.ShapeDtypeStruct((rows, 2 * units), BF),
            jax.ShapeDtypeStruct((rows, 2 * units), BF),
            jax.ShapeDtypeStruct((1, 2 * units), F32),
            jax.ShapeDtypeStruct((1, 2 * units), F32),
            jax.ShapeDtypeStruct((rows, width), F32),
            jax.ShapeDtypeStruct((rows, width), BF),
        ],
        in_specs=[whole] * 5
        + weights.specs()
        + [pl.BlockSpec(memory_space=pl.ANY)] * len(earlier),
        out_specs=[whole] * 6,
        scratch_shapes=weights.scratch(),
        compiler_params=pltpu.CompilerParams(vmem_limit_bytes=56 * 2**20),
        cost_estimate=COST,
        name="hidden_backward",
    )(
        down_low,
        up_proj,
        gate_proj,
        up_scale.reshape(1, -1),
        gate_scale.reshape(1, -1),
        *weights.arrays,
        *earlier,
    )


def per_device(
    tokens,
    cotangent,
    lengths,
    placement,
    query_weight,
    key_weight,
    value_weight,
    out_weight,
    up_weight,
    gate_weight,
    down_weight,
    scoring,
    upscale,
    gatescale,
    attention_rate,
    feedforward_rate,
):
    size = lax.axis_size("fsdp")
    planes = size // 4
    half = lax.axis_index("grp")
    me = lax.axis_index("fsdp")
    core = me % 2
    side = (me // 2) % 2
    plane = me // 4
    half_scalar = half.reshape(1).astype(jnp.int32)
    which = jnp.stack([core, side]).astype(jnp.int32)
    local_seqs = tokens.shape[0] // size
    seq_len = tokens.shape[1] * size
    width = tokens.shape[2]
    own_rows = local_seqs * seq_len
    shard = query_weight.shape[0]
    hidden_shard = down_weight.shape[0]
    part = hidden_shard // 2
    per_row = hidden_shard // shard
    half_width = width // 2

    def swap_core(array):
        return lax.ppermute(array, "fsdp", [(i, i ^ 1) for i in range(size)])

    def swap_side(array):
        return lax.ppermute(array, "fsdp", [(i, i ^ 2) for i in range(size)])

    def next_plane(array):
        return lax.ppermute(array, "fsdp", [(i, (i + 4) % size) for i in range(size)])

    def swap_half(array):
        return lax.ppermute(array, "grp", [(0, 1), (1, 0)])

    def pick(array, index, axis):
        return lax.dynamic_index_in_dim(array, index, axis, keepdims=False)

    first_group = lay_first(
        half_scalar,
        query_weight,
        key_weight,
        value_weight,
        out_weight,
        [scoring, attention_rate, feedforward_rate, upscale, gatescale],
    )
    second_group = lay_second(half_scalar, up_weight, gate_weight, down_weight, planes)
    hidden_width = planes * 4 * part
    core_width = hidden_width // 2
    held = [first_group]
    crossed = []
    for i in range(planes):
        here = after(held[-1], *crossed[-1:]) if crossed else held[-1]
        if i < planes - 1:
            held.append(next_plane(here))
        crossed.append(swap_side(here))
    second_whole = lax.all_gather(
        after(second_group, *held[: GATE + 1], *crossed[:GATE]), "fsdp", axis=0
    )
    (both,) = call(
        "rows",
        place_pair,
        [like(2, *tokens.shape)],
        arrays=[tokens, cotangent],
        earlier=[held[-1], crossed[-2]],
        limit=56,
    )
    arrived = lax.all_to_all(both, "fsdp", split_axis=1, concat_axis=2, tiled=True)
    own_tokens = arrived[0].reshape(own_rows, width)
    other_tokens = swap_half(own_tokens)
    held = held + crossed
    held = held + [swap_core(array) for array in held]
    places = []
    for i in range(4 * planes):
        there_core = 1 - core if i >= 2 * planes else core
        there_side = 1 - side if i // planes % 2 else side
        places.append(((plane - i) % planes * 2 + there_side) * 2 + there_core)
    shards = Shards(held, jnp.stack(places).astype(jnp.int32))

    group_order = placement[0]
    own_slots = lax.dynamic_slice_in_dim(group_order, me * local_seqs, local_seqs)
    own_lengths = jnp.take(lengths[0], own_slots)
    valid = (jnp.arange(seq_len, dtype=jnp.int32)[None, :] < own_lengths[:, None]).reshape(
        own_rows, 1
    )
    own_cot = jnp.where(valid, arrived[1].reshape(own_rows, width), jnp.zeros((), BF))
    token_rows = jnp.concatenate([own_tokens, other_tokens])
    other_cot = swap_half(own_cot)

    qkv, query_unit, key_unit, value_low, mixed_half, mixed_turned, scale_float = attention_forward(
        half_scalar, token_rows, shards, seq_len
    )
    attention_mix = scale_float[1:2]
    feed_mix = scale_float[2:3]

    up_scale, gate_scale = hidden_scales(half_scalar, scale_float, per_row, planes, shard)
    skip = 3 * half_width + 128
    mixed_low, attended, first_state, first_low = first_forward(
        half_scalar, mixed_half, swap_half(mixed_turned), token_rows, attention_mix, shards, skip
    )

    feature = jnp.arange(width, dtype=jnp.int32)
    block = []
    for b in range(2):
        for a in range(2):
            for k in range(planes):
                there_core = core if b == 0 else 1 - core
                there_side = 1 - side if a == 0 else side
                block.append((k * 2 + there_side) * 2 + there_core)
    block = jnp.stack(block).astype(jnp.int32)
    wanted = (block[:, None] * shard + jnp.arange(shard, dtype=jnp.int32)[None, :]).reshape(-1)
    chooser = (feature[:, None] == wanted[None, :]).astype(BF)

    def share_columns(array):
        chosen = matmul(array, chooser).astype(BF)
        return chosen[:, :half_width], swap_core(chosen[:, half_width:])

    def share(array):
        return array, swap_core(array)

    def over_planes(total):
        return lax.psum_scatter(
            total.reshape(planes, total.shape[0] // planes, total.shape[1]),
            "fsdp",
            scatter_dimension=0,
            axis_index_groups=[[k * 4 + j for k in range(planes)] for j in range(4)],
        )

    def joined(kept, arrived_part):
        return (kept.astype(F32) + arrived_part.astype(F32)).astype(BF)

    token_sides = share_columns(token_rows)
    mixed_sides = share_columns(mixed_low)
    first_sides = share_columns(first_low)
    hidden_weights = HiddenWeights(
        after(second_whole, *token_sides, *mixed_sides, *first_sides, other_cot), planes, shard, part
    )
    hidden_low, up_proj, gate_proj, partial, partial_turned = hidden_forward(
        first_low, hidden_weights, up_scale, gate_scale, own_rows
    )
    hidden_other = swap_core(pick(hidden_low, 1 - core, 0))

    layer_own, grad_first, down_low, feed_grad = second_backward(
        partial,
        swap_half(partial_turned),
        first_state,
        own_cot,
        other_cot,
        valid.astype(F32),
        feed_mix,
    )
    down_other = swap_core(down_low)
    down_args = (which, hidden_low, hidden_other, down_low, down_other)
    down_both = down_grads(*down_args, [])
    down_sum = over_planes(down_both)
    up_low, gate_low, upscale_grad, gatescale_grad, partial, partial_turned = hidden_backward(
        down_low, up_proj, gate_proj, hidden_weights, up_scale, gate_scale, own_rows, [down_both]
    )
    up_other = swap_core(up_low)
    partial_other = swap_half(partial_turned)
    gate_other = swap_core(gate_low)
    up_side = [(up_low, up_other, None)]
    gate_side = [(gate_low, gate_other, None)]
    up_sent = side_grads("up_sent", [first_sides], up_side, False, [])
    up_arrived = swap_side(up_sent)
    gate_sent = side_grads("gate_sent", [first_sides], gate_side, False, [up_sent])
    attended_cols, grad_mixed, grad_tokens, attention_grad = first_backward(
        half_scalar,
        grad_first,
        partial,
        partial_other,
        token_rows,
        attended,
        attention_mix,
        shards,
        skip,
        [gate_sent],
    )
    qkv_low, scoring_grad, token_own, token_sent = attention_backward(
        half_scalar, grad_mixed, qkv, query_unit, key_unit, value_low, scale_float, shards, seq_len, []
    )
    up_kept = side_grads("up_kept", [first_sides], up_side, True, [qkv_low])
    gate_arrived = swap_side(after(gate_sent, up_arrived, up_kept))
    attended_other = swap_core(after(attended_cols, up_arrived, up_kept))
    qkv_other = swap_core(after(qkv_low, up_arrived, up_kept))
    token_other = swap_half(after(token_sent, up_arrived, up_kept))
    up_joined = joined(up_kept, after(up_arrived, attended_other))
    up_total = over_planes(up_joined)
    last_args = (
        [mixed_sides, token_sides],
        [(attended_cols, attended_other, None), (qkv_low, qkv_other, (0, 1, 2))],
    )
    last_sent = side_grads("last_sent", *last_args, False, [up_joined, down_sum])
    gate_kept = side_grads("gate_kept", [first_sides], gate_side, True, [last_sent])
    last_kept = side_grads("last_kept", *last_args, True, [gate_kept])
    last_arrived = swap_side(after(last_sent, gate_arrived))
    gate_joined = joined(gate_kept, after(gate_arrived, last_kept, token_other))
    gate_total = over_planes(gate_joined)
    def hidden_spread(grad):
        blocks = jnp.transpose(grad.reshape(2, 2, planes, part), (2, 1, 0, 3))
        blank = jnp.zeros_like(blocks)
        both_halves = jnp.where(
            half == 0, jnp.stack([blocks, blank], axis=3), jnp.stack([blank, blocks], axis=3)
        )
        return both_halves.reshape(size, hidden_shard)

    blank = jnp.zeros_like(scoring_grad)
    scoring_spread = jnp.where(
        half == 0,
        jnp.concatenate([scoring_grad, blank], axis=1),
        jnp.concatenate([blank, scoring_grad], axis=1),
    )
    small = jnp.concatenate(
        [
            scoring_spread.reshape(size, shard),
            attention_grad.reshape(size, shard),
            feed_grad.reshape(size, shard),
            hidden_spread(upscale_grad),
            hidden_spread(gatescale_grad),
        ],
        axis=1,
    )
    (up_part,) = split_hidden(half_scalar, [up_total], planes, part)
    up_swapped = swap_half(up_part)
    (outgoing,) = call(
        "outgoing",
        place_outgoing,
        [like(2, own_rows, width)],
        arrays=[layer_own, grad_tokens, token_own, token_other],
        earlier=[up_part],
    )
    returned = lax.all_to_all(
        outgoing.reshape(2, local_seqs, seq_len, width), "fsdp", split_axis=2, concat_axis=1, tiled=True
    )
    (up_out,) = merge_hidden(half_scalar, [up_total], [up_swapped], planes, part, [returned])
    last_joined = joined(last_kept, after(last_arrived, up_out))
    last_total = over_planes(last_joined).astype(F32)
    down_total = down_sum[:, width:].astype(F32) + swap_side(
        after(down_sum[:, :width], last_joined)
    ).astype(F32)
    down_cols = down_total.reshape(part, 2, half_width)
    mine = pick(down_cols, half, 1)
    theirs = swap_half(pick(down_cols, 1 - half, 1).astype(BF)).astype(F32)
    down_out = jnp.where(
        half == 0, jnp.concatenate([mine, theirs]), jnp.concatenate([theirs, mine])
    )
    (small,) = call(
        "pass", place_whole, [like(*small.shape, dtype=F32)], arrays=[small], earlier=[last_joined]
    )
    small = lax.all_to_all(small, "fsdp", split_axis=0, concat_axis=0, tiled=True)
    (total,) = call("add", sum_whole, [like(1, small.shape[1], dtype=F32)], arrays=[small])
    total = total[0]
    total = total + swap_half(total)

    (gate_part,) = split_hidden(half_scalar, [gate_total], planes, part)
    (gate_out,) = merge_hidden(half_scalar, [gate_total], [swap_half(gate_part)], planes, part, [])
    out_total = last_total[:, :half_width]
    qkv_total = last_total[:, half_width:]

    return (
        returned[0],
        returned[1],
        qkv_total[:, :half_width],
        qkv_total[:, half_width : 2 * half_width],
        qkv_total[:, 2 * half_width :],
        out_total,
        up_out,
        gate_out,
        down_out,
        total[:shard],
        total[3 * shard : 3 * shard + hidden_shard],
        total[3 * shard + hidden_shard :],
        total[shard : 2 * shard],
        total[2 * shard : 3 * shard],
    )


def solution(mesh):
    rows = P("grp", "fsdp", None)
    group = P("grp", None)
    matrix = P("fsdp", None)
    vector = P("fsdp")
    split = P("fsdp", "grp")
    return jax.shard_map(
        per_device,
        mesh=mesh,
        in_specs=(rows, rows, group, group) + (matrix,) * 7 + (vector,) * 5,
        out_specs=(rows, rows) + (split,) * 7 + (vector,) * 5,
        check_vma=False,
    )
```

```python
import math

import jax
import jax.numpy as jnp
from jax import lax
from jax.experimental import pallas as pl
from jax.experimental.pallas import tpu as pltpu
from jax.sharding import PartitionSpec as P

H = 20
DK = 64
BF = jnp.bfloat16
F32 = jnp.float32
GATE = 1
COST = pl.CostEstimate(flops=1000, bytes_accessed=1000, transcendentals=0)


def swiglu(up_proj, gate_proj, upscale, gatescale):
    scaled = gatescale * gate_proj
    return scaled * jax.nn.sigmoid(scaled) * (upscale * up_proj)


def matmul(left_side, right_side):
    return jnp.dot(left_side, right_side, preferred_element_type=F32)


def weight_grad(left_side, right_side):
    return lax.dot_general(
        left_side, right_side, (((0,), (0,)), ((), ())), preferred_element_type=F32
    )


def back_matmul(grad_rows, weight_rows):
    return lax.dot_general(
        grad_rows, weight_rows, (((1,), (1,)), ((), ())), preferred_element_type=F32
    )


def after(value, *earlier):
    return lax.optimization_barrier((value, *earlier))[0]


def like(*shape, dtype=BF):
    return jax.ShapeDtypeStruct(shape, dtype)


def call(name, body, outs, scalars=(), arrays=(), remote=(), scratch=(), earlier=(), limit=16):
    counts = (len(scalars), len(arrays), len(remote), len(earlier), len(outs))

    def kernel(*refs):
        groups = []
        at = 0
        for count in counts:
            groups.append(refs[at : at + count])
            at += count
        body(*groups[0], *groups[1], groups[2], *groups[4], *refs[at:])

    whole = pl.BlockSpec(memory_space=pltpu.VMEM)
    kept = pl.BlockSpec(memory_space=pl.ANY)
    placed = pl.BlockSpec(memory_space=pltpu.HBM)
    return pl.pallas_call(
        kernel,
        out_shape=list(outs),
        in_specs=[pl.BlockSpec(memory_space=pltpu.SMEM)] * counts[0]
        + [whole] * counts[1]
        + [placed] * counts[2]
        + [kept] * counts[3],
        out_specs=[whole] * counts[4],
        scratch_shapes=list(scratch),
        compiler_params=pltpu.CompilerParams(vmem_limit_bytes=limit * 2**20),
        cost_estimate=COST,
        name=name,
    )(*scalars, *arrays, *remote, *earlier)


class Shards:
    def __init__(self, arrays, places):
        self.direct = arrays[0].shape[0] % 16 == 0
        if self.direct:
            self.arrays, self.places = list(arrays), places
        else:
            whole = jnp.zeros((len(arrays),) + arrays[0].shape, BF)
            for i, array in enumerate(arrays):
                whole = lax.dynamic_update_index_in_dim(whole, array, places[i], 0)
            self.arrays = [whole.reshape(-1, arrays[0].shape[1])]
            self.places = jnp.zeros((1,), jnp.int32)
        self.count = len(self.arrays)
        self.height = self.arrays[0].shape[0]

    def scratch(self, width):
        return [
            pltpu.VMEM((self.count, self.height, width), BF),
            pltpu.SemaphoreType.DMA((self.count,)),
        ]

    def copies(self, places, sources, target, sems, begin, width):
        return [
            pltpu.make_async_copy(
                sources[i].at[:, pl.ds(begin, width)], target.at[places[i]], sems.at[i]
            )
            for i in range(self.count)
        ]

    def columns(self, target, begin, width):
        return target[:, :, pl.ds(begin, width)].reshape(self.count * self.height, width)

    def rows(self, target, index, parts, begin, width):
        if self.direct:
            step = self.count // parts
            rows = target[pl.ds(index * step, step), :, pl.ds(begin, width)]
        else:
            step = self.height // parts
            rows = target[:, pl.ds(pl.multiple_of(index * step, step), step), pl.ds(begin, width)]
        return rows.reshape(-1, width)


def inverse_rms(vector):
    return lax.rsqrt(jnp.mean(vector * vector, axis=-1, keepdims=True) + 1e-06)


def head_sums(values, low_head):
    low_sum = jnp.sum(jnp.where(low_head, values, 0.0), axis=-1, keepdims=True)
    high_sum = jnp.sum(jnp.where(low_head, 0.0, values), axis=-1, keepdims=True)
    return low_sum, high_sum


def head_inverse(vector, low_head):
    low_sum, high_sum = head_sums(vector * vector, low_head)
    return jnp.where(low_head, lax.rsqrt(low_sum + 1e-06), lax.rsqrt(high_sum + 1e-06))


def head_probs(query_head, key_unit, seq_len):
    scores = back_matmul(query_head, key_unit) * math.sqrt(DK)
    query_row = lax.broadcasted_iota(jnp.int32, scores.shape, 0)
    key_row = lax.broadcasted_iota(jnp.int32, scores.shape, 1)
    start = query_row - lax.rem(query_row, seq_len)
    scores = jnp.where((key_row <= query_row) & (key_row >= start), scores, -1e30)
    exp_scores = jnp.exp(scores - jnp.max(scores, axis=-1, keepdims=True))
    return exp_scores / jnp.sum(exp_scores, axis=-1, keepdims=True)


def only(mask, values):
    return jnp.where(mask, values.astype(F32), 0.0).astype(BF)


def turn(ref, rows, columns, value):
    ref[pl.ds(0, rows), columns] = value[rows:].astype(BF)
    ref[pl.ds(rows, rows), columns] = value[:rows].astype(BF)


def attention_forward(half, token_rows, shards, seq_len):
    rows, width = token_rows.shape
    half_width = width // 2
    pairs = half_width // 128
    cols = 3 * half_width + 128

    def body(
        places, half_ref, x_ref, sources, qkv_ref, qu_ref, ku_ref, vl_ref, mixed_ref, turned_ref, scale_ref, w_ref, sems
    ):
        copies = shards.copies(places, sources, w_ref, sems, 0, cols)
        for copy in copies:
            copy.start()
        for copy in copies:
            copy.wait()
        scale_ref[...] = jnp.transpose(
            shards.columns(w_ref, 3 * half_width, 128).astype(F32)
        )[:16]
        x = x_ref[...]
        step = 384
        for begin in range(0, 3 * half_width, step):
            qkv_ref[:, pl.ds(begin, step)] = matmul(x, shards.columns(w_ref, begin, step))
        low_head = lax.broadcasted_iota(jnp.int32, (rows, 128), 1) < DK
        later = half_ref[0] == 1

        def pair(i, carry):
            at = pl.multiple_of(i * 128, 128)
            here = pl.ds(at, 128)
            queries = qkv_ref[:, here]
            key_rows = qkv_ref[:, pl.ds(half_width + at, 128)]
            value_low = qkv_ref[:, pl.ds(2 * half_width + at, 128)].astype(BF)
            scaling = jnp.where(
                later, scale_ref[0:1, pl.ds(half_width + at, 128)], scale_ref[0:1, here]
            )
            query_unit = queries * head_inverse(queries, low_head) * scaling
            key_unit = (key_rows * head_inverse(key_rows, low_head) * scaling).astype(BF)
            mixed = None
            for mask in (low_head, ~low_head):
                probs = head_probs(only(mask, query_unit), key_unit, seq_len)
                head = matmul(probs.astype(BF), value_low)
                mixed = head if mixed is None else jnp.where(low_head, mixed, head)
            qu_ref[:, here] = query_unit.astype(BF)
            ku_ref[:, here] = key_unit
            vl_ref[:, here] = value_low
            mixed_ref[:, here] = mixed.astype(BF)
            turn(turned_ref, rows // 2, here, mixed)
            return carry

        lax.fori_loop(0, pairs, pair, 0)

    return call(
        "attention_forward",
        body,
        [like(rows, 3 * half_width, dtype=F32)] + [like(rows, half_width)] * 5 + [like(16, width, dtype=F32)],
        scalars=[shards.places, half],
        arrays=[token_rows],
        remote=shards.arrays,
        limit=24,
        scratch=shards.scratch(cols),
    )


def place_whole(source, _, target):
    target[...] = source[...]


def place_pair(first, later, _, target):
    target[0] = first[...]
    target[1] = later[...]


def place_outgoing(layer, mix, own, other, _, target):
    target[0] = layer[...]
    target[1] = (mix[...] + own[...] + other[...].astype(F32)).astype(BF)


def sum_whole(source, _, target):
    target[...] = jnp.sum(source[...], axis=0, keepdims=True)


def hidden_scales(half, scales, per_row, planes, shard):
    pieces = per_row // 2

    def body(half_ref, scale_ref, _, *targets):
        later = half_ref[0] != 0
        for i, target in enumerate(targets):
            for piece in range(pieces):
                row = 3 + i * per_row + piece
                values = jnp.where(
                    later, scale_ref[row + pieces : row + pieces + 1, :], scale_ref[row : row + 1, :]
                )
                for core in range(2):
                    for side in range(2):
                        for plane in range(planes):
                            begin = ((plane * 2 + side) * 2 + core) * shard
                            place = (((core * 2 + side) * planes + plane) * pieces + piece) * shard
                            target[:, place : place + shard] = values[:, begin : begin + shard]

    width = 4 * planes * pieces * shard
    return call(
        "hidden_scales",
        body,
        [like(1, width, dtype=F32)] * 2,
        scalars=[half],
        arrays=[scales],
    )


def place_halves(half_ref, target, own, other):
    width = own.shape[1]

    @pl.when(half_ref[0] == 0)
    def _():
        target[:, pl.ds(0, width)] = own[...]
        target[:, pl.ds(width, width)] = other[...]

    @pl.when(half_ref[0] != 0)
    def _():
        target[:, pl.ds(0, width)] = other[...]
        target[:, pl.ds(width, width)] = own[...]


def first_forward(half, mixed, mixed_other, token_rows, attention_mix, shards, skip):
    rows, width = token_rows.shape

    def body(
        places, half_ref, own_ref, other_ref, x_ref, mix_ref, sources, mixed_ref, attended_ref, first_ref, low_ref, w_ref, sems
    ):
        copies = shards.copies(places, sources, w_ref, sems, skip, width)
        for copy in copies:
            copy.start()
        place_halves(half_ref, mixed_ref, own_ref, other_ref)
        for copy in copies:
            copy.wait()
        for begin in range(0, width, 256):
            attended_ref[:, pl.ds(begin, 256)] = matmul(
                mixed_ref[...], shards.columns(w_ref, begin, 256)
            )
        x = x_ref[...].astype(F32)
        attended = attended_ref[...]
        mix = x + mix_ref[...] * (attended * inverse_rms(attended) - x)
        first = mix * inverse_rms(mix)
        first_ref[...] = first
        low_ref[...] = first.astype(BF)

    return call(
        "first_forward",
        body,
        [like(rows, width)] + [like(rows, width, dtype=F32)] * 2 + [like(rows, width)],
        scalars=[shards.places, half],
        arrays=[mixed, mixed_other, token_rows, attention_mix],
        remote=shards.arrays,
        limit=20,
        scratch=shards.scratch(width),
    )


def mix_backward(base, branch, rate, grad):
    branch_inverse = inverse_rms(branch)
    branch_unit = branch * branch_inverse
    mix = base + rate * (branch_unit - base)
    inverse = inverse_rms(mix)
    value = mix * inverse
    grad_mix = inverse * (grad - value * jnp.mean(grad * value, axis=-1, keepdims=True))
    grad_unit = grad_mix * rate
    grad_branch = branch_inverse * (
        grad_unit - branch_unit * jnp.mean(grad_unit * branch_unit, axis=-1, keepdims=True)
    )
    return value, grad_mix - grad_unit, grad_branch, grad_mix * (branch_unit - base)


def second_backward(partial, partial_other, first_state, cot, cot_other, valid, feed_mix):
    rows, width = partial.shape
    own = rows // 2
    pieces = 4
    step = rows // pieces

    def body(partial_ref, other_ref, first_ref, cot_ref, cot_other_ref, valid_ref, mix_ref, layer_ref, grad_ref, low_ref, rate_ref):
        mine = pl.program_id(0) < pieces // 2
        down = partial_ref[...] + other_ref[...].astype(F32)
        grad = jnp.where(mine, cot_ref[...].astype(F32), cot_other_ref[...].astype(F32))
        value, grad_first, grad_down, grad_rate = mix_backward(first_ref[...], down, mix_ref[...], grad)
        grad_ref[...] = grad_first
        low_ref[...] = grad_down.astype(BF)

        @pl.when(pl.program_id(0) == 0)
        def _():
            rate_ref[...] = jnp.zeros_like(rate_ref)

        @pl.when(mine)
        def _():
            layer_ref[...] = (value * valid_ref[...]).astype(BF)
            rate_ref[...] += jnp.sum(grad_rate, axis=0, keepdims=True)

    every = pl.BlockSpec((step, width), lambda i: (i, 0))
    first_half = pl.BlockSpec((step, width), lambda i: (jnp.minimum(i, pieces // 2 - 1), 0))
    later_half = pl.BlockSpec((step, width), lambda i: (jnp.maximum(i - pieces // 2, 0), 0))
    vector = pl.BlockSpec((1, width), lambda i: (0, 0))
    return pl.pallas_call(
        body,
        grid=(pieces,),
        out_shape=[like(own, width), like(rows, width, dtype=F32), like(rows, width), like(1, width, dtype=F32)],
        in_specs=[
            every,
            every,
            every,
            first_half,
            later_half,
            pl.BlockSpec((step, 1), lambda i: (jnp.minimum(i, pieces // 2 - 1), 0)),
            vector,
        ],
        out_specs=[first_half, every, every, vector],
        compiler_params=pltpu.CompilerParams(vmem_limit_bytes=56 * 2**20),
        cost_estimate=COST,
        name="second_backward",
    )(partial, partial_other, first_state, cot, cot_other, valid, feed_mix)


def first_backward(half, grad_first, partial, partial_other, token_rows, attended, attention_mix, shards, skip, earlier):
    rows, width = partial.shape
    own = rows // 2
    half_width = width // 2

    def body(
        places, half_ref, grad_ref, partial_ref, other_ref, x_ref, attended_ref, mix_ref, sources, cols_ref, mixed_ref, token_ref, rate_ref, low_ref, w_ref, sems
    ):
        copies = shards.copies(places, sources, w_ref, sems, skip, width)
        for copy in copies:
            copy.start()
        for begin in (0, own):
            here = pl.ds(begin, own)
            grad = grad_ref[here, :] + partial_ref[here, :] + other_ref[here, :].astype(F32)
            _, grad_token, grad_attended, grad_rate = mix_backward(
                x_ref[here, :].astype(F32), attended_ref[here, :], mix_ref[...], grad
            )
            low_ref[here, :] = grad_attended.astype(BF)
            if begin == 0:
                token_ref[...] = grad_token
                rate_ref[...] = jnp.sum(grad_rate, axis=0, keepdims=True)
        at = pl.multiple_of(half_ref[0] * half_width, 128)
        cols_ref[...] = low_ref[:, pl.ds(at, half_width)]
        for copy in copies:
            copy.wait()
        mixed_ref[...] = back_matmul(
            low_ref[...], shards.rows(w_ref, half_ref[0], 2, 0, width)
        ).astype(BF)

    return call(
        "first_backward",
        body,
        [like(rows, half_width)] * 2 + [like(own, width, dtype=F32), like(1, width, dtype=F32)],
        scalars=[shards.places, half],
        arrays=[grad_first, partial, partial_other, token_rows, attended, attention_mix],
        remote=shards.arrays,
        limit=56,
        scratch=[pltpu.VMEM((rows, width), BF)] + shards.scratch(width),
        earlier=earlier,
    )


def attention_backward(half, grad_mixed, qkv, query_unit, key_unit, value_low, scales, shards, seq_len, earlier):
    rows, half_width = grad_mixed.shape
    width = 2 * half_width
    pairs = half_width // 128
    own = rows // 2

    def body(
        places, half_ref, gm_ref, qkv_ref, qu_ref, ku_ref, vl_ref, scale_ref, sources, grads_ref, scoring_ref, own_ref, other_ref, w_ref, sems
    ):
        copies = shards.copies(places, sources, w_ref, sems, 0, 3 * half_width)
        for copy in copies:
            copy.start()
        low_head = lax.broadcasted_iota(jnp.int32, (rows, 128), 1) < DK
        later = half_ref[0] == 1

        def pair(i, carry):
            at = pl.multiple_of(i * 128, 128)
            here = pl.ds(at, 128)
            query_unit = qu_ref[:, here]
            key_unit = ku_ref[:, here]
            value_low = vl_ref[:, here]
            scaling = jnp.where(
                later, scale_ref[0:1, pl.ds(half_width + at, 128)], scale_ref[0:1, here]
            )
            grad_value = grad_qunit = grad_kunit = None
            for mask in (low_head, ~low_head):
                probs = head_probs(only(mask, query_unit), key_unit, seq_len)
                grad_head = only(mask, gm_ref[:, here])
                value_part = weight_grad(probs.astype(BF), grad_head)
                grad_probs = back_matmul(grad_head, value_low)
                grad_scores = (
                    probs * (grad_probs - jnp.sum(grad_probs * probs, axis=-1, keepdims=True))
                ).astype(BF)
                query_part = matmul(grad_scores, key_unit)
                key_part = weight_grad(grad_scores, query_unit)
                if grad_value is None:
                    grad_value, grad_qunit, grad_kunit = value_part, query_part, key_part
                else:
                    grad_value = grad_value + value_part
                    grad_qunit = jnp.where(low_head, grad_qunit, query_part)
                    grad_kunit = jnp.where(low_head, grad_kunit, key_part)
            scoring_grad = None
            for place, grad in ((0, grad_qunit), (1, grad_kunit)):
                raw = qkv_ref[:, pl.ds(place * half_width + at, 128)]
                grad = grad * math.sqrt(DK)
                inverse = head_inverse(raw, low_head)
                unit = raw * inverse
                term = jnp.sum(grad * unit, axis=0, keepdims=True)
                scoring_grad = term if scoring_grad is None else scoring_grad + term
                grad = grad * scaling
                low_sum, high_sum = head_sums(grad * unit, low_head)
                grads_ref[place, :, here] = (
                    inverse * (grad - unit * jnp.where(low_head, low_sum, high_sum))
                ).astype(BF)
            grads_ref[2, :, here] = grad_value.astype(BF)
            scoring_ref[:, here] = scoring_grad
            return carry

        lax.fori_loop(0, pairs, pair, 0)
        for copy in copies:
            copy.wait()
        for piece in range(2):
            total = None
            for j in range(3):
                term = back_matmul(
                    grads_ref[j], shards.rows(w_ref, piece, 2, j * half_width, half_width)
                )
                total = term if total is None else total + term
            columns = pl.ds(piece * half_width, half_width)
            own_ref[:, columns] = total[:own]
            other_ref[:, columns] = total[own:].astype(BF)

    return call(
        "attention_backward",
        body,
        [
            like(3, rows, half_width),
            like(1, half_width, dtype=F32),
            like(own, width, dtype=F32),
            like(own, width),
        ],
        scalars=[shards.places, half],
        arrays=[grad_mixed, qkv, query_unit, key_unit, value_low, scales],
        remote=shards.arrays,
        limit=56,
        scratch=shards.scratch(3 * half_width),
        earlier=earlier,
    )


def down_grads(which, hidden, hidden_other, down, down_other, earlier):
    units = hidden_other.shape[1]
    width = down.shape[1]
    block = units // 2

    def body(which_ref, hidden_ref, hidden_other_ref, down_ref, down_other_ref, _, out_ref):
        def piece(i, carry):
            kept = i // 2
            side = jnp.where(kept == 1, which_ref[1], 1 - which_ref[1])
            columns = pl.ds(pl.multiple_of(side * block, 128), block)
            here = pl.ds(pl.multiple_of(i % 2 * 640, 128), 640)
            total = weight_grad(hidden_ref[which_ref[0], :, columns], down_ref[:, here])
            total = total + weight_grad(hidden_other_ref[:, columns], down_other_ref[:, here])
            out_ref[:, pl.ds(pl.multiple_of(i * 640, 128), 640)] = total.astype(BF)
            return carry

        lax.fori_loop(0, 2 * width // 640, piece, 0)

    return call(
        "down_grads",
        body,
        [like(block, 2 * width)],
        scalars=[which],
        arrays=[hidden, hidden_other, down, down_other],
        earlier=earlier,
    )[0]


def side_grads(name, lefts, rights, kept, earlier):
    block = lefts[0][0].shape[1] // 2
    number = len(lefts)
    total_width = sum(right[0].shape[-1] * len(right[2] or (0,)) for right in rights)

    def body(*refs):
        refs = [ref for ref in refs if not isinstance(ref, tuple)]
        out_ref = refs[-1]
        begin = 0
        for i in range(number):
            own_ref, other_ref, right_ref, right_other_ref = refs[4 * i : 4 * i + 4]
            columns = pl.ds(block if kept else 0, block)
            own = own_ref[:, columns]
            other = other_ref[:, columns]
            for index in rights[i][2] or (None,):
                def piece(j, carry, own=own, other=other, right=right_ref, right_other=right_other_ref, index=index, begin=begin):
                    at = pl.multiple_of(j * 640, 128)
                    here = (slice(None), pl.ds(at, 640))
                    if index is not None:
                        here = (index, *here)
                    total = weight_grad(own, right[here]) + weight_grad(other, right_other[here])
                    out_ref[:, pl.ds(begin + at, 640)] = total.astype(out_ref.dtype)
                    return carry

                count = right_ref.shape[-1] // 640
                lax.fori_loop(0, count, piece, 0)
                begin += 640 * count

    arrays = []
    for left, right in zip(lefts, rights):
        arrays += [*left, *right[:2]]
    return call(
        name,
        body,
        [like(block, total_width)],
        limit=20,
        arrays=arrays,
        earlier=earlier,
    )[0]


def lay_first(half, query_weight, key_weight, value_weight, out_weight, scales):
    shard, width = query_weight.shape
    half_width = width // 2

    def body(half_ref, q_ref, k_ref, v_ref, out_ref, *refs):
        target, square = refs[-2:]
        for i, ref in enumerate((q_ref, k_ref, v_ref)):
            place = pl.ds(i * half_width, half_width)

            @pl.when(half_ref[0] == 0)
            def _():
                target[:, place] = ref[:, pl.ds(0, half_width)]

            @pl.when(half_ref[0] != 0)
            def _():
                target[:, place] = ref[:, pl.ds(half_width, half_width)]

        square[...] = jnp.zeros_like(square)
        row = 0
        for ref in refs[: len(scales)]:
            values = ref[...].astype(F32)
            for begin in range(0, values.shape[1], shard):
                square[pl.ds(row, 1), pl.ds(0, shard)] = values[:, begin : begin + shard]
                row += 1
        target[:, pl.ds(3 * half_width, 128)] = jnp.transpose(square[...])[:shard].astype(BF)
        target[:, pl.ds(3 * half_width + 128, width)] = out_ref[...]

    return call(
        "lay_first",
        body,
        [like(shard, 3 * half_width + 128 + width)],
        limit=56,
        scalars=[half],
        arrays=[query_weight, key_weight, value_weight, out_weight]
        + [scale.reshape(1, -1) for scale in scales],
        scratch=[pltpu.VMEM((128, 128), F32)],
    )[0]


def lay_second(half, up_weight, gate_weight, down_weight, planes):
    shard = up_weight.shape[0]
    part = down_weight.shape[0] // 2
    width = down_weight.shape[1]

    def body(half_ref, up_ref, gate_ref, down_ref, _, target):
        upper = half_ref[0] != 0
        for i, ref in enumerate((up_ref, gate_ref)):
            for core in range(2):
                rows = slice((2 * i + core) * shard, (2 * i + core + 1) * shard)
                for side in range(2):
                    for plane in range(planes):
                        begin = ((plane * 2 + side) * 2 + core) * 2 * part
                        place = (side * planes + plane) * part
                        target[rows, place : place + part] = jnp.where(
                            upper,
                            ref[:, begin + part : begin + 2 * part].astype(F32),
                            ref[:, begin : begin + part].astype(F32),
                        ).astype(BF)

        @pl.when(jnp.logical_not(upper))
        def _():
            target[pl.ds(4 * shard, part), :] = down_ref[pl.ds(0, part), :]

        @pl.when(upper)
        def _():
            target[pl.ds(4 * shard, part), :] = down_ref[pl.ds(part, part), :]

    return call(
        "lay_second",
        body,
        [like(4 * shard + part, width)],
        limit=56,
        scalars=[half],
        arrays=[up_weight, gate_weight, down_weight],
    )[0]


def split_hidden(half, totals, planes, part):
    shard, width = totals[0].shape
    run = planes // 2 * part

    def body(half_ref, *refs):
        for source, target in zip(refs[: len(totals)], refs[-len(totals) :]):
            for i in range(4):
                begin = 2 * i * run
                first, later = source[:, begin : begin + run], source[:, begin + run : begin + 2 * run]
                target[:, i * run : (i + 1) * run] = jnp.where(
                    half_ref[0] == 0, later.astype(F32), first.astype(F32)
                ).astype(BF)

    return call(
        "split_hidden",
        body,
        [like(shard, width // 2)] * len(totals),
        scalars=[half],
        arrays=totals,
    )


def merge_hidden(half, totals, others, planes, part, earlier):
    shard, width = totals[0].shape
    run = planes // 2 * part

    def body(half_ref, *refs):
        number = len(totals)
        upper = half_ref[0] != 0
        for own_ref, other_ref, target in zip(refs[:number], refs[number : 2 * number], refs[-number:]):
            for plane in range(planes // 2):
                for side in range(2):
                    for core in range(2):
                        i = core * 2 + side
                        begin = 2 * i * run + plane * part
                        own = jnp.where(
                            upper,
                            own_ref[:, begin + run : begin + run + part].astype(F32),
                            own_ref[:, begin : begin + part].astype(F32),
                        )
                        begin = i * run + plane * part
                        other = other_ref[:, begin : begin + part].astype(F32)
                        begin = ((plane * 2 + side) * 2 + core) * 2 * part
                        target[:, begin : begin + part] = jnp.where(upper, other, own)
                        target[:, begin + part : begin + 2 * part] = jnp.where(upper, own, other)

    return call(
        "merge_hidden",
        body,
        [like(shard, width, dtype=F32)] * len(totals),
        scalars=[half],
        arrays=[*totals, *others],
        earlier=earlier,
    )


class HiddenWeights:
    def __init__(self, gathered, planes, shard, part):
        width = gathered.shape[2]
        units = 2 * planes * part
        self.direct = shard % 16 == 0 and part % 16 == 0
        self.width, self.units, self.shard, self.part = width, units, shard, part
        if self.direct:
            self.arrays = [gathered.reshape(planes, 2, 2, -1, width)]
            self.matrix = (planes, 2, 2, shard, units)
            self.down = (planes, part, width)
        else:
            blocks = gathered[:, 4 * shard :].reshape(planes, 2, 2, part, width)
            self.arrays = [
                jnp.stack(
                    [gathered[:, i * shard : (i + 1) * shard].reshape(width, width) for i in range(4)]
                ),
                jnp.transpose(blocks, (2, 1, 0, 3, 4)).reshape(2, 2, planes * part, width),
            ]
            self.matrix = (width, units)
            self.down = (planes * part, width)

    def scratch(self):
        return [
            pltpu.VMEM((4,) + self.matrix, BF),
            pltpu.VMEM((2, 2) + self.down, BF),
            pltpu.SemaphoreType.DMA((8,)),
        ]

    def specs(self):
        return [pl.BlockSpec(memory_space=pltpu.HBM)] * len(self.arrays)

    def matrix_copy(self, sources, wide, sems, i):
        if self.direct:
            source = sources[0].at[:, :, :, pl.ds(i * self.shard, self.shard), :]
        else:
            source = sources[0].at[i]
        return pltpu.make_async_copy(source, wide.at[i], sems.at[i])

    def down_copy(self, sources, tall, sems, core, side):
        if self.direct:
            source = sources[0].at[:, side, core, pl.ds(4 * self.shard, self.part), :]
        else:
            source = sources[1].at[core, side]
        return pltpu.make_async_copy(source, tall.at[core, side], sems.at[4 + core * 2 + side])

    def matrix_value(self, wide, i, columns):
        if self.direct:
            return wide[i, :, :, :, :, columns].reshape(self.width, -1)
        return wide[i, :, columns]

    def matrix_rows(self, wide, i, j, parts):
        if self.direct:
            step = self.matrix[0] // parts
            return wide[i, pl.ds(j * step, step)].reshape(self.width // parts, -1)
        step = self.width // parts
        return wide[i, pl.ds(j * step, step)]

    def down_value(self, tall, core, side, columns):
        if self.direct:
            return tall[core, side, :, :, columns].reshape(-1, columns.size)
        return tall[core, side, :, columns]

    def down_rows(self, tall, core, side):
        return tall[core, side].reshape(-1, self.width)


def hidden_forward(first_low, weights, up_scale, gate_scale, own_rows):
    rows, width = first_low.shape
    units = weights.units
    block = units // 2
    step = 256

    def body(first_ref, up_scale_ref, gate_scale_ref, *refs):
        sources = refs[: len(weights.arrays)]
        hidden_ref, up_ref, gate_ref, partial_ref, turned_ref, wide, tall, sems = refs[
            len(weights.arrays) :
        ]
        copies = [weights.matrix_copy(sources, wide, sems, i) for i in (0, 2, 1, 3)]
        down_copies = [
            weights.down_copy(sources, tall, sems, i, j) for i in range(2) for j in range(2)
        ]
        for copy in copies + down_copies:
            copy.start()
        first = first_ref[...]
        for core in range(2):
            copies[2 * core].wait()
            copies[2 * core + 1].wait()

            for begin in range(0, units, step):
                columns = pl.ds(begin, step)
                here = pl.ds(core * units + begin, step)
                up = matmul(first, weights.matrix_value(wide, core, columns))
                gate = matmul(first, weights.matrix_value(wide, 2 + core, columns))
                up_ref[:, here] = up.astype(BF)
                gate_ref[:, here] = gate.astype(BF)
                hidden = swiglu(up, gate, up_scale_ref[:, here], gate_scale_ref[:, here])
                hidden_ref[core, :, columns] = hidden.astype(BF)
        for copy in down_copies:
            copy.wait()

        for begin in range(0, width, step):
            columns = pl.ds(begin, step)
            total = None
            for core in range(2):
                for side in range(2):
                    term = matmul(
                        hidden_ref[core, :, pl.ds(side * block, block)],
                        weights.down_value(tall, core, side, columns),
                    )
                    total = term if total is None else total + term
            partial_ref[:, columns] = total
            turned_ref[pl.ds(0, own_rows), columns] = total[own_rows:].astype(BF)
            turned_ref[pl.ds(own_rows, own_rows), columns] = total[:own_rows].astype(BF)

    whole = pl.BlockSpec(memory_space=pltpu.VMEM)
    return pl.pallas_call(
        body,
        out_shape=[
            jax.ShapeDtypeStruct((2, rows, units), BF),
            jax.ShapeDtypeStruct((rows, 2 * units), BF),
            jax.ShapeDtypeStruct((rows, 2 * units), BF),
            jax.ShapeDtypeStruct((rows, width), F32),
            jax.ShapeDtypeStruct((rows, width), BF),
        ],
        in_specs=[whole] * 3 + weights.specs(),
        out_specs=[whole] * 5,
        scratch_shapes=weights.scratch(),
        compiler_params=pltpu.CompilerParams(vmem_limit_bytes=56 * 2**20),
        cost_estimate=COST,
        name="hidden_forward",
    )(first_low, up_scale.reshape(1, -1), gate_scale.reshape(1, -1), *weights.arrays)


def hidden_backward(down_low, up_proj, gate_proj, weights, up_scale, gate_scale, earlier):
    rows = down_low.shape[0]
    units = weights.units
    block = units // 2

    def body(down_ref, up_ref, gate_ref, up_scale_ref, gate_scale_ref, sources, low_ref, gate_low_ref, up_grad_ref, gate_grad_ref, tall, sems):
        copies = [weights.down_copy(sources, tall, sems, i, j) for i in range(2) for j in range(2)]
        for copy in copies:
            copy.start()
        down = down_ref[...]
        for core in range(2):
            for side in range(2):
                copies[core * 2 + side].wait()
                here = pl.ds((core * 2 + side) * block, block)
                grad_hidden = back_matmul(down, weights.down_rows(tall, core, side))
                up_scaling = up_scale_ref[:, here]
                gate_scaling = gate_scale_ref[:, here]
                up = up_ref[:, here].astype(F32)
                gate = gate_ref[:, here].astype(F32)
                scaled = gate_scaling * gate
                sigmoid = jax.nn.sigmoid(scaled)
                silu = scaled * sigmoid
                grad_scaled_up = grad_hidden * silu
                grad_scaled = grad_hidden * (up_scaling * up) * (sigmoid + silu * (1.0 - sigmoid))
                low_ref[:, here] = (grad_scaled_up * up_scaling).astype(BF)
                gate_low_ref[:, here] = (grad_scaled * gate_scaling).astype(BF)
                up_grad_ref[:, here] = jnp.sum(grad_scaled_up * up, axis=0, keepdims=True)
                gate_grad_ref[:, here] = jnp.sum(grad_scaled * gate, axis=0, keepdims=True)

    return call(
        "hidden_backward",
        body,
        [like(rows, 2 * units)] * 2 + [like(1, 2 * units, dtype=F32)] * 2,
        limit=56,
        arrays=[down_low, up_proj, gate_proj, up_scale, gate_scale],
        remote=weights.arrays,
        scratch=weights.scratch()[1:],
        earlier=earlier,
    )


def first_partial(up_low, gate_low, weights, own_rows, earlier):
    rows = up_low.shape[0]
    units = weights.units
    width = weights.width

    def body(up_ref, gate_ref, sources, partial_ref, turned_ref, wide, sems):
        copies = [weights.matrix_copy(sources, wide, sems, i) for i in range(4)]
        for copy in copies:
            copy.start()
        pieces = 2
        piece = width // pieces
        for i in range(4):
            copies[i].wait()
            left = (up_ref, gate_ref)[i // 2][:, pl.ds((i % 2) * units, units)]
            for j in range(pieces):
                columns = pl.ds(j * piece, piece)
                term = back_matmul(left, weights.matrix_rows(wide, i, j, pieces))
                if i:
                    term = partial_ref[:, columns] + term
                partial_ref[:, columns] = term
        for j in range(pieces):
            columns = pl.ds(j * piece, piece)
            turn(turned_ref, own_rows, columns, partial_ref[:, columns])

    return call(
        "first_partial",
        body,
        [like(rows, width, dtype=F32), like(rows, width)],
        limit=56,
        arrays=[up_low, gate_low],
        remote=weights.arrays,
        scratch=[weights.scratch()[0], weights.scratch()[2]],
        earlier=earlier,
    )


def per_device(
    tokens,
    cotangent,
    lengths,
    placement,
    query_weight,
    key_weight,
    value_weight,
    out_weight,
    up_weight,
    gate_weight,
    down_weight,
    scoring,
    upscale,
    gatescale,
    attention_rate,
    feedforward_rate,
):
    size = lax.axis_size("fsdp")
    planes = size // 4
    half = lax.axis_index("grp")
    me = lax.axis_index("fsdp")
    core = me % 2
    side = (me // 2) % 2
    plane = me // 4
    half_scalar = half.reshape(1).astype(jnp.int32)
    which = jnp.stack([core, side]).astype(jnp.int32)
    local_seqs = tokens.shape[0] // size
    seq_len = tokens.shape[1] * size
    width = tokens.shape[2]
    own_rows = local_seqs * seq_len
    shard = query_weight.shape[0]
    hidden_shard = down_weight.shape[0]
    part = hidden_shard // 2
    per_row = hidden_shard // shard
    half_width = width // 2

    def swap_core(array):
        return lax.ppermute(array, "fsdp", [(i, i ^ 1) for i in range(size)])

    def swap_side(array):
        return lax.ppermute(array, "fsdp", [(i, i ^ 2) for i in range(size)])

    def next_plane(array):
        return lax.ppermute(array, "fsdp", [(i, (i + 4) % size) for i in range(size)])

    def swap_half(array):
        return lax.ppermute(array, "grp", [(0, 1), (1, 0)])

    def pick(array, index, axis):
        return lax.dynamic_index_in_dim(array, index, axis, keepdims=False)

    first_group = lay_first(
        half_scalar,
        query_weight,
        key_weight,
        value_weight,
        out_weight,
        [scoring, attention_rate, feedforward_rate, upscale, gatescale],
    )
    second_group = lay_second(half_scalar, up_weight, gate_weight, down_weight, planes)
    hidden_width = planes * 4 * part
    core_width = hidden_width // 2
    held = [first_group]
    crossed = []
    for i in range(planes):
        here = after(held[-1], *crossed[-1:]) if crossed else held[-1]
        if i < planes - 1:
            held.append(next_plane(here))
        crossed.append(swap_side(here))
    second_whole = lax.all_gather(
        after(second_group, *held[: GATE + 1], *crossed[:GATE]), "fsdp", axis=0
    )
    (both,) = call(
        "rows",
        place_pair,
        [like(2, *tokens.shape)],
        arrays=[tokens, cotangent],
        earlier=[held[-1], crossed[-2]],
        limit=56,
    )
    arrived = lax.all_to_all(both, "fsdp", split_axis=1, concat_axis=2, tiled=True)
    own_tokens = arrived[0].reshape(own_rows, width)
    other_tokens = swap_half(own_tokens)
    held = held + crossed
    held = held + [swap_core(array) for array in held]
    places = []
    for i in range(4 * planes):
        there_core = 1 - core if i >= 2 * planes else core
        there_side = 1 - side if i // planes % 2 else side
        places.append(((plane - i) % planes * 2 + there_side) * 2 + there_core)
    shards = Shards(held, jnp.stack(places).astype(jnp.int32))

    group_order = placement[0]
    own_slots = lax.dynamic_slice_in_dim(group_order, me * local_seqs, local_seqs)
    own_lengths = jnp.take(lengths[0], own_slots)
    valid = (jnp.arange(seq_len, dtype=jnp.int32)[None, :] < own_lengths[:, None]).reshape(
        own_rows, 1
    )
    own_cot = jnp.where(valid, arrived[1].reshape(own_rows, width), jnp.zeros((), BF))
    token_rows = jnp.concatenate([own_tokens, other_tokens])
    other_cot = swap_half(own_cot)

    qkv, query_unit, key_unit, value_low, mixed_half, mixed_turned, scale_float = attention_forward(
        half_scalar, token_rows, shards, seq_len
    )
    attention_mix = scale_float[1:2]
    feed_mix = scale_float[2:3]

    up_scale, gate_scale = hidden_scales(half_scalar, scale_float, per_row, planes, shard)
    skip = 3 * half_width + 128
    mixed_low, attended, first_state, first_low = first_forward(
        half_scalar, mixed_half, swap_half(mixed_turned), token_rows, attention_mix, shards, skip
    )

    feature = jnp.arange(width, dtype=jnp.int32)
    block = []
    for b in range(2):
        for a in range(2):
            for k in range(planes):
                there_core = core if b == 0 else 1 - core
                there_side = 1 - side if a == 0 else side
                block.append((k * 2 + there_side) * 2 + there_core)
    block = jnp.stack(block).astype(jnp.int32)
    wanted = (block[:, None] * shard + jnp.arange(shard, dtype=jnp.int32)[None, :]).reshape(-1)
    chooser = (feature[:, None] == wanted[None, :]).astype(BF)

    def share_columns(array):
        chosen = matmul(array, chooser).astype(BF)
        return chosen[:, :half_width], swap_core(chosen[:, half_width:])

    def share(array):
        return array, swap_core(array)

    def over_planes(total):
        return lax.psum_scatter(
            total.reshape(planes, total.shape[0] // planes, total.shape[1]),
            "fsdp",
            scatter_dimension=0,
            axis_index_groups=[[k * 4 + j for k in range(planes)] for j in range(4)],
        )

    def joined(kept, arrived_part):
        return (kept.astype(F32) + arrived_part.astype(F32)).astype(BF)

    token_sides = share_columns(token_rows)
    mixed_sides = share_columns(mixed_low)
    first_sides = share_columns(first_low)
    hidden_weights = HiddenWeights(
        after(second_whole, *token_sides, *mixed_sides, *first_sides, other_cot), planes, shard, part
    )
    hidden_low, up_proj, gate_proj, partial, partial_turned = hidden_forward(
        first_low, hidden_weights, up_scale, gate_scale, own_rows
    )
    hidden_other = swap_core(pick(hidden_low, 1 - core, 0))

    layer_own, grad_first, down_low, feed_grad = second_backward(
        partial,
        swap_half(partial_turned),
        first_state,
        own_cot,
        other_cot,
        valid.astype(F32),
        feed_mix,
    )
    down_other = swap_core(down_low)
    down_args = (which, hidden_low, hidden_other, down_low, down_other)
    down_both = down_grads(*down_args, [])
    down_sum = over_planes(down_both)
    up_low, gate_low, upscale_grad, gatescale_grad = hidden_backward(
        down_low, up_proj, gate_proj, hidden_weights, up_scale, gate_scale, [down_both]
    )
    up_other = swap_core(up_low)
    gate_other = swap_core(gate_low)
    up_side = [(up_low, up_other, None)]
    gate_side = [(gate_low, gate_other, None)]
    up_sent = side_grads("up_sent", [first_sides], up_side, False, [])
    up_arrived = swap_side(up_sent)
    partial, partial_turned = first_partial(up_low, gate_low, hidden_weights, own_rows, [up_sent])
    partial_other = swap_half(partial_turned)
    gate_sent = side_grads("gate_sent", [first_sides], gate_side, False, [partial])
    up_kept = side_grads("up_kept", [first_sides], up_side, True, [gate_sent])
    attended_cols, grad_mixed, grad_tokens, attention_grad = first_backward(
        half_scalar,
        grad_first,
        partial,
        partial_other,
        token_rows,
        attended,
        attention_mix,
        shards,
        skip,
        [up_kept],
    )
    gate_arrived = swap_side(after(gate_sent, up_arrived))
    attended_other = swap_core(after(attended_cols, up_arrived))
    up_joined = joined(up_kept, after(up_arrived, grad_mixed))
    up_total = over_planes(up_joined)
    qkv_low, scoring_grad, token_own, token_sent = attention_backward(
        half_scalar, grad_mixed, qkv, query_unit, key_unit, value_low, scale_float, shards, seq_len, [up_joined]
    )
    qkv_other = swap_core(qkv_low)
    token_other = swap_half(token_sent)
    last_args = (
        [mixed_sides, token_sides],
        [(attended_cols, attended_other, None), (qkv_low, qkv_other, (0, 1, 2))],
    )
    last_sent = side_grads("last_sent", *last_args, False, [down_sum])
    gate_kept = side_grads("gate_kept", [first_sides], gate_side, True, [last_sent])
    last_kept = side_grads("last_kept", *last_args, True, [gate_kept])
    last_arrived = swap_side(after(last_sent, gate_arrived))
    gate_joined = joined(gate_kept, after(gate_arrived, last_kept, token_other))
    gate_total = over_planes(gate_joined)
    def hidden_spread(grad):
        blocks = jnp.transpose(grad.reshape(2, 2, planes, part), (2, 1, 0, 3))
        blank = jnp.zeros_like(blocks)
        both_halves = jnp.where(
            half == 0, jnp.stack([blocks, blank], axis=3), jnp.stack([blank, blocks], axis=3)
        )
        return both_halves.reshape(size, hidden_shard)

    blank = jnp.zeros_like(scoring_grad)
    scoring_spread = jnp.where(
        half == 0,
        jnp.concatenate([scoring_grad, blank], axis=1),
        jnp.concatenate([blank, scoring_grad], axis=1),
    )
    small = jnp.concatenate(
        [
            scoring_spread.reshape(size, shard),
            attention_grad.reshape(size, shard),
            feed_grad.reshape(size, shard),
            hidden_spread(upscale_grad),
            hidden_spread(gatescale_grad),
        ],
        axis=1,
    )
    (up_part,) = split_hidden(half_scalar, [up_total], planes, part)
    up_swapped = swap_half(up_part)
    (outgoing,) = call(
        "outgoing",
        place_outgoing,
        [like(2, own_rows, width)],
        arrays=[layer_own, grad_tokens, token_own, token_other],
        earlier=[up_part],
    )
    returned = lax.all_to_all(
        outgoing.reshape(2, local_seqs, seq_len, width), "fsdp", split_axis=2, concat_axis=1, tiled=True
    )
    (up_out,) = merge_hidden(half_scalar, [up_total], [up_swapped], planes, part, [returned])
    last_joined = joined(last_kept, after(last_arrived, up_out))
    last_total = over_planes(last_joined).astype(F32)
    down_total = down_sum[:, width:].astype(F32) + swap_side(
        after(down_sum[:, :width], last_joined)
    ).astype(F32)
    down_cols = down_total.reshape(part, 2, half_width)
    mine = pick(down_cols, half, 1)
    theirs = swap_half(pick(down_cols, 1 - half, 1).astype(BF)).astype(F32)
    down_out = jnp.where(
        half == 0, jnp.concatenate([mine, theirs]), jnp.concatenate([theirs, mine])
    )
    (small,) = call(
        "pass", place_whole, [like(*small.shape, dtype=F32)], arrays=[small], earlier=[last_joined]
    )
    small = lax.all_to_all(small, "fsdp", split_axis=0, concat_axis=0, tiled=True)
    (total,) = call("add", sum_whole, [like(1, small.shape[1], dtype=F32)], arrays=[small])
    total = total[0]
    total = total + swap_half(total)

    (gate_part,) = split_hidden(half_scalar, [gate_total], planes, part)
    (gate_out,) = merge_hidden(half_scalar, [gate_total], [swap_half(gate_part)], planes, part, [])
    out_total = last_total[:, :half_width]
    qkv_total = last_total[:, half_width:]

    return (
        returned[0],
        returned[1],
        qkv_total[:, :half_width],
        qkv_total[:, half_width : 2 * half_width],
        qkv_total[:, 2 * half_width :],
        out_total,
        up_out,
        gate_out,
        down_out,
        total[:shard],
        total[3 * shard : 3 * shard + hidden_shard],
        total[3 * shard + hidden_shard :],
        total[shard : 2 * shard],
        total[2 * shard : 3 * shard],
    )


def solution(mesh):
    rows = P("grp", "fsdp", None)
    group = P("grp", None)
    matrix = P("fsdp", None)
    vector = P("fsdp")
    split = P("fsdp", "grp")
    return jax.shard_map(
        per_device,
        mesh=mesh,
        in_specs=(rows, rows, group, group) + (matrix,) * 7 + (vector,) * 5,
        out_specs=(rows, rows) + (split,) * 7 + (vector,) * 5,
        check_vma=False,
    )
```

```python
import math

import jax
import jax.numpy as jnp
from jax import lax
from jax.experimental import pallas as pl
from jax.experimental.pallas import tpu as pltpu
from jax.sharding import PartitionSpec as P

H = 20
DK = 64
BF = jnp.bfloat16
F32 = jnp.float32
GATE = 1
COST = pl.CostEstimate(flops=1000, bytes_accessed=1000, transcendentals=0)


def swiglu(up_proj, gate_proj, upscale, gatescale):
    scaled = gatescale * gate_proj
    return scaled * jax.nn.sigmoid(scaled) * (upscale * up_proj)


def matmul(left_side, right_side):
    return jnp.dot(left_side, right_side, preferred_element_type=F32)


def weight_grad(left_side, right_side):
    return lax.dot_general(
        left_side, right_side, (((0,), (0,)), ((), ())), preferred_element_type=F32
    )


def back_matmul(grad_rows, weight_rows):
    return lax.dot_general(
        grad_rows, weight_rows, (((1,), (1,)), ((), ())), preferred_element_type=F32
    )


def after(value, *earlier):
    return lax.optimization_barrier((value, *earlier))[0]


def like(*shape, dtype=BF):
    return jax.ShapeDtypeStruct(shape, dtype)


def call(name, body, outs, scalars=(), arrays=(), remote=(), scratch=(), earlier=(), limit=16, written=0):
    counts = (len(scalars), len(arrays), len(remote), len(earlier), len(outs))

    def kernel(*refs):
        groups = []
        at = 0
        for count in counts:
            groups.append(refs[at : at + count])
            at += count
        body(*groups[0], *groups[1], groups[2], *groups[4], *refs[at:])

    whole = pl.BlockSpec(memory_space=pltpu.VMEM)
    kept = pl.BlockSpec(memory_space=pl.ANY)
    placed = pl.BlockSpec(memory_space=pltpu.HBM)
    return pl.pallas_call(
        kernel,
        out_shape=list(outs),
        in_specs=[pl.BlockSpec(memory_space=pltpu.SMEM)] * counts[0]
        + [whole] * counts[1]
        + [placed] * counts[2]
        + [kept] * counts[3],
        out_specs=[placed] * written + [whole] * (counts[4] - written),
        scratch_shapes=list(scratch),
        compiler_params=pltpu.CompilerParams(vmem_limit_bytes=limit * 2**20),
        cost_estimate=COST,
        name=name,
    )(*scalars, *arrays, *remote, *earlier)


class Shards:
    def __init__(self, arrays, places):
        self.direct = arrays[0].shape[0] % 16 == 0
        if self.direct:
            self.arrays, self.places = list(arrays), places
        else:
            whole = jnp.zeros((len(arrays),) + arrays[0].shape, BF)
            for i, array in enumerate(arrays):
                whole = lax.dynamic_update_index_in_dim(whole, array, places[i], 0)
            self.arrays = [whole.reshape(-1, arrays[0].shape[1])]
            self.places = jnp.zeros((1,), jnp.int32)
        self.count = len(self.arrays)
        self.height = self.arrays[0].shape[0]

    def scratch(self, width):
        return [
            pltpu.VMEM((self.count, self.height, width), BF),
            pltpu.SemaphoreType.DMA((self.count,)),
        ]

    def copies(self, places, sources, target, sems, begin, width):
        return [
            pltpu.make_async_copy(
                sources[i].at[:, pl.ds(begin, width)], target.at[places[i]], sems.at[i]
            )
            for i in range(self.count)
        ]

    def columns(self, target, begin, width):
        return target[:, :, pl.ds(begin, width)].reshape(self.count * self.height, width)

    def rows(self, target, index, parts, begin, width):
        if self.direct:
            step = self.count // parts
            rows = target[pl.ds(index * step, step), :, pl.ds(begin, width)]
        else:
            step = self.height // parts
            rows = target[:, pl.ds(pl.multiple_of(index * step, step), step), pl.ds(begin, width)]
        return rows.reshape(-1, width)


def inverse_rms(vector):
    return lax.rsqrt(jnp.mean(vector * vector, axis=-1, keepdims=True) + 1e-06)


def head_sums(values, low_head):
    low_sum = jnp.sum(jnp.where(low_head, values, 0.0), axis=-1, keepdims=True)
    high_sum = jnp.sum(jnp.where(low_head, 0.0, values), axis=-1, keepdims=True)
    return low_sum, high_sum


def head_inverse(vector, low_head):
    low_sum, high_sum = head_sums(vector * vector, low_head)
    return jnp.where(low_head, lax.rsqrt(low_sum + 1e-06), lax.rsqrt(high_sum + 1e-06))


def head_probs(query_head, key_unit, seq_len):
    scores = back_matmul(query_head, key_unit) * math.sqrt(DK)
    query_row = lax.broadcasted_iota(jnp.int32, scores.shape, 0)
    key_row = lax.broadcasted_iota(jnp.int32, scores.shape, 1)
    start = query_row - lax.rem(query_row, seq_len)
    scores = jnp.where((key_row <= query_row) & (key_row >= start), scores, -1e30)
    exp_scores = jnp.exp(scores - jnp.max(scores, axis=-1, keepdims=True))
    return exp_scores / jnp.sum(exp_scores, axis=-1, keepdims=True)


def only(mask, values):
    return jnp.where(mask, values.astype(F32), 0.0).astype(BF)


def turn(ref, rows, columns, value):
    ref[pl.ds(0, rows), columns] = value[rows:].astype(BF)
    ref[pl.ds(rows, rows), columns] = value[:rows].astype(BF)


def attention_forward(half, token_rows, shards, seq_len):
    rows, width = token_rows.shape
    half_width = width // 2
    pairs = half_width // 128
    cols = 3 * half_width + 128

    def body(
        places, half_ref, x_ref, sources, qkv_ref, qu_ref, ku_ref, vl_ref, mixed_ref, turned_ref, scale_ref, w_ref, sems
    ):
        copies = shards.copies(places, sources, w_ref, sems, 0, cols)
        for copy in copies:
            copy.start()
        for copy in copies:
            copy.wait()
        scale_ref[...] = jnp.transpose(
            shards.columns(w_ref, 3 * half_width, 128).astype(F32)
        )[:16]
        x = x_ref[...]
        step = 384
        for begin in range(0, 3 * half_width, step):
            qkv_ref[:, pl.ds(begin, step)] = matmul(x, shards.columns(w_ref, begin, step))
        low_head = lax.broadcasted_iota(jnp.int32, (rows, 128), 1) < DK
        later = half_ref[0] == 1

        def pair(i, carry):
            at = pl.multiple_of(i * 128, 128)
            here = pl.ds(at, 128)
            queries = qkv_ref[:, here]
            key_rows = qkv_ref[:, pl.ds(half_width + at, 128)]
            value_low = qkv_ref[:, pl.ds(2 * half_width + at, 128)].astype(BF)
            scaling = jnp.where(
                later, scale_ref[0:1, pl.ds(half_width + at, 128)], scale_ref[0:1, here]
            )
            query_unit = queries * head_inverse(queries, low_head) * scaling
            key_unit = (key_rows * head_inverse(key_rows, low_head) * scaling).astype(BF)
            mixed = None
            for mask in (low_head, ~low_head):
                probs = head_probs(only(mask, query_unit), key_unit, seq_len)
                head = matmul(probs.astype(BF), value_low)
                mixed = head if mixed is None else jnp.where(low_head, mixed, head)
            qu_ref[:, here] = query_unit.astype(BF)
            ku_ref[:, here] = key_unit
            vl_ref[:, here] = value_low
            mixed_ref[:, here] = mixed.astype(BF)
            turn(turned_ref, rows // 2, here, mixed)
            return carry

        lax.fori_loop(0, pairs, pair, 0)

    return call(
        "attention_forward",
        body,
        [like(rows, 3 * half_width, dtype=F32)] + [like(rows, half_width)] * 5 + [like(16, width, dtype=F32)],
        scalars=[shards.places, half],
        arrays=[token_rows],
        remote=shards.arrays,
        limit=24,
        scratch=shards.scratch(cols),
    )


def place_whole(source, _, target):
    target[...] = source[...]


def place_pair(first, later, _, target):
    target[0] = first[...]
    target[1] = later[...]


def place_outgoing(layer, mix, own, other, _, target):
    target[0] = layer[...]
    target[1] = (mix[...] + own[...] + other[...].astype(F32)).astype(BF)


def sum_whole(source, _, target):
    target[...] = jnp.sum(source[...], axis=0, keepdims=True)


def hidden_scales(half, scales, per_row, planes, shard):
    pieces = per_row // 2

    def body(half_ref, scale_ref, _, *targets):
        later = half_ref[0] != 0
        for i, target in enumerate(targets):
            for piece in range(pieces):
                row = 3 + i * per_row + piece
                values = jnp.where(
                    later, scale_ref[row + pieces : row + pieces + 1, :], scale_ref[row : row + 1, :]
                )
                for core in range(2):
                    for side in range(2):
                        for plane in range(planes):
                            begin = ((plane * 2 + side) * 2 + core) * shard
                            place = (((core * 2 + side) * planes + plane) * pieces + piece) * shard
                            target[:, place : place + shard] = values[:, begin : begin + shard]

    width = 4 * planes * pieces * shard
    return call(
        "hidden_scales",
        body,
        [like(1, width, dtype=F32)] * 2,
        scalars=[half],
        arrays=[scales],
    )


def place_halves(half_ref, target, own, other):
    width = own.shape[1]

    @pl.when(half_ref[0] == 0)
    def _():
        target[:, pl.ds(0, width)] = own[...]
        target[:, pl.ds(width, width)] = other[...]

    @pl.when(half_ref[0] != 0)
    def _():
        target[:, pl.ds(0, width)] = other[...]
        target[:, pl.ds(width, width)] = own[...]


def first_forward(half, mixed, mixed_other, token_rows, attention_mix, shards, skip):
    rows, width = token_rows.shape

    def body(
        places, half_ref, own_ref, other_ref, x_ref, mix_ref, sources, mixed_ref, attended_ref, first_ref, low_ref, w_ref, sems
    ):
        copies = shards.copies(places, sources, w_ref, sems, skip, width)
        for copy in copies:
            copy.start()
        place_halves(half_ref, mixed_ref, own_ref, other_ref)
        for copy in copies:
            copy.wait()
        for begin in range(0, width, 256):
            attended_ref[:, pl.ds(begin, 256)] = matmul(
                mixed_ref[...], shards.columns(w_ref, begin, 256)
            )
        x = x_ref[...].astype(F32)
        attended = attended_ref[...]
        mix = x + mix_ref[...] * (attended * inverse_rms(attended) - x)
        first = mix * inverse_rms(mix)
        first_ref[...] = first
        low_ref[...] = first.astype(BF)

    return call(
        "first_forward",
        body,
        [like(rows, width)] + [like(rows, width, dtype=F32)] * 2 + [like(rows, width)],
        scalars=[shards.places, half],
        arrays=[mixed, mixed_other, token_rows, attention_mix],
        remote=shards.arrays,
        limit=20,
        scratch=shards.scratch(width),
    )


def mix_backward(base, branch, rate, grad):
    branch_inverse = inverse_rms(branch)
    branch_unit = branch * branch_inverse
    mix = base + rate * (branch_unit - base)
    inverse = inverse_rms(mix)
    value = mix * inverse
    grad_mix = inverse * (grad - value * jnp.mean(grad * value, axis=-1, keepdims=True))
    grad_unit = grad_mix * rate
    grad_branch = branch_inverse * (
        grad_unit - branch_unit * jnp.mean(grad_unit * branch_unit, axis=-1, keepdims=True)
    )
    return value, grad_mix - grad_unit, grad_branch, grad_mix * (branch_unit - base)


def second_backward(partial, partial_other, first_state, cot, cot_other, valid, feed_mix):
    rows, width = partial.shape
    own = rows // 2
    pieces = 4
    step = rows // pieces

    def body(partial_ref, other_ref, first_ref, cot_ref, cot_other_ref, valid_ref, mix_ref, layer_ref, grad_ref, low_ref, rate_ref):
        mine = pl.program_id(0) < pieces // 2
        down = partial_ref[...] + other_ref[...].astype(F32)
        grad = jnp.where(mine, cot_ref[...].astype(F32), cot_other_ref[...].astype(F32))
        value, grad_first, grad_down, grad_rate = mix_backward(first_ref[...], down, mix_ref[...], grad)
        grad_ref[...] = grad_first
        low_ref[...] = grad_down.astype(BF)

        @pl.when(pl.program_id(0) == 0)
        def _():
            rate_ref[...] = jnp.zeros_like(rate_ref)

        @pl.when(mine)
        def _():
            layer_ref[...] = (value * valid_ref[...]).astype(BF)
            rate_ref[...] += jnp.sum(grad_rate, axis=0, keepdims=True)

    every = pl.BlockSpec((step, width), lambda i: (i, 0))
    first_half = pl.BlockSpec((step, width), lambda i: (jnp.minimum(i, pieces // 2 - 1), 0))
    later_half = pl.BlockSpec((step, width), lambda i: (jnp.maximum(i - pieces // 2, 0), 0))
    vector = pl.BlockSpec((1, width), lambda i: (0, 0))
    return pl.pallas_call(
        body,
        grid=(pieces,),
        out_shape=[like(own, width), like(rows, width, dtype=F32), like(rows, width), like(1, width, dtype=F32)],
        in_specs=[
            every,
            every,
            every,
            first_half,
            later_half,
            pl.BlockSpec((step, 1), lambda i: (jnp.minimum(i, pieces // 2 - 1), 0)),
            vector,
        ],
        out_specs=[first_half, every, every, vector],
        compiler_params=pltpu.CompilerParams(vmem_limit_bytes=56 * 2**20),
        cost_estimate=COST,
        name="second_backward",
    )(partial, partial_other, first_state, cot, cot_other, valid, feed_mix)


def first_backward(half, grad_first, partial, partial_other, token_rows, attended, attention_mix, shards, skip, earlier):
    rows, width = partial.shape
    own = rows // 2
    half_width = width // 2

    def body(
        places, half_ref, grad_ref, partial_ref, other_ref, x_ref, attended_ref, mix_ref, sources, cols_ref, mixed_ref, token_ref, rate_ref, low_ref, w_ref, sems
    ):
        copies = shards.copies(places, sources, w_ref, sems, skip, width)
        for copy in copies:
            copy.start()
        for begin in (0, own):
            here = pl.ds(begin, own)
            grad = grad_ref[here, :] + partial_ref[here, :] + other_ref[here, :].astype(F32)
            _, grad_token, grad_attended, grad_rate = mix_backward(
                x_ref[here, :].astype(F32), attended_ref[here, :], mix_ref[...], grad
            )
            low_ref[here, :] = grad_attended.astype(BF)
            if begin == 0:
                token_ref[...] = grad_token
                rate_ref[...] = jnp.sum(grad_rate, axis=0, keepdims=True)
        at = pl.multiple_of(half_ref[0] * half_width, 128)
        cols_ref[...] = low_ref[:, pl.ds(at, half_width)]
        for copy in copies:
            copy.wait()
        mixed_ref[...] = back_matmul(
            low_ref[...], shards.rows(w_ref, half_ref[0], 2, 0, width)
        ).astype(BF)

    return call(
        "first_backward",
        body,
        [like(rows, half_width)] * 2 + [like(own, width, dtype=F32), like(1, width, dtype=F32)],
        scalars=[shards.places, half],
        arrays=[grad_first, partial, partial_other, token_rows, attended, attention_mix],
        remote=shards.arrays,
        limit=56,
        scratch=[pltpu.VMEM((rows, width), BF)] + shards.scratch(width),
        earlier=earlier,
    )


def attention_backward(half, grad_mixed, qkv, query_unit, key_unit, value_low, scales, shards, seq_len, earlier):
    rows, half_width = grad_mixed.shape
    width = 2 * half_width
    pairs = half_width // 128
    own = rows // 2

    def body(
        places, half_ref, gm_ref, qkv_ref, qu_ref, ku_ref, vl_ref, scale_ref, sources, grads_ref, scoring_ref, own_ref, other_ref, w_ref, sems
    ):
        copies = shards.copies(places, sources, w_ref, sems, 0, 3 * half_width)
        for copy in copies:
            copy.start()
        low_head = lax.broadcasted_iota(jnp.int32, (rows, 128), 1) < DK
        later = half_ref[0] == 1

        def pair(i, carry):
            at = pl.multiple_of(i * 128, 128)
            here = pl.ds(at, 128)
            query_unit = qu_ref[:, here]
            key_unit = ku_ref[:, here]
            value_low = vl_ref[:, here]
            scaling = jnp.where(
                later, scale_ref[0:1, pl.ds(half_width + at, 128)], scale_ref[0:1, here]
            )
            grad_value = grad_qunit = grad_kunit = None
            for mask in (low_head, ~low_head):
                probs = head_probs(only(mask, query_unit), key_unit, seq_len)
                grad_head = only(mask, gm_ref[:, here])
                value_part = weight_grad(probs.astype(BF), grad_head)
                grad_probs = back_matmul(grad_head, value_low)
                grad_scores = (
                    probs * (grad_probs - jnp.sum(grad_probs * probs, axis=-1, keepdims=True))
                ).astype(BF)
                query_part = matmul(grad_scores, key_unit)
                key_part = weight_grad(grad_scores, query_unit)
                if grad_value is None:
                    grad_value, grad_qunit, grad_kunit = value_part, query_part, key_part
                else:
                    grad_value = grad_value + value_part
                    grad_qunit = jnp.where(low_head, grad_qunit, query_part)
                    grad_kunit = jnp.where(low_head, grad_kunit, key_part)
            scoring_grad = None
            for place, grad in ((0, grad_qunit), (1, grad_kunit)):
                raw = qkv_ref[:, pl.ds(place * half_width + at, 128)]
                grad = grad * math.sqrt(DK)
                inverse = head_inverse(raw, low_head)
                unit = raw * inverse
                term = jnp.sum(grad * unit, axis=0, keepdims=True)
                scoring_grad = term if scoring_grad is None else scoring_grad + term
                grad = grad * scaling
                low_sum, high_sum = head_sums(grad * unit, low_head)
                grads_ref[place, :, here] = (
                    inverse * (grad - unit * jnp.where(low_head, low_sum, high_sum))
                ).astype(BF)
            grads_ref[2, :, here] = grad_value.astype(BF)
            scoring_ref[:, here] = scoring_grad
            return carry

        lax.fori_loop(0, pairs, pair, 0)
        for copy in copies:
            copy.wait()
        for piece in range(2):
            total = None
            for j in range(3):
                term = back_matmul(
                    grads_ref[j], shards.rows(w_ref, piece, 2, j * half_width, half_width)
                )
                total = term if total is None else total + term
            columns = pl.ds(piece * half_width, half_width)
            own_ref[:, columns] = total[:own]
            other_ref[:, columns] = total[own:].astype(BF)

    return call(
        "attention_backward",
        body,
        [
            like(3, rows, half_width),
            like(1, half_width, dtype=F32),
            like(own, width, dtype=F32),
            like(own, width),
        ],
        scalars=[shards.places, half],
        arrays=[grad_mixed, qkv, query_unit, key_unit, value_low, scales],
        remote=shards.arrays,
        limit=56,
        scratch=shards.scratch(3 * half_width),
        earlier=earlier,
    )


def down_grads(which, hidden, hidden_other, down, down_other, earlier):
    units = hidden_other.shape[1]
    width = down.shape[1]
    block = units // 2

    def body(which_ref, hidden_ref, hidden_other_ref, down_ref, down_other_ref, _, out_ref):
        def piece(i, carry):
            kept = i // 2
            side = jnp.where(kept == 1, which_ref[1], 1 - which_ref[1])
            columns = pl.ds(pl.multiple_of(side * block, 128), block)
            here = pl.ds(pl.multiple_of(i % 2 * 640, 128), 640)
            total = weight_grad(hidden_ref[which_ref[0], :, columns], down_ref[:, here])
            total = total + weight_grad(hidden_other_ref[:, columns], down_other_ref[:, here])
            out_ref[:, pl.ds(pl.multiple_of(i * 640, 128), 640)] = total.astype(BF)
            return carry

        lax.fori_loop(0, 2 * width // 640, piece, 0)

    return call(
        "down_grads",
        body,
        [like(block, 2 * width)],
        scalars=[which],
        arrays=[hidden, hidden_other, down, down_other],
        earlier=earlier,
    )[0]


def side_grads(name, lefts, rights, kept, earlier):
    block = lefts[0][0].shape[1] // 2
    number = len(lefts)
    total_width = sum(right[0].shape[-1] * len(right[2] or (0,)) for right in rights)

    def body(*refs):
        refs = [ref for ref in refs if not isinstance(ref, tuple)]
        out_ref = refs[-1]
        begin = 0
        for i in range(number):
            own_ref, other_ref, right_ref, right_other_ref = refs[4 * i : 4 * i + 4]
            columns = pl.ds(block if kept else 0, block)
            own = own_ref[:, columns]
            other = other_ref[:, columns]
            for index in rights[i][2] or (None,):
                def piece(j, carry, own=own, other=other, right=right_ref, right_other=right_other_ref, index=index, begin=begin):
                    at = pl.multiple_of(j * 640, 128)
                    here = (slice(None), pl.ds(at, 640))
                    if index is not None:
                        here = (index, *here)
                    total = weight_grad(own, right[here]) + weight_grad(other, right_other[here])
                    out_ref[:, pl.ds(begin + at, 640)] = total.astype(out_ref.dtype)
                    return carry

                count = right_ref.shape[-1] // 640
                lax.fori_loop(0, count, piece, 0)
                begin += 640 * count

    arrays = []
    for left, right in zip(lefts, rights):
        arrays += [*left, *right[:2]]
    return call(
        name,
        body,
        [like(block, total_width)],
        limit=20,
        arrays=arrays,
        earlier=earlier,
    )[0]


def lay_first(half, query_weight, key_weight, value_weight, out_weight, scales):
    shard, width = query_weight.shape
    half_width = width // 2

    def body(half_ref, q_ref, k_ref, v_ref, out_ref, *refs):
        target, square = refs[-2:]
        for i, ref in enumerate((q_ref, k_ref, v_ref)):
            place = pl.ds(i * half_width, half_width)

            @pl.when(half_ref[0] == 0)
            def _():
                target[:, place] = ref[:, pl.ds(0, half_width)]

            @pl.when(half_ref[0] != 0)
            def _():
                target[:, place] = ref[:, pl.ds(half_width, half_width)]

        square[...] = jnp.zeros_like(square)
        row = 0
        for ref in refs[: len(scales)]:
            values = ref[...].astype(F32).reshape(1, -1)
            for begin in range(0, values.shape[1], shard):
                square[pl.ds(row, 1), pl.ds(0, shard)] = values[:, begin : begin + shard]
                row += 1
        target[:, pl.ds(3 * half_width, 128)] = jnp.transpose(square[...])[:shard].astype(BF)
        target[:, pl.ds(3 * half_width + 128, width)] = out_ref[...]

    return call(
        "lay_first",
        body,
        [like(shard, 3 * half_width + 128 + width)],
        limit=56,
        scalars=[half],
        arrays=[query_weight, key_weight, value_weight, out_weight]
        + list(scales),
        scratch=[pltpu.VMEM((128, 128), F32)],
    )[0]


def lay_second(half, up_weight, gate_weight, down_weight, planes):
    shard = up_weight.shape[0]
    part = down_weight.shape[0] // 2
    width = down_weight.shape[1]

    def body(half_ref, up_ref, gate_ref, down_ref, _, target):
        upper = half_ref[0] != 0
        for i, ref in enumerate((up_ref, gate_ref)):
            for core in range(2):
                rows = slice((2 * i + core) * shard, (2 * i + core + 1) * shard)
                for side in range(2):
                    for plane in range(planes):
                        begin = ((plane * 2 + side) * 2 + core) * 2 * part
                        place = (side * planes + plane) * part
                        target[rows, place : place + part] = jnp.where(
                            upper,
                            ref[:, begin + part : begin + 2 * part].astype(F32),
                            ref[:, begin : begin + part].astype(F32),
                        ).astype(BF)

        @pl.when(jnp.logical_not(upper))
        def _():
            target[pl.ds(4 * shard, part), :] = down_ref[pl.ds(0, part), :]

        @pl.when(upper)
        def _():
            target[pl.ds(4 * shard, part), :] = down_ref[pl.ds(part, part), :]

    return call(
        "lay_second",
        body,
        [like(4 * shard + part, width)],
        limit=56,
        scalars=[half],
        arrays=[up_weight, gate_weight, down_weight],
    )[0]


def split_hidden(half, totals, planes, part):
    shard, width = totals[0].shape
    run = planes // 2 * part

    def body(half_ref, *refs):
        for source, target in zip(refs[: len(totals)], refs[-len(totals) :]):
            for i in range(4):
                begin = 2 * i * run
                first, later = source[:, begin : begin + run], source[:, begin + run : begin + 2 * run]
                target[:, i * run : (i + 1) * run] = jnp.where(
                    half_ref[0] == 0, later.astype(F32), first.astype(F32)
                ).astype(BF)

    return call(
        "split_hidden",
        body,
        [like(shard, width // 2)] * len(totals),
        scalars=[half],
        arrays=totals,
    )


def merge_hidden(half, totals, others, planes, part, earlier):
    shard, width = totals[0].shape
    run = planes // 2 * part

    def body(half_ref, *refs):
        number = len(totals)
        upper = half_ref[0] != 0
        for own_ref, other_ref, target in zip(refs[:number], refs[number : 2 * number], refs[-number:]):
            for plane in range(planes // 2):
                for side in range(2):
                    for core in range(2):
                        i = core * 2 + side
                        begin = 2 * i * run + plane * part
                        own = jnp.where(
                            upper,
                            own_ref[:, begin + run : begin + run + part].astype(F32),
                            own_ref[:, begin : begin + part].astype(F32),
                        )
                        begin = i * run + plane * part
                        other = other_ref[:, begin : begin + part].astype(F32)
                        begin = ((plane * 2 + side) * 2 + core) * 2 * part
                        target[:, begin : begin + part] = jnp.where(upper, other, own)
                        target[:, begin + part : begin + 2 * part] = jnp.where(upper, own, other)

    return call(
        "merge_hidden",
        body,
        [like(shard, width, dtype=F32)] * len(totals),
        scalars=[half],
        arrays=[*totals, *others],
        earlier=earlier,
    )


class HiddenWeights:
    def __init__(self, gathered, planes, shard, part):
        width = gathered.shape[2]
        units = 2 * planes * part
        self.direct = shard % 16 == 0 and part % 16 == 0
        self.width, self.units, self.shard, self.part = width, units, shard, part
        if self.direct:
            self.arrays = [gathered.reshape(planes, 2, 2, -1, width)]
            self.matrix = (planes, 2, 2, shard, units)
            self.down = (planes, part, width)
        else:
            blocks = gathered[:, 4 * shard :].reshape(planes, 2, 2, part, width)
            self.arrays = [
                jnp.stack(
                    [gathered[:, i * shard : (i + 1) * shard].reshape(width, width) for i in range(4)]
                ),
                jnp.transpose(blocks, (2, 1, 0, 3, 4)).reshape(2, 2, planes * part, width),
            ]
            self.matrix = (width, units)
            self.down = (planes * part, width)

    def scratch(self):
        return [
            pltpu.VMEM((4,) + self.matrix, BF),
            pltpu.VMEM((2, 2) + self.down, BF),
            pltpu.SemaphoreType.DMA((8,)),
        ]

    def specs(self):
        return [pl.BlockSpec(memory_space=pltpu.HBM)] * len(self.arrays)

    def matrix_copy(self, sources, wide, sems, i):
        if self.direct:
            source = sources[0].at[:, :, :, pl.ds(i * self.shard, self.shard), :]
        else:
            source = sources[0].at[i]
        return pltpu.make_async_copy(source, wide.at[i], sems.at[i])

    def down_copy(self, sources, tall, sems, core, side):
        if self.direct:
            source = sources[0].at[:, side, core, pl.ds(4 * self.shard, self.part), :]
        else:
            source = sources[1].at[core, side]
        return pltpu.make_async_copy(source, tall.at[core, side], sems.at[4 + core * 2 + side])

    def matrix_value(self, wide, i, columns):
        if self.direct:
            return wide[i, :, :, :, :, columns].reshape(self.width, -1)
        return wide[i, :, columns]

    def matrix_rows(self, wide, i, j, parts):
        if self.direct:
            step = self.matrix[0] // parts
            return wide[i, pl.ds(j * step, step)].reshape(self.width // parts, -1)
        step = self.width // parts
        return wide[i, pl.ds(j * step, step)]

    def down_value(self, tall, core, side, columns):
        if self.direct:
            return tall[core, side, :, :, columns].reshape(-1, columns.size)
        return tall[core, side, :, columns]

    def down_rows(self, tall, core, side):
        return tall[core, side].reshape(-1, self.width)


def hidden_forward(first_low, weights, up_scale, gate_scale, own_rows):
    rows, width = first_low.shape
    units = weights.units
    block = units // 2
    step = 256

    def body(first_ref, up_scale_ref, gate_scale_ref, *refs):
        sources = refs[: len(weights.arrays)]
        hidden_out, up_out, gate_out, partial_ref, turned_ref, *rest = refs[len(weights.arrays) :]
        wide, tall, sems, hidden_ref, up_ref, gate_ref, out_sems = rest
        copies = [weights.matrix_copy(sources, wide, sems, i) for i in (0, 2, 1, 3)]
        down_copies = [
            weights.down_copy(sources, tall, sems, i, j) for i in range(2) for j in range(2)
        ]
        for copy in copies + down_copies:
            copy.start()
        first = first_ref[...]
        out_copies = []
        for core in range(2):
            copies[2 * core].wait()
            copies[2 * core + 1].wait()

            for begin in range(0, units, step):
                columns = pl.ds(begin, step)
                here = pl.ds(core * units + begin, step)
                up = matmul(first, weights.matrix_value(wide, core, columns))
                gate = matmul(first, weights.matrix_value(wide, 2 + core, columns))
                up_ref[:, here] = up.astype(BF)
                gate_ref[:, here] = gate.astype(BF)
                hidden = swiglu(up, gate, up_scale_ref[:, here], gate_scale_ref[:, here])
                hidden_ref[core, :, columns] = hidden.astype(BF)

            half = pl.ds(core * units, units)
            out_copies += [
                pltpu.make_async_copy(hidden_ref.at[core], hidden_out.at[core], out_sems.at[3 * core]),
                pltpu.make_async_copy(up_ref.at[:, half], up_out.at[:, half], out_sems.at[3 * core + 1]),
                pltpu.make_async_copy(gate_ref.at[:, half], gate_out.at[:, half], out_sems.at[3 * core + 2]),
            ]
            for copy in out_copies[-3:]:
                copy.start()
        for copy in down_copies:
            copy.wait()

        for begin in range(0, width, step):
            columns = pl.ds(begin, step)
            total = None
            for core in range(2):
                for side in range(2):
                    term = matmul(
                        hidden_ref[core, :, pl.ds(side * block, block)],
                        weights.down_value(tall, core, side, columns),
                    )
                    total = term if total is None else total + term
            partial_ref[:, columns] = total
            turned_ref[pl.ds(0, own_rows), columns] = total[own_rows:].astype(BF)
            turned_ref[pl.ds(own_rows, own_rows), columns] = total[:own_rows].astype(BF)

        for copy in out_copies:
            copy.wait()

    whole = pl.BlockSpec(memory_space=pltpu.VMEM)
    return pl.pallas_call(
        body,
        out_shape=[
            jax.ShapeDtypeStruct((2, rows, units), BF),
            jax.ShapeDtypeStruct((rows, 2 * units), BF),
            jax.ShapeDtypeStruct((rows, 2 * units), BF),
            jax.ShapeDtypeStruct((rows, width), F32),
            jax.ShapeDtypeStruct((rows, width), BF),
        ],
        in_specs=[whole] * 3 + weights.specs(),
        out_specs=[pl.BlockSpec(memory_space=pltpu.HBM)] * 3 + [whole] * 2,
        scratch_shapes=weights.scratch()
        + [
            pltpu.VMEM((2, rows, units), BF),
            pltpu.VMEM((rows, 2 * units), BF),
            pltpu.VMEM((rows, 2 * units), BF),
            pltpu.SemaphoreType.DMA((6,)),
        ],
        compiler_params=pltpu.CompilerParams(vmem_limit_bytes=56 * 2**20),
        cost_estimate=COST,
        name="hidden_forward",
    )(first_low, up_scale.reshape(1, -1), gate_scale.reshape(1, -1), *weights.arrays)


def hidden_backward(down_low, up_proj, gate_proj, weights, up_scale, gate_scale, earlier):
    rows = down_low.shape[0]
    units = weights.units
    block = units // 2

    def body(down_ref, up_ref, gate_ref, up_scale_ref, gate_scale_ref, sources, low_out, gate_low_out, up_grad_ref, gate_grad_ref, tall, sems, low_ref, gate_low_ref, out_sems):
        copies = [weights.down_copy(sources, tall, sems, i, j) for i in range(2) for j in range(2)]
        for copy in copies:
            copy.start()
        down = down_ref[...]
        out_copies = []
        for core in range(2):
            for side in range(2):
                copies[core * 2 + side].wait()
                here = pl.ds((core * 2 + side) * block, block)
                grad_hidden = back_matmul(down, weights.down_rows(tall, core, side))
                up_scaling = up_scale_ref[:, here]
                gate_scaling = gate_scale_ref[:, here]
                up = up_ref[:, here].astype(F32)
                gate = gate_ref[:, here].astype(F32)
                scaled = gate_scaling * gate
                sigmoid = jax.nn.sigmoid(scaled)
                silu = scaled * sigmoid
                grad_scaled_up = grad_hidden * silu
                grad_scaled = grad_hidden * (up_scaling * up) * (sigmoid + silu * (1.0 - sigmoid))
                low_ref[:, here] = (grad_scaled_up * up_scaling).astype(BF)
                gate_low_ref[:, here] = (grad_scaled * gate_scaling).astype(BF)
                up_grad_ref[:, here] = jnp.sum(grad_scaled_up * up, axis=0, keepdims=True)
                gate_grad_ref[:, here] = jnp.sum(grad_scaled * gate, axis=0, keepdims=True)
                i = 2 * (core * 2 + side)
                out_copies += [
                    pltpu.make_async_copy(low_ref.at[:, here], low_out.at[:, here], out_sems.at[i]),
                    pltpu.make_async_copy(gate_low_ref.at[:, here], gate_low_out.at[:, here], out_sems.at[i + 1]),
                ]
                for copy in out_copies[-2:]:
                    copy.start()
        for copy in out_copies:
            copy.wait()

    return call(
        "hidden_backward",
        body,
        [like(rows, 2 * units)] * 2 + [like(1, 2 * units, dtype=F32)] * 2,
        limit=56,
        arrays=[down_low, up_proj, gate_proj, up_scale, gate_scale],
        remote=weights.arrays,
        scratch=weights.scratch()[1:]
        + [pltpu.VMEM((rows, 2 * units), BF)] * 2
        + [pltpu.SemaphoreType.DMA((8,))],
        written=2,
        earlier=earlier,
    )


def first_partial(up_low, gate_low, weights, own_rows, earlier):
    rows = up_low.shape[0]
    units = weights.units
    width = weights.width

    def body(up_ref, gate_ref, sources, partial_ref, turned_ref, wide, sems):
        copies = [weights.matrix_copy(sources, wide, sems, i) for i in range(4)]
        for copy in copies:
            copy.start()
        pieces = 2
        piece = width // pieces
        for i in range(4):
            copies[i].wait()
            left = (up_ref, gate_ref)[i // 2][:, pl.ds((i % 2) * units, units)]
            for j in range(pieces):
                columns = pl.ds(j * piece, piece)
                term = back_matmul(left, weights.matrix_rows(wide, i, j, pieces))
                if i:
                    term = partial_ref[:, columns] + term
                partial_ref[:, columns] = term
        for j in range(pieces):
            columns = pl.ds(j * piece, piece)
            turn(turned_ref, own_rows, columns, partial_ref[:, columns])

    return call(
        "first_partial",
        body,
        [like(rows, width, dtype=F32), like(rows, width)],
        limit=56,
        arrays=[up_low, gate_low],
        remote=weights.arrays,
        scratch=[weights.scratch()[0], weights.scratch()[2]],
        earlier=earlier,
    )


def per_device(
    tokens,
    cotangent,
    lengths,
    placement,
    query_weight,
    key_weight,
    value_weight,
    out_weight,
    up_weight,
    gate_weight,
    down_weight,
    scoring,
    upscale,
    gatescale,
    attention_rate,
    feedforward_rate,
):
    size = lax.axis_size("fsdp")
    planes = size // 4
    half = lax.axis_index("grp")
    me = lax.axis_index("fsdp")
    core = me % 2
    side = (me // 2) % 2
    plane = me // 4
    half_scalar = half.reshape(1).astype(jnp.int32)
    which = jnp.stack([core, side]).astype(jnp.int32)
    local_seqs = tokens.shape[0] // size
    seq_len = tokens.shape[1] * size
    width = tokens.shape[2]
    own_rows = local_seqs * seq_len
    shard = query_weight.shape[0]
    hidden_shard = down_weight.shape[0]
    part = hidden_shard // 2
    per_row = hidden_shard // shard
    half_width = width // 2

    def swap_core(array):
        return lax.ppermute(array, "fsdp", [(i, i ^ 1) for i in range(size)])

    def swap_side(array):
        return lax.ppermute(array, "fsdp", [(i, i ^ 2) for i in range(size)])

    def next_plane(array):
        return lax.ppermute(array, "fsdp", [(i, (i + 4) % size) for i in range(size)])

    def swap_half(array):
        return lax.ppermute(array, "grp", [(0, 1), (1, 0)])

    def pick(array, index, axis):
        return lax.dynamic_index_in_dim(array, index, axis, keepdims=False)

    first_group = lay_first(
        half_scalar,
        query_weight,
        key_weight,
        value_weight,
        out_weight,
        [scoring, attention_rate, feedforward_rate, upscale, gatescale],
    )
    second_group = lay_second(half_scalar, up_weight, gate_weight, down_weight, planes)
    hidden_width = planes * 4 * part
    core_width = hidden_width // 2
    held = [first_group]
    crossed = []
    for i in range(planes):
        here = after(held[-1], *crossed[-1:]) if crossed else held[-1]
        if i < planes - 1:
            held.append(next_plane(here))
        crossed.append(swap_side(here))
    second_whole = lax.all_gather(
        after(second_group, *held[: GATE + 1], *crossed[:GATE]), "fsdp", axis=0
    )
    (both,) = call(
        "rows",
        place_pair,
        [like(2, *tokens.shape)],
        arrays=[tokens, cotangent],
        earlier=[held[-1], crossed[-2]],
        limit=56,
    )
    arrived = lax.all_to_all(both, "fsdp", split_axis=1, concat_axis=2, tiled=True)
    own_tokens = arrived[0].reshape(own_rows, width)
    other_tokens = swap_half(own_tokens)
    held = held + crossed
    held = held + [swap_core(array) for array in held]
    places = []
    for i in range(4 * planes):
        there_core = 1 - core if i >= 2 * planes else core
        there_side = 1 - side if i // planes % 2 else side
        places.append(((plane - i) % planes * 2 + there_side) * 2 + there_core)
    shards = Shards(held, jnp.stack(places).astype(jnp.int32))

    group_order = placement[0]
    own_slots = lax.dynamic_slice_in_dim(group_order, me * local_seqs, local_seqs)
    own_lengths = jnp.take(lengths[0], own_slots)
    valid = (jnp.arange(seq_len, dtype=jnp.int32)[None, :] < own_lengths[:, None]).reshape(
        own_rows, 1
    )
    own_cot = jnp.where(valid, arrived[1].reshape(own_rows, width), jnp.zeros((), BF))
    token_rows = jnp.concatenate([own_tokens, other_tokens])
    other_cot = swap_half(own_cot)

    qkv, query_unit, key_unit, value_low, mixed_half, mixed_turned, scale_float = attention_forward(
        half_scalar, token_rows, shards, seq_len
    )
    attention_mix = scale_float[1:2]
    feed_mix = scale_float[2:3]

    up_scale, gate_scale = hidden_scales(half_scalar, scale_float, per_row, planes, shard)
    skip = 3 * half_width + 128
    mixed_low, attended, first_state, first_low = first_forward(
        half_scalar, mixed_half, swap_half(mixed_turned), token_rows, attention_mix, shards, skip
    )

    feature = jnp.arange(width, dtype=jnp.int32)
    block = []
    for b in range(2):
        for a in range(2):
            for k in range(planes):
                there_core = core if b == 0 else 1 - core
                there_side = 1 - side if a == 0 else side
                block.append((k * 2 + there_side) * 2 + there_core)
    block = jnp.stack(block).astype(jnp.int32)
    wanted = (block[:, None] * shard + jnp.arange(shard, dtype=jnp.int32)[None, :]).reshape(-1)
    chooser = (feature[:, None] == wanted[None, :]).astype(BF)

    def share_columns(array):
        chosen = matmul(array, chooser).astype(BF)
        return chosen[:, :half_width], swap_core(chosen[:, half_width:])

    def share(array):
        return array, swap_core(array)

    def over_planes(total):
        return lax.psum_scatter(
            total.reshape(planes, total.shape[0] // planes, total.shape[1]),
            "fsdp",
            scatter_dimension=0,
            axis_index_groups=[[k * 4 + j for k in range(planes)] for j in range(4)],
        )

    def joined(kept, arrived_part):
        return (kept.astype(F32) + arrived_part.astype(F32)).astype(BF)

    token_sides = share_columns(token_rows)
    mixed_sides = share_columns(mixed_low)
    first_sides = share_columns(first_low)
    hidden_weights = HiddenWeights(
        after(second_whole, *token_sides, *mixed_sides, *first_sides, other_cot), planes, shard, part
    )
    hidden_low, up_proj, gate_proj, partial, partial_turned = hidden_forward(
        first_low, hidden_weights, up_scale, gate_scale, own_rows
    )
    hidden_other = swap_core(pick(hidden_low, 1 - core, 0))

    layer_own, grad_first, down_low, feed_grad = second_backward(
        partial,
        swap_half(partial_turned),
        first_state,
        own_cot,
        other_cot,
        valid.astype(F32),
        feed_mix,
    )
    down_other = swap_core(down_low)
    down_args = (which, hidden_low, hidden_other, down_low, down_other)
    down_both = down_grads(*down_args, [])
    down_sum = over_planes(down_both)
    up_low, gate_low, upscale_grad, gatescale_grad = hidden_backward(
        down_low, up_proj, gate_proj, hidden_weights, up_scale, gate_scale, [down_both]
    )
    up_other = swap_core(up_low)
    gate_other = swap_core(gate_low)
    up_side = [(up_low, up_other, None)]
    gate_side = [(gate_low, gate_other, None)]
    up_sent = side_grads("up_sent", [first_sides], up_side, False, [])
    up_arrived = swap_side(up_sent)
    partial, partial_turned = first_partial(up_low, gate_low, hidden_weights, own_rows, [up_sent])
    partial_other = swap_half(partial_turned)
    gate_sent = side_grads("gate_sent", [first_sides], gate_side, False, [partial])
    up_kept = side_grads("up_kept", [first_sides], up_side, True, [gate_sent])
    attended_cols, grad_mixed, grad_tokens, attention_grad = first_backward(
        half_scalar,
        grad_first,
        partial,
        partial_other,
        token_rows,
        attended,
        attention_mix,
        shards,
        skip,
        [up_kept],
    )
    gate_arrived = swap_side(after(gate_sent, up_arrived))
    attended_other = swap_core(after(attended_cols, up_arrived))
    up_joined = joined(up_kept, after(up_arrived, grad_mixed))
    up_total = over_planes(up_joined)
    qkv_low, scoring_grad, token_own, token_sent = attention_backward(
        half_scalar, grad_mixed, qkv, query_unit, key_unit, value_low, scale_float, shards, seq_len, [up_joined]
    )
    qkv_other = swap_core(qkv_low)
    token_other = swap_half(token_sent)
    last_args = (
        [mixed_sides, token_sides],
        [(attended_cols, attended_other, None), (qkv_low, qkv_other, (0, 1, 2))],
    )
    last_sent = side_grads("last_sent", *last_args, False, [down_sum])
    gate_kept = side_grads("gate_kept", [first_sides], gate_side, True, [last_sent])
    last_kept = side_grads("last_kept", *last_args, True, [gate_kept])
    last_arrived = swap_side(after(last_sent, gate_arrived))
    gate_joined = joined(gate_kept, after(gate_arrived, last_kept, token_other))
    gate_total = over_planes(gate_joined)
    def hidden_spread(grad):
        blocks = jnp.transpose(grad.reshape(2, 2, planes, part), (2, 1, 0, 3))
        blank = jnp.zeros_like(blocks)
        both_halves = jnp.where(
            half == 0, jnp.stack([blocks, blank], axis=3), jnp.stack([blank, blocks], axis=3)
        )
        return both_halves.reshape(size, hidden_shard)

    blank = jnp.zeros_like(scoring_grad)
    scoring_spread = jnp.where(
        half == 0,
        jnp.concatenate([scoring_grad, blank], axis=1),
        jnp.concatenate([blank, scoring_grad], axis=1),
    )
    small = jnp.concatenate(
        [
            scoring_spread.reshape(size, shard),
            attention_grad.reshape(size, shard),
            feed_grad.reshape(size, shard),
            hidden_spread(upscale_grad),
            hidden_spread(gatescale_grad),
        ],
        axis=1,
    )
    (up_part,) = split_hidden(half_scalar, [up_total], planes, part)
    up_swapped = swap_half(up_part)
    (outgoing,) = call(
        "outgoing",
        place_outgoing,
        [like(2, own_rows, width)],
        arrays=[layer_own, grad_tokens, token_own, token_other],
        earlier=[last_kept],
    )
    returned = lax.all_to_all(
        outgoing.reshape(2, local_seqs, seq_len, width), "fsdp", split_axis=2, concat_axis=1, tiled=True
    )
    (up_out,) = merge_hidden(half_scalar, [up_total], [up_swapped], planes, part, [returned])
    last_joined = joined(last_kept, after(last_arrived, up_out))
    last_total = over_planes(last_joined).astype(F32)
    down_total = down_sum[:, width:].astype(F32) + swap_side(
        after(down_sum[:, :width], last_joined)
    ).astype(F32)
    down_cols = down_total.reshape(part, 2, half_width)
    mine = pick(down_cols, half, 1)
    theirs = swap_half(pick(down_cols, 1 - half, 1).astype(BF)).astype(F32)
    down_out = jnp.where(
        half == 0, jnp.concatenate([mine, theirs]), jnp.concatenate([theirs, mine])
    )
    (small,) = call(
        "pass", place_whole, [like(*small.shape, dtype=F32)], arrays=[small], earlier=[last_joined]
    )
    small = lax.all_to_all(small, "fsdp", split_axis=0, concat_axis=0, tiled=True)
    (total,) = call("add", sum_whole, [like(1, small.shape[1], dtype=F32)], arrays=[small])
    total = total[0]
    total = total + swap_half(total)

    (gate_part,) = split_hidden(half_scalar, [gate_total], planes, part)
    (gate_out,) = merge_hidden(half_scalar, [gate_total], [swap_half(gate_part)], planes, part, [])
    out_total = last_total[:, :half_width]
    qkv_total = last_total[:, half_width:]

    return (
        returned[0],
        returned[1],
        qkv_total[:, :half_width],
        qkv_total[:, half_width : 2 * half_width],
        qkv_total[:, 2 * half_width :],
        out_total,
        up_out,
        gate_out,
        down_out,
        total[:shard],
        total[3 * shard : 3 * shard + hidden_shard],
        total[3 * shard + hidden_shard :],
        total[shard : 2 * shard],
        total[2 * shard : 3 * shard],
    )


def solution(mesh):
    rows = P("grp", "fsdp", None)
    group = P("grp", None)
    matrix = P("fsdp", None)
    vector = P("fsdp")
    split = P("fsdp", "grp")
    return jax.shard_map(
        per_device,
        mesh=mesh,
        in_specs=(rows, rows, group, group) + (matrix,) * 7 + (vector,) * 5,
        out_specs=(rows, rows) + (split,) * 7 + (vector,) * 5,
        check_vma=False,
    )
```

```python
import math

import jax
import jax.numpy as jnp
from jax import lax
from jax.experimental import pallas as pl
from jax.experimental.pallas import tpu as pltpu
from jax.sharding import PartitionSpec as P

H = 20
DK = 64
BF = jnp.bfloat16
F32 = jnp.float32
GATE = 1
COST = pl.CostEstimate(flops=1000, bytes_accessed=1000, transcendentals=0)


def swiglu(up_proj, gate_proj, upscale, gatescale):
    scaled = gatescale * gate_proj
    return scaled * jax.nn.sigmoid(scaled) * (upscale * up_proj)


def matmul(left_side, right_side):
    return jnp.dot(left_side, right_side, preferred_element_type=F32)


def weight_grad(left_side, right_side):
    return lax.dot_general(
        left_side, right_side, (((0,), (0,)), ((), ())), preferred_element_type=F32
    )


def back_matmul(grad_rows, weight_rows):
    return lax.dot_general(
        grad_rows, weight_rows, (((1,), (1,)), ((), ())), preferred_element_type=F32
    )


def after(value, *earlier):
    return lax.optimization_barrier((value, *earlier))[0]


def like(*shape, dtype=BF):
    return jax.ShapeDtypeStruct(shape, dtype)


def call(name, body, outs, scalars=(), arrays=(), remote=(), scratch=(), earlier=(), limit=16, written=0):
    counts = (len(scalars), len(arrays), len(remote), len(earlier), len(outs))

    def kernel(*refs):
        groups = []
        at = 0
        for count in counts:
            groups.append(refs[at : at + count])
            at += count
        body(*groups[0], *groups[1], groups[2], *groups[4], *refs[at:])

    whole = pl.BlockSpec(memory_space=pltpu.VMEM)
    kept = pl.BlockSpec(memory_space=pl.ANY)
    placed = pl.BlockSpec(memory_space=pltpu.HBM)
    return pl.pallas_call(
        kernel,
        out_shape=list(outs),
        in_specs=[pl.BlockSpec(memory_space=pltpu.SMEM)] * counts[0]
        + [whole] * counts[1]
        + [placed] * counts[2]
        + [kept] * counts[3],
        out_specs=[placed] * written + [whole] * (counts[4] - written),
        scratch_shapes=list(scratch),
        compiler_params=pltpu.CompilerParams(vmem_limit_bytes=limit * 2**20),
        cost_estimate=COST,
        name=name,
    )(*scalars, *arrays, *remote, *earlier)


class Shards:
    def __init__(self, arrays, places):
        self.direct = arrays[0].shape[0] % 16 == 0
        if self.direct:
            self.arrays, self.places = list(arrays), places
        else:
            whole = jnp.zeros((len(arrays),) + arrays[0].shape, BF)
            for i, array in enumerate(arrays):
                whole = lax.dynamic_update_index_in_dim(whole, array, places[i], 0)
            self.arrays = [whole.reshape(-1, arrays[0].shape[1])]
            self.places = jnp.zeros((1,), jnp.int32)
        self.count = len(self.arrays)
        self.height = self.arrays[0].shape[0]

    def scratch(self, width):
        return [
            pltpu.VMEM((self.count, self.height, width), BF),
            pltpu.SemaphoreType.DMA((self.count,)),
        ]

    def copies(self, places, sources, target, sems, begin, width):
        return [
            pltpu.make_async_copy(
                sources[i].at[:, pl.ds(begin, width)], target.at[places[i]], sems.at[i]
            )
            for i in range(self.count)
        ]

    def columns(self, target, begin, width):
        return target[:, :, pl.ds(begin, width)].reshape(self.count * self.height, width)

    def rows(self, target, index, parts, begin, width):
        if self.direct:
            step = self.count // parts
            rows = target[pl.ds(index * step, step), :, pl.ds(begin, width)]
        else:
            step = self.height // parts
            rows = target[:, pl.ds(pl.multiple_of(index * step, step), step), pl.ds(begin, width)]
        return rows.reshape(-1, width)


def inverse_rms(vector):
    return lax.rsqrt(jnp.mean(vector * vector, axis=-1, keepdims=True) + 1e-06)


def head_sums(values, low_head):
    low_sum = jnp.sum(jnp.where(low_head, values, 0.0), axis=-1, keepdims=True)
    high_sum = jnp.sum(jnp.where(low_head, 0.0, values), axis=-1, keepdims=True)
    return low_sum, high_sum


def head_inverse(vector, low_head):
    low_sum, high_sum = head_sums(vector * vector, low_head)
    return jnp.where(low_head, lax.rsqrt(low_sum + 1e-06), lax.rsqrt(high_sum + 1e-06))


def head_probs(query_head, key_unit, seq_len):
    scores = back_matmul(query_head, key_unit) * math.sqrt(DK)
    query_row = lax.broadcasted_iota(jnp.int32, scores.shape, 0)
    key_row = lax.broadcasted_iota(jnp.int32, scores.shape, 1)
    start = query_row - lax.rem(query_row, seq_len)
    scores = jnp.where((key_row <= query_row) & (key_row >= start), scores, -1e30)
    exp_scores = jnp.exp(scores - jnp.max(scores, axis=-1, keepdims=True))
    return exp_scores / jnp.sum(exp_scores, axis=-1, keepdims=True)


def only(mask, values):
    return jnp.where(mask, values.astype(F32), 0.0).astype(BF)


def turn(ref, rows, columns, value):
    ref[pl.ds(0, rows), columns] = value[rows:].astype(BF)
    ref[pl.ds(rows, rows), columns] = value[:rows].astype(BF)


def attention_forward(half, token_rows, shards, seq_len):
    rows, width = token_rows.shape
    half_width = width // 2
    pairs = half_width // 128
    cols = 3 * half_width + 128

    def body(
        places, half_ref, x_ref, sources, qkv_ref, qu_ref, ku_ref, vl_ref, mixed_ref, turned_ref, scale_ref, w_ref, sems
    ):
        copies = shards.copies(places, sources, w_ref, sems, 0, cols)
        for copy in copies:
            copy.start()
        for copy in copies:
            copy.wait()
        scale_ref[...] = jnp.transpose(
            shards.columns(w_ref, 3 * half_width, 128).astype(F32)
        )[:16]
        x = x_ref[...]
        step = 384
        for begin in range(0, 3 * half_width, step):
            qkv_ref[:, pl.ds(begin, step)] = matmul(x, shards.columns(w_ref, begin, step))
        low_head = lax.broadcasted_iota(jnp.int32, (rows, 128), 1) < DK
        later = half_ref[0] == 1

        def pair(i, carry):
            at = pl.multiple_of(i * 128, 128)
            here = pl.ds(at, 128)
            queries = qkv_ref[:, here]
            key_rows = qkv_ref[:, pl.ds(half_width + at, 128)]
            value_low = qkv_ref[:, pl.ds(2 * half_width + at, 128)].astype(BF)
            scaling = jnp.where(
                later, scale_ref[0:1, pl.ds(half_width + at, 128)], scale_ref[0:1, here]
            )
            query_unit = queries * head_inverse(queries, low_head) * scaling
            key_unit = (key_rows * head_inverse(key_rows, low_head) * scaling).astype(BF)
            mixed = None
            for mask in (low_head, ~low_head):
                probs = head_probs(only(mask, query_unit), key_unit, seq_len)
                head = matmul(probs.astype(BF), value_low)
                mixed = head if mixed is None else jnp.where(low_head, mixed, head)
            qu_ref[:, here] = query_unit.astype(BF)
            ku_ref[:, here] = key_unit
            vl_ref[:, here] = value_low
            mixed_ref[:, here] = mixed.astype(BF)
            turn(turned_ref, rows // 2, here, mixed)
            return carry

        lax.fori_loop(0, pairs, pair, 0)

    return call(
        "attention_forward",
        body,
        [like(rows, 3 * half_width, dtype=F32)] + [like(rows, half_width)] * 5 + [like(16, width, dtype=F32)],
        scalars=[shards.places, half],
        arrays=[token_rows],
        remote=shards.arrays,
        limit=24,
        scratch=shards.scratch(cols),
    )


def place_whole(source, _, target):
    target[...] = source[...]


def place_pair(first, later, _, target):
    target[0] = first[...]
    target[1] = later[...]


def place_outgoing(layer, mix, own, other, _, target):
    target[0] = layer[...]
    target[1] = (mix[...] + own[...] + other[...].astype(F32)).astype(BF)


def sum_whole(source, _, target):
    target[...] = jnp.sum(source[...], axis=0, keepdims=True)


def hidden_scales(half, scales, per_row, planes, shard):
    pieces = per_row // 2

    def body(half_ref, scale_ref, _, *targets):
        later = half_ref[0] != 0
        for i, target in enumerate(targets):
            for piece in range(pieces):
                row = 3 + i * per_row + piece
                values = jnp.where(
                    later, scale_ref[row + pieces : row + pieces + 1, :], scale_ref[row : row + 1, :]
                )
                for core in range(2):
                    for side in range(2):
                        for plane in range(planes):
                            begin = ((plane * 2 + side) * 2 + core) * shard
                            place = (((core * 2 + side) * planes + plane) * pieces + piece) * shard
                            target[:, place : place + shard] = values[:, begin : begin + shard]

    width = 4 * planes * pieces * shard
    return call(
        "hidden_scales",
        body,
        [like(1, width, dtype=F32)] * 2,
        scalars=[half],
        arrays=[scales],
    )


def place_halves(half_ref, target, own, other):
    width = own.shape[1]

    @pl.when(half_ref[0] == 0)
    def _():
        target[:, pl.ds(0, width)] = own[...]
        target[:, pl.ds(width, width)] = other[...]

    @pl.when(half_ref[0] != 0)
    def _():
        target[:, pl.ds(0, width)] = other[...]
        target[:, pl.ds(width, width)] = own[...]


def first_forward(half, mixed, mixed_other, token_rows, attention_mix, shards, skip):
    rows, width = token_rows.shape

    def body(
        places, half_ref, own_ref, other_ref, x_ref, mix_ref, sources, mixed_ref, attended_ref, first_ref, low_ref, w_ref, sems
    ):
        copies = shards.copies(places, sources, w_ref, sems, skip, width)
        for copy in copies:
            copy.start()
        place_halves(half_ref, mixed_ref, own_ref, other_ref)
        for copy in copies:
            copy.wait()
        for begin in range(0, width, 256):
            attended_ref[:, pl.ds(begin, 256)] = matmul(
                mixed_ref[...], shards.columns(w_ref, begin, 256)
            )
        x = x_ref[...].astype(F32)
        attended = attended_ref[...]
        mix = x + mix_ref[...] * (attended * inverse_rms(attended) - x)
        first = mix * inverse_rms(mix)
        first_ref[...] = first
        low_ref[...] = first.astype(BF)

    return call(
        "first_forward",
        body,
        [like(rows, width)] + [like(rows, width, dtype=F32)] * 2 + [like(rows, width)],
        scalars=[shards.places, half],
        arrays=[mixed, mixed_other, token_rows, attention_mix],
        remote=shards.arrays,
        limit=20,
        scratch=shards.scratch(width),
    )


def mix_backward(base, branch, rate, grad):
    branch_inverse = inverse_rms(branch)
    branch_unit = branch * branch_inverse
    mix = base + rate * (branch_unit - base)
    inverse = inverse_rms(mix)
    value = mix * inverse
    grad_mix = inverse * (grad - value * jnp.mean(grad * value, axis=-1, keepdims=True))
    grad_unit = grad_mix * rate
    grad_branch = branch_inverse * (
        grad_unit - branch_unit * jnp.mean(grad_unit * branch_unit, axis=-1, keepdims=True)
    )
    return value, grad_mix - grad_unit, grad_branch, grad_mix * (branch_unit - base)


def second_backward(partial, partial_other, first_state, cot, cot_other, valid, feed_mix):
    rows, width = partial.shape
    own = rows // 2
    pieces = 4
    step = rows // pieces

    def body(partial_ref, other_ref, first_ref, cot_ref, cot_other_ref, valid_ref, mix_ref, layer_ref, grad_ref, low_ref, rate_ref):
        mine = pl.program_id(0) < pieces // 2
        down = partial_ref[...] + other_ref[...].astype(F32)
        grad = jnp.where(mine, cot_ref[...].astype(F32), cot_other_ref[...].astype(F32))
        value, grad_first, grad_down, grad_rate = mix_backward(first_ref[...], down, mix_ref[...], grad)
        grad_ref[...] = grad_first
        low_ref[...] = grad_down.astype(BF)

        @pl.when(pl.program_id(0) == 0)
        def _():
            rate_ref[...] = jnp.zeros_like(rate_ref)

        @pl.when(mine)
        def _():
            layer_ref[...] = (value * valid_ref[...]).astype(BF)
            rate_ref[...] += jnp.sum(grad_rate, axis=0, keepdims=True)

    every = pl.BlockSpec((step, width), lambda i: (i, 0))
    first_half = pl.BlockSpec((step, width), lambda i: (jnp.minimum(i, pieces // 2 - 1), 0))
    later_half = pl.BlockSpec((step, width), lambda i: (jnp.maximum(i - pieces // 2, 0), 0))
    vector = pl.BlockSpec((1, width), lambda i: (0, 0))
    return pl.pallas_call(
        body,
        grid=(pieces,),
        out_shape=[like(own, width), like(rows, width, dtype=F32), like(rows, width), like(1, width, dtype=F32)],
        in_specs=[
            every,
            every,
            every,
            first_half,
            later_half,
            pl.BlockSpec((step, 1), lambda i: (jnp.minimum(i, pieces // 2 - 1), 0)),
            vector,
        ],
        out_specs=[first_half, every, every, vector],
        compiler_params=pltpu.CompilerParams(vmem_limit_bytes=24 * 2**20),
        cost_estimate=COST,
        name="second_backward",
    )(partial, partial_other, first_state, cot, cot_other, valid, feed_mix)


def first_backward(half, grad_first, partial, partial_other, token_rows, attended, attention_mix, shards, skip, earlier):
    rows, width = partial.shape
    own = rows // 2
    half_width = width // 2

    def body(
        places, half_ref, grad_ref, partial_ref, other_ref, x_ref, attended_ref, mix_ref, sources, cols_ref, mixed_ref, token_ref, rate_ref, low_ref, w_ref, sems
    ):
        copies = shards.copies(places, sources, w_ref, sems, skip, width)
        for copy in copies:
            copy.start()
        for begin in (0, own):
            here = pl.ds(begin, own)
            grad = grad_ref[here, :] + partial_ref[here, :] + other_ref[here, :].astype(F32)
            _, grad_token, grad_attended, grad_rate = mix_backward(
                x_ref[here, :].astype(F32), attended_ref[here, :], mix_ref[...], grad
            )
            low_ref[here, :] = grad_attended.astype(BF)
            if begin == 0:
                token_ref[...] = grad_token
                rate_ref[...] = jnp.sum(grad_rate, axis=0, keepdims=True)
        at = pl.multiple_of(half_ref[0] * half_width, 128)
        cols_ref[...] = low_ref[:, pl.ds(at, half_width)]
        for copy in copies:
            copy.wait()
        mixed_ref[...] = back_matmul(
            low_ref[...], shards.rows(w_ref, half_ref[0], 2, 0, width)
        ).astype(BF)

    return call(
        "first_backward",
        body,
        [like(rows, half_width)] * 2 + [like(own, width, dtype=F32), like(1, width, dtype=F32)],
        scalars=[shards.places, half],
        arrays=[grad_first, partial, partial_other, token_rows, attended, attention_mix],
        remote=shards.arrays,
        limit=56,
        scratch=[pltpu.VMEM((rows, width), BF)] + shards.scratch(width),
        earlier=earlier,
    )


def attention_backward(half, grad_mixed, qkv, query_unit, key_unit, value_low, scales, shards, seq_len, earlier):
    rows, half_width = grad_mixed.shape
    width = 2 * half_width
    pairs = half_width // 128
    own = rows // 2

    def body(
        places, half_ref, gm_ref, qkv_ref, qu_ref, ku_ref, vl_ref, scale_ref, sources, grads_ref, scoring_ref, own_ref, other_ref, w_ref, sems
    ):
        copies = shards.copies(places, sources, w_ref, sems, 0, 3 * half_width)
        for copy in copies:
            copy.start()
        low_head = lax.broadcasted_iota(jnp.int32, (rows, 128), 1) < DK
        later = half_ref[0] == 1

        def pair(i, carry):
            at = pl.multiple_of(i * 128, 128)
            here = pl.ds(at, 128)
            query_unit = qu_ref[:, here]
            key_unit = ku_ref[:, here]
            value_low = vl_ref[:, here]
            scaling = jnp.where(
                later, scale_ref[0:1, pl.ds(half_width + at, 128)], scale_ref[0:1, here]
            )
            grad_value = grad_qunit = grad_kunit = None
            for mask in (low_head, ~low_head):
                probs = head_probs(only(mask, query_unit), key_unit, seq_len)
                grad_head = only(mask, gm_ref[:, here])
                value_part = weight_grad(probs.astype(BF), grad_head)
                grad_probs = back_matmul(grad_head, value_low)
                grad_scores = (
                    probs * (grad_probs - jnp.sum(grad_probs * probs, axis=-1, keepdims=True))
                ).astype(BF)
                query_part = matmul(grad_scores, key_unit)
                key_part = weight_grad(grad_scores, query_unit)
                if grad_value is None:
                    grad_value, grad_qunit, grad_kunit = value_part, query_part, key_part
                else:
                    grad_value = grad_value + value_part
                    grad_qunit = jnp.where(low_head, grad_qunit, query_part)
                    grad_kunit = jnp.where(low_head, grad_kunit, key_part)
            scoring_grad = None
            for place, grad in ((0, grad_qunit), (1, grad_kunit)):
                raw = qkv_ref[:, pl.ds(place * half_width + at, 128)]
                grad = grad * math.sqrt(DK)
                inverse = head_inverse(raw, low_head)
                unit = raw * inverse
                term = jnp.sum(grad * unit, axis=0, keepdims=True)
                scoring_grad = term if scoring_grad is None else scoring_grad + term
                grad = grad * scaling
                low_sum, high_sum = head_sums(grad * unit, low_head)
                grads_ref[place, :, here] = (
                    inverse * (grad - unit * jnp.where(low_head, low_sum, high_sum))
                ).astype(BF)
            grads_ref[2, :, here] = grad_value.astype(BF)
            scoring_ref[:, here] = scoring_grad
            return carry

        lax.fori_loop(0, pairs, pair, 0)
        for copy in copies:
            copy.wait()
        for piece in range(2):
            total = None
            for j in range(3):
                term = back_matmul(
                    grads_ref[j], shards.rows(w_ref, piece, 2, j * half_width, half_width)
                )
                total = term if total is None else total + term
            columns = pl.ds(piece * half_width, half_width)
            own_ref[:, columns] = total[:own]
            other_ref[:, columns] = total[own:].astype(BF)

    return call(
        "attention_backward",
        body,
        [
            like(3, rows, half_width),
            like(1, half_width, dtype=F32),
            like(own, width, dtype=F32),
            like(own, width),
        ],
        scalars=[shards.places, half],
        arrays=[grad_mixed, qkv, query_unit, key_unit, value_low, scales],
        remote=shards.arrays,
        limit=56,
        scratch=shards.scratch(3 * half_width),
        earlier=earlier,
    )


def down_grads(which, hidden, hidden_other, down, down_other, earlier):
    units = hidden_other.shape[1]
    width = down.shape[1]
    block = units // 2

    def body(which_ref, hidden_ref, hidden_other_ref, down_ref, down_other_ref, _, out_ref):
        def piece(kept, carry):
            side = jnp.where(kept == 1, which_ref[1], 1 - which_ref[1])
            columns = pl.ds(pl.multiple_of(side * block, 128), block)
            total = weight_grad(hidden_ref[which_ref[0], :, columns], down_ref[...])
            total = total + weight_grad(hidden_other_ref[:, columns], down_other_ref[...])
            out_ref[:, pl.ds(pl.multiple_of(kept * width, 128), width)] = total.astype(BF)
            return carry

        lax.fori_loop(0, 2, piece, 0)

    return call(
        "down_grads",
        body,
        [like(block, 2 * width)],
        scalars=[which],
        arrays=[hidden, hidden_other, down, down_other],
        earlier=earlier,
    )[0]


def side_grads(name, lefts, rights, kept, earlier):
    block = lefts[0][0].shape[1] // 2
    number = len(lefts)
    total_width = sum(right[0].shape[-1] * len(right[2] or (0,)) for right in rights)

    def body(*refs):
        refs = [ref for ref in refs if not isinstance(ref, tuple)]
        out_ref = refs[-1]
        begin = 0
        for i in range(number):
            own_ref, other_ref, right_ref, right_other_ref = refs[4 * i : 4 * i + 4]
            columns = pl.ds(block if kept else 0, block)
            own = own_ref[:, columns]
            other = other_ref[:, columns]
            for index in rights[i][2] or (None,):
                step = min(right_ref.shape[-1], 1280)

                def piece(j, carry, own=own, other=other, right=right_ref, right_other=right_other_ref, index=index, begin=begin, step=step):
                    at = pl.multiple_of(j * step, 128)
                    here = (slice(None), pl.ds(at, step))
                    if index is not None:
                        here = (index, *here)
                    total = weight_grad(own, right[here]) + weight_grad(other, right_other[here])
                    out_ref[:, pl.ds(begin + at, step)] = total.astype(out_ref.dtype)
                    return carry

                count = right_ref.shape[-1] // step
                lax.fori_loop(0, count, piece, 0)
                begin += step * count

    arrays = []
    for left, right in zip(lefts, rights):
        arrays += [*left, *right[:2]]
    return call(
        name,
        body,
        [like(block, total_width)],
        limit=20,
        arrays=arrays,
        earlier=earlier,
    )[0]


def lay_first(half, query_weight, key_weight, value_weight, out_weight, scales):
    shard, width = query_weight.shape
    half_width = width // 2

    def body(half_ref, q_ref, k_ref, v_ref, out_ref, *refs):
        target, square = refs[-2:]
        for i, ref in enumerate((q_ref, k_ref, v_ref)):
            place = pl.ds(i * half_width, half_width)

            @pl.when(half_ref[0] == 0)
            def _():
                target[:, place] = ref[:, pl.ds(0, half_width)]

            @pl.when(half_ref[0] != 0)
            def _():
                target[:, place] = ref[:, pl.ds(half_width, half_width)]

        square[...] = jnp.zeros_like(square)
        row = 0
        for ref in refs[: len(scales)]:
            values = ref[...].astype(F32).reshape(1, -1)
            for begin in range(0, values.shape[1], shard):
                square[pl.ds(row, 1), pl.ds(0, shard)] = values[:, begin : begin + shard]
                row += 1
        target[:, pl.ds(3 * half_width, 128)] = jnp.transpose(square[...])[:shard].astype(BF)
        target[:, pl.ds(3 * half_width + 128, width)] = out_ref[...]

    return call(
        "lay_first",
        body,
        [like(shard, 3 * half_width + 128 + width)],
        limit=56,
        scalars=[half],
        arrays=[query_weight, key_weight, value_weight, out_weight]
        + list(scales),
        scratch=[pltpu.VMEM((128, 128), F32)],
    )[0]


def lay_second(half, up_weight, gate_weight, down_weight, planes):
    shard = up_weight.shape[0]
    part = down_weight.shape[0] // 2
    width = down_weight.shape[1]

    def body(half_ref, up_ref, gate_ref, down_ref, _, target):
        upper = half_ref[0] != 0
        for i, ref in enumerate((up_ref, gate_ref)):
            for core in range(2):
                rows = slice((2 * i + core) * shard, (2 * i + core + 1) * shard)
                for side in range(2):
                    for plane in range(planes):
                        begin = ((plane * 2 + side) * 2 + core) * 2 * part
                        place = (side * planes + plane) * part
                        target[rows, place : place + part] = jnp.where(
                            upper,
                            ref[:, begin + part : begin + 2 * part].astype(F32),
                            ref[:, begin : begin + part].astype(F32),
                        ).astype(BF)

        @pl.when(jnp.logical_not(upper))
        def _():
            target[pl.ds(4 * shard, part), :] = down_ref[pl.ds(0, part), :]

        @pl.when(upper)
        def _():
            target[pl.ds(4 * shard, part), :] = down_ref[pl.ds(part, part), :]

    return call(
        "lay_second",
        body,
        [like(4 * shard + part, width)],
        limit=56,
        scalars=[half],
        arrays=[up_weight, gate_weight, down_weight],
    )[0]


def split_hidden(half, totals, planes, part):
    shard, width = totals[0].shape
    run = planes // 2 * part

    def body(half_ref, *refs):
        for source, target in zip(refs[: len(totals)], refs[-len(totals) :]):
            for i in range(4):
                begin = 2 * i * run
                first, later = source[:, begin : begin + run], source[:, begin + run : begin + 2 * run]
                target[:, i * run : (i + 1) * run] = jnp.where(
                    half_ref[0] == 0, later.astype(F32), first.astype(F32)
                ).astype(BF)

    return call(
        "split_hidden",
        body,
        [like(shard, width // 2)] * len(totals),
        scalars=[half],
        arrays=totals,
    )


def merge_hidden(half, totals, others, planes, part, earlier):
    shard, width = totals[0].shape
    run = planes // 2 * part

    def body(half_ref, *refs):
        number = len(totals)
        upper = half_ref[0] != 0
        for own_ref, other_ref, target in zip(refs[:number], refs[number : 2 * number], refs[-number:]):
            for plane in range(planes // 2):
                for side in range(2):
                    for core in range(2):
                        i = core * 2 + side
                        begin = 2 * i * run + plane * part
                        own = jnp.where(
                            upper,
                            own_ref[:, begin + run : begin + run + part].astype(F32),
                            own_ref[:, begin : begin + part].astype(F32),
                        )
                        begin = i * run + plane * part
                        other = other_ref[:, begin : begin + part].astype(F32)
                        begin = ((plane * 2 + side) * 2 + core) * 2 * part
                        target[:, begin : begin + part] = jnp.where(upper, other, own)
                        target[:, begin + part : begin + 2 * part] = jnp.where(upper, own, other)

    return call(
        "merge_hidden",
        body,
        [like(shard, width, dtype=F32)] * len(totals),
        scalars=[half],
        arrays=[*totals, *others],
        earlier=earlier,
    )


class HiddenWeights:
    def __init__(self, gathered, planes, shard, part):
        width = gathered.shape[2]
        units = 2 * planes * part
        self.direct = shard % 16 == 0 and part % 16 == 0
        self.width, self.units, self.shard, self.part = width, units, shard, part
        if self.direct:
            self.arrays = [gathered.reshape(planes, 2, 2, -1, width)]
            self.matrix = (planes, 2, 2, shard, units)
            self.down = (planes, part, width)
        else:
            blocks = gathered[:, 4 * shard :].reshape(planes, 2, 2, part, width)
            self.arrays = [
                jnp.stack(
                    [gathered[:, i * shard : (i + 1) * shard].reshape(width, width) for i in range(4)]
                ),
                jnp.transpose(blocks, (2, 1, 0, 3, 4)).reshape(2, 2, planes * part, width),
            ]
            self.matrix = (width, units)
            self.down = (planes * part, width)

    def scratch(self):
        return [
            pltpu.VMEM((4,) + self.matrix, BF),
            pltpu.VMEM((2, 2) + self.down, BF),
            pltpu.SemaphoreType.DMA((8,)),
        ]

    def specs(self):
        return [pl.BlockSpec(memory_space=pltpu.HBM)] * len(self.arrays)

    def matrix_copy(self, sources, wide, sems, i):
        if self.direct:
            source = sources[0].at[:, :, :, pl.ds(i * self.shard, self.shard), :]
        else:
            source = sources[0].at[i]
        return pltpu.make_async_copy(source, wide.at[i], sems.at[i])

    def down_copy(self, sources, tall, sems, core, side):
        if self.direct:
            source = sources[0].at[:, side, core, pl.ds(4 * self.shard, self.part), :]
        else:
            source = sources[1].at[core, side]
        return pltpu.make_async_copy(source, tall.at[core, side], sems.at[4 + core * 2 + side])

    def matrix_value(self, wide, i, columns):
        if self.direct:
            return wide[i, :, :, :, :, columns].reshape(self.width, -1)
        return wide[i, :, columns]

    def matrix_rows(self, wide, i, j, parts):
        if self.direct:
            step = self.matrix[0] // parts
            return wide[i, pl.ds(j * step, step)].reshape(self.width // parts, -1)
        step = self.width // parts
        return wide[i, pl.ds(j * step, step)]

    def down_value(self, tall, core, side, columns):
        if self.direct:
            return tall[core, side, :, :, columns].reshape(-1, columns.size)
        return tall[core, side, :, columns]

    def down_rows(self, tall, core, side):
        return tall[core, side].reshape(-1, self.width)


def hidden_forward(first_low, weights, up_scale, gate_scale, own_rows):
    rows, width = first_low.shape
    units = weights.units
    block = units // 2
    step = 256

    def body(first_ref, up_scale_ref, gate_scale_ref, *refs):
        sources = refs[: len(weights.arrays)]
        hidden_ref, up_ref, gate_ref, partial_ref, turned_ref, wide, tall, sems = refs[
            len(weights.arrays) :
        ]
        copies = [weights.matrix_copy(sources, wide, sems, i) for i in (0, 2, 1, 3)]
        down_copies = [
            weights.down_copy(sources, tall, sems, i, j) for i in range(2) for j in range(2)
        ]
        for copy in copies + down_copies:
            copy.start()
        first = first_ref[...]
        for core in range(2):
            copies[2 * core].wait()
            copies[2 * core + 1].wait()

            for begin in range(0, units, step):
                columns = pl.ds(begin, step)
                here = pl.ds(core * units + begin, step)
                up = matmul(first, weights.matrix_value(wide, core, columns))
                gate = matmul(first, weights.matrix_value(wide, 2 + core, columns))
                up_ref[:, here] = up.astype(BF)
                gate_ref[:, here] = gate.astype(BF)
                hidden = swiglu(up, gate, up_scale_ref[:, here], gate_scale_ref[:, here])
                hidden_ref[core, :, columns] = hidden.astype(BF)
        for copy in down_copies:
            copy.wait()

        for begin in range(0, width, step):
            columns = pl.ds(begin, step)
            total = None
            for core in range(2):
                for side in range(2):
                    term = matmul(
                        hidden_ref[core, :, pl.ds(side * block, block)],
                        weights.down_value(tall, core, side, columns),
                    )
                    total = term if total is None else total + term
            partial_ref[:, columns] = total
            turned_ref[pl.ds(0, own_rows), columns] = total[own_rows:].astype(BF)
            turned_ref[pl.ds(own_rows, own_rows), columns] = total[:own_rows].astype(BF)

    whole = pl.BlockSpec(memory_space=pltpu.VMEM)
    return pl.pallas_call(
        body,
        out_shape=[
            jax.ShapeDtypeStruct((2, rows, units), BF),
            jax.ShapeDtypeStruct((rows, 2 * units), BF),
            jax.ShapeDtypeStruct((rows, 2 * units), BF),
            jax.ShapeDtypeStruct((rows, width), F32),
            jax.ShapeDtypeStruct((rows, width), BF),
        ],
        in_specs=[whole] * 3 + weights.specs(),
        out_specs=[whole] * 5,
        scratch_shapes=weights.scratch(),
        compiler_params=pltpu.CompilerParams(vmem_limit_bytes=56 * 2**20),
        cost_estimate=COST,
        name="hidden_forward",
    )(first_low, up_scale.reshape(1, -1), gate_scale.reshape(1, -1), *weights.arrays)


def hidden_backward(down_low, up_proj, gate_proj, weights, up_scale, gate_scale, earlier):
    rows = down_low.shape[0]
    units = weights.units
    block = units // 2

    def body(down_ref, up_ref, gate_ref, up_scale_ref, gate_scale_ref, sources, low_out, gate_low_out, up_grad_ref, gate_grad_ref, tall, sems, low_ref, gate_low_ref, out_sems):
        copies = [weights.down_copy(sources, tall, sems, i, j) for i in range(2) for j in range(2)]
        for copy in copies:
            copy.start()
        down = down_ref[...]
        out_copies = []
        for core in range(2):
            for side in range(2):
                copies[core * 2 + side].wait()
                here = pl.ds((core * 2 + side) * block, block)
                grad_hidden = back_matmul(down, weights.down_rows(tall, core, side))
                up_scaling = up_scale_ref[:, here]
                gate_scaling = gate_scale_ref[:, here]
                up = up_ref[:, here].astype(F32)
                gate = gate_ref[:, here].astype(F32)
                scaled = gate_scaling * gate
                sigmoid = jax.nn.sigmoid(scaled)
                silu = scaled * sigmoid
                grad_scaled_up = grad_hidden * silu
                grad_scaled = grad_hidden * (up_scaling * up) * (sigmoid + silu * (1.0 - sigmoid))
                low_ref[:, here] = (grad_scaled_up * up_scaling).astype(BF)
                gate_low_ref[:, here] = (grad_scaled * gate_scaling).astype(BF)
                up_grad_ref[:, here] = jnp.sum(grad_scaled_up * up, axis=0, keepdims=True)
                gate_grad_ref[:, here] = jnp.sum(grad_scaled * gate, axis=0, keepdims=True)
                i = 2 * (core * 2 + side)
                out_copies += [
                    pltpu.make_async_copy(low_ref.at[:, here], low_out.at[:, here], out_sems.at[i]),
                    pltpu.make_async_copy(gate_low_ref.at[:, here], gate_low_out.at[:, here], out_sems.at[i + 1]),
                ]
                for copy in out_copies[-2:]:
                    copy.start()
        for copy in out_copies:
            copy.wait()

    return call(
        "hidden_backward",
        body,
        [like(rows, 2 * units)] * 2 + [like(1, 2 * units, dtype=F32)] * 2,
        limit=30,
        arrays=[down_low, up_proj, gate_proj, up_scale, gate_scale],
        remote=weights.arrays,
        scratch=weights.scratch()[1:]
        + [pltpu.VMEM((rows, 2 * units), BF)] * 2
        + [pltpu.SemaphoreType.DMA((8,))],
        written=2,
        earlier=earlier,
    )


def first_partial(up_low, gate_low, weights, own_rows, earlier):
    rows = up_low.shape[0]
    units = weights.units
    width = weights.width

    def body(up_ref, gate_ref, sources, partial_ref, turned_ref, wide, sems):
        copies = [weights.matrix_copy(sources, wide, sems, i) for i in range(4)]
        for copy in copies:
            copy.start()
        pieces = 2
        piece = width // pieces
        for i in range(4):
            copies[i].wait()
            left = (up_ref, gate_ref)[i // 2][:, pl.ds((i % 2) * units, units)]
            for j in range(pieces):
                columns = pl.ds(j * piece, piece)
                term = back_matmul(left, weights.matrix_rows(wide, i, j, pieces))
                if i:
                    term = partial_ref[:, columns] + term
                partial_ref[:, columns] = term
        for j in range(pieces):
            columns = pl.ds(j * piece, piece)
            turn(turned_ref, own_rows, columns, partial_ref[:, columns])

    return call(
        "first_partial",
        body,
        [like(rows, width, dtype=F32), like(rows, width)],
        limit=30,
        arrays=[up_low, gate_low],
        remote=weights.arrays,
        scratch=[weights.scratch()[0], weights.scratch()[2]],
        earlier=earlier,
    )


def per_device(
    tokens,
    cotangent,
    lengths,
    placement,
    query_weight,
    key_weight,
    value_weight,
    out_weight,
    up_weight,
    gate_weight,
    down_weight,
    scoring,
    upscale,
    gatescale,
    attention_rate,
    feedforward_rate,
):
    size = lax.axis_size("fsdp")
    planes = size // 4
    half = lax.axis_index("grp")
    me = lax.axis_index("fsdp")
    core = me % 2
    side = (me // 2) % 2
    plane = me // 4
    half_scalar = half.reshape(1).astype(jnp.int32)
    which = jnp.stack([core, side]).astype(jnp.int32)
    local_seqs = tokens.shape[0] // size
    seq_len = tokens.shape[1] * size
    width = tokens.shape[2]
    own_rows = local_seqs * seq_len
    shard = query_weight.shape[0]
    hidden_shard = down_weight.shape[0]
    part = hidden_shard // 2
    per_row = hidden_shard // shard
    half_width = width // 2

    def swap_core(array):
        return lax.ppermute(array, "fsdp", [(i, i ^ 1) for i in range(size)])

    def swap_side(array):
        return lax.ppermute(array, "fsdp", [(i, i ^ 2) for i in range(size)])

    def next_plane(array):
        return lax.ppermute(array, "fsdp", [(i, (i + 4) % size) for i in range(size)])

    def swap_half(array):
        return lax.ppermute(array, "grp", [(0, 1), (1, 0)])

    def pick(array, index, axis):
        return lax.dynamic_index_in_dim(array, index, axis, keepdims=False)

    first_group = lay_first(
        half_scalar,
        query_weight,
        key_weight,
        value_weight,
        out_weight,
        [scoring, attention_rate, feedforward_rate, upscale, gatescale],
    )
    second_group = lay_second(half_scalar, up_weight, gate_weight, down_weight, planes)
    hidden_width = planes * 4 * part
    core_width = hidden_width // 2
    held = [first_group]
    crossed = []
    for i in range(planes):
        here = after(held[-1], *crossed[-1:]) if crossed else held[-1]
        if i < planes - 1:
            held.append(next_plane(here))
        crossed.append(swap_side(here))
    second_whole = lax.all_gather(
        after(second_group, *held[: GATE + 1], *crossed[:GATE]), "fsdp", axis=0
    )
    (both,) = call(
        "rows",
        place_pair,
        [like(2, *tokens.shape)],
        arrays=[tokens, cotangent],
        earlier=[held[-1], crossed[-2]],
        limit=56,
    )
    arrived = lax.all_to_all(both, "fsdp", split_axis=1, concat_axis=2, tiled=True)
    own_tokens = arrived[0].reshape(own_rows, width)
    other_tokens = swap_half(own_tokens)
    held = held + crossed
    held = held + [swap_core(array) for array in held]
    places = []
    for i in range(4 * planes):
        there_core = 1 - core if i >= 2 * planes else core
        there_side = 1 - side if i // planes % 2 else side
        places.append(((plane - i) % planes * 2 + there_side) * 2 + there_core)
    shards = Shards(held, jnp.stack(places).astype(jnp.int32))

    group_order = placement[0]
    own_slots = lax.dynamic_slice_in_dim(group_order, me * local_seqs, local_seqs)
    own_lengths = jnp.take(lengths[0], own_slots)
    valid = (jnp.arange(seq_len, dtype=jnp.int32)[None, :] < own_lengths[:, None]).reshape(
        own_rows, 1
    )
    own_cot = jnp.where(valid, arrived[1].reshape(own_rows, width), jnp.zeros((), BF))
    token_rows = jnp.concatenate([own_tokens, other_tokens])
    other_cot = swap_half(own_cot)

    qkv, query_unit, key_unit, value_low, mixed_half, mixed_turned, scale_float = attention_forward(
        half_scalar, token_rows, shards, seq_len
    )
    attention_mix = scale_float[1:2]
    feed_mix = scale_float[2:3]

    up_scale, gate_scale = hidden_scales(half_scalar, scale_float, per_row, planes, shard)
    skip = 3 * half_width + 128
    mixed_low, attended, first_state, first_low = first_forward(
        half_scalar, mixed_half, swap_half(mixed_turned), token_rows, attention_mix, shards, skip
    )

    feature = jnp.arange(width, dtype=jnp.int32)
    block = []
    for b in range(2):
        for a in range(2):
            for k in range(planes):
                there_core = core if b == 0 else 1 - core
                there_side = 1 - side if a == 0 else side
                block.append((k * 2 + there_side) * 2 + there_core)
    block = jnp.stack(block).astype(jnp.int32)
    wanted = (block[:, None] * shard + jnp.arange(shard, dtype=jnp.int32)[None, :]).reshape(-1)
    chooser = (feature[:, None] == wanted[None, :]).astype(BF)

    def share_columns(array):
        chosen = matmul(array, chooser).astype(BF)
        return chosen[:, :half_width], swap_core(chosen[:, half_width:])

    def share(array):
        return array, swap_core(array)

    def over_planes(total):
        return lax.psum_scatter(
            total.reshape(planes, total.shape[0] // planes, total.shape[1]),
            "fsdp",
            scatter_dimension=0,
            axis_index_groups=[[k * 4 + j for k in range(planes)] for j in range(4)],
        )

    def joined(kept, arrived_part):
        return (kept.astype(F32) + arrived_part.astype(F32)).astype(BF)

    token_sides = share_columns(token_rows)
    mixed_sides = share_columns(mixed_low)
    first_sides = share_columns(first_low)
    hidden_weights = HiddenWeights(
        after(second_whole, *token_sides, *mixed_sides, *first_sides, other_cot), planes, shard, part
    )
    hidden_low, up_proj, gate_proj, partial, partial_turned = hidden_forward(
        first_low, hidden_weights, up_scale, gate_scale, own_rows
    )
    hidden_other = swap_core(pick(hidden_low, 1 - core, 0))

    layer_own, grad_first, down_low, feed_grad = second_backward(
        partial,
        swap_half(partial_turned),
        first_state,
        own_cot,
        other_cot,
        valid.astype(F32),
        feed_mix,
    )
    down_other = swap_core(down_low)
    down_args = (which, hidden_low, hidden_other, down_low, down_other)
    down_both = down_grads(*down_args, [])
    down_sum = over_planes(down_both)
    up_low, gate_low, upscale_grad, gatescale_grad = hidden_backward(
        down_low, up_proj, gate_proj, hidden_weights, up_scale, gate_scale, [down_both]
    )
    up_other = swap_core(up_low)
    gate_other = swap_core(gate_low)
    up_side = [(up_low, up_other, None)]
    gate_side = [(gate_low, gate_other, None)]
    up_sent = side_grads("up_sent", [first_sides], up_side, False, [])
    up_arrived = swap_side(up_sent)
    partial, partial_turned = first_partial(up_low, gate_low, hidden_weights, own_rows, [up_sent])
    partial_other = swap_half(partial_turned)
    gate_sent = side_grads("gate_sent", [first_sides], gate_side, False, [partial])
    up_kept = side_grads("up_kept", [first_sides], up_side, True, [gate_sent])
    attended_cols, grad_mixed, grad_tokens, attention_grad = first_backward(
        half_scalar,
        grad_first,
        partial,
        partial_other,
        token_rows,
        attended,
        attention_mix,
        shards,
        skip,
        [up_kept],
    )
    gate_arrived = swap_side(after(gate_sent, up_arrived))
    attended_other = swap_core(after(attended_cols, up_arrived))
    up_joined = joined(up_kept, after(up_arrived, grad_mixed))
    up_total = over_planes(up_joined)
    qkv_low, scoring_grad, token_own, token_sent = attention_backward(
        half_scalar, grad_mixed, qkv, query_unit, key_unit, value_low, scale_float, shards, seq_len, [up_joined]
    )
    qkv_other = swap_core(qkv_low)
    token_other = swap_half(token_sent)
    last_args = (
        [mixed_sides, token_sides],
        [(attended_cols, attended_other, None), (qkv_low, qkv_other, (0, 1, 2))],
    )
    last_sent = side_grads("last_sent", *last_args, False, [down_sum])
    gate_kept = side_grads("gate_kept", [first_sides], gate_side, True, [last_sent])
    last_kept = side_grads("last_kept", *last_args, True, [gate_kept])
    last_arrived = swap_side(after(last_sent, gate_arrived))
    gate_joined = joined(gate_kept, after(gate_arrived, last_kept, token_other))
    gate_total = over_planes(gate_joined)
    def hidden_spread(grad):
        blocks = jnp.transpose(grad.reshape(2, 2, planes, part), (2, 1, 0, 3))
        blank = jnp.zeros_like(blocks)
        both_halves = jnp.where(
            half == 0, jnp.stack([blocks, blank], axis=3), jnp.stack([blank, blocks], axis=3)
        )
        return both_halves.reshape(size, hidden_shard)

    blank = jnp.zeros_like(scoring_grad)
    scoring_spread = jnp.where(
        half == 0,
        jnp.concatenate([scoring_grad, blank], axis=1),
        jnp.concatenate([blank, scoring_grad], axis=1),
    )
    small = jnp.concatenate(
        [
            scoring_spread.reshape(size, shard),
            attention_grad.reshape(size, shard),
            feed_grad.reshape(size, shard),
            hidden_spread(upscale_grad),
            hidden_spread(gatescale_grad),
        ],
        axis=1,
    )
    (up_part,) = split_hidden(half_scalar, [up_total], planes, part)
    up_swapped = swap_half(up_part)
    (outgoing,) = call(
        "outgoing",
        place_outgoing,
        [like(2, own_rows, width)],
        arrays=[layer_own, grad_tokens, token_own, token_other],
        earlier=[last_kept],
    )
    returned = lax.all_to_all(
        outgoing.reshape(2, local_seqs, seq_len, width), "fsdp", split_axis=2, concat_axis=1, tiled=True
    )
    (up_out,) = merge_hidden(half_scalar, [up_total], [up_swapped], planes, part, [returned])
    last_joined = joined(last_kept, after(last_arrived, up_out))
    last_total = over_planes(last_joined).astype(F32)
    down_total = down_sum[:, width:].astype(F32) + swap_side(
        after(down_sum[:, :width], last_joined)
    ).astype(F32)
    down_cols = down_total.reshape(part, 2, half_width)
    mine = pick(down_cols, half, 1)
    theirs = swap_half(pick(down_cols, 1 - half, 1).astype(BF)).astype(F32)
    down_out = jnp.where(
        half == 0, jnp.concatenate([mine, theirs]), jnp.concatenate([theirs, mine])
    )
    (small,) = call(
        "pass", place_whole, [like(*small.shape, dtype=F32)], arrays=[small], earlier=[last_joined]
    )
    small = lax.all_to_all(small, "fsdp", split_axis=0, concat_axis=0, tiled=True)
    (total,) = call("add", sum_whole, [like(1, small.shape[1], dtype=F32)], arrays=[small])
    total = total[0]
    total = total + swap_half(total)

    (gate_part,) = split_hidden(half_scalar, [gate_total], planes, part)
    (gate_out,) = merge_hidden(half_scalar, [gate_total], [swap_half(gate_part)], planes, part, [])
    out_total = last_total[:, :half_width]
    qkv_total = last_total[:, half_width:]

    return (
        returned[0],
        returned[1],
        qkv_total[:, :half_width],
        qkv_total[:, half_width : 2 * half_width],
        qkv_total[:, 2 * half_width :],
        out_total,
        up_out,
        gate_out,
        down_out,
        total[:shard],
        total[3 * shard : 3 * shard + hidden_shard],
        total[3 * shard + hidden_shard :],
        total[shard : 2 * shard],
        total[2 * shard : 3 * shard],
    )


def solution(mesh):
    rows = P("grp", "fsdp", None)
    group = P("grp", None)
    matrix = P("fsdp", None)
    vector = P("fsdp")
    split = P("fsdp", "grp")
    return jax.shard_map(
        per_device,
        mesh=mesh,
        in_specs=(rows, rows, group, group) + (matrix,) * 7 + (vector,) * 5,
        out_specs=(rows, rows) + (split,) * 7 + (vector,) * 5,
        check_vma=False,
    )
```

```python
import math

import jax
import jax.numpy as jnp
from jax import lax
from jax.experimental import pallas as pl
from jax.experimental.pallas import tpu as pltpu
from jax.sharding import PartitionSpec as P

H = 20
DK = 64
BF = jnp.bfloat16
F32 = jnp.float32
GATE = 1
COST = pl.CostEstimate(flops=1000, bytes_accessed=1000, transcendentals=0)


def swiglu(up_proj, gate_proj, upscale, gatescale):
    scaled = gatescale * gate_proj
    return scaled * jax.nn.sigmoid(scaled) * (upscale * up_proj)


def matmul(left_side, right_side):
    return jnp.dot(left_side, right_side, preferred_element_type=F32)


def weight_grad(left_side, right_side):
    return lax.dot_general(
        left_side, right_side, (((0,), (0,)), ((), ())), preferred_element_type=F32
    )


def back_matmul(grad_rows, weight_rows):
    return lax.dot_general(
        grad_rows, weight_rows, (((1,), (1,)), ((), ())), preferred_element_type=F32
    )


def after(value, *earlier):
    return lax.optimization_barrier((value, *earlier))[0]


def like(*shape, dtype=BF):
    return jax.ShapeDtypeStruct(shape, dtype)


def call(name, body, outs, scalars=(), arrays=(), remote=(), scratch=(), earlier=(), limit=16, written=0):
    counts = (len(scalars), len(arrays), len(remote), len(earlier), len(outs))

    def kernel(*refs):
        groups = []
        at = 0
        for count in counts:
            groups.append(refs[at : at + count])
            at += count
        body(*groups[0], *groups[1], groups[2], *groups[4], *refs[at:])

    whole = pl.BlockSpec(memory_space=pltpu.VMEM)
    kept = pl.BlockSpec(memory_space=pl.ANY)
    placed = pl.BlockSpec(memory_space=pltpu.HBM)
    return pl.pallas_call(
        kernel,
        out_shape=list(outs),
        in_specs=[pl.BlockSpec(memory_space=pltpu.SMEM)] * counts[0]
        + [whole] * counts[1]
        + [placed] * counts[2]
        + [kept] * counts[3],
        out_specs=[placed] * written + [whole] * (counts[4] - written),
        scratch_shapes=list(scratch),
        compiler_params=pltpu.CompilerParams(vmem_limit_bytes=limit * 2**20),
        cost_estimate=COST,
        name=name,
    )(*scalars, *arrays, *remote, *earlier)


class Shards:
    def __init__(self, arrays, places):
        self.direct = arrays[0].shape[0] % 16 == 0
        if self.direct:
            self.arrays, self.places = list(arrays), places
        else:
            whole = jnp.zeros((len(arrays),) + arrays[0].shape, BF)
            for i, array in enumerate(arrays):
                whole = lax.dynamic_update_index_in_dim(whole, array, places[i], 0)
            self.arrays = [whole.reshape(-1, arrays[0].shape[1])]
            self.places = jnp.zeros((1,), jnp.int32)
        self.count = len(self.arrays)
        self.height = self.arrays[0].shape[0]

    def scratch(self, width):
        return [
            pltpu.VMEM((self.count, self.height, width), BF),
            pltpu.SemaphoreType.DMA((self.count,)),
        ]

    def copies(self, places, sources, target, sems, begin, width):
        return [
            pltpu.make_async_copy(
                sources[i].at[:, pl.ds(begin, width)], target.at[places[i]], sems.at[i]
            )
            for i in range(self.count)
        ]

    def columns(self, target, begin, width):
        return target[:, :, pl.ds(begin, width)].reshape(self.count * self.height, width)

    def rows(self, target, index, parts, begin, width):
        if self.direct:
            step = self.count // parts
            rows = target[pl.ds(index * step, step), :, pl.ds(begin, width)]
        else:
            step = self.height // parts
            rows = target[:, pl.ds(pl.multiple_of(index * step, step), step), pl.ds(begin, width)]
        return rows.reshape(-1, width)


def inverse_rms(vector):
    return lax.rsqrt(jnp.mean(vector * vector, axis=-1, keepdims=True) + 1e-06)


def head_sums(values, low_head):
    low_sum = jnp.sum(jnp.where(low_head, values, 0.0), axis=-1, keepdims=True)
    high_sum = jnp.sum(jnp.where(low_head, 0.0, values), axis=-1, keepdims=True)
    return low_sum, high_sum


def head_inverse(vector, low_head):
    low_sum, high_sum = head_sums(vector * vector, low_head)
    return jnp.where(low_head, lax.rsqrt(low_sum + 1e-06), lax.rsqrt(high_sum + 1e-06))


def head_probs(query_head, key_unit, seq_len):
    scores = back_matmul(query_head, key_unit) * math.sqrt(DK)
    query_row = lax.broadcasted_iota(jnp.int32, scores.shape, 0)
    key_row = lax.broadcasted_iota(jnp.int32, scores.shape, 1)
    start = query_row - lax.rem(query_row, seq_len)
    scores = jnp.where((key_row <= query_row) & (key_row >= start), scores, -1e30)
    exp_scores = jnp.exp(scores - jnp.max(scores, axis=-1, keepdims=True))
    return exp_scores / jnp.sum(exp_scores, axis=-1, keepdims=True)


def only(mask, values):
    return jnp.where(mask, values.astype(F32), 0.0).astype(BF)


def turn(ref, rows, columns, value):
    ref[pl.ds(0, rows), columns] = value[rows:].astype(BF)
    ref[pl.ds(rows, rows), columns] = value[:rows].astype(BF)


def attention_forward(half, token_rows, shards, seq_len):
    rows, width = token_rows.shape
    half_width = width // 2
    pairs = half_width // 128
    cols = 3 * half_width + 128

    def body(
        places, half_ref, x_ref, sources, qkv_ref, qu_ref, ku_ref, vl_ref, mixed_ref, turned_ref, scale_ref, w_ref, sems
    ):
        copies = shards.copies(places, sources, w_ref, sems, 0, cols)
        for copy in copies:
            copy.start()
        for copy in copies:
            copy.wait()
        scale_ref[...] = jnp.transpose(
            shards.columns(w_ref, 3 * half_width, 128).astype(F32)
        )[:16]
        x = x_ref[...]
        step = 384
        for begin in range(0, 3 * half_width, step):
            qkv_ref[:, pl.ds(begin, step)] = matmul(x, shards.columns(w_ref, begin, step))
        low_head = lax.broadcasted_iota(jnp.int32, (rows, 128), 1) < DK
        later = half_ref[0] == 1

        def pair(i, carry):
            at = pl.multiple_of(i * 128, 128)
            here = pl.ds(at, 128)
            queries = qkv_ref[:, here]
            key_rows = qkv_ref[:, pl.ds(half_width + at, 128)]
            value_low = qkv_ref[:, pl.ds(2 * half_width + at, 128)].astype(BF)
            scaling = jnp.where(
                later, scale_ref[0:1, pl.ds(half_width + at, 128)], scale_ref[0:1, here]
            )
            query_unit = queries * head_inverse(queries, low_head) * scaling
            key_unit = (key_rows * head_inverse(key_rows, low_head) * scaling).astype(BF)
            mixed = None
            for mask in (low_head, ~low_head):
                probs = head_probs(only(mask, query_unit), key_unit, seq_len)
                head = matmul(probs.astype(BF), value_low)
                mixed = head if mixed is None else jnp.where(low_head, mixed, head)
            qu_ref[:, here] = query_unit.astype(BF)
            ku_ref[:, here] = key_unit
            vl_ref[:, here] = value_low
            mixed_ref[:, here] = mixed.astype(BF)
            turn(turned_ref, rows // 2, here, mixed)
            return carry

        lax.fori_loop(0, pairs, pair, 0)

    return call(
        "attention_forward",
        body,
        [like(rows, 3 * half_width, dtype=F32)] + [like(rows, half_width)] * 5 + [like(16, width, dtype=F32)],
        scalars=[shards.places, half],
        arrays=[token_rows],
        remote=shards.arrays,
        limit=24,
        scratch=shards.scratch(cols),
    )


def place_whole(source, _, target):
    target[...] = source[...]


def place_pair(first, later, _, target):
    target[0] = first[...]
    target[1] = later[...]


def place_outgoing(layer, mix, own, other, _, target):
    target[0] = layer[...]
    target[1] = (mix[...] + own[...] + other[...].astype(F32)).astype(BF)


def sum_whole(source, _, target):
    target[...] = jnp.sum(source[...], axis=0, keepdims=True)


def hidden_scales(half, scales, per_row, planes, shard):
    pieces = per_row // 2

    def body(half_ref, scale_ref, _, *targets):
        later = half_ref[0] != 0
        for i, target in enumerate(targets):
            for piece in range(pieces):
                row = 3 + i * per_row + piece
                values = jnp.where(
                    later, scale_ref[row + pieces : row + pieces + 1, :], scale_ref[row : row + 1, :]
                )
                for core in range(2):
                    for side in range(2):
                        for plane in range(planes):
                            begin = ((plane * 2 + side) * 2 + core) * shard
                            place = (((core * 2 + side) * planes + plane) * pieces + piece) * shard
                            target[:, place : place + shard] = values[:, begin : begin + shard]

    width = 4 * planes * pieces * shard
    return call(
        "hidden_scales",
        body,
        [like(1, width, dtype=F32)] * 2,
        scalars=[half],
        arrays=[scales],
    )


def place_halves(half_ref, target, own, other):
    width = own.shape[1]

    @pl.when(half_ref[0] == 0)
    def _():
        target[:, pl.ds(0, width)] = own[...]
        target[:, pl.ds(width, width)] = other[...]

    @pl.when(half_ref[0] != 0)
    def _():
        target[:, pl.ds(0, width)] = other[...]
        target[:, pl.ds(width, width)] = own[...]


def first_forward(half, mixed, mixed_other, token_rows, attention_mix, shards, skip):
    rows, width = token_rows.shape

    def body(
        places, half_ref, own_ref, other_ref, x_ref, mix_ref, sources, mixed_ref, attended_ref, first_ref, low_ref, w_ref, sems
    ):
        copies = shards.copies(places, sources, w_ref, sems, skip, width)
        for copy in copies:
            copy.start()
        place_halves(half_ref, mixed_ref, own_ref, other_ref)
        for copy in copies:
            copy.wait()
        for begin in range(0, width, 256):
            attended_ref[:, pl.ds(begin, 256)] = matmul(
                mixed_ref[...], shards.columns(w_ref, begin, 256)
            )
        x = x_ref[...].astype(F32)
        attended = attended_ref[...]
        mix = x + mix_ref[...] * (attended * inverse_rms(attended) - x)
        first = mix * inverse_rms(mix)
        first_ref[...] = first
        low_ref[...] = first.astype(BF)

    return call(
        "first_forward",
        body,
        [like(rows, width)] + [like(rows, width, dtype=F32)] * 2 + [like(rows, width)],
        scalars=[shards.places, half],
        arrays=[mixed, mixed_other, token_rows, attention_mix],
        remote=shards.arrays,
        limit=20,
        scratch=shards.scratch(width),
    )


def mix_backward(base, branch, rate, grad):
    branch_inverse = inverse_rms(branch)
    branch_unit = branch * branch_inverse
    mix = base + rate * (branch_unit - base)
    inverse = inverse_rms(mix)
    value = mix * inverse
    grad_mix = inverse * (grad - value * jnp.mean(grad * value, axis=-1, keepdims=True))
    grad_unit = grad_mix * rate
    grad_branch = branch_inverse * (
        grad_unit - branch_unit * jnp.mean(grad_unit * branch_unit, axis=-1, keepdims=True)
    )
    return value, grad_mix - grad_unit, grad_branch, grad_mix * (branch_unit - base)


def second_backward(partial, partial_other, first_state, cot, cot_other, valid, feed_mix):
    rows, width = partial.shape
    own = rows // 2
    pieces = 4
    step = rows // pieces

    def body(partial_ref, other_ref, first_ref, cot_ref, cot_other_ref, valid_ref, mix_ref, layer_ref, grad_ref, low_ref, rate_ref):
        mine = pl.program_id(0) < pieces // 2
        down = partial_ref[...] + other_ref[...].astype(F32)
        grad = jnp.where(mine, cot_ref[...].astype(F32), cot_other_ref[...].astype(F32))
        value, grad_first, grad_down, grad_rate = mix_backward(first_ref[...], down, mix_ref[...], grad)
        grad_ref[...] = grad_first
        low_ref[...] = grad_down.astype(BF)

        @pl.when(pl.program_id(0) == 0)
        def _():
            rate_ref[...] = jnp.zeros_like(rate_ref)

        @pl.when(mine)
        def _():
            layer_ref[...] = (value * valid_ref[...]).astype(BF)
            rate_ref[...] += jnp.sum(grad_rate, axis=0, keepdims=True)

    every = pl.BlockSpec((step, width), lambda i: (i, 0))
    first_half = pl.BlockSpec((step, width), lambda i: (jnp.minimum(i, pieces // 2 - 1), 0))
    later_half = pl.BlockSpec((step, width), lambda i: (jnp.maximum(i - pieces // 2, 0), 0))
    vector = pl.BlockSpec((1, width), lambda i: (0, 0))
    return pl.pallas_call(
        body,
        grid=(pieces,),
        out_shape=[like(own, width), like(rows, width, dtype=F32), like(rows, width), like(1, width, dtype=F32)],
        in_specs=[
            every,
            every,
            every,
            first_half,
            later_half,
            pl.BlockSpec((step, 1), lambda i: (jnp.minimum(i, pieces // 2 - 1), 0)),
            vector,
        ],
        out_specs=[first_half, every, every, vector],
        compiler_params=pltpu.CompilerParams(vmem_limit_bytes=24 * 2**20),
        cost_estimate=COST,
        name="second_backward",
    )(partial, partial_other, first_state, cot, cot_other, valid, feed_mix)


def first_backward(half, grad_first, partial, partial_other, token_rows, attended, attention_mix, shards, skip, earlier):
    rows, width = partial.shape
    own = rows // 2
    half_width = width // 2

    def body(
        places, half_ref, grad_ref, partial_ref, other_ref, x_ref, attended_ref, mix_ref, sources, cols_ref, mixed_ref, token_ref, rate_ref, low_ref, w_ref, sems
    ):
        copies = shards.copies(places, sources, w_ref, sems, skip, width)
        for copy in copies:
            copy.start()
        for begin in (0, own):
            here = pl.ds(begin, own)
            grad = grad_ref[here, :] + partial_ref[here, :] + other_ref[here, :].astype(F32)
            _, grad_token, grad_attended, grad_rate = mix_backward(
                x_ref[here, :].astype(F32), attended_ref[here, :], mix_ref[...], grad
            )
            low_ref[here, :] = grad_attended.astype(BF)
            if begin == 0:
                token_ref[...] = grad_token
                rate_ref[...] = jnp.sum(grad_rate, axis=0, keepdims=True)
        at = pl.multiple_of(half_ref[0] * half_width, 128)
        cols_ref[...] = low_ref[:, pl.ds(at, half_width)]
        for copy in copies:
            copy.wait()
        mixed_ref[...] = back_matmul(
            low_ref[...], shards.rows(w_ref, half_ref[0], 2, 0, width)
        ).astype(BF)

    return call(
        "first_backward",
        body,
        [like(rows, half_width)] * 2 + [like(own, width, dtype=F32), like(1, width, dtype=F32)],
        scalars=[shards.places, half],
        arrays=[grad_first, partial, partial_other, token_rows, attended, attention_mix],
        remote=shards.arrays,
        limit=56,
        scratch=[pltpu.VMEM((rows, width), BF)] + shards.scratch(width),
        earlier=earlier,
    )


def attention_backward(half, grad_mixed, qkv, query_unit, key_unit, value_low, scales, shards, seq_len, earlier):
    rows, half_width = grad_mixed.shape
    width = 2 * half_width
    pairs = half_width // 128
    own = rows // 2

    def body(
        places, half_ref, gm_ref, qkv_ref, qu_ref, ku_ref, vl_ref, scale_ref, sources, grads_ref, scoring_ref, own_ref, other_ref, w_ref, sems
    ):
        copies = shards.copies(places, sources, w_ref, sems, 0, 3 * half_width)
        for copy in copies:
            copy.start()
        low_head = lax.broadcasted_iota(jnp.int32, (rows, 128), 1) < DK
        later = half_ref[0] == 1

        def pair(i, carry):
            at = pl.multiple_of(i * 128, 128)
            here = pl.ds(at, 128)
            query_unit = qu_ref[:, here]
            key_unit = ku_ref[:, here]
            value_low = vl_ref[:, here]
            scaling = jnp.where(
                later, scale_ref[0:1, pl.ds(half_width + at, 128)], scale_ref[0:1, here]
            )
            grad_value = grad_qunit = grad_kunit = None
            for mask in (low_head, ~low_head):
                probs = head_probs(only(mask, query_unit), key_unit, seq_len)
                grad_head = only(mask, gm_ref[:, here])
                value_part = weight_grad(probs.astype(BF), grad_head)
                grad_probs = back_matmul(grad_head, value_low)
                grad_scores = (
                    probs * (grad_probs - jnp.sum(grad_probs * probs, axis=-1, keepdims=True))
                ).astype(BF)
                query_part = matmul(grad_scores, key_unit)
                key_part = weight_grad(grad_scores, query_unit)
                if grad_value is None:
                    grad_value, grad_qunit, grad_kunit = value_part, query_part, key_part
                else:
                    grad_value = grad_value + value_part
                    grad_qunit = jnp.where(low_head, grad_qunit, query_part)
                    grad_kunit = jnp.where(low_head, grad_kunit, key_part)
            scoring_grad = None
            for place, grad in ((0, grad_qunit), (1, grad_kunit)):
                raw = qkv_ref[:, pl.ds(place * half_width + at, 128)]
                grad = grad * math.sqrt(DK)
                inverse = head_inverse(raw, low_head)
                unit = raw * inverse
                term = jnp.sum(grad * unit, axis=0, keepdims=True)
                scoring_grad = term if scoring_grad is None else scoring_grad + term
                grad = grad * scaling
                low_sum, high_sum = head_sums(grad * unit, low_head)
                grads_ref[place, :, here] = (
                    inverse * (grad - unit * jnp.where(low_head, low_sum, high_sum))
                ).astype(BF)
            grads_ref[2, :, here] = grad_value.astype(BF)
            scoring_ref[:, here] = scoring_grad
            return carry

        lax.fori_loop(0, pairs, pair, 0)
        for copy in copies:
            copy.wait()
        for piece in range(2):
            total = None
            for j in range(3):
                term = back_matmul(
                    grads_ref[j], shards.rows(w_ref, piece, 2, j * half_width, half_width)
                )
                total = term if total is None else total + term
            columns = pl.ds(piece * half_width, half_width)
            own_ref[:, columns] = total[:own]
            other_ref[:, columns] = total[own:].astype(BF)

    return call(
        "attention_backward",
        body,
        [
            like(3, rows, half_width),
            like(1, half_width, dtype=F32),
            like(own, width, dtype=F32),
            like(own, width),
        ],
        scalars=[shards.places, half],
        arrays=[grad_mixed, qkv, query_unit, key_unit, value_low, scales],
        remote=shards.arrays,
        limit=56,
        scratch=shards.scratch(3 * half_width),
        earlier=earlier,
    )


def down_grads(which, hidden, hidden_other, down, down_other, earlier):
    units = hidden_other.shape[1]
    width = down.shape[1]
    block = units // 2

    def body(which_ref, hidden_ref, hidden_other_ref, down_ref, down_other_ref, _, out_ref):
        def piece(kept, carry):
            side = jnp.where(kept == 1, which_ref[1], 1 - which_ref[1])
            columns = pl.ds(pl.multiple_of(side * block, 128), block)
            total = weight_grad(hidden_ref[which_ref[0], :, columns], down_ref[...])
            total = total + weight_grad(hidden_other_ref[:, columns], down_other_ref[...])
            out_ref[:, pl.ds(pl.multiple_of(kept * width, 128), width)] = total.astype(BF)
            return carry

        lax.fori_loop(0, 2, piece, 0)

    return call(
        "down_grads",
        body,
        [like(block, 2 * width)],
        scalars=[which],
        arrays=[hidden, hidden_other, down, down_other],
        earlier=earlier,
    )[0]


def side_grads(name, lefts, rights, kept, earlier):
    block = lefts[0][0].shape[1] // 2
    number = len(lefts)
    total_width = sum(right[0].shape[-1] * len(right[2] or (0,)) for right in rights)

    def body(*refs):
        refs = [ref for ref in refs if not isinstance(ref, tuple)]
        out_ref = refs[-1]
        begin = 0
        for i in range(number):
            own_ref, other_ref, right_ref, right_other_ref = refs[4 * i : 4 * i + 4]
            columns = pl.ds(block if kept else 0, block)
            own = own_ref[:, columns]
            other = other_ref[:, columns]
            for index in rights[i][2] or (None,):
                step = min(right_ref.shape[-1], 1280)

                def piece(j, carry, own=own, other=other, right=right_ref, right_other=right_other_ref, index=index, begin=begin, step=step):
                    at = pl.multiple_of(j * step, 128)
                    here = (slice(None), pl.ds(at, step))
                    if index is not None:
                        here = (index, *here)
                    total = weight_grad(own, right[here]) + weight_grad(other, right_other[here])
                    out_ref[:, pl.ds(begin + at, step)] = total.astype(out_ref.dtype)
                    return carry

                count = right_ref.shape[-1] // step
                lax.fori_loop(0, count, piece, 0)
                begin += step * count

    arrays = []
    for left, right in zip(lefts, rights):
        arrays += [*left, *right[:2]]
    return call(
        name,
        body,
        [like(block, total_width)],
        limit=20,
        arrays=arrays,
        earlier=earlier,
    )[0]


def lay_first(half, query_weight, key_weight, value_weight, out_weight, scales):
    shard, width = query_weight.shape
    half_width = width // 2

    def body(half_ref, q_ref, k_ref, v_ref, out_ref, *refs):
        target, square = refs[-2:]
        for i, ref in enumerate((q_ref, k_ref, v_ref)):
            place = pl.ds(i * half_width, half_width)

            @pl.when(half_ref[0] == 0)
            def _():
                target[:, place] = ref[:, pl.ds(0, half_width)]

            @pl.when(half_ref[0] != 0)
            def _():
                target[:, place] = ref[:, pl.ds(half_width, half_width)]

        square[...] = jnp.zeros_like(square)
        row = 0
        for ref in refs[: len(scales)]:
            values = ref[...].astype(F32).reshape(1, -1)
            for begin in range(0, values.shape[1], shard):
                square[pl.ds(row, 1), pl.ds(0, shard)] = values[:, begin : begin + shard]
                row += 1
        target[:, pl.ds(3 * half_width, 128)] = jnp.transpose(square[...])[:shard].astype(BF)
        target[:, pl.ds(3 * half_width + 128, width)] = out_ref[...]

    return call(
        "lay_first",
        body,
        [like(shard, 3 * half_width + 128 + width)],
        limit=56,
        scalars=[half],
        arrays=[query_weight, key_weight, value_weight, out_weight]
        + list(scales),
        scratch=[pltpu.VMEM((128, 128), F32)],
    )[0]


def lay_second(half, up_weight, gate_weight, down_weight, planes):
    shard = up_weight.shape[0]
    part = down_weight.shape[0] // 2
    width = down_weight.shape[1]

    def body(half_ref, up_ref, gate_ref, down_ref, _, target):
        upper = half_ref[0] != 0
        for i, ref in enumerate((up_ref, gate_ref)):
            for core in range(2):
                rows = slice((2 * i + core) * shard, (2 * i + core + 1) * shard)
                for side in range(2):
                    for plane in range(planes):
                        begin = ((plane * 2 + side) * 2 + core) * 2 * part
                        place = (side * planes + plane) * part
                        target[rows, place : place + part] = jnp.where(
                            upper,
                            ref[:, begin + part : begin + 2 * part].astype(F32),
                            ref[:, begin : begin + part].astype(F32),
                        ).astype(BF)

        @pl.when(jnp.logical_not(upper))
        def _():
            target[pl.ds(4 * shard, part), :] = down_ref[pl.ds(0, part), :]

        @pl.when(upper)
        def _():
            target[pl.ds(4 * shard, part), :] = down_ref[pl.ds(part, part), :]

    return call(
        "lay_second",
        body,
        [like(4 * shard + part, width)],
        limit=56,
        scalars=[half],
        arrays=[up_weight, gate_weight, down_weight],
    )[0]


def split_hidden(half, totals, planes, part):
    shard, width = totals[0].shape
    run = planes // 2 * part

    def body(half_ref, *refs):
        for source, target in zip(refs[: len(totals)], refs[-len(totals) :]):
            for i in range(4):
                begin = 2 * i * run
                first, later = source[:, begin : begin + run], source[:, begin + run : begin + 2 * run]
                target[:, i * run : (i + 1) * run] = jnp.where(
                    half_ref[0] == 0, later.astype(F32), first.astype(F32)
                ).astype(BF)

    return call(
        "split_hidden",
        body,
        [like(shard, width // 2)] * len(totals),
        scalars=[half],
        arrays=totals,
    )


def merge_hidden(half, totals, others, planes, part, earlier):
    shard, width = totals[0].shape
    run = planes // 2 * part

    def body(half_ref, *refs):
        number = len(totals)
        upper = half_ref[0] != 0
        for own_ref, other_ref, target in zip(refs[:number], refs[number : 2 * number], refs[-number:]):
            for plane in range(planes // 2):
                for side in range(2):
                    for core in range(2):
                        i = core * 2 + side
                        begin = 2 * i * run + plane * part
                        own = jnp.where(
                            upper,
                            own_ref[:, begin + run : begin + run + part].astype(F32),
                            own_ref[:, begin : begin + part].astype(F32),
                        )
                        begin = i * run + plane * part
                        other = other_ref[:, begin : begin + part].astype(F32)
                        begin = ((plane * 2 + side) * 2 + core) * 2 * part
                        target[:, begin : begin + part] = jnp.where(upper, other, own)
                        target[:, begin + part : begin + 2 * part] = jnp.where(upper, own, other)

    return call(
        "merge_hidden",
        body,
        [like(shard, width, dtype=F32)] * len(totals),
        scalars=[half],
        arrays=[*totals, *others],
        earlier=earlier,
    )


class HiddenWeights:
    def __init__(self, gathered, planes, shard, part):
        width = gathered.shape[2]
        units = 2 * planes * part
        self.direct = shard % 16 == 0 and part % 16 == 0
        self.width, self.units, self.shard, self.part = width, units, shard, part
        if self.direct:
            self.arrays = [gathered.reshape(planes, 2, 2, -1, width)]
            self.matrix = (planes, 2, 2, shard, units)
            self.down = (planes, part, width)
        else:
            blocks = gathered[:, 4 * shard :].reshape(planes, 2, 2, part, width)
            self.arrays = [
                jnp.stack(
                    [gathered[:, i * shard : (i + 1) * shard].reshape(width, width) for i in range(4)]
                ),
                jnp.transpose(blocks, (2, 1, 0, 3, 4)).reshape(2, 2, planes * part, width),
            ]
            self.matrix = (width, units)
            self.down = (planes * part, width)

    def scratch(self):
        return [
            pltpu.VMEM((4,) + self.matrix, BF),
            pltpu.VMEM((2, 2) + self.down, BF),
            pltpu.SemaphoreType.DMA((8,)),
        ]

    def specs(self):
        return [pl.BlockSpec(memory_space=pltpu.HBM)] * len(self.arrays)

    def matrix_copy(self, sources, wide, sems, i):
        if self.direct:
            source = sources[0].at[:, :, :, pl.ds(i * self.shard, self.shard), :]
        else:
            source = sources[0].at[i]
        return pltpu.make_async_copy(source, wide.at[i], sems.at[i])

    def down_copy(self, sources, tall, sems, core, side):
        if self.direct:
            source = sources[0].at[:, side, core, pl.ds(4 * self.shard, self.part), :]
        else:
            source = sources[1].at[core, side]
        return pltpu.make_async_copy(source, tall.at[core, side], sems.at[4 + core * 2 + side])

    def matrix_value(self, wide, i, columns):
        if self.direct:
            return wide[i, :, :, :, :, columns].reshape(self.width, -1)
        return wide[i, :, columns]

    def matrix_rows(self, wide, i, j, parts):
        if self.direct:
            step = self.matrix[0] // parts
            return wide[i, pl.ds(j * step, step)].reshape(self.width // parts, -1)
        step = self.width // parts
        return wide[i, pl.ds(j * step, step)]

    def down_value(self, tall, core, side, columns):
        if self.direct:
            return tall[core, side, :, :, columns].reshape(-1, columns.size)
        return tall[core, side, :, columns]

    def down_rows(self, tall, core, side):
        return tall[core, side].reshape(-1, self.width)


def hidden_forward(first_low, weights, up_scale, gate_scale, own_rows):
    rows, width = first_low.shape
    units = weights.units
    block = units // 2
    step = 256

    def body(first_ref, up_scale_ref, gate_scale_ref, *refs):
        sources = refs[: len(weights.arrays)]
        hidden_ref, up_ref, gate_ref, partial_ref, turned_ref, wide, tall, sems = refs[
            len(weights.arrays) :
        ]
        copies = [weights.matrix_copy(sources, wide, sems, i) for i in (0, 2, 1, 3)]
        down_copies = [
            weights.down_copy(sources, tall, sems, i, j) for i in range(2) for j in range(2)
        ]
        for copy in copies + down_copies:
            copy.start()
        first = first_ref[...]
        for core in range(2):
            copies[2 * core].wait()
            copies[2 * core + 1].wait()

            for begin in range(0, units, step):
                columns = pl.ds(begin, step)
                here = pl.ds(core * units + begin, step)
                up = matmul(first, weights.matrix_value(wide, core, columns))
                gate = matmul(first, weights.matrix_value(wide, 2 + core, columns))
                up_ref[:, here] = up.astype(BF)
                gate_ref[:, here] = gate.astype(BF)
                hidden = swiglu(up, gate, up_scale_ref[:, here], gate_scale_ref[:, here])
                hidden_ref[core, :, columns] = hidden.astype(BF)
        for copy in down_copies:
            copy.wait()

        for begin in range(0, width, step):
            columns = pl.ds(begin, step)
            total = None
            for core in range(2):
                for side in range(2):
                    term = matmul(
                        hidden_ref[core, :, pl.ds(side * block, block)],
                        weights.down_value(tall, core, side, columns),
                    )
                    total = term if total is None else total + term
            partial_ref[:, columns] = total
            turned_ref[pl.ds(0, own_rows), columns] = total[own_rows:].astype(BF)
            turned_ref[pl.ds(own_rows, own_rows), columns] = total[:own_rows].astype(BF)

    whole = pl.BlockSpec(memory_space=pltpu.VMEM)
    return pl.pallas_call(
        body,
        out_shape=[
            jax.ShapeDtypeStruct((2, rows, units), BF),
            jax.ShapeDtypeStruct((rows, 2 * units), BF),
            jax.ShapeDtypeStruct((rows, 2 * units), BF),
            jax.ShapeDtypeStruct((rows, width), F32),
            jax.ShapeDtypeStruct((rows, width), BF),
        ],
        in_specs=[whole] * 3 + weights.specs(),
        out_specs=[whole] * 5,
        scratch_shapes=weights.scratch(),
        compiler_params=pltpu.CompilerParams(vmem_limit_bytes=56 * 2**20),
        cost_estimate=COST,
        name="hidden_forward",
    )(first_low, up_scale.reshape(1, -1), gate_scale.reshape(1, -1), *weights.arrays)


def hidden_backward(down_low, up_proj, gate_proj, weights, up_scale, gate_scale, earlier):
    rows = down_low.shape[0]
    units = weights.units
    block = units // 2

    def body(down_ref, up_ref, gate_ref, up_scale_ref, gate_scale_ref, sources, low_out, gate_low_out, up_grad_ref, gate_grad_ref, tall, sems, low_ref, gate_low_ref, out_sems):
        copies = [weights.down_copy(sources, tall, sems, i, j) for i in range(2) for j in range(2)]
        for copy in copies:
            copy.start()
        down = down_ref[...]
        out_copies = []
        for core in range(2):
            for side in range(2):
                copies[core * 2 + side].wait()
                here = pl.ds((core * 2 + side) * block, block)
                grad_hidden = back_matmul(down, weights.down_rows(tall, core, side))
                up_scaling = up_scale_ref[:, here]
                gate_scaling = gate_scale_ref[:, here]
                up = up_ref[:, here].astype(F32)
                gate = gate_ref[:, here].astype(F32)
                scaled = gate_scaling * gate
                sigmoid = jax.nn.sigmoid(scaled)
                silu = scaled * sigmoid
                grad_scaled_up = grad_hidden * silu
                grad_scaled = grad_hidden * (up_scaling * up) * (sigmoid + silu * (1.0 - sigmoid))
                low_ref[:, here] = (grad_scaled_up * up_scaling).astype(BF)
                gate_low_ref[:, here] = (grad_scaled * gate_scaling).astype(BF)
                up_grad_ref[:, here] = jnp.sum(grad_scaled_up * up, axis=0, keepdims=True)
                gate_grad_ref[:, here] = jnp.sum(grad_scaled * gate, axis=0, keepdims=True)
                i = 2 * (core * 2 + side)
                out_copies += [
                    pltpu.make_async_copy(low_ref.at[:, here], low_out.at[:, here], out_sems.at[i]),
                    pltpu.make_async_copy(gate_low_ref.at[:, here], gate_low_out.at[:, here], out_sems.at[i + 1]),
                ]
                for copy in out_copies[-2:]:
                    copy.start()
        for copy in out_copies:
            copy.wait()

    return call(
        "hidden_backward",
        body,
        [like(rows, 2 * units)] * 2 + [like(1, 2 * units, dtype=F32)] * 2,
        limit=30,
        arrays=[down_low, up_proj, gate_proj, up_scale, gate_scale],
        remote=weights.arrays,
        scratch=weights.scratch()[1:]
        + [pltpu.VMEM((rows, 2 * units), BF)] * 2
        + [pltpu.SemaphoreType.DMA((8,))],
        written=2,
        earlier=earlier,
    )


def first_partial(up_low, gate_low, weights, own_rows, earlier):
    rows = up_low.shape[0]
    units = weights.units
    width = weights.width

    def body(up_ref, gate_ref, sources, partial_ref, turned_ref, wide, sems):
        copies = [weights.matrix_copy(sources, wide, sems, i) for i in range(4)]
        for copy in copies:
            copy.start()
        pieces = 2
        piece = width // pieces
        for i in range(4):
            copies[i].wait()
            left = (up_ref, gate_ref)[i // 2][:, pl.ds((i % 2) * units, units)]
            for j in range(pieces):
                columns = pl.ds(j * piece, piece)
                term = back_matmul(left, weights.matrix_rows(wide, i, j, pieces))
                if i:
                    term = partial_ref[:, columns] + term
                partial_ref[:, columns] = term
        for j in range(pieces):
            columns = pl.ds(j * piece, piece)
            turn(turned_ref, own_rows, columns, partial_ref[:, columns])

    return call(
        "first_partial",
        body,
        [like(rows, width, dtype=F32), like(rows, width)],
        limit=30,
        arrays=[up_low, gate_low],
        remote=weights.arrays,
        scratch=[weights.scratch()[0], weights.scratch()[2]],
        earlier=earlier,
    )


def per_device(
    tokens,
    cotangent,
    lengths,
    placement,
    query_weight,
    key_weight,
    value_weight,
    out_weight,
    up_weight,
    gate_weight,
    down_weight,
    scoring,
    upscale,
    gatescale,
    attention_rate,
    feedforward_rate,
):
    size = lax.axis_size("fsdp")
    planes = size // 4
    half = lax.axis_index("grp")
    me = lax.axis_index("fsdp")
    core = me % 2
    side = (me // 2) % 2
    plane = me // 4
    half_scalar = half.reshape(1).astype(jnp.int32)
    which = jnp.stack([core, side]).astype(jnp.int32)
    local_seqs = tokens.shape[0] // size
    seq_len = tokens.shape[1] * size
    width = tokens.shape[2]
    own_rows = local_seqs * seq_len
    shard = query_weight.shape[0]
    hidden_shard = down_weight.shape[0]
    part = hidden_shard // 2
    per_row = hidden_shard // shard
    half_width = width // 2

    def swap_core(array):
        return lax.ppermute(array, "fsdp", [(i, i ^ 1) for i in range(size)])

    def swap_side(array):
        return lax.ppermute(array, "fsdp", [(i, i ^ 2) for i in range(size)])

    def next_plane(array):
        return lax.ppermute(array, "fsdp", [(i, (i + 4) % size) for i in range(size)])

    def swap_half(array):
        return lax.ppermute(array, "grp", [(0, 1), (1, 0)])

    def pick(array, index, axis):
        return lax.dynamic_index_in_dim(array, index, axis, keepdims=False)

    first_group = lay_first(
        half_scalar,
        query_weight,
        key_weight,
        value_weight,
        out_weight,
        [scoring, attention_rate, feedforward_rate, upscale, gatescale],
    )
    second_group = lay_second(half_scalar, up_weight, gate_weight, down_weight, planes)
    hidden_width = planes * 4 * part
    core_width = hidden_width // 2
    held = [first_group]
    crossed = []
    for i in range(planes):
        here = after(held[-1], *crossed[-1:]) if crossed else held[-1]
        if i < planes - 1:
            held.append(next_plane(here))
        crossed.append(swap_side(here))
    second_whole = lax.all_gather(
        after(second_group, *held[: GATE + 1], *crossed[:GATE]), "fsdp", axis=0
    )
    (both,) = call(
        "rows",
        place_pair,
        [like(2, *tokens.shape)],
        arrays=[tokens, cotangent],
        earlier=[held[-1], crossed[-2]],
        limit=56,
    )
    arrived = lax.all_to_all(both, "fsdp", split_axis=1, concat_axis=2, tiled=True)
    own_tokens = arrived[0].reshape(own_rows, width)
    other_tokens = swap_half(own_tokens)
    held = held + crossed
    held = held + [swap_core(array) for array in held]
    places = []
    for i in range(4 * planes):
        there_core = 1 - core if i >= 2 * planes else core
        there_side = 1 - side if i // planes % 2 else side
        places.append(((plane - i) % planes * 2 + there_side) * 2 + there_core)
    shards = Shards(held, jnp.stack(places).astype(jnp.int32))

    group_order = placement[0]
    own_slots = lax.dynamic_slice_in_dim(group_order, me * local_seqs, local_seqs)
    own_lengths = jnp.take(lengths[0], own_slots)
    valid = (jnp.arange(seq_len, dtype=jnp.int32)[None, :] < own_lengths[:, None]).reshape(
        own_rows, 1
    )
    own_cot = jnp.where(valid, arrived[1].reshape(own_rows, width), jnp.zeros((), BF))
    token_rows = jnp.concatenate([own_tokens, other_tokens])
    other_cot = swap_half(own_cot)

    qkv, query_unit, key_unit, value_low, mixed_half, mixed_turned, scale_float = attention_forward(
        half_scalar, token_rows, shards, seq_len
    )
    attention_mix = scale_float[1:2]
    feed_mix = scale_float[2:3]

    up_scale, gate_scale = hidden_scales(half_scalar, scale_float, per_row, planes, shard)
    skip = 3 * half_width + 128
    mixed_low, attended, first_state, first_low = first_forward(
        half_scalar, mixed_half, swap_half(mixed_turned), token_rows, attention_mix, shards, skip
    )

    feature = jnp.arange(width, dtype=jnp.int32)
    block = []
    for b in range(2):
        for a in range(2):
            for k in range(planes):
                there_core = core if b == 0 else 1 - core
                there_side = 1 - side if a == 0 else side
                block.append((k * 2 + there_side) * 2 + there_core)
    block = jnp.stack(block).astype(jnp.int32)
    wanted = (block[:, None] * shard + jnp.arange(shard, dtype=jnp.int32)[None, :]).reshape(-1)
    chooser = (feature[:, None] == wanted[None, :]).astype(BF)

    def share_columns(array):
        chosen = matmul(array, chooser).astype(BF)
        return chosen[:, :half_width], swap_core(chosen[:, half_width:])

    def share(array):
        return array, swap_core(array)

    def over_planes(total):
        return lax.psum_scatter(
            total.reshape(planes, total.shape[0] // planes, total.shape[1]),
            "fsdp",
            scatter_dimension=0,
            axis_index_groups=[[k * 4 + j for k in range(planes)] for j in range(4)],
        )

    def joined(kept, arrived_part):
        return (kept.astype(F32) + arrived_part.astype(F32)).astype(BF)

    token_sides = share_columns(token_rows)
    mixed_sides = share_columns(mixed_low)
    first_sides = share_columns(first_low)
    hidden_weights = HiddenWeights(
        after(second_whole, *token_sides, *mixed_sides, *first_sides, other_cot), planes, shard, part
    )
    hidden_low, up_proj, gate_proj, partial, partial_turned = hidden_forward(
        first_low, hidden_weights, up_scale, gate_scale, own_rows
    )
    hidden_other = swap_core(pick(hidden_low, 1 - core, 0))

    layer_own, grad_first, down_low, feed_grad = second_backward(
        partial,
        swap_half(partial_turned),
        first_state,
        own_cot,
        other_cot,
        valid.astype(F32),
        feed_mix,
    )
    down_other = swap_core(down_low)
    down_args = (which, hidden_low, hidden_other, down_low, down_other)
    down_both = down_grads(*down_args, [])
    down_sum = over_planes(down_both)
    up_low, gate_low, upscale_grad, gatescale_grad = hidden_backward(
        down_low, up_proj, gate_proj, hidden_weights, up_scale, gate_scale, [down_both]
    )
    up_other = swap_core(up_low)
    gate_other = swap_core(gate_low)
    up_side = [(up_low, up_other, None)]
    gate_side = [(gate_low, gate_other, None)]
    up_sent = side_grads("up_sent", [first_sides], up_side, False, [])
    up_arrived = swap_side(up_sent)
    partial, partial_turned = first_partial(up_low, gate_low, hidden_weights, own_rows, [up_sent])
    partial_other = swap_half(partial_turned)
    gate_sent = side_grads("gate_sent", [first_sides], gate_side, False, [partial])
    up_kept = side_grads("up_kept", [first_sides], up_side, True, [gate_sent])
    attended_cols, grad_mixed, grad_tokens, attention_grad = first_backward(
        half_scalar,
        grad_first,
        partial,
        partial_other,
        token_rows,
        attended,
        attention_mix,
        shards,
        skip,
        [up_kept],
    )
    gate_arrived = swap_side(after(gate_sent, up_arrived))
    attended_other = swap_core(after(attended_cols, up_arrived))
    up_joined = joined(up_kept, after(up_arrived, grad_mixed))
    up_total = over_planes(up_joined)
    qkv_low, scoring_grad, token_own, token_sent = attention_backward(
        half_scalar, grad_mixed, qkv, query_unit, key_unit, value_low, scale_float, shards, seq_len, [up_joined]
    )
    qkv_other = swap_core(qkv_low)
    token_other = swap_half(token_sent)
    last_args = (
        [mixed_sides, token_sides],
        [(attended_cols, attended_other, None), (qkv_low, qkv_other, (0, 1, 2))],
    )
    last_sent = side_grads("last_sent", *last_args, False, [down_sum])
    gate_kept = side_grads("gate_kept", [first_sides], gate_side, True, [last_sent])
    last_kept = side_grads("last_kept", *last_args, True, [gate_kept])
    last_arrived = swap_side(after(last_sent, gate_arrived))
    gate_joined = joined(gate_kept, after(gate_arrived, last_kept, token_other))
    gate_total = over_planes(gate_joined)
    def hidden_spread(grad):
        blocks = jnp.transpose(grad.reshape(2, 2, planes, part), (2, 1, 0, 3))
        blank = jnp.zeros_like(blocks)
        both_halves = jnp.where(
            half == 0, jnp.stack([blocks, blank], axis=3), jnp.stack([blank, blocks], axis=3)
        )
        return both_halves.reshape(size, hidden_shard)

    blank = jnp.zeros_like(scoring_grad)
    scoring_spread = jnp.where(
        half == 0,
        jnp.concatenate([scoring_grad, blank], axis=1),
        jnp.concatenate([blank, scoring_grad], axis=1),
    )
    small = jnp.concatenate(
        [
            scoring_spread.reshape(size, shard),
            attention_grad.reshape(size, shard),
            feed_grad.reshape(size, shard),
            hidden_spread(upscale_grad),
            hidden_spread(gatescale_grad),
        ],
        axis=1,
    )
    (up_part,) = split_hidden(half_scalar, [up_total], planes, part)
    up_swapped = swap_half(up_part)
    (outgoing,) = call(
        "outgoing",
        place_outgoing,
        [like(2, own_rows, width)],
        arrays=[layer_own, grad_tokens, token_own, token_other],
        earlier=[last_kept],
    )
    returned = lax.all_to_all(
        outgoing.reshape(2, local_seqs, seq_len, width), "fsdp", split_axis=2, concat_axis=1, tiled=True
    )
    (up_out,) = merge_hidden(half_scalar, [up_total], [up_swapped], planes, part, [])
    (small,) = call(
        "pass", place_whole, [like(*small.shape, dtype=F32)], arrays=[small], earlier=[returned]
    )
    last_joined = joined(last_kept, after(last_arrived, small))
    last_total = over_planes(last_joined).astype(F32)
    down_total = down_sum[:, width:].astype(F32) + swap_side(
        after(down_sum[:, :width], last_joined)
    ).astype(F32)
    down_cols = down_total.reshape(part, 2, half_width)
    mine = pick(down_cols, half, 1)
    theirs = swap_half(pick(down_cols, 1 - half, 1).astype(BF)).astype(F32)
    down_out = jnp.where(
        half == 0, jnp.concatenate([mine, theirs]), jnp.concatenate([theirs, mine])
    )
    small = lax.all_to_all(small, "fsdp", split_axis=0, concat_axis=0, tiled=True)
    (total,) = call("add", sum_whole, [like(1, small.shape[1], dtype=F32)], arrays=[small])
    total = total[0]
    total = total + swap_half(total)

    (gate_part,) = split_hidden(half_scalar, [gate_total], planes, part)
    (gate_out,) = merge_hidden(half_scalar, [gate_total], [swap_half(gate_part)], planes, part, [])
    out_total = last_total[:, :half_width]
    qkv_total = last_total[:, half_width:]

    return (
        returned[0],
        returned[1],
        qkv_total[:, :half_width],
        qkv_total[:, half_width : 2 * half_width],
        qkv_total[:, 2 * half_width :],
        out_total,
        up_out,
        gate_out,
        down_out,
        total[:shard],
        total[3 * shard : 3 * shard + hidden_shard],
        total[3 * shard + hidden_shard :],
        total[shard : 2 * shard],
        total[2 * shard : 3 * shard],
    )


def solution(mesh):
    rows = P("grp", "fsdp", None)
    group = P("grp", None)
    matrix = P("fsdp", None)
    vector = P("fsdp")
    split = P("fsdp", "grp")
    return jax.shard_map(
        per_device,
        mesh=mesh,
        in_specs=(rows, rows, group, group) + (matrix,) * 7 + (vector,) * 5,
        out_specs=(rows, rows) + (split,) * 7 + (vector,) * 5,
        check_vma=False,
    )
```
